128 devices in a mesh: dp: 128 (over y, x, z, core).
Axes of the slice: x: 4, y: 4, z: 4, core: 2. Of those that a mesh axis runs over, the one named last changes fastest.
Arguments:
- inputs: bfloat16 [4, 16384, 768], P(None, 'dp')
- cotangent: bfloat16 [4, 16384, 768], P(None, 'dp'), may hold values from -6 to 6
- joined: int32 [4, 128], P(None, 'dp'), may hold values 0 or 1
- half_lengths: int32 [4, 128, 2], P(None, 'dp'), may hold values from 32 to 64
- attention_master: float32 [4, 768, 768], P(None, 'dp')
- attention_first: float32 [4, 768, 768], P(None, 'dp'), may hold values from -0.00061035156 to 0.00061035156
- attention_second: float32 [4, 768, 768], P(None, 'dp'), may hold values from 1.4110135e-10 to 5.644054e-10
- hidden_master: float32 [2, 768, 3072], P(None, 'dp')
- hidden_first: float32 [2, 768, 3072], P(None, 'dp'), may hold values from -0.00061035156 to 0.00061035156
- hidden_second: float32 [2, 768, 3072], P(None, 'dp'), may hold values from 1.4110135e-10 to 5.644054e-10
- vector_master: float32 [12, 768], P(None, 'dp')
- vector_first: float32 [12, 768], P(None, 'dp'), may hold values from -0.00061035156 to 0.00061035156
- vector_second: float32 [12, 768], P(None, 'dp'), may hold values from 1.4110135e-10 to 5.644054e-10
Outputs:
- layer_output: bfloat16 [4, 16384, 768], P(None, 'dp')
- input_grad: float32 [4, 16384, 768], P(None, 'dp')
- grad_norm: float32 [], replicated
- attention_weights: float32 [4, 768, 768], P(None, 'dp')
- attention_means: float32 [4, 768, 768], P(None, 'dp')
- attention_squares: float32 [4, 768, 768], P(None, 'dp')
- hidden_weights: float32 [2, 768, 3072], P(None, 'dp')
- hidden_means: float32 [2, 768, 3072], P(None, 'dp')
- hidden_squares: float32 [2, 768, 3072], P(None, 'dp')
- vector_weights: float32 [12, 768], P(None, 'dp')
- vector_means: float32 [12, 768], P(None, 'dp')
- vector_squares: float32 [12, 768], P(None, 'dp')
The draws below stay inside these ranges and needn't reach their ends.
All inputs are finite; a program needn't handle non-finite values. No bound on the sum of `joined` on one device may be relied on, other than what follows from the above.
Results may differ from the reference program's by a relative error of at most 0.013.
Values may be sent and summed in bfloat16 or wider, within the bound.
A program may use at most 256 MiB of HBM per device.

```python
import math
import jax
import jax.numpy as jnp
from jax import lax

D = 768
FF = 3072
HEADS = 12
LEN = 128
MB = 4
STEP = 10
SEQS = 128
ROWS = 16384
PARAMS = 7087104


def rising(count, highest):
    return jnp.exp(jnp.linspace(0.0, math.log(highest), count)).astype(jnp.float32)


def draw_inputs(key, part):
    key = jax.random.fold_in(key, 11)
    normal_part = jax.random.normal(key, (MB, SEQS * LEN, D), jnp.float32)
    scales = rising(D, 1.7)
    return (normal_part * scales[None, None, :]).astype(jnp.bfloat16)


def draw_attention_master(key, part):
    key = jax.random.fold_in(key, 17)
    normal_part = jax.random.normal(key, (4, D, D), jnp.float32)
    factors = jnp.asarray([(4.0 * D) ** (-0.5), (4.0 * D) ** (-0.5), D ** (-0.5), max(D // 64, 1) ** (-0.5)], jnp.float32)
    return normal_part * factors[:, None, None]


def draw_hidden_master(key, part):
    key = jax.random.fold_in(key, 19)
    normal_part = jax.random.normal(key, (2, D, FF), jnp.float32)
    factors = jnp.asarray([D ** (-0.5), FF ** (-0.5)], jnp.float32)
    return normal_part * factors[:, None, None]


def draw_vector_master(key, part):
    key = jax.random.fold_in(key, 23)
    count_rows = 8 + FF // D
    normal_part = jax.random.normal(key, (count_rows, D), jnp.float32) * 0.3
    spread = jax.random.uniform(jax.random.fold_in(key, 1), (count_rows, D), jnp.float32, 0.8, 1.25)
    gain_rows = rising(D, 1.7)[None, :] * spread
    row_index = jnp.arange(count_rows)[:, None]
    return jnp.where((row_index == 3) | (row_index == 5), gain_rows, normal_part)


def touch_ends(result, key, smallest, high):
    dims = result.shape
    spot = [jax.random.randint(jax.random.fold_in(key, axis), (), 0, dims[axis]) for axis in range(len(dims))]
    result = result.at[tuple(spot)].set(smallest)
    longest = dims.index(max(dims))
    spot[longest] = (spot[longest] + 1) % dims[longest]
    return result.at[tuple(spot)].set(high)


def block_scale(own_key, shape, split, least, top_value):
    loudness, own = 1.0, jax.random.fold_in(own_key, 6)
    for position, blocks in split:
        steps = jnp.exp(jax.random.uniform(jax.random.fold_in(own, position), (blocks,), jnp.float32, least / len(split), top_value / len(split)))
        loudness = loudness * jnp.repeat(steps, shape[position] // blocks).reshape([-1 if axis == position else 1 for axis in range(len(shape))])
    return loudness


def gaussian(rng, dims, deviation, limit, shards=(), kind=jnp.bfloat16):
    values = deviation * jax.random.normal(rng, dims, jnp.float32)
    if shards:
        values = values * block_scale(rng, dims, shards, -0.22, 0.18)
    return jnp.clip(values, -limit, limit).astype(kind)


def setup_inputs(seed: int = 0) -> dict:
    key_list = jax.random.split(jax.random.key(seed), 14)
    inputs = draw_inputs(jax.random.fold_in(key_list[13], 71), 0)
    cotangent = gaussian(key_list[1], (MB, ROWS, D), 1.0, 6.0, ((1, 128),))
    joined = touch_ends((jax.random.randint(key_list[2], (MB, SEQS), 0, 2) < 1).astype(jnp.int32), jax.random.fold_in(key_list[2], 1), 0, 1)
    half_lengths = touch_ends(jax.random.randint(key_list[3], (MB, SEQS, 2), LEN // 4, LEN // 2 + 1), jax.random.fold_in(key_list[3], 1), LEN // 4, (LEN // 2 + 1) - 1).astype(jnp.int32)
    attention_master = draw_attention_master(jax.random.fold_in(key_list[13], 71), 0)
    attention_first = gaussian(key_list[5], (4, D, D), (0.11 / PARAMS ** 0.5), 0.00061035156, ((1, 128),), jnp.float32)
    attention_second = jnp.clip(jnp.exp(math.log(5.644054112963204e-10) - 1.3862944 * jax.random.uniform(key_list[6], (4, D, D), jnp.float32) ** block_scale(key_list[6], (4, D, D), ((1, 128),), -0.2, 0.2)), 1.411013528240801e-10, 5.644054112963204e-10)
    hidden_master = draw_hidden_master(jax.random.fold_in(key_list[13], 71), 0)
    hidden_first = gaussian(key_list[8], (2, D, FF), (0.11 / PARAMS ** 0.5), 0.00061035156, ((1, 128),), jnp.float32)
    hidden_second = jnp.clip(jnp.exp(math.log(5.644054112963204e-10) - 1.3862944 * jax.random.uniform(key_list[9], (2, D, FF), jnp.float32) ** block_scale(key_list[9], (2, D, FF), ((1, 128),), -0.2, 0.2)), 1.411013528240801e-10, 5.644054112963204e-10)
    vector_master = draw_vector_master(jax.random.fold_in(key_list[13], 71), 0)
    vector_first = gaussian(key_list[11], (8 + FF // D, D), (0.11 / PARAMS ** 0.5), 0.00061035156, ((1, 128),), jnp.float32)
    vector_second = jnp.clip(jnp.exp(math.log(5.644054112963204e-10) - 1.3862944 * jax.random.uniform(key_list[12], (8 + FF // D, D), jnp.float32) ** block_scale(key_list[12], (8 + FF // D, D), ((1, 128),), -0.2, 0.2)), 1.411013528240801e-10, 5.644054112963204e-10)
    return dict(inputs=inputs, cotangent=cotangent, joined=joined, half_lengths=half_lengths, attention_master=attention_master, attention_first=attention_first, attention_second=attention_second, hidden_master=hidden_master, hidden_first=hidden_first, hidden_second=hidden_second, vector_master=vector_master, vector_first=vector_first, vector_second=vector_second)


@jax.custom_vjp
def low(v):
    return lax.optimization_barrier(v.astype(jnp.bfloat16)).astype(jnp.float32)

@jax.custom_vjp
def low_back(v):
    return v

def low_keep(v):
    return (low(v), None)

def low_pass(kept, grad):
    return (grad,)

def back_keep(v):
    return (v, None)

def back_low(kept, grad):
    return (low(grad),)
low.defvjp(low_keep, low_pass)
low_back.defvjp(back_keep, back_low)
NORM_EPS = 1e-05
ADAM_EPS = 1e-08
BETA_ONE = 0.9
BETA_TWO = 0.999
CLIP_NORM = 1.0
WEIGHT_DECAY = 0.01
ATTENTION_RATES = (0.02, 0.02, 0.04, 0.3)
HIDDEN_RATES = (0.04, 0.02)
VECTOR_RATE = 0.5
MASKED = -1e+30
HIGH = lax.Precision.HIGHEST

def key_allowed(joined, half_lengths, length):
    places = jnp.arange(length, dtype=jnp.int32)
    middle = length // 2
    upper_half = (places >= middle).astype(jnp.int32)
    joined_col = joined[:, None]
    document = (1 - joined_col) * upper_half[None, :]
    lower_count = half_lengths[:, 0:1]
    upper_count = half_lengths[:, 1:2]
    within = jnp.where(upper_half[None, :] == 1, upper_count, lower_count)
    present = jnp.where(joined_col == 1, places[None, :] < middle + upper_count, places[None, :] - middle * upper_half[None, :] < within)
    return (document[:, :, None] == document[:, None, :]) & present[:, None, :]

def layer_norm(values, gain, shift):
    center = values - lax.optimization_barrier(jnp.mean(values, -1, keepdims=True))
    inverse = lax.rsqrt(lax.optimization_barrier(jnp.mean(center * center, -1, keepdims=True)) + NORM_EPS)
    return center * inverse * gain + shift

def attend(block):
    query_part, key_part, value_part, allowed = block
    scores = low_back(jnp.einsum('gqhe,gkhe->ghqk', query_part, key_part, precision=HIGH) * 0.125)
    scores = jnp.where(allowed[:, None], scores, MASKED)
    highest = lax.optimization_barrier(jnp.max(scores, -1, keepdims=True))
    exponent = jnp.exp(scores - highest)
    probabilities = exponent / lax.optimization_barrier(jnp.sum(exponent, -1, keepdims=True))
    return jnp.einsum('ghqk,gkhe->gqhe', low(probabilities), value_part, precision=HIGH)

def forward(attention_master, hidden_master, vector_master, tokens, allowed):
    attention = low(attention_master)
    hidden = low(hidden_master)
    vectors = low(vector_master)
    row_count, model_width = tokens.shape
    head_size = model_width // HEADS
    query_rows = low(low_back(jnp.dot(tokens, attention[0], precision=HIGH, preferred_element_type=jnp.float32) + vectors[0]))
    key_rows = low(low_back(jnp.dot(tokens, attention[1], precision=HIGH, preferred_element_type=jnp.float32)))
    value_rows = low(low_back(jnp.dot(tokens, attention[2], precision=HIGH, preferred_element_type=jnp.float32) + vectors[1]))
    group = math.gcd(SEQS, max(1, 4096 // LEN))
    shape_blocks = (SEQS // group, group, LEN, HEADS, head_size)
    context = lax.map(jax.checkpoint(attend), (query_rows.reshape(shape_blocks), key_rows.reshape(shape_blocks), value_rows.reshape(shape_blocks), allowed.reshape(SEQS // group, group, LEN, LEN)))
    context = low(low_back(context.reshape(row_count, model_width)))
    attended = low_back(jnp.dot(context, attention[3].T, precision=HIGH, preferred_element_type=jnp.float32) + vectors[2])
    first_out = layer_norm(tokens + attended, vectors[3], vectors[4])
    inner_pre = low_back(jnp.dot(low(first_out), hidden[0], precision=HIGH, preferred_element_type=jnp.float32) + vectors[8:].reshape(-1))
    activated = low(jax.nn.gelu(inner_pre, approximate=False))
    branch = low_back(jnp.dot(activated, hidden[1].T, precision=HIGH, preferred_element_type=jnp.float32) + vectors[7])
    return layer_norm(first_out + branch, vectors[5], vectors[6])

def adam_step(master, first, second, gradient, rates, decay):
    first_new = BETA_ONE * first + (1.0 - BETA_ONE) * gradient
    second_new = BETA_TWO * second + (1.0 - BETA_TWO) * gradient * gradient
    first_hat = first_new / (1.0 - BETA_ONE ** STEP)
    second_hat = second_new / (1.0 - BETA_TWO ** STEP)
    master_new = master - rates * (first_hat / (jnp.sqrt(second_hat) + ADAM_EPS) + decay * master)
    return (master_new, first_new, second_new)

def reference(inputs, cotangent, joined, half_lengths, attention_master, attention_first, attention_second, hidden_master, hidden_first, hidden_second, vector_master, vector_first, vector_second):
    summed = (jnp.zeros_like(attention_master), jnp.zeros_like(hidden_master), jnp.zeros_like(vector_master))
    outputs = []
    input_grads = []
    for batch_index in range(MB):
        allowed = key_allowed(joined[batch_index], half_lengths[batch_index], LEN)
        tokens = inputs[batch_index].astype(jnp.float32)

        def run(attention, hidden, vectors, rows_in):
            return forward(attention, hidden, vectors, rows_in, allowed)
        output, pull = jax.vjp(run, attention_master, hidden_master, vector_master, tokens)
        gradients = pull(cotangent[batch_index].astype(jnp.float32))
        summed = tuple((total + gradient for total, gradient in zip(summed, gradients[:3])))
        outputs.append(output.astype(jnp.bfloat16))
        input_grads.append(gradients[3])
    squares = sum((jnp.sum(gradient * gradient) for gradient in summed))
    grad_norm = jnp.sqrt(squares)
    factor = CLIP_NORM / jnp.maximum(grad_norm, CLIP_NORM)
    attention_new = adam_step(attention_master, attention_first, attention_second, summed[0] * factor, jnp.asarray(ATTENTION_RATES)[:, None, None], WEIGHT_DECAY)
    hidden_new = adam_step(hidden_master, hidden_first, hidden_second, summed[1] * factor, jnp.asarray(HIDDEN_RATES)[:, None, None], WEIGHT_DECAY)
    vector_new = adam_step(vector_master, vector_first, vector_second, summed[2] * factor, VECTOR_RATE, 0.0)
    return (jnp.stack(outputs), jnp.stack(input_grads), grad_norm, attention_new[0], attention_new[1], attention_new[2], hidden_new[0], hidden_new[1], hidden_new[2], vector_new[0], vector_new[1], vector_new[2])
```

```python
import functools
import jax
import jax.numpy as jnp
import numpy as np
from jax import lax
from jax.experimental import pallas as pl
from jax.experimental.pallas import tpu as pltpu
from jax.sharding import PartitionSpec as P

F32 = jnp.float32
BF16 = jnp.bfloat16
D = 768
FF = 3072
ROWS = 512
SLOTS = 4
LEN = 128
PAIRS = 6
TILE = 256
NORM_EPS = 1e-05
MASKED = -1e30
NN = (((1,), (0,)), ((), ()))
NT = (((1,), (1,)), ((), ()))
TN = (((0,), (0,)), ((), ()))
PLACE_Q, PLACE_K, PLACE_V, PLACE_O = 0, 2, 6, 8
PLACE_UP = (1, 3, 7, 9)
PLACE_DOWN = (4, 5, 10, 11)
V_BQ, V_BV, V_BO, V_G1, V_C1, V_G2, V_C2, V_B2, V_B1 = range(9)


def dot(a, b, dims=NN):
    return lax.dot_general(a, b, dims, preferred_element_type=F32)


def block(ref, place):
    return ref[place].reshape(D, D)


def columns(ref, place, start, size):
    return ref[place, :, :, :, pl.ds(start, size)].reshape(D, size)


def put_columns(ref, place, start, size, value):
    ref[place, :, :, :, pl.ds(start, size)] = value.reshape(4, 4, 48, size)


def loop(count, body):
    lax.fori_loop(0, count, lambda i, c: (body(i), c)[1], 0)


def at(i, size):
    return pl.ds(pl.multiple_of(i * size, size), size)


def qkv(W, V, xb, q, k, v):
    def tile(n):
        cols = at(n, TILE)
        x = xb[...]
        q[:, cols] = ((dot(x, columns(W, PLACE_Q, cols.start, TILE)) + V[V_BQ, cols]).astype(BF16) * 0.125).astype(BF16)
        k[:, cols] = dot(x, columns(W, PLACE_K, cols.start, TILE)).astype(BF16)
        v[:, cols] = (dot(x, columns(W, PLACE_V, cols.start, TILE)) + V[V_BV, cols]).astype(BF16)

    loop(D // TILE, tile)


def halves(value):
    lane = lax.broadcasted_iota(jnp.int32, value.shape, 1)
    zero = jnp.zeros_like(value)
    return jnp.concatenate([jnp.where(lane < 64, value, zero), jnp.where(lane < 64, zero, value)], 0)


def joined_halves(value):
    lane = lax.broadcasted_iota(jnp.int32, (LEN, LEN), 1)
    return jnp.where(lane < 64, value[:LEN], value[LEN:])


def fill_masks(joined, half_lengths, bias):
    query = lax.broadcasted_iota(jnp.int32, (LEN, LEN), 0)
    key = lax.broadcasted_iota(jnp.int32, (LEN, LEN), 1)
    for slot in range(SLOTS):
        is_joined = joined[slot, 0]
        low = half_lengths[slot, 0, 0]
        high = half_lengths[slot, 0, 1]
        upper = (key >= 64).astype(jnp.int32)
        limit = is_joined * (64 + high) + (1 - is_joined) * (upper * (64 + high) + (1 - upper) * low)
        apart = (1 - is_joined) * jnp.abs((query >= 64).astype(jnp.int32) - upper)
        bias[slot] = jnp.where((key < limit) & (apart == 0), 0.0, MASKED)


def attend(q, k, v, bias, p, ctx):
    def unit(i):
        slot = i // PAIRS
        pair = i - slot * PAIRS
        rows, cols = at(slot, LEN), at(pair, LEN)
        s = dot(halves(q[rows, cols]), k[rows, cols], NT)
        m = bias[slot]
        s = jnp.where(jnp.concatenate([m, m], 0) < 0, MASKED, s)
        e = jnp.exp(s - jnp.max(s, -1, keepdims=True))
        low = (e * (1.0 / jnp.sum(e, -1, keepdims=True))).astype(BF16)
        p[i] = low
        ctx[rows, cols] = joined_halves(dot(low, v[rows, cols])).astype(BF16)

    loop(SLOTS * PAIRS, unit)


def attend_back(q, k, v, p, dctx):
    def unit(i):
        slot = i // PAIRS
        pair = i - slot * PAIRS
        rows, cols = at(slot, LEN), at(pair, LEN)
        low = p[i]
        two = halves(dctx[rows, cols])
        q2 = halves(q[rows, cols])
        dp = dot(two, v[rows, cols], NT)
        dv = dot(low, two, TN)
        full = low.astype(F32)
        ds = (full * (dp - jnp.sum(dp * full, -1, keepdims=True))).astype(BF16)
        dq = joined_halves(dot(ds, k[rows, cols])) * 0.125
        dk = dot(ds, q2, TN)
        v[rows, cols] = dv.astype(BF16)
        q[rows, cols] = dq.astype(BF16)
        k[rows, cols] = dk.astype(BF16)

    loop(SLOTS * PAIRS, unit)


STRIP = 64


def first_norm(W, V, xb, ctx, A, inv1, F, y1b):
    def tile(i):
        rows = at(i, TILE)
        A[rows, :] = dot(ctx[rows, :], block(W, PLACE_O), NT)

    loop(ROWS // TILE, tile)

    def strip(i):
        rows = at(i, STRIP)
        a = xb[rows, :].astype(F32) + A[rows, :] + V[V_BO : V_BO + 1, :]
        center = a - jnp.mean(a, -1, keepdims=True)
        inverse = lax.rsqrt(jnp.mean(center * center, -1, keepdims=True) + NORM_EPS)
        n = center * inverse
        A[rows, :] = n
        inv1[rows, :] = inverse
        y = n * V[V_G1 : V_G1 + 1, :] + V[V_C1 : V_C1 + 1, :]
        y1b[rows, :] = y.astype(BF16)
        F[rows, :] = y + V[V_B2 : V_B2 + 1, :]

    loop(ROWS // STRIP, strip)


def gelu_parts(u):
    x = jnp.abs(u) * 0.7071067811865476
    e = jnp.exp(-0.5 * u * u)
    t = 1.0 / (1.0 + 0.3275911 * x)
    poly = ((((1.061405429 * t - 1.453152027) * t + 1.421413741) * t - 0.284496736) * t + 0.254829592) * t
    tail = 0.5 * poly * e
    cdf = jnp.where(u >= 0, 1.0 - tail, tail)
    return u * cdf, cdf + u * e * 0.3989422804014327


def up(W, V, y1b, h, gp, part):
    def one(place, j):
        def half(i):
            rows = at(i, TILE)
            start = j * D + part * TILE
            cols = pl.ds(start, TILE)
            u = dot(y1b[rows, :], columns(W, place, part * TILE, TILE)) + V[V_B1 + j : V_B1 + j + 1, pl.ds(part * TILE, TILE)]
            value, slope = gelu_parts(u)
            h[rows, cols] = value.astype(BF16)
            gp[rows, cols] = slope.astype(BF16)
        loop(ROWS // TILE, half)

    for j, place in enumerate(PLACE_UP):
        one(place, j)


def down(W, h, FP, part):
    def half(i):
        rows = at(i, TILE)
        acc = None
        for j, place in enumerate(PLACE_DOWN):
            term = dot(h[rows, pl.ds(j * D + part * TILE, TILE)], columns(W, place, part * TILE, TILE), NT)
            acc = term if acc is None else acc + term
        FP[rows, :] = acc if part == 0 else FP[rows, :] + acc

    loop(ROWS // TILE, half)


def second_norm(V, perm, FP, F, gb, outb, dfb, sums):
    def tile(i):
        rows = at(i, TILE)
        F[rows, :] += dot(FP[rows, :].astype(BF16), perm[...])

    loop(ROWS // TILE, tile)

    def strip(i, carry):
        dg, dc, db = carry
        rows = at(i, STRIP)
        z = F[rows, :]
        center = z - jnp.mean(z, -1, keepdims=True)
        inverse = lax.rsqrt(jnp.mean(center * center, -1, keepdims=True) + NORM_EPS)
        n = center * inverse
        gain = V[V_G2 : V_G2 + 1, :]
        g = gb[rows, :].astype(F32)
        outb[rows, :] = (n * gain + V[V_C2 : V_C2 + 1, :]).astype(BF16)
        gn = g * n
        e = g * gain
        dz = inverse * (e - jnp.mean(e, -1, keepdims=True) - n * jnp.mean(gn * gain, -1, keepdims=True))
        low = dz.astype(BF16)
        F[rows, :] = dz
        dfb[rows, :] = low
        return (
            dg + jnp.sum(gn, 0, keepdims=True),
            dc + jnp.sum(g, 0, keepdims=True),
            db + jnp.sum(low.astype(F32), 0, keepdims=True),
        )

    zero = jnp.zeros((1, D), F32)
    dg, dc, db = lax.fori_loop(0, ROWS // STRIP, strip, (zero, zero, zero))
    sums[V_G2 : V_G2 + 1, :] = dg
    sums[V_C2 : V_C2 + 1, :] = dc
    sums[V_B2 : V_B2 + 1, :] = db


def turn(source, target):
    for i in range(ROWS // LEN):
        target[:, i * LEN : (i + 1) * LEN] = source[i * LEN : (i + 1) * LEN, :].T


def first_back(W, V, A, inv1, gp, F, dob, sums):
    def tile(i):
        rows = at(i, TILE)
        acc = F[rows, :]
        for j, place in enumerate(PLACE_UP):
            acc = acc + dot(gp[rows, j * D : (j + 1) * D], block(W, place), NT)
        F[rows, :] = acc

    loop(ROWS // TILE, tile)

    def strip(i, carry):
        dg, dc, db = carry
        rows = at(i, STRIP)
        dy = F[rows, :]
        n = A[rows, :]
        gain = V[V_G1 : V_G1 + 1, :]
        dyn = dy * n
        e = dy * gain
        da = inv1[rows, :] * (e - jnp.mean(e, -1, keepdims=True) - n * jnp.mean(dyn * gain, -1, keepdims=True))
        low = da.astype(BF16)
        F[rows, :] = da
        dob[rows, :] = low
        return (
            dg + jnp.sum(dyn, 0, keepdims=True),
            dc + jnp.sum(dy, 0, keepdims=True),
            db + jnp.sum(low.astype(F32), 0, keepdims=True),
        )

    zero = jnp.zeros((1, D), F32)
    dg, dc, db = lax.fori_loop(0, ROWS // STRIP, strip, (zero, zero, zero))
    sums[V_G1 : V_G1 + 1, :] = dg
    sums[V_C1 : V_C1 + 1, :] = dc
    sums[V_BO : V_BO + 1, :] = db


def output_back(W, dob, dctx):
    def tile(n):
        cols = at(n, TILE)
        dctx[:, cols] = dot(dob[...], columns(W, PLACE_O, cols.start, TILE)).astype(BF16)

    loop(D // TILE, tile)


def column_sums(source, sums, row):
    sums[row : row + 1, :] = jnp.sum(source[...].astype(F32), 0, keepdims=True)


def input_back(W, q, k, v, F):
    def tile(i):
        rows = at(i, TILE)
        F[rows, :] = (
            F[rows, :]
            + dot(q[rows, :], block(W, PLACE_Q), NT)
            + dot(k[rows, :], block(W, PLACE_K), NT)
            + dot(v[rows, :], block(W, PLACE_V), NT)
        )

    loop(ROWS // TILE, tile)


def to_down_order(dfb, perm, dfp):
    def tile(i):
        rows = at(i, TILE)
        dfp[rows, :] = dot(dfb[rows, :], perm[...], NT).astype(BF16)

    loop(ROWS // TILE, tile)


def permutation():
    r = np.arange(D)
    y, x, z, j = r // 192, r // 48 % 4, r // 12 % 4, r % 12
    p = np.zeros((D, D), np.float32)
    p[192 * z + 48 * y + 12 * x + j, r] = 1
    return p


MESH = pl.DeviceIdType.MESH
STEP = 10
ADAM_EPS = 1e-08
BETA_ONE = 0.9
BETA_TWO = 0.999
CLIP_NORM = 1.0
WEIGHT_DECAY = 0.01
ATTENTION_RATES = (0.02, 0.02, 0.04, 0.3)
HIDDEN_RATES = (0.04, 0.02)
VECTOR_RATE = 0.5
COPIES = 256
VECTORS = 12
SHARE = 6


class Net:
    def __init__(self, send_sem, recv_sem):
        self.send_sem, self.recv_sem, self.count, self.open = send_sem, recv_sem, 0, []

    def send(self, source, target, device):
        assert self.count < COPIES
        copy = pltpu.make_async_remote_copy(
            src_ref=source,
            dst_ref=target,
            send_sem=self.send_sem.at[self.count],
            recv_sem=self.recv_sem.at[self.count],
            device_id=(device,),
            device_id_type=MESH,
        )
        self.count += 1
        copy.start()
        self.open.append(copy)
        return copy

    def sent(self, copy):
        copy.wait_send()
        self.open = [one for one in self.open if one is not copy]

    def close(self):
        for copy in self.open:
            copy.wait_send()
        self.open = []


def adam(master, first, second, gradient, rate, decay):
    first_new = BETA_ONE * first + (1.0 - BETA_ONE) * gradient
    second_new = BETA_TWO * second + (1.0 - BETA_TWO) * gradient * gradient
    first_hat = first_new / (1.0 - BETA_ONE**STEP)
    second_hat = second_new / (1.0 - BETA_TWO**STEP)
    master_new = master - rate * (first_hat / (jnp.sqrt(second_hat) + ADAM_EPS) + decay * master)
    return master_new, first_new, second_new


SCRATCH = dict(
    W=pltpu.VMEM((12, 4, 4, 48, D), BF16),
    G=pltpu.VMEM((SHARE, 4, 4, 48, D), BF16),
    pair_in=pltpu.VMEM((SHARE, 4, 4, 48, D), BF16),
    pair_out=pltpu.VMEM((2, 2, 4, 4, 48, TILE), BF16),
    half_in=pltpu.VMEM((SHARE, 2, 2, 48, D), BF16),
    block_in=pltpu.VMEM((SHARE, 2, 4, 48, D), BF16),
    strip_in=pltpu.VMEM((SHARE, 3, 48, D), BF16),
    piece_in=pltpu.VMEM((3, SHARE, 16, D), BF16),
    first_out=pltpu.VMEM((SHARE, 8, D), F32),
    first_own=pltpu.VMEM((SHARE, 8, D), F32),
    first_in=pltpu.VMEM((SHARE, 8, D), F32),
    vec_own=pltpu.VMEM((8, LEN), F32),
    vec_in=pltpu.VMEM((8, LEN), F32),
    pieces=pltpu.VMEM((4, SHARE, 16, D), BF16),
    vec_pieces=pltpu.VMEM((4, 16, LEN), BF16),
    VT=pltpu.VMEM((4, 4, 48, LEN), BF16),
    line=pltpu.VMEM((48, D), F32),
    square=pltpu.VMEM((LEN, LEN), F32),
    turned_sums=pltpu.VMEM((D + 8, LEN), F32),
    sums_in=pltpu.VMEM((4, 3, 16, D), F32),
    sums_out=pltpu.VMEM((4, 16, D), F32),
    norm_out=pltpu.VMEM((4, 8, LEN), F32),
    norm_in=pltpu.VMEM((4, 3, 8, LEN), F32),
    V=pltpu.VMEM((16, D), F32),
    sums=pltpu.VMEM((16, D), F32),
    bias=pltpu.VMEM((SLOTS, LEN, LEN), F32),
    act=pltpu.VMEM((4, ROWS, D), BF16),
    p=pltpu.VMEM((SLOTS * PAIRS, 2 * LEN, LEN), BF16),
    A=pltpu.VMEM((ROWS, D), F32),
    F=pltpu.VMEM((ROWS, D), F32),
    FP=pltpu.VMEM((ROWS, D), F32),
    inv1=pltpu.VMEM((ROWS, 1), F32),
    y1b=pltpu.VMEM((ROWS, D), BF16),
    turned=pltpu.VMEM((2, D, ROWS), BF16),
    h=pltpu.VMEM((ROWS, FF), BF16),
    gp=pltpu.VMEM((ROWS, FF), BF16),
    dfb=pltpu.VMEM((ROWS, D), BF16),
    dfp=pltpu.VMEM((ROWS, D), BF16),
    xb=pltpu.VMEM((ROWS, D), BF16),
    gb=pltpu.VMEM((ROWS, D), BF16),
    perm=pltpu.VMEM((D, D), BF16),
    load_sem=pltpu.SemaphoreType.DMA((16,)),
    store_sem=pltpu.SemaphoreType.DMA((16,)),
    send_sem=pltpu.SemaphoreType.DMA((COPIES,)),
    recv_sem=pltpu.SemaphoreType.DMA((COPIES,)),
)
NAMES = tuple(SCRATCH)


def step_kernel(
    x_hbm,
    g_hbm,
    perm_hbm,
    joined,
    half_lengths,
    att_w,
    hid_w,
    vec_w,
    att_m,
    att_v,
    hid_m,
    hid_v,
    vec_m,
    vec_v,
    out_hbm,
    grad_hbm,
    norm_out_ref,
    att_w_new,
    att_m_new,
    att_v_new,
    hid_w_new,
    hid_m_new,
    hid_v_new,
    vec_w_new,
    vec_m_new,
    vec_v_new,
    *scratch,
):
    s = dict(zip(NAMES, scratch))
    W, G, V = s["W"], s["G"], s["V"]
    xb, gb, perm = s["xb"], s["gb"], s["perm"]
    net = Net(s["send_sem"], s["recv_sem"])

    me = lax.axis_index("dp")
    c = lax.rem(me, 2)
    z = lax.rem(lax.div(me, 2), 4)
    x = lax.rem(lax.div(me, 8), 4)
    y = lax.div(me, 32)
    other = 1 - c

    def wrap(value):
        return lax.rem(value + 4, 4)

    def peer(axis, step):
        moved = {"x": x, "y": y, "z": z}
        moved[axis] = wrap(moved[axis] + step)
        return ((moved["y"] * 4 + moved["x"]) * 4 + moved["z"]) * 2 + c

    sibling = me + 1 - 2 * c

    loads = []
    for i in range(SLOTS):
        loads.append(pltpu.make_async_copy(x_hbm.at[i], xb.at[pl.ds(i * LEN, LEN)], s["load_sem"].at[i]))
        loads.append(pltpu.make_async_copy(g_hbm.at[i], gb.at[pl.ds(i * LEN, LEN)], s["load_sem"].at[4 + i]))
    loads.append(pltpu.make_async_copy(perm_hbm, perm, s["load_sem"].at[8]))
    for copy in loads:
        copy.start()

    barrier = pltpu.get_barrier_semaphore()
    partners = [sibling] + [peer(axis, step) for axis in "xyz" for step in (1, 2, 3)]
    for partner in partners:
        pl.semaphore_signal(barrier, inc=1, device_id=(partner,), device_id_type=MESH)
    pl.semaphore_wait(barrier, len(partners))

    def master_part(core, l):
        if l in (0, 2):
            return att_w[2 * core + l // 2]
        if l in (1, 3):
            return hid_w[0, :, pl.ds(pl.multiple_of((2 * core + l // 2) * D, LEN), D)]
        return hid_w[1, :, pl.ds(pl.multiple_of((2 * core + l - 4) * D, LEN), D)]

    for l in range(SHARE):
        s["first_own"][l, 0:6, :] = master_part(c, l)
        s["first_out"][l, 0:6, :] = master_part(other, l)
    s["square"][...] = jnp.zeros((LEN, LEN), F32)
    s["square"][0:VECTORS, 0:6] = vec_w[...]
    s["vec_own"][...] = s["square"][...].T[0:8]
    pair = net.send(s["first_out"], s["first_in"], sibling)
    pair_vec = net.send(s["vec_own"], s["vec_in"], sibling)
    pair.wait_recv()
    pair_vec.wait_recv()

    line = s["line"]
    pieces, vec_pieces = s["pieces"], s["vec_pieces"]
    line[0:16, :] = jnp.zeros((16, D), F32)
    for l in range(SHARE):
        own, far = s["first_own"][l, 0:6], s["first_in"][l, 0:6]
        line[0:6, :] = jnp.where(c == 0, own, far)
        line[6:12, :] = jnp.where(c == 0, far, own)
        pieces[z if l < 4 else x, l] = line[0:16, :].astype(BF16)
    own, far = s["vec_own"][0:6], s["vec_in"][0:6]
    line[0:6, 0:LEN] = jnp.where(c == 0, own, far)
    line[6:12, 0:LEN] = jnp.where(c == 0, far, own)
    vec_pieces[z] = line[0:16, 0:LEN].astype(BF16)

    arriving = []
    for step in (1, 2, 3):
        near = pieces.at[z, pl.ds(0, 4)]
        arriving.append(net.send(near, near, peer("z", step)))
        near = vec_pieces.at[z]
        arriving.append(net.send(near, near, peer("z", step)))
        near = pieces.at[x, pl.ds(4, 2)]
        arriving.append(net.send(near, near, peer("x", step)))
    for copy in arriving:
        copy.wait_recv()
    early = [pair, pair_vec] + arriving

    VT = s["VT"]

    def spread(l):
        for i in range(4):
            line[12 * i : 12 * i + 12, :] = pieces[i, l].astype(F32)[0:12]
        first, second = (y, x) if l < 4 else (z, y)
        W[6 * c + l, first, second] = line[...].astype(BF16)

    def strips(l):
        m = 6 * c + l
        first, second = (y, x) if l < 4 else (z, y)
        near = W.at[m, first, second]
        return [net.send(near, near, peer("x" if l in (2, 3) else "y", step)) for step in (1, 2, 3)]

    for i in range(4):
        line[12 * i : 12 * i + 12, 0:LEN] = vec_pieces[i].astype(F32)[0:12]
    VT[y, x] = line[:, 0:LEN].astype(BF16)
    near = VT.at[y, x]
    vec_strips = [net.send(near, near, peer("x", step)) for step in (1, 2, 3)]
    strip_copies = {}
    for l in (0, 2, 4, 5, 1, 3):
        spread(l)
        strip_copies[l] = strips(l)

    def strips_in(l):
        for copy in strip_copies[l]:
            copy.wait_recv()

    def region(ref, l, m, index, half, cols):
        part = pl.ds(0, 4) if half is None else pl.ds(2 * half, 2)
        if l < 2:
            return ref.at[m, part, index, :, cols]
        return ref.at[m, index, part, :, cols]

    def axis_of(l):
        return "x" if l < 2 else "y" if l < 4 else "z"

    def position(l):
        return x if l < 2 else y if l < 4 else z

    def gather_start(l, cols):
        m = 6 * c + l
        near = region(W, l, m, position(l), None, cols)
        up = net.send(near, near, peer(axis_of(l), 1))
        down = net.send(near, near, peer(axis_of(l), 3))
        return l, cols, up, down

    def gather_pass(state):
        l, cols, up, down = state
        m = 6 * c + l
        up.wait_recv()
        low = region(W, l, m, wrap(position(l) - 1), 0, cols)
        up = net.send(low, low, peer(axis_of(l), 1))
        down.wait_recv()
        high = region(W, l, m, wrap(position(l) + 1), 1, cols)
        down = net.send(high, high, peer(axis_of(l), 3))
        return l, cols, up, down

    def gather_share(state):
        l, cols, up, down = state
        up.wait_recv()
        down.wait_recv()
        whole = W.at[6 * c + l, :, :, :, cols]
        return net.send(whole, whole, sibling)

    def vec_start():
        near = VT.at[y]
        return net.send(near, near, peer("y", 1)), net.send(near, near, peer("y", 3))

    def vec_pass(state):
        up, down = state
        up.wait_recv()
        low = VT.at[wrap(y - 1), pl.ds(0, 2)]
        up = net.send(low, low, peer("y", 1))
        down.wait_recv()
        high = VT.at[wrap(y + 1), pl.ds(2, 2)]
        down = net.send(high, high, peer("y", 3))
        return up, down

    every = pl.ds(0, D)
    part_cols = [pl.ds(part * TILE, TILE) for part in range(3)]
    for copy in vec_strips:
        copy.wait_recv()
    vec_state = vec_start()
    first = []
    for l in (0, 2):
        strips_in(l)
        first.append(gather_start(l, every))
    strips_in(4)
    strips_in(5)
    later = [[], [], []]
    for l in (4, 5):
        later[0].append(gather_start(l, part_cols[0]))
    strips_in(1)
    strips_in(3)

    fill_masks(joined, half_lengths, s["bias"])
    for copy in loads:
        copy.wait()

    vec_state = vec_pass(vec_state)
    first = [gather_pass(state) for state in first]
    for l in (1, 3):
        later[0].append(gather_start(l, part_cols[0]))
    later[0][:2] = [gather_pass(state) for state in later[0][:2]]
    for l in (4, 5):
        later[1].append(gather_start(l, part_cols[1]))
    for copy in vec_state:
        copy.wait_recv()
    first = [gather_share(state) for state in first]
    vectors = VT[...].reshape(D, LEN).astype(F32)
    V[...] = vectors.T[0:16]
    later[0][2:] = [gather_pass(state) for state in later[0][2:]]
    for l in (1, 3):
        later[1].append(gather_start(l, part_cols[1]))
    for copy in first:
        copy.wait_recv()

    act, p = s["act"], s["p"]
    q, k, v, ctx = (act.at[i] for i in range(4))
    A, F, FP, inv1, y1b = s["A"], s["F"], s["FP"], s["inv1"], s["y1b"]
    h, gp, dfb, dfp, sums = s["h"], s["gp"], s["dfb"], s["dfp"], s["sums"]
    turned = s["turned"]

    qkv(W, V, xb, q, k, v)
    later[0] = [gather_share(state) for state in later[0]]
    later[1] = [gather_pass(state) for state in later[1]]
    for l in (4, 5, 1, 3):
        later[2].append(gather_start(l, part_cols[2]))
    attend(q, k, v, s["bias"], p, ctx)
    later[1] = [gather_share(state) for state in later[1]]
    later[2] = [gather_pass(state) for state in later[2]]
    first_norm(W, V, xb, ctx, A, inv1, F, y1b)
    for part in range(3):
        if part == 1:
            later[2] = [gather_share(state) for state in later[2]]
        for copy in later[part]:
            copy.wait_recv()
        up(W, V, y1b, h, gp, part)
        down(W, h, FP, part)
    second_norm(V, perm, FP, F, gb, gb, dfb, sums)
    stores = []
    for i in range(SLOTS):
        stores.append(pltpu.make_async_copy(gb.at[pl.ds(i * LEN, LEN)], out_hbm.at[i], s["store_sem"].at[i]))
        stores[-1].start()
    to_down_order(dfb, perm, dfp)
    turn(dfp, turned.at[0])
    turn(y1b, turned.at[1])

    pair_in, pair_out = s["pair_in"], s["pair_out"]

    def hidden_grad(core, e, part, finish):
        j = 2 * core + e
        at_h = pl.ds(pl.multiple_of(j * D + part * TILE, LEN), TILE)
        finish(4 + e, dot(turned[0], h[:, at_h]))
        finish(1 + 2 * e, dot(turned[1], gp[:, at_h]))

    def hidden_slope(core, e, part):
        j = 2 * core + e
        at_h = pl.ds(pl.multiple_of(j * D + part * TILE, LEN), TILE)
        place = 6 * core + 4 + e

        def half(i, total):
            rows = at(i, TILE)
            dh = dot(dfp[rows, :], columns(W, place, part * TILE, TILE))
            du = (dh * gp[rows, at_h].astype(F32)).astype(BF16)
            gp[rows, at_h] = du
            return total + jnp.sum(du.astype(F32), 0, keepdims=True)

        total = lax.fori_loop(0, ROWS // TILE, half, jnp.zeros((1, TILE), F32))
        sums[pl.ds(V_B1 + j, 1), pl.ds(part * TILE, TILE)] = total

    def share_of(slot, which, l, cols):
        return net.send(pair_out.at[slot, which], pair_in.at[l, :, :, :, cols], sibling)

    G_half, G_block = s["half_in"], s["block_in"]

    def reduce_start(l, cols):
        lo = region(G, l, l, wrap(position(l) + 2), 0, cols)
        hi = region(G, l, l, wrap(position(l) + 2), 1, cols)
        return (
            l,
            cols,
            net.send(lo, G_half.at[l, 0, :, :, cols], peer(axis_of(l), 1)),
            net.send(hi, G_half.at[l, 1, :, :, cols], peer(axis_of(l), 3)),
        )

    def add_into(ref, index, *others):
        total = ref[index].astype(F32)
        for other_ref, other_index in others:
            total = total + other_ref[other_index].astype(F32)
        ref[index] = total.astype(BF16)

    def cell(l, index, i, cols):
        return (l, i, index, slice(None), cols) if l < 2 else (l, index, i, slice(None), cols)

    def reduce_pass(state):
        l, cols, up, down = state
        axis, here = axis_of(l), position(l)
        up.wait_recv()
        for i in range(2):
            add_into(G, cell(l, wrap(here + 1), i, cols), (G_half, (l, 0, i, slice(None), cols)))
        up = net.send(region(G, l, l, wrap(here + 1), None, cols), G_block.at[l, 0, :, :, cols], peer(axis, 1))
        down.wait_recv()
        for i in range(2):
            add_into(G, cell(l, wrap(here - 1), 2 + i, cols), (G_half, (l, 1, i, slice(None), cols)))
        down = net.send(region(G, l, l, wrap(here - 1), None, cols), G_block.at[l, 1, :, :, cols], peer(axis, 3))
        return l, cols, up, down

    def reduce_end(state):
        l, cols, up, down = state
        up.wait_recv()
        down.wait_recv()
        for i in range(4):
            add_into(
                G,
                cell(l, position(l), i, cols),
                (G_block, (l, 0, i, slice(None), cols)),
                (G_block, (l, 1, i, slice(None), cols)),
            )

    strip_in = s["strip_in"]

    def strip_place(l, moved):
        if l < 2:
            return l, moved, x
        if l < 4:
            return l, y, moved
        return l, z, moved

    def second_position(l):
        return x if l in (2, 3) else y

    def strips_out(l):
        copies = []
        for step in (1, 2, 3):
            target = wrap(second_position(l) + step)
            copies.append(
                net.send(G.at[strip_place(l, target)], strip_in.at[l, step - 1], peer("x" if l in (2, 3) else "y", step))
            )
        return copies

    for copy in early:
        net.sent(copy)
    piece_out, piece_in = pieces, s["piece_in"]

    def strips_sum(l, copies):
        for copy in copies:
            copy.wait_recv()
        total = G[strip_place(l, second_position(l))].astype(F32)
        for i in range(3):
            total = total + strip_in[l, i].astype(F32)
        line[...] = total
        for i in range(4):
            piece_out[i, l, 0:16, :] = jnp.concatenate([line[12 * i : 12 * i + 12, :], jnp.zeros((4, D), F32)], 0).astype(BF16)

    flows = [[], [], []]
    pair_copies = {}
    for part in range(3):
        cols = part_cols[part]
        for e in range(2):
            hidden_slope(other, e, part)

            def finish(l, value):
                slot = 0 if l >= 4 else 1
                if (e, slot) in pair_copies:
                    net.sent(pair_copies[e, slot])
                pair_out[e, slot] = value.astype(BF16).reshape(4, 4, 48, TILE)
                pair_copies[e, slot] = share_of(e, slot, l, cols)

            hidden_grad(other, e, part, finish)
        for e in range(2):
            hidden_slope(c, e, part)

            def finish(l, value):
                pair_copies[e, 0 if l >= 4 else 1].wait_recv()
                G[l, :, :, :, cols] = (
                    value + pair_in[l, :, :, :, cols].reshape(D, TILE).astype(F32)
                ).astype(BF16).reshape(4, 4, 48, TILE)
                flows[part].append(reduce_start(l, cols))

            hidden_grad(c, e, part, finish)
        if part:
            flows[part - 1] = [reduce_pass(state) for state in flows[part - 1]]

    first_back(W, V, A, inv1, gp, F, dfb, sums)
    flows[2] = [reduce_pass(state) for state in flows[2]]
    turn(dfb, turned.at[1])
    output_back(W, dfb, y1b)
    for state in flows[0]:
        reduce_end(state)
    attend_back(q, k, v, p, y1b)
    turn(xb, turned.at[0])
    for state in flows[1] + flows[2]:
        reduce_end(state)
    strip_states = {l: strips_out(l) for l in (1, 3, 4, 5)}

    def projection_grad(core, l, n):
        left = core if l == 2 else 0
        return dot(turned[left], act[2 * core + l // 2, :, n * TILE : (n + 1) * TILE])

    for l in (0, 2):
        for n in range(3):
            slot = (n + (l // 2)) % 2, n % 2
            if slot in pair_copies:
                net.sent(pair_copies.pop(slot))
            cols = part_cols[n]
            pair_out[slot] = projection_grad(other, l, n).astype(BF16).reshape(4, 4, 48, TILE)
            pair_copies[slot] = share_of(*slot, l, cols)
            pair_copies[l, n, "in"] = pair_copies[slot]
    last = []
    for l in (0, 2):
        for n in range(3):
            cols = part_cols[n]
            value = projection_grad(c, l, n)
            pair_copies[l, n, "in"].wait_recv()
            G[l, :, :, :, cols] = (
                value + pair_in[l, :, :, :, cols].reshape(D, TILE).astype(F32)
            ).astype(BF16).reshape(4, 4, 48, TILE)
        last.append(reduce_start(l, every))
    column_sums(q, sums, V_BQ)
    column_sums(v, sums, V_BV)

    sums[VECTORS:16, :] = jnp.zeros((16 - VECTORS, D), F32)
    sums_in, sums_out = s["sums_in"], s["sums_out"]
    sums_out[0] = sums[...]
    sums_copies = [net.send(sums_out.at[0], sums_in.at[0, 0], sibling)]
    input_back(W, q, k, v, F)
    for i in range(SLOTS):
        stores.append(pltpu.make_async_copy(F.at[pl.ds(i * LEN, LEN)], grad_hbm.at[i], s["store_sem"].at[4 + i]))
        stores[-1].start()

    def sums_step(stage, copies, axis):
        total = sums_out[stage]
        for i, copy in enumerate(copies):
            copy.wait_recv()
            total = total + sums_in[stage, i]
        if axis is None:
            return total
        sums_out[stage + 1] = total
        return [net.send(sums_out.at[stage + 1], sums_in.at[stage + 1, step - 1], peer(axis, step)) for step in (1, 2, 3)]

    sums_copies = sums_step(0, sums_copies, "z")
    last = [reduce_pass(state) for state in last]
    sums_copies = sums_step(1, sums_copies, "x")
    for l in (1, 3, 4, 5):
        strips_sum(l, strip_states[l])
    sums_copies = sums_step(2, sums_copies, "y")
    for state in last:
        reduce_end(state)
        strip_states[state[0]] = strips_out(state[0])
    vec_total = sums_step(3, sums_copies, None)
    turned_sums = s["turned_sums"]
    turned_sums[0:D, :] = jnp.concatenate([vec_total, jnp.zeros((LEN - 16, D), F32)], 0).T
    for l in (0, 2):
        strips_sum(l, strip_states[l])

    copies = []
    for step in (1, 2, 3):
        copies.append(net.send(piece_out.at[wrap(z + step), pl.ds(0, 4)], piece_in.at[step - 1, pl.ds(0, 4)], peer("z", step)))
        copies.append(net.send(piece_out.at[wrap(x + step), pl.ds(4, 2)], piece_in.at[step - 1, pl.ds(4, 2)], peer("x", step)))
    for copy in copies:
        copy.wait_recv()
    rows_out, rows_own, rows_in = s["first_out"], s["first_own"], s["first_in"]
    squares = jnp.zeros((1, D), F32)
    for l in range(SHARE):
        total = piece_out[z if l < 4 else x, l].astype(F32)
        for i in range(3):
            total = total + piece_in[i, l].astype(F32)
        squares = squares + jnp.sum(total * total, 0, keepdims=True)
        line[0:16, :] = total
        top, bottom = line[0:6, :], line[6:12, :]
        rows_own[l, 0:6, :] = jnp.where(c == 0, top, bottom)
        rows_out[l, 0:6, :] = jnp.where(c == 0, bottom, top)
    rows_copy = net.send(rows_out, rows_in, sibling)
    vec_grad = turned_sums[pl.ds(6 * me, 8), :][0:6]
    squares = jnp.sum(squares, keepdims=True) + jnp.sum(vec_grad * vec_grad, keepdims=True)
    norm_out, norm_in = s["norm_out"], s["norm_in"]
    total = jnp.broadcast_to(squares, (8, LEN))
    norm_out[0] = total
    copies = [net.send(norm_out.at[0], norm_in.at[0, 0], sibling)]
    for stage, axis in ((0, "z"), (1, "x"), (2, "y"), (3, None)):
        total = norm_out[stage]
        for i, copy in enumerate(copies):
            copy.wait_recv()
            total = total + norm_in[stage, i]
        if axis is not None:
            norm_out[stage + 1] = total
            copies = [
                net.send(norm_out.at[stage + 1], norm_in.at[stage + 1, step - 1], peer(axis, step)) for step in (1, 2, 3)
            ]
    norm = jnp.sqrt(total)
    norm_out_ref[...] = norm[0:1, 0:1]
    factor = (CLIP_NORM / jnp.maximum(norm, CLIP_NORM))[0:1, 0:1]
    rows_copy.wait_recv()

    def gradient(core, l):
        return jnp.where(c == core, rows_own[l, 0:6], rows_in[l, 0:6]) * factor

    for i in range(4):
        new = adam(att_w[i], att_m[i], att_v[i], gradient(i // 2, 2 * (i % 2)), ATTENTION_RATES[i], WEIGHT_DECAY)
        att_w_new[i], att_m_new[i], att_v_new[i] = new
    for i in range(2):
        for j in range(4):
            cols = pl.ds(j * D, D)
            l = 1 + 2 * (j % 2) if i == 0 else 4 + j % 2
            new = adam(
                hid_w[i, :, cols], hid_m[i, :, cols], hid_v[i, :, cols], gradient(j // 2, l), HIDDEN_RATES[i], WEIGHT_DECAY
            )
            hid_w_new[i, :, cols], hid_m_new[i, :, cols], hid_v_new[i, :, cols] = new
    square = s["square"]
    square[0:6, :] = vec_grad * factor
    vec_step = square[...].T[0:VECTORS, 0:6]
    vec_w_new[...], vec_m_new[...], vec_v_new[...] = adam(vec_w[...], vec_m[...], vec_v[...], vec_step, VECTOR_RATE, 0.0)
    for copy in stores:
        copy.wait()
    net.close()


def on_device(
    inputs,
    cotangent,
    joined,
    half_lengths,
    attention_master,
    attention_first,
    attention_second,
    hidden_master,
    hidden_first,
    hidden_second,
    vector_master,
    vector_first,
    vector_second,
):
    any_space = pl.BlockSpec(memory_space=pl.ANY)
    vmem = pl.BlockSpec(memory_space=pltpu.VMEM)
    smem = pl.BlockSpec(memory_space=pltpu.SMEM)
    like = lambda a: jax.ShapeDtypeStruct(a.shape, a.dtype)
    outs = pl.pallas_call(
        step_kernel,
        out_shape=(
            like(inputs),
            jax.ShapeDtypeStruct(inputs.shape, F32),
            jax.ShapeDtypeStruct((1, 1), F32),
            *([like(attention_master)] * 3),
            *([like(hidden_master)] * 3),
            *([like(vector_master)] * 3),
        ),
        in_specs=[any_space] * 3 + [smem] * 2 + [vmem] * 9,
        out_specs=(any_space, any_space) + (vmem,) * 10,
        scratch_shapes=list(SCRATCH.values()),
        compiler_params=pltpu.CompilerParams(collective_id=0, has_side_effects=True, vmem_limit_bytes=64 << 20),
        cost_estimate=pl.CostEstimate(flops=22 * 10**9, bytes_accessed=6 * 10**6, transcendentals=4 * 10**6),
    )(
        inputs,
        cotangent,
        jnp.asarray(permutation(), BF16),
        joined,
        half_lengths,
        attention_master,
        hidden_master,
        vector_master,
        attention_first,
        attention_second,
        hidden_first,
        hidden_second,
        vector_first,
        vector_second,
    )
    output, input_grad, norm, *params = outs
    return (output, input_grad, norm.reshape(()), *params)


def solution(mesh):
    shard = P(None, "dp", None)
    flat = P(None, "dp")
    return jax.shard_map(
        on_device,
        mesh=mesh,
        in_specs=(shard, shard, flat, shard, shard, shard, shard, shard, shard, shard, flat, flat, flat),
        out_specs=(shard, shard, P(), shard, shard, shard, shard, shard, shard, flat, flat, flat),
        check_vma=False,
    )
```

```python
import functools
import jax
import jax.numpy as jnp
import numpy as np
from jax import lax
from jax.experimental import pallas as pl
from jax.experimental.pallas import tpu as pltpu
from jax.sharding import PartitionSpec as P

F32 = jnp.float32
BF16 = jnp.bfloat16
D = 768
FF = 3072
ROWS = 512
SLOTS = 4
LEN = 128
PAIRS = 6
TILE = 256
NORM_EPS = 1e-05
MASKED = -1e30
NN = (((1,), (0,)), ((), ()))
NT = (((1,), (1,)), ((), ()))
TN = (((0,), (0,)), ((), ()))
PLACE_Q, PLACE_K, PLACE_V, PLACE_O = 0, 1, 6, 7
PLACE_UP = (2, 3, 8, 9)
PLACE_DOWN = (4, 5, 10, 11)
V_BQ, V_BV, V_BO, V_G1, V_C1, V_G2, V_C2, V_B2, V_B1 = range(9)


def dot(a, b, dims=NN):
    return lax.dot_general(a, b, dims, preferred_element_type=F32)


def block(ref, place):
    return ref[place].reshape(D, D)


def columns(ref, place, start, size):
    return ref[place, :, :, :, pl.ds(start, size)].reshape(D, size)


def put_columns(ref, place, start, size, value):
    ref[place, :, :, :, pl.ds(start, size)] = value.reshape(4, 4, 48, size)


def loop(count, body):
    lax.fori_loop(0, count, lambda i, c: (body(i), c)[1], 0)


def at(i, size):
    return pl.ds(pl.multiple_of(i * size, size), size)


def qkv(W, V, xb, q, k, v):
    def tile(n):
        cols = at(n, TILE)
        x = xb[...]
        q[:, cols] = ((dot(x, columns(W, PLACE_Q, cols.start, TILE)) + V[V_BQ, cols]).astype(BF16) * 0.125).astype(BF16)
        k[:, cols] = dot(x, columns(W, PLACE_K, cols.start, TILE)).astype(BF16)
        v[:, cols] = (dot(x, columns(W, PLACE_V, cols.start, TILE)) + V[V_BV, cols]).astype(BF16)

    loop(D // TILE, tile)


def halves(value):
    lane = lax.broadcasted_iota(jnp.int32, value.shape, 1)
    zero = jnp.zeros_like(value)
    return jnp.concatenate([jnp.where(lane < 64, value, zero), jnp.where(lane < 64, zero, value)], 0)


def joined_halves(value):
    lane = lax.broadcasted_iota(jnp.int32, (LEN, LEN), 1)
    return jnp.where(lane < 64, value[:LEN], value[LEN:])


def fill_masks(joined, half_lengths, bias):
    query = lax.broadcasted_iota(jnp.int32, (LEN, LEN), 0)
    key = lax.broadcasted_iota(jnp.int32, (LEN, LEN), 1)
    for slot in range(SLOTS):
        is_joined = joined[0, slot]
        low = half_lengths[0, 0, slot]
        high = half_lengths[0, 1, slot]
        upper = (key >= 64).astype(jnp.int32)
        limit = is_joined * (64 + high) + (1 - is_joined) * (upper * (64 + high) + (1 - upper) * low)
        apart = (1 - is_joined) * jnp.abs((query >= 64).astype(jnp.int32) - upper)
        bias[slot] = jnp.where((key < limit) & (apart == 0), 0.0, MASKED)


GROUP = 6


def attend(q, k, v, bias, p, ctx):
    def units(slot):
        rows = at(slot, LEN)
        m = bias[slot]
        hidden = jnp.concatenate([m, m], 0) < 0
        cols = [pl.ds(pair * LEN, LEN) for pair in range(PAIRS)]
        for start in range(0, PAIRS, GROUP):
            some = range(start, start + GROUP)
            s = [dot(halves(q[rows, cols[i]]), k[rows, cols[i]], NT) for i in some]
            values = [v[rows, cols[i]] for i in some]
            s = [jnp.where(hidden, MASKED, one) for one in s]
            e = [jnp.exp(one - jnp.max(one, -1, keepdims=True)) for one in s]
            low = [(one * (1.0 / jnp.sum(one, -1, keepdims=True))).astype(BF16) for one in e]
            out = [joined_halves(dot(one, value)).astype(BF16) for one, value in zip(low, values)]
            for i, one, result in zip(some, low, out):
                p[slot * PAIRS + i] = one
                ctx[rows, cols[i]] = result

    loop(SLOTS, units)


def attend_back(q, k, v, p, dctx):
    def units(slot):
        rows = at(slot, LEN)
        cols = [pl.ds(pair * LEN, LEN) for pair in range(PAIRS)]
        for start in range(0, PAIRS, BACK_GROUP):
            some = range(start, start + BACK_GROUP)
            low = [p[slot * PAIRS + i] for i in some]
            two = [halves(dctx[rows, cols[i]]) for i in some]
            q2 = [halves(q[rows, cols[i]]) for i in some]
            keys = [k[rows, cols[i]] for i in some]
            dp = [dot(a, v[rows, cols[i]], NT) for a, i in zip(two, some)]
            dv = [dot(a, b, TN) for a, b in zip(low, two)]
            full = [a.astype(F32) for a in low]
            ds = [(a * (b - jnp.sum(a * b, -1, keepdims=True))).astype(BF16) for a, b in zip(full, dp)]
            dq = [joined_halves(dot(a, b)) * 0.125 for a, b in zip(ds, keys)]
            dk = [dot(a, b, TN) for a, b in zip(ds, q2)]
            for n, i in enumerate(some):
                v[rows, cols[i]] = dv[n].astype(BF16)
                q[rows, cols[i]] = dq[n].astype(BF16)
                k[rows, cols[i]] = dk[n].astype(BF16)

    loop(SLOTS, units)


BACK_GROUP = 3


STRIP = 256


def first_norm(W, V, xb, ctx, A, inv1, F, y1b):
    A[...] = dot(ctx[...], block(W, PLACE_O), NT)

    def strip(i):
        rows = at(i, STRIP)
        a = xb[rows, :].astype(F32) + A[rows, :] + V[V_BO : V_BO + 1, :]
        center = a - jnp.mean(a, -1, keepdims=True)
        inverse = lax.rsqrt(jnp.mean(center * center, -1, keepdims=True) + NORM_EPS)
        n = center * inverse
        A[rows, :] = n
        inv1[rows, :] = inverse
        y = n * V[V_G1 : V_G1 + 1, :] + V[V_C1 : V_C1 + 1, :]
        y1b[rows, :] = y.astype(BF16)
        F[rows, :] = y + V[V_B2 : V_B2 + 1, :]

    loop(ROWS // STRIP, strip)


def gelu_parts(u):
    e = jnp.exp(-0.5 * (u * u))
    t = pl.reciprocal(1.0 + 0.23164190 * jnp.abs(u), approx=True)
    poly = ((((0.5307027145 * t - 0.726576013) * t + 0.7107068705) * t - 0.142248368) * t + 0.127414796) * t
    tail = poly * e
    cdf = jnp.where(u >= 0, 1.0 - tail, tail)
    return u * cdf, cdf + (u * 0.3989422804014327) * e


def up(W, V, y1b, h, gp, part):
    def half(i):
        rows = at(i, TILE)
        y = y1b[rows, :]
        for j, place in enumerate(PLACE_UP):
            cols = pl.ds(j * D + part * TILE, TILE)
            u = dot(y, columns(W, place, part * TILE, TILE)) + V[V_B1 + j : V_B1 + j + 1, pl.ds(part * TILE, TILE)]
            value, slope = gelu_parts(u)
            h[rows, cols] = value.astype(BF16)
            gp[rows, cols] = slope.astype(BF16)

    loop(ROWS // TILE, half)


def down(W, h, FP, part):
    left = jnp.concatenate([h[:, pl.ds(j * D + part * TILE, TILE)] for j in range(4)], 1)
    right = jnp.concatenate([columns(W, place, part * TILE, TILE) for place in PLACE_DOWN], 1)
    total = dot(left, right, NT)
    FP[...] = total if part == 0 else FP[...] + total


def second_norm(V, perm, FP, F, gb, outb, dfb, sums):
    F[...] += dot(FP[...].astype(BF16), perm[...])

    def strip(i, carry):
        dg, dc, db = carry
        rows = at(i, STRIP)
        z = F[rows, :]
        center = z - jnp.mean(z, -1, keepdims=True)
        inverse = lax.rsqrt(jnp.mean(center * center, -1, keepdims=True) + NORM_EPS)
        n = center * inverse
        gain = V[V_G2 : V_G2 + 1, :]
        g = gb[rows, :].astype(F32)
        outb[rows, :] = (n * gain + V[V_C2 : V_C2 + 1, :]).astype(BF16)
        gn = g * n
        e = g * gain
        dz = inverse * (e - jnp.mean(e, -1, keepdims=True) - n * jnp.mean(gn * gain, -1, keepdims=True))
        low = dz.astype(BF16)
        F[rows, :] = dz
        dfb[rows, :] = low
        return (
            dg + jnp.sum(gn, 0, keepdims=True),
            dc + jnp.sum(g, 0, keepdims=True),
            db + jnp.sum(low.astype(F32), 0, keepdims=True),
        )

    zero = jnp.zeros((1, D), F32)
    dg, dc, db = lax.fori_loop(0, ROWS // STRIP, strip, (zero, zero, zero))
    sums[V_G2 : V_G2 + 1, :] = dg
    sums[V_C2 : V_C2 + 1, :] = dc
    sums[V_B2 : V_B2 + 1, :] = db


def turn(source, target):
    for i in range(ROWS // LEN):
        target[:, i * LEN : (i + 1) * LEN] = source[i * LEN : (i + 1) * LEN, :].T


def first_back(W, V, A, inv1, gp, F, dob, sums):
    right = jnp.concatenate([block(W, place) for place in PLACE_UP], 1)
    F[...] += dot(gp[...], right, NT)

    def strip(i, carry):
        dg, dc, db = carry
        rows = at(i, STRIP)
        dy = F[rows, :]
        n = A[rows, :]
        gain = V[V_G1 : V_G1 + 1, :]
        dyn = dy * n
        e = dy * gain
        da = inv1[rows, :] * (e - jnp.mean(e, -1, keepdims=True) - n * jnp.mean(dyn * gain, -1, keepdims=True))
        low = da.astype(BF16)
        F[rows, :] = da
        dob[rows, :] = low
        return (
            dg + jnp.sum(dyn, 0, keepdims=True),
            dc + jnp.sum(dy, 0, keepdims=True),
            db + jnp.sum(low.astype(F32), 0, keepdims=True),
        )

    zero = jnp.zeros((1, D), F32)
    dg, dc, db = lax.fori_loop(0, ROWS // STRIP, strip, (zero, zero, zero))
    sums[V_G1 : V_G1 + 1, :] = dg
    sums[V_C1 : V_C1 + 1, :] = dc
    sums[V_BO : V_BO + 1, :] = db


def output_back(W, dob, dctx):
    def tile(n):
        cols = at(n, TILE)
        dctx[:, cols] = dot(dob[...], columns(W, PLACE_O, cols.start, TILE)).astype(BF16)

    loop(D // TILE, tile)


def column_sums(source, sums, row):
    sums[row : row + 1, :] = jnp.sum(source[...].astype(F32), 0, keepdims=True)


def input_back(W, q, k, v, F):
    left = jnp.concatenate([q[...], k[...], v[...]], 1)
    right = jnp.concatenate([block(W, place) for place in (PLACE_Q, PLACE_K, PLACE_V)], 1)
    F[...] += dot(left, right, NT)


def to_down_order(dfb, perm, dfp):
    dfp[...] = dot(dfb[...], perm[...], NT).astype(BF16)


def permutation():
    r = np.arange(D)
    y, x, z, j = r // 192, r // 48 % 4, r // 12 % 4, r % 12
    p = np.zeros((D, D), np.float32)
    p[192 * z + 48 * x + 12 * y + j, r] = 1
    return p


MESH = pl.DeviceIdType.MESH
STEP = 10
ADAM_EPS = 1e-08
BETA_ONE = 0.9
BETA_TWO = 0.999
CLIP_NORM = 1.0
WEIGHT_DECAY = 0.01
ATTENTION_RATES = (0.02, 0.02, 0.04, 0.3)
HIDDEN_RATES = (0.04, 0.02)
VECTOR_RATE = 0.5
COPIES = 340
VECTORS = 12
SHARE = 6


class Net:
    def __init__(self, send_sem, recv_sem):
        self.send_sem, self.recv_sem, self.count, self.open = send_sem, recv_sem, 0, []

    def send(self, source, target, device):
        assert self.count < COPIES
        copy = pltpu.make_async_remote_copy(
            src_ref=source,
            dst_ref=target,
            send_sem=self.send_sem.at[self.count],
            recv_sem=self.recv_sem.at[self.count],
            device_id=(device,),
            device_id_type=MESH,
        )
        self.count += 1
        copy.start()
        self.open.append(copy)
        return copy

    def sent(self, copy):
        copy.wait_send()
        self.open = [one for one in self.open if one is not copy]

    def close(self):
        for copy in self.open:
            copy.wait_send()
        self.open = []


def adam(master, first, second, gradient, rate, decay):
    first_new = BETA_ONE * first + (1.0 - BETA_ONE) * gradient
    second_new = BETA_TWO * second + (1.0 - BETA_TWO) * gradient * gradient
    first_hat = first_new / (1.0 - BETA_ONE**STEP)
    second_hat = second_new / (1.0 - BETA_TWO**STEP)
    master_new = master - rate * (first_hat / (jnp.sqrt(second_hat) + ADAM_EPS) + decay * master)
    return master_new, first_new, second_new


SCRATCH = dict(
    W=pltpu.VMEM((12, 4, 4, 48, D), BF16),
    G=pltpu.VMEM((SHARE, 4, 4, 48, D), BF16),
    pair_in=pltpu.VMEM((SHARE, 4, 4, 48, D), BF16),
    pair_out=pltpu.VMEM((4, 4, 4, 48, TILE), BF16),
    half_in=pltpu.VMEM((SHARE, 2, 2, 48, D), BF16),
    strip_in=pltpu.VMEM((SHARE, 3, 48, D), BF16),
    piece_in=pltpu.VMEM((3, SHARE, 16, D), BF16),
    first_out=pltpu.VMEM((SHARE, 8, D), F32),
    first_own=pltpu.VMEM((SHARE, 8, D), F32),
    first_in=pltpu.VMEM((SHARE, 8, D), F32),
    vec_own=pltpu.VMEM((8, LEN), F32),
    vec_in=pltpu.VMEM((8, LEN), F32),
    pieces=pltpu.VMEM((4, SHARE, 16, D), BF16),
    vec_pieces=pltpu.VMEM((4, 16, LEN), BF16),
    VT=pltpu.VMEM((4, 4, 48, LEN), BF16),
    line=pltpu.VMEM((48, D), F32),
    sums_in=pltpu.VMEM((10, 16, D), F32),
    sums_out=pltpu.VMEM((4, 16, D), F32),
    norm_out=pltpu.VMEM((3, 8, LEN), F32),
    norm_in=pltpu.VMEM((3, 7, 8, LEN), F32),
    V=pltpu.VMEM((16, D), F32),
    sums=pltpu.VMEM((16, D), F32),
    bias=pltpu.VMEM((SLOTS, LEN, LEN), F32),
    act=pltpu.VMEM((4, ROWS, D), BF16),
    p=pltpu.VMEM((SLOTS * PAIRS, 2 * LEN, LEN), BF16),
    A=pltpu.VMEM((ROWS, D), F32),
    F=pltpu.VMEM((ROWS, D), F32),
    FP=pltpu.VMEM((ROWS, D), F32),
    inv1=pltpu.VMEM((ROWS, 1), F32),
    y1b=pltpu.VMEM((ROWS, D), BF16),
    turned=pltpu.VMEM((2, D, ROWS), BF16),
    h=pltpu.VMEM((ROWS, FF), BF16),
    gp=pltpu.VMEM((ROWS, FF), BF16),
    dfb=pltpu.VMEM((ROWS, D), BF16),
    xb=pltpu.VMEM((ROWS, D), BF16),
    gb=pltpu.VMEM((ROWS, D), BF16),
    perm=pltpu.VMEM((D, D), BF16),
    load_sem=pltpu.SemaphoreType.DMA((16,)),
    store_sem=pltpu.SemaphoreType.DMA((16,)),
    send_sem=pltpu.SemaphoreType.DMA((COPIES,)),
    recv_sem=pltpu.SemaphoreType.DMA((COPIES,)),
)
NAMES = tuple(SCRATCH)


def step_kernel(
    x_hbm,
    g_hbm,
    perm_hbm,
    joined,
    half_lengths,
    att_w,
    hid_w,
    vec_w,
    att_m,
    att_v,
    hid_m,
    hid_v,
    vec_m,
    vec_v,
    out_hbm,
    grad_hbm,
    norm_out_ref,
    att_w_new,
    att_m_new,
    att_v_new,
    hid_w_new,
    hid_m_new,
    hid_v_new,
    vec_w_new,
    vec_m_new,
    vec_v_new,
    *scratch,
):
    s = dict(zip(NAMES, scratch))
    W, G, V = s["W"], s["G"], s["V"]
    xb, gb, perm = s["xb"], s["gb"], s["perm"]
    net = Net(s["send_sem"], s["recv_sem"])

    me = lax.axis_index("dp")
    c = lax.rem(me, 2)
    z = lax.rem(lax.div(me, 2), 4)
    x = lax.rem(lax.div(me, 8), 4)
    y = lax.div(me, 32)
    other = 1 - c

    def wrap(value):
        return lax.rem(value + 4, 4)

    def peer(axis, step):
        moved = {"x": x, "y": y, "z": z}
        moved[axis] = wrap(moved[axis] + step)
        return ((moved["y"] * 4 + moved["x"]) * 4 + moved["z"]) * 2 + c

    sibling = me + 1 - 2 * c

    def far_peer(step):
        return ((y * 4 + x) * 4 + wrap(z + step)) * 2 + other

    loads = []
    for i in range(SLOTS):
        loads.append(pltpu.make_async_copy(x_hbm.at[i], xb.at[pl.ds(i * LEN, LEN)], s["load_sem"].at[i]))
        loads.append(pltpu.make_async_copy(g_hbm.at[i], gb.at[pl.ds(i * LEN, LEN)], s["load_sem"].at[4 + i]))
    loads.append(pltpu.make_async_copy(perm_hbm, perm, s["load_sem"].at[8]))
    for copy in loads:
        copy.start()

    barrier = pltpu.get_barrier_semaphore()
    partners = [sibling] + [peer(axis, step) for axis in "xyz" for step in (1, 2, 3)]
    partners += [far_peer(step) for step in (1, 2, 3)]
    for partner in partners:
        pl.semaphore_signal(barrier, inc=1, device_id=(partner,), device_id_type=MESH)

    masters = [[att_w[:, 2 * core + l, :] for l in range(2)] for core in range(2)]
    for core in range(2):
        masters[core] += [hid_w[:, i, (2 * core + l) * D : (2 * core + l + 1) * D] for i in range(2) for l in range(2)]
    for l in range(SHARE):
        s["first_own"][l, 0:6, :] = jnp.where(c == 0, masters[0][l], masters[1][l])
        s["first_out"][l, 0:6, :] = jnp.where(c == 0, masters[1][l], masters[0][l])
    s["vec_own"][...] = jnp.zeros((8, LEN), F32)
    s["vec_own"][0:6, 0:VECTORS] = vec_w[...]
    line = s["line"]
    line[...] = jnp.zeros((48, D), F32)
    pl.semaphore_wait(barrier, len(partners))

    pair = [
        net.send(s["first_out"].at[pl.ds(0, 2)], s["first_in"].at[pl.ds(0, 2)], sibling),
        net.send(s["first_out"].at[pl.ds(2, 4)], s["first_in"].at[pl.ds(2, 4)], sibling),
        net.send(s["vec_own"], s["vec_in"], sibling),
    ]
    fill_masks(joined, half_lengths, s["bias"])

    ALONG = ("x", "y", "x", "y", "z", "z")
    SECOND = ("y", "z", "y", "z", "x", "x")
    FIRST = ("z", "x", "z", "x", "y", "y")
    HERE = {"x": x, "y": y, "z": z}
    pieces, vec_pieces = s["pieces"], s["vec_pieces"]

    def make_piece(l):
        own, far = s["first_own"][l, 0:6], s["first_in"][l, 0:6]
        line[0:6, :] = jnp.where(c == 0, own, far)
        line[6:12, :] = jnp.where(c == 0, far, own)
        pieces[HERE[FIRST[l]], l] = line[0:16, :].astype(BF16)

    def send_pieces(l, count=1):
        near = pieces.at[HERE[FIRST[l]], pl.ds(l, count)]
        return [net.send(near, near, peer(FIRST[l], step)) for step in (1, 2, 3)]

    pair[0].wait_recv()
    for l in (0, 1):
        make_piece(l)
    piece_copies = {0: send_pieces(0), 1: send_pieces(1)}
    pair[2].wait_recv()
    own, far = s["vec_own"][0:6], s["vec_in"][0:6]
    line[0:6, 0:LEN] = jnp.where(c == 0, own, far)
    line[6:12, 0:LEN] = jnp.where(c == 0, far, own)
    vec_pieces[z] = line[0:16, 0:LEN].astype(BF16)
    near = vec_pieces.at[z]
    vec_copies = [net.send(near, near, peer("z", step)) for step in (1, 2, 3)]
    pair[1].wait_recv()
    for l in (4, 5):
        make_piece(l)
    piece_copies[4] = send_pieces(4, 2)
    piece_copies[5] = []
    for l in (2, 3):
        make_piece(l)
        piece_copies[l] = send_pieces(l)
    early = pair + vec_copies

    VT = s["VT"]

    def stage(ref, l, index):
        return ref.at[pl.ds(pl.multiple_of(index * 48, 16), 48), pl.ds((l // 2) * D, D)]

    def spread(l):
        for copy in piece_copies[l]:
            copy.wait_recv()
        early.extend(piece_copies[l])
        for i in range(4):
            line[12 * i : 12 * i + 12, :] = pieces[i, l].astype(F32)[0:12]
        if ALONG[l] == "y":
            stage(s["gp"], l, z)[...] = line[...].astype(BF16)
        else:
            W[(6 * c + l,) + ((y, x) if ALONG[l] == "x" else (z, x))] = line[...].astype(BF16)

    def strips(l, cols):
        if ALONG[l] == "y":
            near = stage(s["gp"], l, z)
        else:
            near = W.at[(6 * c + l,) + ((y, x) if ALONG[l] == "x" else (z, x)) + (slice(None), cols)]
        return [net.send(near, near, peer(SECOND[l], step)) for step in (1, 2, 3)]

    def strips_in(l, copies):
        for copy in copies:
            copy.wait_recv()
        if ALONG[l] == "y":
            for i in range(4):
                FP[48 * i : 48 * i + 48, :] = stage(s["gp"], l, i)[...].astype(F32)
            for i in range(4):
                for j in range(4):
                    line[12 * j : 12 * j + 12, :] = FP[48 * j + 12 * i : 48 * j + 12 * i + 12, :]
                W[6 * c + l, y, i] = line[...].astype(BF16)

    def region(ref, l, m, index, half, cols):
        part = pl.ds(0, 4) if half is None else pl.ds(2 * half, 2)
        if ALONG[l] == "x":
            return ref.at[m, part, index, :, cols]
        return ref.at[m, index, part, :, cols]

    def position(l):
        return HERE[ALONG[l]]

    def gather_start(l, cols):
        near = region(W, l, 6 * c + l, position(l), None, cols)
        up = net.send(near, near, peer(ALONG[l], 1))
        down = net.send(near, near, peer(ALONG[l], 3))
        return l, cols, up, down

    def gather_pass(state):
        l, cols, up, down = state
        m = 6 * c + l
        up.wait_recv()
        low = region(W, l, m, wrap(position(l) - 1), 0, cols)
        up = net.send(low, low, peer(ALONG[l], 1))
        down.wait_recv()
        high = region(W, l, m, wrap(position(l) + 1), 1, cols)
        down = net.send(high, high, peer(ALONG[l], 3))
        return l, cols, up, down

    def gather_share(state):
        l, cols, up, down = state
        up.wait_recv()
        down.wait_recv()
        whole = W.at[6 * c + l, :, :, :, cols]
        return net.send(whole, whole, sibling)

    def vec_start():
        near = VT.at[y]
        return net.send(near, near, peer("y", 1)), net.send(near, near, peer("y", 3))

    def vec_pass(state):
        up, down = state
        up.wait_recv()
        low = VT.at[wrap(y - 1), pl.ds(0, 2)]
        up = net.send(low, low, peer("y", 1))
        down.wait_recv()
        high = VT.at[wrap(y + 1), pl.ds(2, 2)]
        down = net.send(high, high, peer("y", 3))
        return up, down

    act, p = s["act"], s["p"]
    q, k, v, ctx = (act.at[i] for i in range(4))
    A, F, FP, inv1, y1b = s["A"], s["F"], s["FP"], s["inv1"], s["y1b"]
    h, gp, dfb, dfp, sums = s["h"], s["gp"], s["dfb"], y1b, s["sums"]
    turned = s["turned"]

    every = pl.ds(0, D)
    part_cols = [pl.ds(part * TILE, TILE) for part in range(3)]
    rest_cols = pl.ds(TILE, 2 * TILE)
    strip_copies = {}
    for l in (0, 1):
        spread(l)
        strip_copies[l] = strips(l, every)
    for copy in vec_copies:
        copy.wait_recv()
    for i in range(4):
        line[12 * i : 12 * i + 12, 0:LEN] = vec_pieces[i].astype(F32)[0:12]
    VT[y, x] = line[:, 0:LEN].astype(BF16)
    near = VT.at[y, x]
    vec_strips = [net.send(near, near, peer("x", step)) for step in (1, 2, 3)]
    for l in (4, 5):
        spread(l)
        strip_copies[l] = strips(l, part_cols[0])
    first = []
    for l in (0, 1):
        strips_in(l, strip_copies[l])
        first.append(gather_start(l, every))
    for copy in vec_strips:
        copy.wait_recv()
    vec_state = vec_start()
    later = [[], [], []]
    for l in (4, 5):
        strips_in(l, strip_copies[l])
        later[0].append(gather_start(l, part_cols[0]))
    for l in (2, 3):
        spread(l)
    for copy in loads:
        copy.wait()

    vec_state = vec_pass(vec_state)
    first = [gather_pass(state) for state in first]
    for l in (2, 3):
        strip_copies[l] = strips(l, every)
    for l in (4, 5):
        strip_copies[l] = strips(l, rest_cols)
    later[0] = [gather_pass(state) for state in later[0]]
    for copy in vec_state:
        copy.wait_recv()
    V[...] = VT[...].reshape(D, LEN).astype(F32).T[0:16]
    first = [gather_share(state) for state in first]
    for l in (2, 3):
        strips_in(l, strip_copies[l])
        later[0].append(gather_start(l, part_cols[0]))
    for l in (4, 5):
        strips_in(l, strip_copies[l])
        later[1].append(gather_start(l, part_cols[1]))
    for copy in first:
        copy.wait_recv()

    qkv(W, V, xb, q, k, v)
    later[0] = [gather_share(state) for state in later[0][:2]] + [gather_pass(state) for state in later[0][2:]]
    for l in (2, 3):
        later[1].append(gather_start(l, part_cols[1]))
    attend(q, k, v, s["bias"], p, ctx)
    later[1][:2] = [gather_pass(state) for state in later[1][:2]]
    for l in (4, 5):
        later[2].append(gather_start(l, part_cols[2]))
    first_norm(W, V, xb, ctx, A, inv1, F, y1b)
    later[0] = later[0][:2] + [gather_share(state) for state in later[0][2:]]
    later[1][2:] = [gather_pass(state) for state in later[1][2:]]
    for l in (2, 3):
        later[2].append(gather_start(l, part_cols[2]))
    turn(y1b, turned.at[1])
    for copy in later[0]:
        copy.wait_recv()
    for copy in strip_copies[1] + strip_copies[3]:
        net.sent(copy)
    up(W, V, y1b, h, gp, 0)
    later[1] = [gather_share(state) for state in later[1]]
    later[2] = [gather_pass(state) for state in later[2]]
    down(W, h, FP, 0)
    for copy in later[1]:
        copy.wait_recv()
    up(W, V, y1b, h, gp, 1)
    later[2] = [gather_share(state) for state in later[2]]
    down(W, h, FP, 1)
    for copy in later[2]:
        copy.wait_recv()
    up(W, V, y1b, h, gp, 2)
    down(W, h, FP, 2)
    second_norm(V, perm, FP, F, gb, gb, dfb, sums)
    stores = []
    for i in range(SLOTS):
        stores.append(pltpu.make_async_copy(gb.at[pl.ds(i * LEN, LEN)], out_hbm.at[i], s["store_sem"].at[i]))
        stores[-1].start()
    to_down_order(dfb, perm, dfp)
    dfpT = turned.at[0]
    y1T = turned.at[1]
    turn(dfp, dfpT)

    pair_in, pair_out = s["pair_in"], s["pair_out"]

    def share_of(slot, l, cols):
        return net.send(pair_out.at[slot], pair_in.at[l, :, :, :, cols], sibling)

    G_half = s["half_in"]
    G_block = pair_in

    def reduce_start(l, cols):
        lo = region(G, l, l, wrap(position(l) + 2), 0, cols)
        hi = region(G, l, l, wrap(position(l) + 2), 1, cols)
        return (
            l,
            cols,
            net.send(lo, G_half.at[l, 0, :, :, cols], peer(ALONG[l], 1)),
            net.send(hi, G_half.at[l, 1, :, :, cols], peer(ALONG[l], 3)),
        )

    def add_into(ref, index, *others):
        total = ref[index].astype(F32)
        for other_ref, other_index in others:
            total = total + other_ref[other_index].astype(F32)
        ref[index] = total.astype(BF16)

    def cell(l, index, i, cols):
        return (l, i, index, slice(None), cols) if ALONG[l] == "x" else (l, index, i, slice(None), cols)

    def reduce_pass(state):
        l, cols, up, down = state
        axis, here = ALONG[l], position(l)
        up.wait_recv()
        down.wait_recv()
        for i in range(2):
            add_into(G, cell(l, wrap(here + 1), i, cols), (G_half, (l, 0, i, slice(None), cols)))
            add_into(G, cell(l, wrap(here - 1), 2 + i, cols), (G_half, (l, 1, i, slice(None), cols)))
        up = net.send(region(G, l, l, wrap(here + 1), None, cols), G_block.at[l, 0, :, :, cols], peer(axis, 1))
        down = net.send(region(G, l, l, wrap(here - 1), None, cols), G_block.at[l, 1, :, :, cols], peer(axis, 3))
        return l, cols, up, down

    def reduce_end(state):
        l, cols, up, down = state
        up.wait_recv()
        down.wait_recv()
        for i in range(4):
            add_into(
                G,
                cell(l, position(l), i, cols),
                (G_block, (l, 0, i, slice(None), cols)),
                (G_block, (l, 1, i, slice(None), cols)),
            )

    strip_in = s["strip_in"]

    def strip_place(l, moved):
        return (l, moved, x) if ALONG[l] == "x" else (l, z, moved)

    def strips_out(l):
        if ALONG[l] == "y":
            for i in range(4):
                FP[48 * i : 48 * i + 48, :] = G[l, y, i].astype(F32)
            for j in range(4):
                for i in range(4):
                    line[12 * i : 12 * i + 12, :] = FP[48 * i + 12 * j : 48 * i + 12 * j + 12, :]
                stage(h, l, j)[...] = line[...].astype(BF16)
        copies = []
        for step in (1, 2, 3):
            target = wrap(HERE[SECOND[l]] + step)
            source = stage(h, l, target) if ALONG[l] == "y" else G.at[strip_place(l, target)]
            copies.append(net.send(source, strip_in.at[l, step - 1], peer(SECOND[l], step)))
        return copies

    piece_out, piece_in = pieces, s["piece_in"]

    def strips_sum(l, copies):
        for copy in copies:
            copy.wait_recv()
        own = stage(h, l, z)[...] if ALONG[l] == "y" else G[strip_place(l, HERE[SECOND[l]])]
        total = own.astype(F32)
        for i in range(3):
            total = total + strip_in[l, i].astype(F32)
        line[...] = total
        for i in range(4):
            piece_out[i, l, 0:16, :] = jnp.concatenate([line[12 * i : 12 * i + 12, :], jnp.zeros((4, D), F32)], 0).astype(BF16)

    def pieces_out(l, count=1):
        return [
            net.send(
                piece_out.at[wrap(HERE[FIRST[l]] + step), pl.ds(l, count)],
                piece_in.at[step - 1, pl.ds(l, count)],
                peer(FIRST[l], step),
            )
            for step in (1, 2, 3)
        ]

    rows_out, rows_own, rows_in = s["first_out"], s["first_own"], s["first_in"]

    def pieces_sum(l):
        total = piece_out[HERE[FIRST[l]], l].astype(F32)
        for i in range(3):
            total = total + piece_in[i, l].astype(F32)
        line[0:16, :] = total
        top, bottom = line[0:6, :], line[6:12, :]
        rows_own[l, 0:6, :] = jnp.where(c == 0, top, bottom)
        rows_out[l, 0:6, :] = jnp.where(c == 0, bottom, top)
        return jnp.sum(top * top, 0, keepdims=True) + jnp.sum(bottom * bottom, 0, keepdims=True)

    flows = [[], [], []]
    slots = [None] * 4

    def other_tile(slot, l, cols, value):
        if slots[slot] is not None:
            net.sent(slots[slot])
        pair_out[slot] = value.astype(BF16).reshape(4, 4, 48, TILE)
        slots[slot] = share_of(slot, l, cols)
        return slots[slot]

    def own_tile(copy, l, cols, value):
        copy.wait_recv()
        value = value + pair_in[l, :, :, :, cols].reshape(D, TILE).astype(F32)
        G[l, :, :, :, cols] = value.astype(BF16).reshape(4, 4, 48, TILE)
        return reduce_start(l, cols)

    def hidden_slopes(core, part):
        places = [pl.ds(pl.multiple_of((2 * core + e) * D + part * TILE, LEN), TILE) for e in range(2)]
        slopes = []
        for e in range(2):
            dh = dot(dfp[...], columns(W, 6 * core + 4 + e, part * TILE, TILE))
            du = (dh * gp[:, places[e]].astype(F32)).astype(BF16)
            slopes.append(du)
            sums[pl.ds(V_B1 + 2 * core + e, 1), part_cols[part]] = jnp.sum(du.astype(F32), 0, keepdims=True)
        return places, slopes

    for part in range(3):
        cols = part_cols[part]
        places, slopes = hidden_slopes(other, part)
        shared = {}
        for e in range(2):
            shared[4 + e] = other_tile(e, 4 + e, cols, dot(dfpT[...], h[:, places[e]]))
        for e in range(2):
            shared[2 + e] = other_tile(2 + e, 2 + e, cols, dot(y1T[...], slopes[e]))
            gp[:, places[e]] = slopes[e]
        places, slopes = hidden_slopes(c, part)
        for e in range(2):
            flows[part].append(own_tile(shared[4 + e], 4 + e, cols, dot(dfpT[...], h[:, places[e]])))
        for e in range(2):
            flows[part].append(own_tile(shared[2 + e], 2 + e, cols, dot(y1T[...], slopes[e])))
            gp[:, places[e]] = slopes[e]
        if part:
            flows[part - 1] = [reduce_pass(state) for state in flows[part - 1]]

    first_back(W, V, A, inv1, gp, F, dfb, sums)
    flows[2] = [reduce_pass(state) for state in flows[2]]
    for state in flows[0]:
        reduce_end(state)
    doT = turned.at[1]
    turn(dfb, doT)
    output_back(W, dfb, y1b)
    for state in flows[1]:
        reduce_end(state)
    attend_back(q, k, v, p, y1b)
    turn(xb, turned.at[0])
    for state in flows[2]:
        reduce_end(state)
    for copy in early:
        net.sent(copy)
    strip_states = {l: strips_out(l) for l in (4, 5, 2, 3)}

    def projection_grad(core, l, n):
        left = core if l == 1 else 0
        return dot(turned[left], act[2 * core + l, :, n * TILE : (n + 1) * TILE])

    shared = {}

    def other_projection(n):
        for l in (0, 1):
            shared[l, n] = other_tile((2 * n + l) % 4, l, part_cols[n], projection_grad(other, l, n))

    last = []

    def own_projection(n):
        last.append([own_tile(shared[l, n], l, part_cols[n], projection_grad(c, l, n)) for l in (0, 1)])

    other_projection(0)
    other_projection(1)
    own_projection(0)
    other_projection(2)
    own_projection(1)
    own_projection(2)
    column_sums(q, sums, V_BQ)
    column_sums(v, sums, V_BV)

    sums[VECTORS:16, :] = jnp.zeros((16 - VECTORS, D), F32)
    sums_in, sums_out = s["sums_in"], s["sums_out"]
    sums_out[0] = sums[...]
    sums_copies = [net.send(sums_out.at[0], sums_in.at[0], sibling)]

    def sums_step(stage, copies, axis):
        total = sums_out[stage]
        for i, copy in enumerate(copies):
            copy.wait_recv()
            total = total + sums_in[3 * stage - 2 + i if stage else 0]
        if axis is None:
            return total
        sums_out[stage + 1] = total
        return [net.send(sums_out.at[stage + 1], sums_in.at[3 * stage + step], peer(axis, step)) for step in (1, 2, 3)]

    last[0] = [reduce_pass(state) for state in last[0]]
    last[1] = [reduce_pass(state) for state in last[1]]
    last[2] = [reduce_pass(state) for state in last[2]]
    sums_copies = sums_step(0, sums_copies, "z")
    input_back(W, q, k, v, F)
    for i in range(SLOTS):
        stores.append(pltpu.make_async_copy(F.at[pl.ds(i * LEN, LEN)], grad_hbm.at[i], s["store_sem"].at[4 + i]))
        stores[-1].start()
    sums_copies = sums_step(1, sums_copies, "x")
    piece_copies = {}
    for l in (4, 5, 2, 3):
        strips_sum(l, strip_states[l])
        if l != 4:
            piece_copies[l] = pieces_out(4, 2) if l == 5 else pieces_out(l)
    sums_copies = sums_step(2, sums_copies, "y")
    for some in last:
        for state in some:
            reduce_end(state)
    for l in (0, 1):
        strip_states[l] = strips_out(l)
    vec_total = sums_step(3, sums_copies, None)
    place = lax.broadcasted_iota(jnp.int32, (8, D), 1) - 6 * me
    pick = (place == lax.broadcasted_iota(jnp.int32, (8, D), 0)).astype(BF16)
    vec_grad = jnp.zeros((8, 16), F32)
    for _ in range(3):
        low = vec_total.astype(BF16)
        vec_grad = vec_grad + dot(pick, low, NT)
        vec_total = vec_total - low.astype(F32)
    vec_grad = vec_grad[0:6, 0:VECTORS]
    squares = jnp.zeros((1, D), F32)
    for l in (5, 2, 3):
        for copy in piece_copies[l]:
            copy.wait_recv()
    for l in (4, 5, 2, 3):
        squares = squares + pieces_sum(l)
    rows_copies = [net.send(rows_out.at[pl.ds(2, 4)], rows_in.at[pl.ds(2, 4)], sibling)]
    for l in (0, 1):
        strips_sum(l, strip_states[l])
        piece_copies[l] = pieces_out(l)
    for l in (0, 1):
        for copy in piece_copies[l]:
            copy.wait_recv()
        squares = squares + pieces_sum(l)
    total = jnp.sum(squares, keepdims=True) + jnp.sum(vec_grad * vec_grad, keepdims=True)
    norm_out, norm_in = s["norm_out"], s["norm_in"]
    norm_out[0] = jnp.broadcast_to(total, (8, LEN))
    copies = [net.send(norm_out.at[0], norm_in.at[0, step - 1], peer("x", step)) for step in (1, 2, 3)]
    rows_copies.append(net.send(rows_out.at[pl.ds(0, 2)], rows_in.at[pl.ds(0, 2)], sibling))
    for copy in rows_copies:
        copy.wait_recv()
    att_grad, hid_grad = att_m_new, hid_m_new
    for core in range(2):
        for l in range(SHARE):
            value = jnp.where(c == core, rows_own[l, 0:6], rows_in[l, 0:6])
            if l < 2:
                att_grad[:, 2 * core + l, :] = value
            else:
                i, j = (l - 2) // 2, 2 * core + l % 2
                hid_grad[:, i, j * D : (j + 1) * D] = value

    def norm_step(index, copies):
        total = norm_out[index]
        for copy in copies:
            copy.wait_recv()
        for i in range(len(copies)):
            total = total + norm_in[index, i]
        return total

    norm_out[1] = norm_step(0, copies)
    copies = [net.send(norm_out.at[1], norm_in.at[1, step - 1], peer("y", step)) for step in (1, 2, 3)]
    norm_out[2] = norm_step(1, copies)
    copies = [net.send(norm_out.at[2], norm_in.at[2, 0], sibling)]
    for step in (1, 2, 3):
        copies.append(net.send(norm_out.at[2], norm_in.at[2, step], peer("z", step)))
        copies.append(net.send(norm_out.at[2], norm_in.at[2, 3 + step], far_peer(step)))
    norm = jnp.sqrt(norm_step(2, copies))
    norm_out_ref[...] = norm[0:1, 0:1]
    factor = (CLIP_NORM / jnp.maximum(norm, CLIP_NORM))[0:1, 0:1]

    def rates(values, shape):
        index = lax.broadcasted_iota(jnp.int32, shape, 1)
        rate = jnp.full(shape, values[0], F32)
        for i, value in enumerate(values[1:]):
            rate = jnp.where(index == i + 1, value, rate)
        return rate

    att_w_new[...], att_m_new[...], att_v_new[...] = adam(
        att_w[...], att_m[...], att_v[...], att_grad[...] * factor, rates(ATTENTION_RATES, (6, 4, D)), WEIGHT_DECAY
    )
    hid_w_new[...], hid_m_new[...], hid_v_new[...] = adam(
        hid_w[...], hid_m[...], hid_v[...], hid_grad[...] * factor, rates(HIDDEN_RATES, (6, 2, FF)), WEIGHT_DECAY
    )
    vec_w_new[...], vec_m_new[...], vec_v_new[...] = adam(
        vec_w[...], vec_m[...], vec_v[...], vec_grad * factor, VECTOR_RATE, 0.0
    )
    for copy in stores:
        copy.wait()
    net.close()


def on_device(
    inputs,
    cotangent,
    joined,
    half_lengths,
    attention_master,
    attention_first,
    attention_second,
    hidden_master,
    hidden_first,
    hidden_second,
    vector_master,
    vector_first,
    vector_second,
):
    any_space = pl.BlockSpec(memory_space=pl.ANY)
    vmem = pl.BlockSpec(memory_space=pltpu.VMEM)
    smem = pl.BlockSpec(memory_space=pltpu.SMEM)
    like = lambda a: jax.ShapeDtypeStruct(a.shape, a.dtype)
    swap = lambda a: jnp.transpose(a, (1, 0, 2))
    attention = [swap(a) for a in (attention_master, attention_first, attention_second)]
    hidden = [swap(a) for a in (hidden_master, hidden_first, hidden_second)]
    vectors = [a.T for a in (vector_master, vector_first, vector_second)]
    outs = pl.pallas_call(
        step_kernel,
        out_shape=(
            like(inputs),
            jax.ShapeDtypeStruct(inputs.shape, F32),
            jax.ShapeDtypeStruct((1, 1), F32),
            *([like(attention[0])] * 3),
            *([like(hidden[0])] * 3),
            *([like(vectors[0])] * 3),
        ),
        in_specs=[any_space] * 3 + [smem] * 2 + [vmem] * 9,
        out_specs=(any_space, any_space) + (vmem,) * 10,
        scratch_shapes=list(SCRATCH.values()),
        compiler_params=pltpu.CompilerParams(collective_id=0, has_side_effects=True, vmem_limit_bytes=64 << 20),
        cost_estimate=pl.CostEstimate(flops=22 * 10**9, bytes_accessed=6 * 10**6, transcendentals=4 * 10**6),
    )(
        inputs,
        cotangent,
        jnp.asarray(permutation(), BF16),
        joined.T,
        jnp.transpose(half_lengths, (1, 2, 0)),
        attention[0],
        hidden[0],
        vectors[0],
        *attention[1:],
        *hidden[1:],
        *vectors[1:],
    )
    output, input_grad, norm, *params = outs
    return (output, input_grad, norm.reshape(()), *[swap(a) for a in params[:6]], *[a.T for a in params[6:]])


def solution(mesh):
    shard = P(None, "dp", None)
    flat = P(None, "dp")
    return jax.shard_map(
        on_device,
        mesh=mesh,
        in_specs=(shard, shard, flat, shard, shard, shard, shard, shard, shard, shard, flat, flat, flat),
        out_specs=(shard, shard, P(), shard, shard, shard, shard, shard, shard, flat, flat, flat),
        check_vma=False,
    )
```

```python
import functools
import jax
import jax.numpy as jnp
import numpy as np
from jax import lax
from jax.experimental import pallas as pl
from jax.experimental.pallas import tpu as pltpu
from jax.sharding import PartitionSpec as P

F32 = jnp.float32
BF16 = jnp.bfloat16
D = 768
FF = 3072
ROWS = 512
SLOTS = 4
LEN = 128
PAIRS = 6
TILE = 256
NORM_EPS = 1e-05
MASKED = -1e30
NN = (((1,), (0,)), ((), ()))
NT = (((1,), (1,)), ((), ()))
TN = (((0,), (0,)), ((), ()))
PLACE_Q, PLACE_K, PLACE_V, PLACE_O = 0, 1, 6, 7
PLACE_UP = (2, 3, 8, 9)
PLACE_DOWN = (4, 5, 10, 11)
V_BQ, V_BV, V_BO, V_G1, V_C1, V_G2, V_C2, V_B2, V_B1 = range(9)


def dot(a, b, dims=NN):
    return lax.dot_general(a, b, dims, preferred_element_type=F32)


def block(ref, place):
    return ref[place].reshape(D, D)


def columns(ref, place, start, size):
    return ref[place, :, :, :, pl.ds(start, size)].reshape(D, size)


def put_columns(ref, place, start, size, value):
    ref[place, :, :, :, pl.ds(start, size)] = value.reshape(4, 4, 48, size)


def loop(count, body):
    lax.fori_loop(0, count, lambda i, c: (body(i), c)[1], 0)


def at(i, size):
    return pl.ds(pl.multiple_of(i * size, size), size)


def qkv(W, V, xb, q, k, v):
    def tile(n):
        cols = at(n, TILE)
        x = xb[...]
        q[:, cols] = ((dot(x, columns(W, PLACE_Q, cols.start, TILE)) + V[V_BQ, cols]).astype(BF16) * 0.125).astype(BF16)
        k[:, cols] = dot(x, columns(W, PLACE_K, cols.start, TILE)).astype(BF16)
        v[:, cols] = (dot(x, columns(W, PLACE_V, cols.start, TILE)) + V[V_BV, cols]).astype(BF16)

    loop(D // TILE, tile)


def halves(value):
    lane = lax.broadcasted_iota(jnp.int32, value.shape, 1)
    zero = jnp.zeros_like(value)
    return jnp.concatenate([jnp.where(lane < 64, value, zero), jnp.where(lane < 64, zero, value)], 0)


def joined_halves(value):
    lane = lax.broadcasted_iota(jnp.int32, (LEN, LEN), 1)
    return jnp.where(lane < 64, value[:LEN], value[LEN:])


def fill_masks(joined, half_lengths, bias):
    query = lax.broadcasted_iota(jnp.int32, (LEN, LEN), 0)
    key = lax.broadcasted_iota(jnp.int32, (LEN, LEN), 1)
    for slot in range(SLOTS):
        is_joined = joined[0, slot]
        low = half_lengths[0, 0, slot]
        high = half_lengths[0, 1, slot]
        upper = (key >= 64).astype(jnp.int32)
        limit = is_joined * (64 + high) + (1 - is_joined) * (upper * (64 + high) + (1 - upper) * low)
        apart = (1 - is_joined) * jnp.abs((query >= 64).astype(jnp.int32) - upper)
        bias[slot] = jnp.where((key < limit) & (apart == 0), 0.0, MASKED)


GROUP = 6


def attend(q, k, v, bias, p, ctx):
    def units(slot):
        rows = at(slot, LEN)
        m = bias[slot]
        hidden = jnp.concatenate([m, m], 0) < 0
        cols = [pl.ds(pair * LEN, LEN) for pair in range(PAIRS)]
        for start in range(0, PAIRS, GROUP):
            some = range(start, start + GROUP)
            s = [dot(halves(q[rows, cols[i]]), k[rows, cols[i]], NT) for i in some]
            values = [v[rows, cols[i]] for i in some]
            s = [jnp.where(hidden, MASKED, one) for one in s]
            e = [jnp.exp(one - jnp.max(one, -1, keepdims=True)) for one in s]
            low = [(one * (1.0 / jnp.sum(one, -1, keepdims=True))).astype(BF16) for one in e]
            out = [joined_halves(dot(one, value)).astype(BF16) for one, value in zip(low, values)]
            for i, one, result in zip(some, low, out):
                p[slot * PAIRS + i] = one
                ctx[rows, cols[i]] = result

    loop(SLOTS, units)


def attend_back(q, k, v, p, dctx):
    def units(slot):
        rows = at(slot, LEN)
        cols = [pl.ds(pair * LEN, LEN) for pair in range(PAIRS)]
        for start in range(0, PAIRS, BACK_GROUP):
            some = range(start, start + BACK_GROUP)
            low = [p[slot * PAIRS + i] for i in some]
            two = [halves(dctx[rows, cols[i]]) for i in some]
            q2 = [halves(q[rows, cols[i]]) for i in some]
            keys = [k[rows, cols[i]] for i in some]
            dp = [dot(a, v[rows, cols[i]], NT) for a, i in zip(two, some)]
            dv = [dot(a, b, TN) for a, b in zip(low, two)]
            full = [a.astype(F32) for a in low]
            ds = [(a * (b - jnp.sum(a * b, -1, keepdims=True))).astype(BF16) for a, b in zip(full, dp)]
            dq = [joined_halves(dot(a, b)) * 0.125 for a, b in zip(ds, keys)]
            dk = [dot(a, b, TN) for a, b in zip(ds, q2)]
            for n, i in enumerate(some):
                v[rows, cols[i]] = dv[n].astype(BF16)
                q[rows, cols[i]] = dq[n].astype(BF16)
                k[rows, cols[i]] = dk[n].astype(BF16)

    loop(SLOTS, units)


BACK_GROUP = 3


STRIP = 256


def first_norm(W, V, xb, ctx, A, inv1, F, y1b):
    A[...] = dot(ctx[...], block(W, PLACE_O), NT)

    def strip(i):
        rows = at(i, STRIP)
        a = xb[rows, :].astype(F32) + A[rows, :] + V[V_BO : V_BO + 1, :]
        center = a - jnp.mean(a, -1, keepdims=True)
        inverse = lax.rsqrt(jnp.mean(center * center, -1, keepdims=True) + NORM_EPS)
        n = center * inverse
        A[rows, :] = n
        inv1[rows, :] = inverse
        y = n * V[V_G1 : V_G1 + 1, :] + V[V_C1 : V_C1 + 1, :]
        y1b[rows, :] = y.astype(BF16)
        F[rows, :] = y + V[V_B2 : V_B2 + 1, :]

    loop(ROWS // STRIP, strip)


def gelu_parts(u):
    e = jnp.exp(-0.5 * (u * u))
    t = pl.reciprocal(1.0 + 0.23164190 * jnp.abs(u), approx=True)
    poly = ((((0.5307027145 * t - 0.726576013) * t + 0.7107068705) * t - 0.142248368) * t + 0.127414796) * t
    tail = poly * e
    cdf = jnp.where(u >= 0, 1.0 - tail, tail)
    return u * cdf, cdf + (u * 0.3989422804014327) * e


def up(W, V, y1b, h, gp, part):
    def half(i):
        rows = at(i, TILE)
        y = y1b[rows, :]
        for j, place in enumerate(PLACE_UP):
            cols = pl.ds(j * D + part * TILE, TILE)
            u = dot(y, columns(W, place, part * TILE, TILE)) + V[V_B1 + j : V_B1 + j + 1, pl.ds(part * TILE, TILE)]
            value, slope = gelu_parts(u)
            h[rows, cols] = value.astype(BF16)
            gp[rows, cols] = slope.astype(BF16)

    loop(ROWS // TILE, half)


def down_(W, h, FP, part):
    left = jnp.concatenate([h[:, pl.ds(j * D + part * TILE, TILE)] for j in range(4)], 1)
    right = jnp.concatenate([columns(W, place, part * TILE, TILE) for place in PLACE_DOWN], 1)
    total = dot(left, right, NT)
    FP[...] = total if part == 0 else FP[...] + total


def second_norm(V, perm, FP, F, gb, outb, dfb, sums):
    F[...] += dot(FP[...].astype(BF16), perm[...])

    def strip(i, carry):
        dg, dc, db = carry
        rows = at(i, STRIP)
        z = F[rows, :]
        center = z - jnp.mean(z, -1, keepdims=True)
        inverse = lax.rsqrt(jnp.mean(center * center, -1, keepdims=True) + NORM_EPS)
        n = center * inverse
        gain = V[V_G2 : V_G2 + 1, :]
        g = gb[rows, :].astype(F32)
        outb[rows, :] = (n * gain + V[V_C2 : V_C2 + 1, :]).astype(BF16)
        gn = g * n
        e = g * gain
        dz = inverse * (e - jnp.mean(e, -1, keepdims=True) - n * jnp.mean(gn * gain, -1, keepdims=True))
        low = dz.astype(BF16)
        F[rows, :] = dz
        dfb[rows, :] = low
        return (
            dg + jnp.sum(gn, 0, keepdims=True),
            dc + jnp.sum(g, 0, keepdims=True),
            db + jnp.sum(low.astype(F32), 0, keepdims=True),
        )

    zero = jnp.zeros((1, D), F32)
    dg, dc, db = lax.fori_loop(0, ROWS // STRIP, strip, (zero, zero, zero))
    sums[V_G2 : V_G2 + 1, :] = dg
    sums[V_C2 : V_C2 + 1, :] = dc
    sums[V_B2 : V_B2 + 1, :] = db


def turn(source, target):
    for i in range(ROWS // LEN):
        target[:, i * LEN : (i + 1) * LEN] = source[i * LEN : (i + 1) * LEN, :].T


def first_back_product(W, gp, F):
    right = jnp.concatenate([block(W, place) for place in PLACE_UP], 1)
    F[...] += dot(gp[...], right, NT)


def first_back(V, A, inv1, F, dob, sums):
    def strip(i, carry):
        dg, dc, db = carry
        rows = at(i, STRIP)
        dy = F[rows, :]
        n = A[rows, :]
        gain = V[V_G1 : V_G1 + 1, :]
        dyn = dy * n
        e = dy * gain
        da = inv1[rows, :] * (e - jnp.mean(e, -1, keepdims=True) - n * jnp.mean(dyn * gain, -1, keepdims=True))
        low = da.astype(BF16)
        F[rows, :] = da
        dob[rows, :] = low
        return (
            dg + jnp.sum(dyn, 0, keepdims=True),
            dc + jnp.sum(dy, 0, keepdims=True),
            db + jnp.sum(low.astype(F32), 0, keepdims=True),
        )

    zero = jnp.zeros((1, D), F32)
    dg, dc, db = lax.fori_loop(0, ROWS // STRIP, strip, (zero, zero, zero))
    sums[V_G1 : V_G1 + 1, :] = dg
    sums[V_C1 : V_C1 + 1, :] = dc
    sums[V_BO : V_BO + 1, :] = db


def output_back(W, dob, dctx):
    def tile(n):
        cols = at(n, TILE)
        dctx[:, cols] = dot(dob[...], columns(W, PLACE_O, cols.start, TILE)).astype(BF16)

    loop(D // TILE, tile)


def column_sums(source, sums, row):
    sums[row : row + 1, :] = jnp.sum(source[...].astype(F32), 0, keepdims=True)


def input_back(W, q, k, v, F):
    left = jnp.concatenate([q[...], k[...], v[...]], 1)
    right = jnp.concatenate([block(W, place) for place in (PLACE_Q, PLACE_K, PLACE_V)], 1)
    F[...] += dot(left, right, NT)


def to_down_order(dfb, perm, dfp):
    dfp[...] = dot(dfb[...], perm[...], NT).astype(BF16)


def permutation():
    r = np.arange(D)
    y, x, z, j = r // 192, r // 48 % 4, r // 12 % 4, r % 12
    p = np.zeros((D, D), np.float32)
    p[192 * z + 48 * x + 12 * y + j, r] = 1
    return p


MESH = pl.DeviceIdType.MESH
STEP = 10
ADAM_EPS = 1e-08
BETA_ONE = 0.9
BETA_TWO = 0.999
CLIP_NORM = 1.0
WEIGHT_DECAY = 0.01
ATTENTION_RATES = (0.02, 0.02, 0.04, 0.3)
HIDDEN_RATES = (0.04, 0.02)
VECTOR_RATE = 0.5
COPIES = 98
VECTORS = 12
SHARE = 6


class Net:
    def __init__(self, send_sem, recv_sem):
        self.send_sem, self.recv_sem, self.count, self.open = send_sem, recv_sem, 0, []

    def send(self, copies, whole):
        assert self.count < COPIES
        sems = dict(send_sem=self.send_sem.at[self.count], recv_sem=self.recv_sem.at[self.count])
        self.count += 1
        made = [
            pltpu.make_async_remote_copy(src_ref=a, dst_ref=b, device_id=(d,), device_id_type=MESH, **sems)
            for a, b, d in copies
        ]
        for copy in made:
            copy.start()
        group = pltpu.make_async_remote_copy(
            src_ref=whole, dst_ref=whole, device_id=(copies[0][2],), device_id_type=MESH, **sems
        )
        self.open.append(group)
        return group

    def sent(self, group):
        if any(one is group for one in self.open):
            group.wait_send()
            self.open = [one for one in self.open if one is not group]

    def close(self):
        for group in self.open:
            group.wait_send()
        self.open = []


def adam(master, first, second, gradient, rate, decay):
    first_new = BETA_ONE * first + (1.0 - BETA_ONE) * gradient
    second_new = BETA_TWO * second + (1.0 - BETA_TWO) * gradient * gradient
    first_hat = first_new / (1.0 - BETA_ONE**STEP)
    second_hat = second_new / (1.0 - BETA_TWO**STEP)
    master_new = master - rate * (first_hat / (jnp.sqrt(second_hat) + ADAM_EPS) + decay * master)
    return master_new, first_new, second_new


SCRATCH = dict(
    W=pltpu.VMEM((12, 4, 4, 48, D), BF16),
    G=pltpu.VMEM((SHARE, 4, 4, 48, D), BF16),
    pair_in=pltpu.VMEM((SHARE, 4, 4, 48, D), BF16),
    pair_out=pltpu.VMEM((8, 4, 4, 48, TILE), BF16),
    half_in=pltpu.VMEM((SHARE, 2, 2, 48, D), BF16),
    strip_in=pltpu.VMEM((SHARE, 3, 48, D), BF16),
    piece_in=pltpu.VMEM((3, SHARE, 16, D), BF16),
    first_out=pltpu.VMEM((SHARE, 8, D), F32),
    first_own=pltpu.VMEM((SHARE, 8, D), F32),
    first_in=pltpu.VMEM((SHARE, 8, D), F32),
    vec_own=pltpu.VMEM((8, LEN), F32),
    vec_in=pltpu.VMEM((8, LEN), F32),
    pieces=pltpu.VMEM((4, SHARE, 16, D), BF16),
    vec_pieces=pltpu.VMEM((4, 16, LEN), BF16),
    VT=pltpu.VMEM((4, 4, 48, LEN), BF16),
    line=pltpu.VMEM((48, D), F32),
    sums_in=pltpu.VMEM((2, 10, 8, D), F32),
    sums_out=pltpu.VMEM((2, 4, 8, D), F32),
    packed=pltpu.VMEM((4, 48, LEN), BF16),
    norm_out=pltpu.VMEM((3, 8, LEN), F32),
    norm_in=pltpu.VMEM((3, 7, 8, LEN), F32),
    V=pltpu.VMEM((16, D), F32),
    sums=pltpu.VMEM((16, D), F32),
    bias=pltpu.VMEM((SLOTS, LEN, LEN), F32),
    act=pltpu.VMEM((4, ROWS, D), BF16),
    p=pltpu.VMEM((SLOTS * PAIRS, 2 * LEN, LEN), BF16),
    A=pltpu.VMEM((ROWS, D), F32),
    F=pltpu.VMEM((ROWS, D), F32),
    FP=pltpu.VMEM((ROWS, D), F32),
    inv1=pltpu.VMEM((ROWS, 1), F32),
    y1b=pltpu.VMEM((ROWS, D), BF16),
    turned=pltpu.VMEM((2, D, ROWS), BF16),
    h=pltpu.VMEM((ROWS, FF), BF16),
    gp=pltpu.VMEM((ROWS, FF), BF16),
    dfb=pltpu.VMEM((ROWS, D), BF16),
    xb=pltpu.VMEM((ROWS, D), BF16),
    gb=pltpu.VMEM((ROWS, D), BF16),
    perm=pltpu.VMEM((D, D), BF16),
    att_w=pltpu.VMEM((6, 4, D), F32),
    hid_w=pltpu.VMEM((6, 2, FF), F32),
    vec_w=pltpu.VMEM((6, VECTORS), F32),
    load_sem=pltpu.SemaphoreType.DMA((16,)),
    store_sem=pltpu.SemaphoreType.DMA((16,)),
    send_sem=pltpu.SemaphoreType.DMA((COPIES,)),
    recv_sem=pltpu.SemaphoreType.DMA((COPIES,)),
)
NAMES = tuple(SCRATCH)


def step_kernel(
    x_hbm,
    g_hbm,
    perm_hbm,
    joined,
    half_lengths,
    att_hbm,
    hid_hbm,
    vec_hbm,
    out_hbm,
    grad_hbm,
    norm_out_ref,
    att_out,
    hid_out,
    vec_out,
    *scratch,
):
    s = dict(zip(NAMES, scratch))
    W, G, V = s["W"], s["G"], s["V"]
    xb, gb, perm = s["xb"], s["gb"], s["perm"]
    net = Net(s["send_sem"], s["recv_sem"])

    me = lax.axis_index("dp")
    c = lax.rem(me, 2)
    z = lax.rem(lax.div(me, 2), 4)
    x = lax.rem(lax.div(me, 8), 4)
    y = lax.div(me, 32)
    other = 1 - c

    def wrap(value):
        return lax.rem(value + 4, 4)

    def peer(axis, step):
        moved = {"x": x, "y": y, "z": z}
        moved[axis] = wrap(moved[axis] + step)
        return ((moved["y"] * 4 + moved["x"]) * 4 + moved["z"]) * 2 + c

    sibling = me + 1 - 2 * c

    def far_peer(step):
        return ((y * 4 + x) * 4 + wrap(z + step)) * 2 + other

    att_w, hid_w, vec_w = s["att_w"], s["hid_w"], s["vec_w"]
    masters_in = [
        pltpu.make_async_copy(source, target, s["load_sem"].at[9 + i])
        for i, (source, target) in enumerate(((att_hbm, att_w), (hid_hbm, hid_w), (vec_hbm, vec_w)))
    ]
    loads = []
    for i in range(SLOTS):
        loads.append(pltpu.make_async_copy(x_hbm.at[i], xb.at[pl.ds(i * LEN, LEN)], s["load_sem"].at[i]))
        loads.append(pltpu.make_async_copy(g_hbm.at[i], gb.at[pl.ds(i * LEN, LEN)], s["load_sem"].at[4 + i]))
    loads.append(pltpu.make_async_copy(perm_hbm, perm, s["load_sem"].at[8]))
    for copy in masters_in + loads:
        copy.start()

    barrier = pltpu.get_barrier_semaphore()
    partners = [sibling] + [peer(axis, step) for axis in "xyz" for step in (1, 2, 3)]
    partners += [far_peer(step) for step in (1, 2, 3)]
    for partner in partners:
        pl.semaphore_signal(barrier, inc=1, device_id=(partner,), device_id_type=MESH)

    for copy in masters_in:
        copy.wait()
    masters = [[att_w[:, 2 * core + l, :] for l in range(2)] for core in range(2)]
    for core in range(2):
        masters[core] += [hid_w[:, i, (2 * core + l) * D : (2 * core + l + 1) * D] for i in range(2) for l in range(2)]
    for l in range(SHARE):
        s["first_own"][l, 0:6, :] = jnp.where(c == 0, masters[0][l], masters[1][l])
        s["first_out"][l, 0:6, :] = jnp.where(c == 0, masters[1][l], masters[0][l])
    s["vec_own"][...] = jnp.zeros((8, LEN), F32)
    s["vec_own"][0:6, 0:VECTORS] = vec_w[...]
    line = s["line"]
    line[...] = jnp.zeros((48, D), F32)
    pl.semaphore_wait(barrier, len(partners))

    FIRST = {"x": "z", "y": "x", "z": "y"}
    SECOND = {"x": "y", "y": "z", "z": "x"}
    HERE = {"x": x, "y": y, "z": z}
    every = pl.ds(0, D)
    wide = pl.ds(0, 2 * TILE)
    part_cols = [pl.ds(part * TILE, TILE) for part in range(3)]
    third = part_cols[2]

    def span(count, size):
        for n in (4, 3, 2, 1):
            for k in (4, 3, 2, 1):
                if count % (n * k) == 0 and count // (n * k) <= 12:
                    return W.at[pl.ds(0, count // (n * k)), pl.ds(0, k), pl.ds(0, n), :, pl.ds(0, size)]
        raise ValueError

    def to_three(axis, copies):
        return [(source(step), target(step), peer(axis, step)) for source, target in copies for step in (1, 2, 3)]

    pair = [
        net.send([(a, b, sibling)], a)
        for a, b in (
            (s["first_out"].at[pl.ds(0, 2)], s["first_in"].at[pl.ds(0, 2)]),
            (s["vec_own"], s["vec_in"]),
            (s["first_out"].at[pl.ds(2, 4)], s["first_in"].at[pl.ds(2, 4)]),
        )
    ]
    fill_masks(joined, half_lengths, s["bias"])
    pieces, vec_pieces = s["pieces"], s["vec_pieces"]
    ATT = ((0, "x", wide), (1, "y", wide), (0, "z", third), (1, "z", third))
    p0, p1, p2 = part_cols
    PARTS = (
        ((2, "x", p0), (3, "y", p0), (4, "z", p0), (5, "z", p0)),
        ((2, "x", p1), (4, "x", p1), (3, "y", p1), (5, "z", p1)),
        ((2, "x", p2), (3, "y", p2), (5, "y", p2), (4, "z", p2)),
    )
    HID = (
        (2, "x", every),
        (3, "y", every),
        (4, "z", p0),
        (4, "x", p1),
        (4, "z", p2),
        (5, "z", pl.ds(0, 2 * TILE)),
        (5, "y", p2),
    )

    def turns(l, route):
        return (route == "z") != (l >= 4)

    def make_piece(l, route, cols):
        own, far = s["first_own"][l, 0:6, cols], s["first_in"][l, 0:6, cols]
        line[0:6, cols] = jnp.where(c == 0, own, far)
        line[6:12, cols] = jnp.where(c == 0, far, own)
        pieces[HERE[FIRST[route]], l, :, cols] = line[0:16, cols].astype(BF16)

    def send_pieces(some, units):
        copies = []
        for l, route, cols in some:
            near = pieces.at[HERE[FIRST[route]], l, :, cols]
            copies += [(near, near, peer(FIRST[route], step)) for step in (1, 2, 3)]
        return net.send(copies, span(units, D))

    pair[0].wait_recv()
    for some in ATT:
        make_piece(*some)
    att_pieces = send_pieces(ATT, 2)
    pair[1].wait_recv()
    own, far = s["vec_own"][0:6], s["vec_in"][0:6]
    line[0:6, 0:LEN] = jnp.where(c == 0, own, far)
    line[6:12, 0:LEN] = jnp.where(c == 0, far, own)
    vec_pieces[z] = line[0:16, 0:LEN].astype(BF16)
    near = vec_pieces.at[z]
    vec_copies = net.send([(near, near, peer("z", step)) for step in (1, 2, 3)], span(1, LEN))
    pair[2].wait_recv()
    for some in HID:
        make_piece(*some)

    VT, packed = s["VT"], s["packed"]

    def stage(ref, l, index):
        return ref.at[pl.ds(pl.multiple_of(index * 48, 16), 48), pl.ds((l // 2) * D, D)]

    def spread(l, route, cols):
        for i in range(4):
            line[12 * i : 12 * i + 12, cols] = pieces[i, l, :, cols].astype(F32)[0:12]
        rows = line[:, cols].astype(BF16)
        if route == "x":
            W[6 * c + l, y, x, :, cols] = rows
        elif route == "y":
            stage(s["gp"], l, z)[:, cols] = rows
        else:
            W[6 * c + l, z, x, :, cols] = rows

    def strips(some, units):
        copies = []
        for l, route, cols in some:
            if route == "x":
                near = W.at[6 * c + l, y, x, :, cols]
            elif route == "y":
                near = stage(s["gp"], l, z).at[:, cols]
            else:
                near = W.at[6 * c + l, z, x, :, cols]
            copies += [(near, near, peer(SECOND[route], step)) for step in (1, 2, 3)]
        return net.send(copies, span(3 * units, copies[0][0].shape[-1]))

    def order_strips(l, cols):
        size = cols.size
        for i in range(4):
            FP[48 * i : 48 * i + 48, 0:size] = stage(s["gp"], l, i)[:, cols].astype(F32)
        for i in range(4):
            for j in range(4):
                line[12 * j : 12 * j + 12, 0:size] = FP[48 * j + 12 * i : 48 * j + 12 * i + 12, 0:size]
            W[6 * c + l, y, i, :, cols] = line[:, 0:size].astype(BF16)

    def turn_rows(ref, place, cols):
        rows = ref[place, :, :, :, cols].reshape(D, cols.size)
        ref[place, :, :, :, cols] = dot(perm[...], rows).astype(BF16).reshape(4, 4, 48, cols.size)

    def region(ref, place, route, index, half, cols):
        part = pl.ds(0, 4) if half is None else pl.ds(2 * half, 2)
        if route == "x":
            return ref.at[place, part, index, :, cols]
        return ref.at[place, index, part, :, cols]

    def gather_start(some):
        copies = []
        for l, route, cols in some:
            near = region(W, 6 * c + l, route, HERE[route], None, cols)
            copies += [(near, near, peer(route, 1)), (near, near, peer(route, 3))]
        group = net.send(copies, span(8 * len(some), some[0][2].size))
        return some, group, [group]

    def gather_pass(state):
        some, group, sends = state
        group.wait_recv()
        copies = []
        for l, route, cols in some:
            low = region(W, 6 * c + l, route, wrap(HERE[route] - 1), 0, cols)
            high = region(W, 6 * c + l, route, wrap(HERE[route] + 1), 1, cols)
            copies += [(low, low, peer(route, 1)), (high, high, peer(route, 3))]
        group = net.send(copies, span(4 * len(some), some[0][2].size))
        return some, group, sends + [group]

    def gather_share(state):
        some, group, sends = state
        group.wait_recv()
        if any(turns(l, route) for l, route, _ in some):
            for sent in sends:
                net.sent(sent)
        copies = []
        for l, route, cols in some:
            if turns(l, route):
                turn_rows(W, 6 * c + l, cols)
            near = W.at[6 * c + l, :, :, :, cols]
            copies.append((near, near, sibling))
        return net.send(copies, span(16 * len(some), some[0][2].size))

    act, p = s["act"], s["p"]
    q, k, v, ctx = (act.at[i] for i in range(4))
    A, F, FP, inv1, y1b = s["A"], s["F"], s["FP"], s["inv1"], s["y1b"]
    h, gp, dfb, dfp, sums = s["h"], s["gp"], s["dfb"], y1b, s["sums"]
    turned = s["turned"]

    att_pieces.wait_recv()
    att_strips = []
    for group in (ATT[:1], ATT[1:2], ATT[2:]):
        for some in group:
            spread(*some)
        att_strips.append(strips(group, len(group)))
    hid_pieces = send_pieces(HID, 4)
    vec_copies.wait_recv()
    for i in range(4):
        line[12 * i : 12 * i + 12, 0:LEN] = vec_pieces[i].astype(F32)[0:12]
    VT[y, x] = line[:, 0:LEN].astype(BF16)
    near = VT.at[y, x]
    vec_strips = net.send([(near, near, peer("x", step)) for step in (1, 2, 3)], span(3, LEN))
    starts = {}
    att_strips[0].wait_recv()
    for part in range(2):
        starts["x", part] = gather_start([(0, "x", part_cols[part])])
    att_strips[1].wait_recv()
    order_strips(1, wide)
    for part in range(2):
        starts["y", part] = gather_start([(1, "y", part_cols[part])])
    att_strips[2].wait_recv()
    starts["t", 0] = gather_start(ATT[2:])
    hid_pieces.wait_recv()
    for some in HID:
        spread(*some)
    z_strips = [strips(PARTS[0][2:], 2)]
    y_strips = strips(HID[1:2], 1)
    x_strips = strips(HID[:1], 1)
    vec_strips.wait_recv()
    near = packed.at[y]
    packed[y] = sum(
        pltpu.roll(VT[y, i].astype(F32), 32 * i, 1) if i else VT[y, i].astype(F32) for i in range(4)
    ).astype(BF16)
    vec_last = net.send([(near, near, peer("y", step)) for step in (1, 2, 3)], span(3, LEN))
    for copy in loads:
        copy.wait()
    starts["x", 0] = gather_pass(starts["x", 0])
    starts["y", 0] = gather_pass(starts["y", 0])
    starts["x", 1] = gather_pass(starts["x", 1])
    starts["y", 1] = gather_pass(starts["y", 1])
    starts["t", 0] = gather_pass(starts["t", 0])
    flows = {}

    def begin(part, route):
        flows[part, route] = gather_start([some for some in PARTS[part] if some[1] == route])

    def passing(part, routes="xyz"):
        for route in routes:
            flows[part, route] = gather_pass(flows[part, route])

    def sharing(part, routes="xyz"):
        for route in routes:
            flows[part, route] = gather_share(flows[part, route])

    z_strips[0].wait_recv()
    begin(0, "z")
    z_strips.append(strips([(5, "z", p1), (4, "z", p2)], 2))
    x_rest = strips([(4, "x", p1)], 1)
    y_rest = strips([(5, "y", p2)], 1)
    x_strips.wait_recv()
    begin(0, "x")
    y_strips.wait_recv()
    order_strips(3, every)
    begin(0, "y")
    vec_last.wait_recv()
    net.sent(vec_strips)
    for i in range(4):
        block_i = packed[i].astype(F32)
        for j in range(4):
            VT[i, j] = (pltpu.roll(block_i, LEN - 32 * j, 1) if j else block_i).astype(BF16)
    V[...] = VT[...].reshape(D, LEN).astype(F32).T[0:16]
    shares = [gather_share(starts[key]) for key in (("x", 0), ("y", 0))]
    net.sent(att_strips[2])
    shares += [gather_share(starts[key]) for key in (("x", 1), ("y", 1), ("t", 0))]
    z_strips[1].wait_recv()
    begin(1, "z")
    x_rest.wait_recv()
    begin(1, "x")
    begin(1, "y")
    y_rest.wait_recv()
    order_strips(5, p2)
    for copy in shares:
        copy.wait_recv()
    qkv(W, V, xb, q, k, v)
    passing(0)
    begin(2, "z")
    begin(2, "x")
    begin(2, "y")
    attend(q, k, v, s["bias"], p, ctx)
    sharing(0)
    passing(1)
    first_norm(W, V, xb, ctx, A, inv1, F, y1b)
    turn(y1b, turned.at[1])
    net.sent(x_rest)
    sharing(1)
    passing(2)

    def arrived(part):
        for route in "xyz":
            flows[part, route].wait_recv()

    arrived(0)
    net.sent(att_strips[1])
    net.sent(y_strips)
    net.sent(y_rest)
    up(W, V, y1b, h, gp, 0)
    down_(W, h, FP, 0)
    sharing(2)
    arrived(1)
    up(W, V, y1b, h, gp, 1)
    down_(W, h, FP, 1)
    arrived(2)
    up(W, V, y1b, h, gp, 2)
    down_(W, h, FP, 2)
    second_norm(V, perm, FP, F, gb, gb, dfb, sums)
    stores = []
    for i in range(SLOTS):
        stores.append(pltpu.make_async_copy(gb.at[pl.ds(i * LEN, LEN)], out_hbm.at[i], s["store_sem"].at[i]))
        stores[-1].start()
    to_down_order(dfb, perm, dfp)
    dfpT = turned.at[0]
    y1T = turned.at[1]
    turn(dfp, dfpT)

    pair_in, pair_out = s["pair_in"], s["pair_out"]
    G_half = s["half_in"]
    G_block = pair_in
    slots = [None] * 8

    def send_tiles(tiles):
        for slot, _, _, _ in tiles:
            if slots[slot] is not None:
                net.sent(slots[slot])
        values = [value() for _, _, _, value in tiles]
        for (slot, _, _, _), value in zip(tiles, values):
            pair_out[slot] = value.astype(BF16).reshape(4, 4, 48, TILE)
        group = net.send(
            [(pair_out.at[slot], pair_in.at[l, :, :, :, cols], sibling) for slot, l, cols, _ in tiles],
            span(16 * len(tiles), TILE),
        )
        for slot, _, _, _ in tiles:
            slots[slot] = group
        return group

    def add_into(ref, index, *others):
        total = ref[index].astype(F32)
        for other_ref, other_index in others:
            total = total + other_ref[other_index].astype(F32)
        ref[index] = total.astype(BF16)

    def cell(l, route, index, i, cols):
        return (l, i, index, slice(None), cols) if route == "x" else (l, index, i, slice(None), cols)

    def reduce_start(some):
        copies = []
        for l, route, cols in some:
            across = wrap(HERE[route] + 2)
            for half, step in ((0, 1), (1, 3)):
                copies.append((region(G, l, route, across, half, cols), G_half.at[l, half, :, :, cols], peer(route, step)))
        return some, net.send(copies, span(4 * len(some), TILE))

    def reduce_pass(state):
        some, group = state
        group.wait_recv()
        copies = []
        for l, route, cols in some:
            here = HERE[route]
            for i in range(2):
                add_into(G, cell(l, route, wrap(here + 1), i, cols), (G_half, (l, 0, i, slice(None), cols)))
                add_into(G, cell(l, route, wrap(here - 1), 2 + i, cols), (G_half, (l, 1, i, slice(None), cols)))
            for half, step in ((0, 1), (1, 3)):
                copies.append(
                    (region(G, l, route, wrap(here + step), None, cols), G_block.at[l, half, :, :, cols], peer(route, step))
                )
        return some, net.send(copies, span(8 * len(some), TILE))

    strip_in = s["strip_in"]

    def strip_place(l, route, moved):
        return (l, moved, x) if route == "x" else (l, z, moved)

    def reduce_end(state):
        some, group = state
        group.wait_recv()
        copies = []
        for l, route, cols in some:
            for i in range(4):
                add_into(
                    G,
                    cell(l, route, HERE[route], i, cols),
                    (G_block, (l, 0, i, slice(None), cols)),
                    (G_block, (l, 1, i, slice(None), cols)),
                )
            if route == "y":
                for i in range(4):
                    FP[48 * i : 48 * i + 48, 0:TILE] = G[l, y, i, :, cols].astype(F32)
                for j in range(4):
                    for i in range(4):
                        line[12 * i : 12 * i + 12, 0:TILE] = FP[48 * i + 12 * j : 48 * i + 12 * j + 12, 0:TILE]
                    stage(h, l, j)[:, cols] = line[:, 0:TILE].astype(BF16)
            for step in (1, 2, 3):
                target = wrap(HERE[SECOND[route]] + step)
                if route == "y":
                    source = stage(h, l, target).at[:, cols]
                else:
                    source = G.at[strip_place(l, route, target) + (slice(None), cols)]
                copies.append((source, strip_in.at[l, step - 1, :, cols], peer(SECOND[route], step)))
        return some, net.send(copies, span(3 * len(some), TILE))

    piece_out, piece_in = pieces, s["piece_in"]

    def strips_sum(state):
        some, group = state
        group.wait_recv()
        for l, route, cols in some:
            if route == "y":
                own = stage(h, l, z)[:, cols]
            else:
                own = G[strip_place(l, route, HERE[SECOND[route]]) + (slice(None), cols)]
            total = own.astype(F32)
            for i in range(3):
                total = total + strip_in[l, i, :, cols].astype(F32)
            line[:, 0:TILE] = total
            gap = jnp.zeros((4, TILE), F32)
            for i in range(4):
                rows = jnp.concatenate([line[12 * i : 12 * i + 12, 0:TILE], gap], 0)
                piece_out[i, l, :, cols] = rows.astype(BF16)

    def pieces_out(some, units):
        copies = []
        for l, route, cols in some:
            for step in (1, 2, 3):
                source = piece_out.at[wrap(HERE[FIRST[route]] + step), l, :, cols]
                copies.append((source, piece_in.at[step - 1, l, :, cols], peer(FIRST[route], step)))
        return net.send(copies, span(units, D))

    rows_out, rows_own, rows_in = s["first_out"], s["first_own"], s["first_in"]

    def pieces_sum(l, route, cols):
        total = piece_out[HERE[FIRST[route]], l, :, cols].astype(F32)
        for i in range(3):
            total = total + piece_in[i, l, :, cols].astype(F32)
        line[0:16, cols] = total
        top, bottom = line[0:6, cols], line[6:12, cols]
        rows_own[l, 0:6, cols] = jnp.where(c == 0, top, bottom)
        rows_out[l, 0:6, cols] = jnp.where(c == 0, bottom, top)
        return jnp.sum(top * top + bottom * bottom, keepdims=True)

    def hidden_slopes(core, part):
        places = [pl.ds(pl.multiple_of((2 * core + e) * D + part * TILE, LEN), TILE) for e in range(2)]
        slopes = []
        for e in range(2):
            dh = dot(dfp[...], columns(W, 6 * core + 4 + e, part * TILE, TILE))
            du = (dh * gp[:, places[e]].astype(F32)).astype(BF16)
            slopes.append(du)
            sums[pl.ds(V_B1 + 2 * core + e, 1), part_cols[part]] = jnp.sum(du.astype(F32), 0, keepdims=True)
        return places, slopes

    def keep_tiles(group, tiles):
        group.wait_recv()
        for l, cols, value in tiles:
            total = value() + pair_in[l, :, :, :, cols].reshape(D, TILE).astype(F32)
            G[l, :, :, :, cols] = total.astype(BF16).reshape(4, 4, 48, TILE)

    def hidden_tiles(places, slopes, cols):
        tiles = [(4 + e, cols, lambda e=e: dot(dfpT[...], h[:, places[e]])) for e in range(2)]
        return tiles + [(2 + e, cols, lambda e=e: dot(y1T[...], slopes[e])) for e in range(2)]

    shared = {}

    def others(part):
        places, slopes = hidden_slopes(other, part)
        tiles = hidden_tiles(places, slopes, part_cols[part])
        shared[part] = send_tiles([(4 * (part % 2) + i,) + tile for i, tile in enumerate(tiles)])
        for e in range(2):
            gp[:, places[e]] = slopes[e]

    def own_slopes(part):
        places, slopes = hidden_slopes(c, part)
        for e in range(2):
            gp[:, places[e]] = slopes[e]

    def own_tiles(part):
        places = [pl.ds(pl.multiple_of((2 * c + e) * D + part * TILE, LEN), TILE) for e in range(2)]
        keep_tiles(shared[part], hidden_tiles(places, [gp[:, place] for place in places], part_cols[part]))
        for l, route, cols in PARTS[part]:
            if turns(l, route):
                turn_rows(G, l, cols)
        return reduce_start(PARTS[part])

    others(0)
    others(1)
    own_slopes(0)
    flows[0] = own_tiles(0)
    others(2)
    own_slopes(1)
    flows[1] = own_tiles(1)
    flows[0] = reduce_pass(flows[0])
    own_slopes(2)
    flows[2] = own_tiles(2)
    first_back_product(W, gp, F)
    flows[1] = reduce_pass(flows[1])
    first_back(V, A, inv1, F, dfb, sums)
    flows[2] = reduce_pass(flows[2])

    sums[VECTORS:16, :] = jnp.zeros((16 - VECTORS, D), F32)
    sums_in, sums_out = s["sums_in"], s["sums_out"]

    def sums_step(place, stage_, group, axis):
        if group is None:
            total = sums[8 * place : 8 * place + 8, :]
        else:
            total = sums_out[place, stage_ - 1]
            group.wait_recv()
            for i in range(1 if stage_ == 1 else 3):
                total = total + sums_in[place, 0 if stage_ == 1 else 3 * stage_ - 5 + i]
        if axis is None:
            return total
        sums_out[place, stage_] = total
        near = sums_out.at[place, stage_]
        if stage_ == 0:
            return net.send([(near, sums_in.at[place, 0], sibling)], near)
        base = 3 * stage_ - 3
        return net.send(
            [(near, sums_in.at[place, base + step], peer(axis, step)) for step in (1, 2, 3)],
            sums_in.at[place, pl.ds(0, 3)],
        )

    up_sums = sums_step(1, 0, None, "sibling")
    doT = turned.at[1]
    turn(dfb, doT)
    output_back(W, dfb, y1b)
    up_sums = sums_step(1, 1, up_sums, "z")
    flows[0] = reduce_end(flows[0])
    attend_back(q, k, v, p, y1b)
    turn(xb, turned.at[0])
    flows[1] = reduce_end(flows[1])

    def projection_grad(core, l, n):
        left = core if l == 1 else 0
        return dot(turned[left], act[2 * core + l, :, n * TILE : (n + 1) * TILE])

    def projection_tiles(core, n):
        return [(l, part_cols[n], lambda l=l: projection_grad(core, l, n)) for l in (0, 1)]

    ORDER = (2, 0, 1)
    for n in ORDER:
        shared["p", n] = send_tiles([(2 * n + i,) + tile for i, tile in enumerate(projection_tiles(other, n))])
    column_sums(q, sums, V_BQ)
    column_sums(v, sums, V_BV)
    first_sums = sums_step(0, 0, None, "sibling")
    last = []
    for n in ORDER:
        keep_tiles(shared["p", n], projection_tiles(c, n))
        if n == 2:
            for l in (0, 1):
                turn_rows(G, l, third)
        last.append(reduce_start([(l, "z" if n == 2 else "xy"[l], part_cols[n]) for l in (0, 1)]))
    first_sums = sums_step(0, 1, first_sums, "z")
    up_sums = sums_step(1, 2, up_sums, "x")
    last[0] = reduce_pass(last[0])
    flows[2] = reduce_end(flows[2])
    last[1] = reduce_pass(last[1])
    first_sums = sums_step(0, 2, first_sums, "x")
    last[2] = reduce_pass(last[2])
    input_back(W, q, k, v, F)
    for i in range(SLOTS):
        stores.append(pltpu.make_async_copy(F.at[pl.ds(i * LEN, LEN)], grad_hbm.at[i], s["store_sem"].at[4 + i]))
        stores[-1].start()
    for group in pair + [att_pieces, hid_pieces]:
        net.sent(group)
    strips_sum(flows[0])
    for n in range(3):
        last[n] = reduce_end(last[n])
    first_sums = sums_step(0, 3, first_sums, "y")
    up_sums = sums_step(1, 3, up_sums, "y")
    strips_sum(flows[1])
    strips_sum(flows[2])
    hid_pieces = pieces_out(HID, 4)
    for n in range(3):
        strips_sum(last[n])
    att_pieces = pieces_out(ATT, 2)
    hid_pieces.wait_recv()
    squares = jnp.zeros((1, 1), F32)
    for some in HID:
        squares = squares + pieces_sum(*some)
    rows_copies = [net.send([(rows_out.at[pl.ds(2, 4)], rows_in.at[pl.ds(2, 4)], sibling)], rows_out.at[pl.ds(2, 4)])]
    vec_total = jnp.concatenate([sums_step(0, 4, first_sums, None), sums_step(1, 4, up_sums, None)], 0)
    place = lax.broadcasted_iota(jnp.int32, (8, D), 1) - 6 * me
    pick = (place == lax.broadcasted_iota(jnp.int32, (8, D), 0)).astype(BF16)
    vec_grad = jnp.zeros((8, 16), F32)
    for _ in range(3):
        low = vec_total.astype(BF16)
        vec_grad = vec_grad + dot(pick, low, NT)
        vec_total = vec_total - low.astype(F32)
    vec_grad = vec_grad[0:6, 0:VECTORS]
    squares = squares + jnp.sum(vec_grad * vec_grad, keepdims=True)
    att_pieces.wait_recv()
    for some in ATT:
        squares = squares + pieces_sum(*some)
    norm_out, norm_in = s["norm_out"], s["norm_in"]
    norm_out[0] = jnp.broadcast_to(squares, (8, LEN))
    norm_group = net.send(
        [(norm_out.at[0], norm_in.at[0, step - 1], peer("x", step)) for step in (1, 2, 3)], norm_in.at[0, pl.ds(0, 3)]
    )
    rows_copies.append(
        net.send([(rows_out.at[pl.ds(0, 2)], rows_in.at[pl.ds(0, 2)], sibling)], rows_out.at[pl.ds(0, 2)])
    )
    for copy in rows_copies:
        copy.wait_recv()
    att_grad, hid_grad, vec_grad_at = att_w, hid_w, vec_w
    vec_grad_at[...] = vec_grad
    for core in range(2):
        for l in range(SHARE):
            value = jnp.where(c == core, rows_own[l, 0:6], rows_in[l, 0:6])
            if l < 2:
                att_grad[:, 2 * core + l, :] = value
            else:
                i, j = (l - 2) // 2, 2 * core + l % 2
                hid_grad[:, i, j * D : (j + 1) * D] = value
    for i, (source, target) in enumerate(((att_grad, att_out), (hid_grad, hid_out), (vec_grad_at, vec_out))):
        stores.append(pltpu.make_async_copy(source, target, s["store_sem"].at[8 + i]))
        stores[-1].start()

    def norm_step(index, group, count):
        group.wait_recv()
        total = norm_out[index]
        for i in range(count):
            total = total + norm_in[index, i]
        return total

    norm_out[1] = norm_step(0, norm_group, 3)
    norm_group = net.send(
        [(norm_out.at[1], norm_in.at[1, step - 1], peer("y", step)) for step in (1, 2, 3)], norm_in.at[1, pl.ds(0, 3)]
    )
    norm_out[2] = norm_step(1, norm_group, 3)
    copies = [(norm_out.at[2], norm_in.at[2, 0], sibling)]
    for step in (1, 2, 3):
        copies.append((norm_out.at[2], norm_in.at[2, step], peer("z", step)))
        copies.append((norm_out.at[2], norm_in.at[2, 3 + step], far_peer(step)))
    norm_group = net.send(copies, norm_in.at[2])
    norm = jnp.sqrt(norm_step(2, norm_group, 7))
    norm_out_ref[...] = norm[0:1, 0:1]
    for copy in stores:
        copy.wait()
    net.close()


def rates(values, shape):
    index = lax.broadcasted_iota(jnp.int32, shape, 1)
    rate = jnp.full(shape, values[0], F32)
    for i, value in enumerate(values[1:]):
        rate = jnp.where(index == i + 1, value, rate)
    return rate


def update_kernel(out_in, grad_in, norm, *refs):
    sources, (out_hbm, grad_hbm), targets = refs[:12], refs[12:14], refs[14:23]
    out_at, grad_at = refs[23:25]
    held, sems = refs[25:37], refs[37]
    loads = [pltpu.make_async_copy(a, b, sems.at[i]) for i, (a, b) in enumerate(zip(sources, held))]
    passing = [pltpu.make_async_copy(out_in, out_at, sems.at[12]), pltpu.make_async_copy(grad_in, grad_at, sems.at[13])]
    for copy in loads + passing:
        copy.start()
    stores = [pltpu.make_async_copy(out_at, out_hbm, sems.at[14]), pltpu.make_async_copy(grad_at, grad_hbm, sems.at[15])]
    factor = CLIP_NORM / jnp.maximum(norm[...], CLIP_NORM)
    settings = (
        (rates(ATTENTION_RATES, (6, 4, D)), WEIGHT_DECAY),
        (rates(HIDDEN_RATES, (6, 2, FF)), WEIGHT_DECAY),
        (VECTOR_RATE, 0.0),
    )
    for i in (1, 0, 2):
        for j in (i, 3 + 3 * i, 4 + 3 * i, 5 + 3 * i):
            loads[j].wait()
        state = held[3 + 3 * i : 6 + 3 * i]
        new = adam(state[0][...], state[1][...], state[2][...], held[i][...] * factor, *settings[i])
        for j in range(3):
            state[j][...] = new[j]
            stores.append(pltpu.make_async_copy(state[j], targets[3 * i + j], sems.at[16 + 3 * i + j]))
        if i == 1:
            for load, copy in zip(passing, stores):
                load.wait()
                copy.start()
        for copy in stores[-3:]:
            copy.start()
    for copy in stores:
        copy.wait()


def on_device(
    inputs,
    cotangent,
    joined,
    half_lengths,
    attention_master,
    attention_first,
    attention_second,
    hidden_master,
    hidden_first,
    hidden_second,
    vector_master,
    vector_first,
    vector_second,
):
    any_space = pl.BlockSpec(memory_space=pl.ANY)
    vmem = pl.BlockSpec(memory_space=pltpu.VMEM)
    smem = pl.BlockSpec(memory_space=pltpu.SMEM)
    like = lambda a: jax.ShapeDtypeStruct(a.shape, a.dtype)
    swap = lambda a: jnp.transpose(a, (1, 0, 2))
    attention = [swap(a) for a in (attention_master, attention_first, attention_second)]
    hidden = [swap(a) for a in (hidden_master, hidden_first, hidden_second)]
    vectors = [a.T for a in (vector_master, vector_first, vector_second)]
    params = attention + hidden + vectors
    out_like = jax.ShapeDtypeStruct(inputs.shape, BF16)
    grad_like = jax.ShapeDtypeStruct(inputs.shape, F32)
    results = pl.pallas_call(
        step_kernel,
        out_shape=(
            out_like,
            grad_like,
            jax.ShapeDtypeStruct((1, 1), F32),
            like(attention[0]),
            like(hidden[0]),
            like(vectors[0]),
        ),
        in_specs=[any_space] * 3 + [smem] * 2 + [any_space] * 3,
        out_specs=(any_space, any_space, vmem) + (any_space,) * 3,
        scratch_shapes=list(SCRATCH.values()),
        compiler_params=pltpu.CompilerParams(collective_id=0, has_side_effects=True, vmem_limit_bytes=64 << 20),
        cost_estimate=pl.CostEstimate(flops=22 * 10**9, bytes_accessed=6 * 10**6, transcendentals=4 * 10**6),
    )(
        inputs,
        cotangent,
        jnp.asarray(permutation(), BF16),
        joined.T,
        jnp.transpose(half_lengths, (1, 2, 0)),
        attention[0],
        hidden[0],
        vectors[0],
    )
    outs = pl.pallas_call(
        update_kernel,
        out_shape=(out_like, grad_like) + tuple(like(a) for a in params),
        in_specs=[any_space] * 2 + [vmem] + [any_space] * 12,
        out_specs=(any_space,) * 11,
        scratch_shapes=[
            pltpu.VMEM(inputs.shape, BF16),
            pltpu.VMEM(inputs.shape, F32),
            *[pltpu.VMEM(a.shape, F32) for a in (attention[0], hidden[0], vectors[0], *params)],
            pltpu.SemaphoreType.DMA((25,)),
        ],
        cost_estimate=pl.CostEstimate(flops=2 * 10**6, bytes_accessed=7 * 10**6, transcendentals=10**5),
    )(*results, *params)
    output, input_grad, *new = outs
    norm = results[2].reshape(())
    return (output, input_grad, norm, *[swap(a) for a in new[:6]], *[a.T for a in new[6:]])


def solution(mesh):
    shard = P(None, "dp", None)
    flat = P(None, "dp")
    return jax.shard_map(
        on_device,
        mesh=mesh,
        in_specs=(shard, shard, flat, shard, shard, shard, shard, shard, shard, shard, flat, flat, flat),
        out_specs=(shard, shard, P(), shard, shard, shard, shard, shard, shard, flat, flat, flat),
        check_vma=False,
    )
```

```python
import functools
import jax
import jax.numpy as jnp
import numpy as np
from jax import lax
from jax.experimental import pallas as pl
from jax.experimental.pallas import tpu as pltpu
from jax.sharding import PartitionSpec as P

F32 = jnp.float32
BF16 = jnp.bfloat16
D = 768
FF = 3072
ROWS = 512
SLOTS = 4
LEN = 128
PAIRS = 6
TILE = 256
NORM_EPS = 1e-05
MASKED = -1e30
NN = (((1,), (0,)), ((), ()))
NT = (((1,), (1,)), ((), ()))
TN = (((0,), (0,)), ((), ()))
PLACE_Q, PLACE_K, PLACE_V, PLACE_O = 0, 1, 6, 7
PLACE_UP = (2, 3, 8, 9)
PLACE_DOWN = (4, 5, 10, 11)
V_BQ, V_BV, V_BO, V_G1, V_C1, V_G2, V_C2, V_B2, V_B1 = range(9)


def dot(a, b, dims=NN):
    return lax.dot_general(a, b, dims, preferred_element_type=F32)


def block(ref, place):
    return ref[place].reshape(D, D)


def columns(ref, place, start, size):
    return ref[place, :, :, :, pl.ds(start, size)].reshape(D, size)


def put_columns(ref, place, start, size, value):
    ref[place, :, :, :, pl.ds(start, size)] = value.reshape(4, 4, 48, size)


def loop(count, body):
    lax.fori_loop(0, count, lambda i, c: (body(i), c)[1], 0)


def at(i, size):
    return pl.ds(pl.multiple_of(i * size, size), size)


def qkv(W, V, xb, q, k, v):
    x = xb[...]
    for n in range(D // TILE):
        cols = pl.ds(n * TILE, TILE)
        q[:, cols] = ((dot(x, columns(W, PLACE_Q, n * TILE, TILE)) + V[V_BQ, cols]).astype(BF16) * 0.125).astype(BF16)
        k[:, cols] = dot(x, columns(W, PLACE_K, n * TILE, TILE)).astype(BF16)
        v[:, cols] = (dot(x, columns(W, PLACE_V, n * TILE, TILE)) + V[V_BV, cols]).astype(BF16)


def halves(value):
    lane = lax.broadcasted_iota(jnp.int32, value.shape, 1)
    zero = jnp.zeros_like(value)
    return jnp.concatenate([jnp.where(lane < 64, value, zero), jnp.where(lane < 64, zero, value)], 0)


def joined_halves(value):
    lane = lax.broadcasted_iota(jnp.int32, (LEN, LEN), 1)
    return jnp.where(lane < 64, value[:LEN], value[LEN:])


def fill_masks(joined, half_lengths, bias):
    query = lax.broadcasted_iota(jnp.int32, (LEN, LEN), 0)
    key = lax.broadcasted_iota(jnp.int32, (LEN, LEN), 1)
    for slot in range(SLOTS):
        is_joined = joined[0, slot]
        low = half_lengths[0, 0, slot]
        high = half_lengths[0, 1, slot]
        upper = (key >= 64).astype(jnp.int32)
        limit = is_joined * (64 + high) + (1 - is_joined) * (upper * (64 + high) + (1 - upper) * low)
        apart = (1 - is_joined) * jnp.abs((query >= 64).astype(jnp.int32) - upper)
        bias[slot] = jnp.where((key < limit) & (apart == 0), 0.0, MASKED)


GROUP = 6


def attend(q, k, v, bias, p, ctx):
    def units(slot):
        rows = at(slot, LEN)
        m = bias[slot]
        hidden = jnp.concatenate([m, m], 0) < 0
        cols = [pl.ds(pair * LEN, LEN) for pair in range(PAIRS)]
        for start in range(0, PAIRS, GROUP):
            some = range(start, start + GROUP)
            s = [dot(halves(q[rows, cols[i]]), k[rows, cols[i]], NT) for i in some]
            values = [v[rows, cols[i]] for i in some]
            s = [jnp.where(hidden, MASKED, one) for one in s]
            e = [jnp.exp(one - jnp.max(one, -1, keepdims=True)) for one in s]
            low = [(one * (1.0 / jnp.sum(one, -1, keepdims=True))).astype(BF16) for one in e]
            out = [joined_halves(dot(one, value)).astype(BF16) for one, value in zip(low, values)]
            for i, one, result in zip(some, low, out):
                p[slot * PAIRS + i] = one
                ctx[rows, cols[i]] = result

    loop(SLOTS, units)


def attend_back(q, k, v, p, dctx):
    def units(slot):
        rows = at(slot, LEN)
        cols = [pl.ds(pair * LEN, LEN) for pair in range(PAIRS)]
        for start in range(0, PAIRS, BACK_GROUP):
            some = range(start, start + BACK_GROUP)
            low = [p[slot * PAIRS + i] for i in some]
            two = [halves(dctx[rows, cols[i]]) for i in some]
            q2 = [halves(q[rows, cols[i]]) for i in some]
            keys = [k[rows, cols[i]] for i in some]
            dp = [dot(a, v[rows, cols[i]], NT) for a, i in zip(two, some)]
            dv = [dot(a, b, TN) for a, b in zip(low, two)]
            full = [a.astype(F32) for a in low]
            ds = [(a * (b - jnp.sum(a * b, -1, keepdims=True))).astype(BF16) for a, b in zip(full, dp)]
            dq = [joined_halves(dot(a, b)) * 0.125 for a, b in zip(ds, keys)]
            dk = [dot(a, b, TN) for a, b in zip(ds, q2)]
            for n, i in enumerate(some):
                v[rows, cols[i]] = dv[n].astype(BF16)
                q[rows, cols[i]] = dq[n].astype(BF16)
                k[rows, cols[i]] = dk[n].astype(BF16)

    loop(SLOTS, units)


BACK_GROUP = 6


STRIP = 256


def first_norm(W, V, xb, ctx, A, inv1, F, y1b):
    A[...] = dot(ctx[...], block(W, PLACE_O), NT)

    def strip(i):
        rows = at(i, STRIP)
        a = xb[rows, :].astype(F32) + A[rows, :] + V[V_BO : V_BO + 1, :]
        center = a - jnp.mean(a, -1, keepdims=True)
        inverse = lax.rsqrt(jnp.mean(center * center, -1, keepdims=True) + NORM_EPS)
        n = center * inverse
        A[rows, :] = n
        inv1[rows, :] = inverse
        y = n * V[V_G1 : V_G1 + 1, :] + V[V_C1 : V_C1 + 1, :]
        y1b[rows, :] = y.astype(BF16)
        F[rows, :] = y + V[V_B2 : V_B2 + 1, :]

    loop(ROWS // STRIP, strip)


def gelu_parts(u):
    e = jnp.exp(-0.5 * (u * u))
    t = pl.reciprocal(1.0 + 0.23164190 * jnp.abs(u), approx=True)
    poly = ((((0.5307027145 * t - 0.726576013) * t + 0.7107068705) * t - 0.142248368) * t + 0.127414796) * t
    tail = poly * e
    cdf = jnp.where(u >= 0, 1.0 - tail, tail)
    return u * cdf, cdf + (u * 0.3989422804014327) * e


def up(W, V, y1b, h, gp, part):
    for j, place in enumerate(PLACE_UP):
        cols = pl.ds(j * D + part * TILE, TILE)
        u = dot(y1b[...], columns(W, place, part * TILE, TILE)) + V[V_B1 + j : V_B1 + j + 1, pl.ds(part * TILE, TILE)]
        value, slope = gelu_parts(u)
        h[:, cols] = value.astype(BF16)
        gp[:, cols] = slope.astype(BF16)


def down_(W, h, FP, part):
    left = jnp.concatenate([h[:, pl.ds(j * D + part * TILE, TILE)] for j in range(4)], 1)
    right = jnp.concatenate([columns(W, place, part * TILE, TILE) for place in PLACE_DOWN], 1)
    total = dot(left, right, NT)
    FP[...] = total if part == 0 else FP[...] + total


def second_norm(V, perm, FP, F, gb, outb, dfb, sums):
    F[...] += dot(FP[...].astype(BF16), perm[...])

    def strip(i, carry):
        dg, dc, db = carry
        rows = at(i, STRIP)
        z = F[rows, :]
        center = z - jnp.mean(z, -1, keepdims=True)
        inverse = lax.rsqrt(jnp.mean(center * center, -1, keepdims=True) + NORM_EPS)
        n = center * inverse
        gain = V[V_G2 : V_G2 + 1, :]
        g = gb[rows, :].astype(F32)
        outb[rows, :] = (n * gain + V[V_C2 : V_C2 + 1, :]).astype(BF16)
        gn = g * n
        e = g * gain
        dz = inverse * (e - jnp.mean(e, -1, keepdims=True) - n * jnp.mean(gn * gain, -1, keepdims=True))
        low = dz.astype(BF16)
        F[rows, :] = dz
        dfb[rows, :] = low
        return (
            dg + jnp.sum(gn, 0, keepdims=True),
            dc + jnp.sum(g, 0, keepdims=True),
            db + jnp.sum(low.astype(F32), 0, keepdims=True),
        )

    zero = jnp.zeros((1, D), F32)
    dg, dc, db = lax.fori_loop(0, ROWS // STRIP, strip, (zero, zero, zero))
    sums[V_G2 : V_G2 + 1, :] = dg
    sums[V_C2 : V_C2 + 1, :] = dc
    sums[V_B2 : V_B2 + 1, :] = db


def turn(source, target):
    for i in range(ROWS // LEN):
        target[:, i * LEN : (i + 1) * LEN] = source[i * LEN : (i + 1) * LEN, :].T


def first_back_product(W, gp, F):
    for i in range(ROWS // TILE):
        rows = pl.ds(i * TILE, TILE)
        F[rows, :] += dot(gp[rows, :], jnp.concatenate([block(W, place) for place in PLACE_UP], 1), NT)


def first_back(V, A, inv1, F, dob, sums):
    def strip(i, carry):
        dg, dc, db = carry
        rows = at(i, STRIP)
        dy = F[rows, :]
        n = A[rows, :]
        gain = V[V_G1 : V_G1 + 1, :]
        dyn = dy * n
        e = dy * gain
        da = inv1[rows, :] * (e - jnp.mean(e, -1, keepdims=True) - n * jnp.mean(dyn * gain, -1, keepdims=True))
        low = da.astype(BF16)
        F[rows, :] = da
        dob[rows, :] = low
        return (
            dg + jnp.sum(dyn, 0, keepdims=True),
            dc + jnp.sum(dy, 0, keepdims=True),
            db + jnp.sum(low.astype(F32), 0, keepdims=True),
        )

    zero = jnp.zeros((1, D), F32)
    dg, dc, db = lax.fori_loop(0, ROWS // STRIP, strip, (zero, zero, zero))
    sums[V_G1 : V_G1 + 1, :] = dg
    sums[V_C1 : V_C1 + 1, :] = dc
    sums[V_BO : V_BO + 1, :] = db


def output_back(W, dob, dctx):
    def tile(n):
        cols = at(n, TILE)
        dctx[:, cols] = dot(dob[...], columns(W, PLACE_O, cols.start, TILE)).astype(BF16)

    loop(D // TILE, tile)


def column_sums(source, sums, row):
    sums[row : row + 1, :] = jnp.sum(source[...].astype(F32), 0, keepdims=True)


def input_back(W, q, k, v, F):
    for i in range(ROWS // TILE):
        rows = pl.ds(i * TILE, TILE)
        left = jnp.concatenate([q[rows, :], k[rows, :], v[rows, :]], 1)
        right = jnp.concatenate([block(W, place) for place in (PLACE_Q, PLACE_K, PLACE_V)], 1)
        F[rows, :] += dot(left, right, NT)


def to_down_order(dfb, perm, dfp):
    dfp[...] = dot(dfb[...], perm[...], NT).astype(BF16)


def permutation():
    r = np.arange(D)
    y, x, z, j = r // 192, r // 48 % 4, r // 12 % 4, r % 12
    p = np.zeros((D, D), np.float32)
    p[192 * z + 48 * x + 12 * y + j, r] = 1
    return p


MESH = pl.DeviceIdType.MESH
STEP = 10
ADAM_EPS = 1e-08
BETA_ONE = 0.9
BETA_TWO = 0.999
CLIP_NORM = 1.0
WEIGHT_DECAY = 0.01
ATTENTION_RATES = (0.02, 0.02, 0.04, 0.3)
HIDDEN_RATES = (0.04, 0.02)
VECTOR_RATE = 0.5
COPIES = 80
VECTORS = 12
SHARE = 6


class Net:
    def __init__(self, send_sem, recv_sem):
        self.send_sem, self.recv_sem, self.count, self.open = send_sem, recv_sem, 0, []

    def send(self, copies, whole):
        assert self.count < COPIES
        sems = dict(send_sem=self.send_sem.at[self.count], recv_sem=self.recv_sem.at[self.count])
        self.count += 1
        made = [
            pltpu.make_async_remote_copy(src_ref=a, dst_ref=b, device_id=(d,), device_id_type=MESH, **sems)
            for a, b, d in copies
        ]
        for copy in made:
            copy.start()
        group = pltpu.make_async_remote_copy(
            src_ref=whole, dst_ref=whole, device_id=(copies[0][2],), device_id_type=MESH, **sems
        )
        self.open.append(group)
        return group

    def sent(self, group):
        if any(one is group for one in self.open):
            group.wait_send()
            self.open = [one for one in self.open if one is not group]

    def close(self):
        for group in self.open:
            group.wait_send()
        self.open = []


def adam(master, first, second, gradient, rate, decay):
    first_new = BETA_ONE * first + (1.0 - BETA_ONE) * gradient
    second_new = BETA_TWO * second + (1.0 - BETA_TWO) * gradient * gradient
    first_hat = first_new / (1.0 - BETA_ONE**STEP)
    second_hat = second_new / (1.0 - BETA_TWO**STEP)
    master_new = master - rate * (first_hat / (jnp.sqrt(second_hat) + ADAM_EPS) + decay * master)
    return master_new, first_new, second_new


SCRATCH = dict(
    W=pltpu.VMEM((12, 4, 4, 48, D), BF16),
    G=pltpu.VMEM((SHARE, 4, 4, 48, D), BF16),
    pair_in=pltpu.VMEM((SHARE, 4, 4, 48, D), BF16),
    pair_out=pltpu.VMEM((8, 4, 4, 48, TILE), BF16),
    half_in=pltpu.VMEM((4, 2, 2, 48, D), BF16),
    strip_in=pltpu.VMEM((SHARE, 3, 48, D), BF16),
    piece_in=pltpu.VMEM((3, SHARE, 16, D), BF16),
    first_out=pltpu.VMEM((SHARE, 8, D), F32),
    first_own=pltpu.VMEM((SHARE, 8, D), F32),
    first_in=pltpu.VMEM((SHARE, 8, D), F32),
    vec_own=pltpu.VMEM((8, LEN), F32),
    vec_in=pltpu.VMEM((8, LEN), F32),
    pieces=pltpu.VMEM((4, SHARE, 16, D), BF16),
    vec_pieces=pltpu.VMEM((4, 16, LEN), BF16),
    VT=pltpu.VMEM((4, 4, 48, LEN), BF16),
    line=pltpu.VMEM((48, D), F32),
    sums_in=pltpu.VMEM((2, 10, 8, D), F32),
    sums_out=pltpu.VMEM((2, 4, 8, D), F32),
    packed=pltpu.VMEM((4, 48, LEN), BF16),
    norm_out=pltpu.VMEM((2, 8, LEN), F32),
    norm_in=pltpu.VMEM((2, 15, 8, LEN), F32),
    V=pltpu.VMEM((16, D), F32),
    sums=pltpu.VMEM((16, D), F32),
    bias=pltpu.VMEM((SLOTS, LEN, LEN), F32),
    act=pltpu.VMEM((4, ROWS, D), BF16),
    p=pltpu.VMEM((SLOTS * PAIRS, 2 * LEN, LEN), BF16),
    A=pltpu.VMEM((ROWS, D), F32),
    F=pltpu.VMEM((ROWS, D), F32),
    FP=pltpu.VMEM((ROWS, D), F32),
    inv1=pltpu.VMEM((ROWS, 1), F32),
    y1b=pltpu.VMEM((ROWS, D), BF16),
    turned=pltpu.VMEM((2, D, ROWS), BF16),
    h=pltpu.VMEM((ROWS, FF), BF16),
    gp=pltpu.VMEM((ROWS, FF), BF16),
    dfb=pltpu.VMEM((ROWS, D), BF16),
    xb=pltpu.VMEM((ROWS, D), BF16),
    gb=pltpu.VMEM((ROWS, D), BF16),
    perm=pltpu.VMEM((D, D), BF16),
    att_w=pltpu.VMEM((6, 4, D), F32),
    hid_w=pltpu.VMEM((6, 2, FF), F32),
    vec_w=pltpu.VMEM((6, VECTORS), F32),
    load_sem=pltpu.SemaphoreType.DMA((12,)),
    store_sem=pltpu.SemaphoreType.DMA((11,)),
    send_sem=pltpu.SemaphoreType.DMA((COPIES,)),
    recv_sem=pltpu.SemaphoreType.DMA((COPIES,)),
)
NAMES = tuple(SCRATCH)


def step_kernel(
    x_hbm,
    g_hbm,
    perm_hbm,
    joined,
    half_lengths,
    att_hbm,
    hid_hbm,
    vec_hbm,
    out_hbm,
    grad_hbm,
    norm_out_ref,
    att_out,
    hid_out,
    vec_out,
    *scratch,
):
    s = dict(zip(NAMES, scratch))
    W, G, V = s["W"], s["G"], s["V"]
    xb, gb, perm = s["xb"], s["gb"], s["perm"]
    net = Net(s["send_sem"], s["recv_sem"])

    me = lax.axis_index("dp")
    c = lax.rem(me, 2)
    z = lax.rem(lax.div(me, 2), 4)
    x = lax.rem(lax.div(me, 8), 4)
    y = lax.div(me, 32)
    other = 1 - c

    def wrap(value):
        return lax.rem(value + 4, 4)

    def peer(axis, step):
        moved = {"x": x, "y": y, "z": z}
        moved[axis] = wrap(moved[axis] + step)
        return ((moved["y"] * 4 + moved["x"]) * 4 + moved["z"]) * 2 + c

    sibling = me + 1 - 2 * c

    def far_peer(step):
        return ((y * 4 + x) * 4 + wrap(z + step)) * 2 + other

    plane_peers = [((wrap(y + i // 4) * 4 + wrap(x + i % 4)) * 4 + z) * 2 + c for i in range(1, 16)]

    att_w, hid_w, vec_w = s["att_w"], s["hid_w"], s["vec_w"]
    masters_in = [
        pltpu.make_async_copy(source, target, s["load_sem"].at[9 + i])
        for i, (source, target) in enumerate(((att_hbm, att_w), (hid_hbm, hid_w), (vec_hbm, vec_w)))
    ]
    loads = []
    for i in range(SLOTS):
        loads.append(pltpu.make_async_copy(x_hbm.at[i], xb.at[pl.ds(i * LEN, LEN)], s["load_sem"].at[i]))
        loads.append(pltpu.make_async_copy(g_hbm.at[i], gb.at[pl.ds(i * LEN, LEN)], s["load_sem"].at[4 + i]))
    loads.append(pltpu.make_async_copy(perm_hbm, perm, s["load_sem"].at[8]))
    for copy in masters_in + loads:
        copy.start()

    barrier = pltpu.get_barrier_semaphore()
    partners = [sibling] + [peer(axis, step) for axis in "xyz" for step in (1, 2, 3)]
    for partner in partners:
        pl.semaphore_signal(barrier, inc=1, device_id=(partner,), device_id_type=MESH)

    for copy in masters_in:
        copy.wait()
    masters = [[att_w[:, 2 * core + l, :] for l in range(2)] for core in range(2)]
    for core in range(2):
        masters[core] += [hid_w[:, i, (2 * core + l) * D : (2 * core + l + 1) * D] for i in range(2) for l in range(2)]
    for l in range(SHARE):
        s["first_own"][l, 0:6, :] = jnp.where(c == 0, masters[0][l], masters[1][l])
        s["first_out"][l, 0:6, :] = jnp.where(c == 0, masters[1][l], masters[0][l])
    s["vec_own"][...] = jnp.zeros((8, LEN), F32)
    s["vec_own"][0:6, 0:VECTORS] = vec_w[...]
    line = s["line"]
    line[...] = jnp.zeros((48, D), F32)
    pl.semaphore_wait(barrier, len(partners))

    FIRST = {"x": "z", "y": "x", "z": "y"}
    SECOND = {"x": "y", "y": "z", "z": "x"}
    HERE = {"x": x, "y": y, "z": z}
    every = pl.ds(0, D)
    wide = pl.ds(0, 2 * TILE)
    part_cols = [pl.ds(part * TILE, TILE) for part in range(3)]
    third = part_cols[2]

    def span(count, size):
        for n in (4, 3, 2, 1):
            for k in (4, 3, 2, 1):
                if count % (n * k) == 0 and count // (n * k) <= 12:
                    return W.at[pl.ds(0, count // (n * k)), pl.ds(0, k), pl.ds(0, n), :, pl.ds(0, size)]
        raise ValueError

    def to_three(axis, copies):
        return [(source(step), target(step), peer(axis, step)) for source, target in copies for step in (1, 2, 3)]

    pair = [
        net.send([(a, b, sibling)], a)
        for a, b in (
            (s["first_out"].at[pl.ds(0, 2)], s["first_in"].at[pl.ds(0, 2)]),
            (s["vec_own"], s["vec_in"]),
            (s["first_out"].at[pl.ds(2, 4)], s["first_in"].at[pl.ds(2, 4)]),
        )
    ]
    fill_masks(joined, half_lengths, s["bias"])
    pieces, vec_pieces = s["pieces"], s["vec_pieces"]
    ATT = ((0, "x", wide), (1, "y", wide), (0, "z", third), (1, "z", third))
    p0, p1, p2 = part_cols
    PARTS = (
        ((2, "x", p0), (3, "y", p0), (4, "z", p0), (5, "z", p0)),
        ((2, "x", p1), (4, "x", p1), (3, "y", p1), (5, "z", p1)),
        ((2, "x", p2), (3, "y", p2), (5, "y", p2), (4, "z", p2)),
    )
    HID = (
        (2, "x", every),
        (3, "y", every),
        (4, "z", p0),
        (4, "x", p1),
        (4, "z", p2),
        (5, "z", pl.ds(0, 2 * TILE)),
        (5, "y", p2),
    )

    def turns(l, route):
        return (route == "z") != (l >= 4)

    def make_piece(l, route, cols):
        own, far = s["first_own"][l, 0:6, cols], s["first_in"][l, 0:6, cols]
        line[0:6, cols] = jnp.where(c == 0, own, far)
        line[6:12, cols] = jnp.where(c == 0, far, own)
        pieces[HERE[FIRST[route]], l, :, cols] = line[0:16, cols].astype(BF16)

    def send_pieces(some, units):
        copies = []
        for l, route, cols in some:
            near = pieces.at[HERE[FIRST[route]], l, :, cols]
            copies += [(near, near, peer(FIRST[route], step)) for step in (1, 2, 3)]
        return net.send(copies, span(units, D))

    pair[0].wait_recv()
    for some in ATT:
        make_piece(*some)
    att_pieces = send_pieces(ATT, 2)
    pair[2].wait_recv()
    for some in HID:
        make_piece(*some)
    hid_pieces = send_pieces(HID, 4)
    pair[1].wait_recv()
    own, far = s["vec_own"][0:6], s["vec_in"][0:6]
    line[0:6, 0:LEN] = jnp.where(c == 0, own, far)
    line[6:12, 0:LEN] = jnp.where(c == 0, far, own)
    vec_pieces[z] = line[0:16, 0:LEN].astype(BF16)
    near = vec_pieces.at[z]
    vec_copies = net.send([(near, near, peer("z", step)) for step in (1, 2, 3)], span(1, LEN))

    VT, packed = s["VT"], s["packed"]

    def stage(ref, l, index):
        return ref.at[pl.ds(pl.multiple_of(index * 48, 16), 48), pl.ds((l // 2) * D, D)]

    def spread(l, route, cols):
        for i in range(4):
            line[12 * i : 12 * i + 12, cols] = pieces[i, l, :, cols].astype(F32)[0:12]
        rows = line[:, cols].astype(BF16)
        if route == "x":
            W[6 * c + l, y, x, :, cols] = rows
        elif route == "y":
            stage(s["gp"], l, z)[:, cols] = rows
        else:
            W[6 * c + l, z, x, :, cols] = rows

    def strips(some, units):
        copies = []
        for l, route, cols in some:
            if route == "x":
                near = W.at[6 * c + l, y, x, :, cols]
            elif route == "y":
                near = stage(s["gp"], l, z).at[:, cols]
            else:
                near = W.at[6 * c + l, z, x, :, cols]
            copies += [(near, near, peer(SECOND[route], step)) for step in (1, 2, 3)]
        return net.send(copies, span(3 * units, copies[0][0].shape[-1]))

    def order_strips(l, cols):
        size = cols.size
        for i in range(4):
            FP[48 * i : 48 * i + 48, 0:size] = stage(s["gp"], l, i)[:, cols].astype(F32)
        for i in range(4):
            for j in range(4):
                line[12 * j : 12 * j + 12, 0:size] = FP[48 * j + 12 * i : 48 * j + 12 * i + 12, 0:size]
            W[6 * c + l, y, i, :, cols] = line[:, 0:size].astype(BF16)

    def turn_rows(ref, place, cols):
        rows = ref[place, :, :, :, cols].reshape(D, cols.size)
        ref[place, :, :, :, cols] = dot(perm[...], rows).astype(BF16).reshape(4, 4, 48, cols.size)

    def region(ref, place, route, index, half, cols):
        part = pl.ds(0, 4) if half is None else pl.ds(2 * half, 2)
        if route == "x":
            return ref.at[place, part, index, :, cols]
        return ref.at[place, index, part, :, cols]

    def gather_start(some):
        copies = []
        for l, route, cols in some:
            near = region(W, 6 * c + l, route, HERE[route], None, cols)
            copies += [(near, near, peer(route, step)) for step in (1, 2, 3)]
        return some, net.send(copies, span(12 * len(some), some[0][2].size))

    def gather_share(state):
        some, group = state
        group.wait_recv()
        if any(turns(l, route) for l, route, _ in some):
            net.sent(group)
        copies = []
        for l, route, cols in some:
            if turns(l, route):
                turn_rows(W, 6 * c + l, cols)
            near = W.at[6 * c + l, :, :, :, cols]
            copies.append((near, near, sibling))
        return net.send(copies, span(16 * len(some), some[0][2].size))

    act, p = s["act"], s["p"]
    q, k, v, ctx = (act.at[i] for i in range(4))
    A, F, FP, inv1, y1b = s["A"], s["F"], s["FP"], s["inv1"], s["y1b"]
    h, gp, dfb, dfp, sums = s["h"], s["gp"], s["dfb"], y1b, s["sums"]
    turned = s["turned"]

    att_pieces.wait_recv()
    att_strips = []
    for group in (ATT[:1], ATT[1:2], ATT[2:]):
        for some in group:
            spread(*some)
        att_strips.append(strips(group, len(group)))
    hid_pieces.wait_recv()
    for some in HID:
        spread(*some)
    z_strips = [strips(PARTS[0][2:], 2)]
    x_strips = strips(HID[:1], 1)
    y_strips = strips(HID[1:2], 1)
    z_strips.append(strips([(5, "z", p1), (4, "z", p2)], 2))
    x_rest = strips([(4, "x", p1)], 1)
    y_rest = strips([(5, "y", p2)], 1)
    vec_copies.wait_recv()
    for i in range(4):
        line[12 * i : 12 * i + 12, 0:LEN] = vec_pieces[i].astype(F32)[0:12]
    VT[y, x] = line[:, 0:LEN].astype(BF16)
    near = VT.at[y, x]
    vec_strips = net.send([(near, near, peer("x", step)) for step in (1, 2, 3)], span(3, LEN))
    starts = {}
    att_strips[0].wait_recv()
    for part in range(2):
        starts["x", part] = gather_start([(0, "x", part_cols[part])])
    att_strips[1].wait_recv()
    order_strips(1, wide)
    for part in range(2):
        starts["y", part] = gather_start([(1, "y", part_cols[part])])
    att_strips[2].wait_recv()
    starts["t", 0] = gather_start(ATT[2:])
    vec_strips.wait_recv()
    near = packed.at[y]
    packed[y] = sum(
        pltpu.roll(VT[y, i].astype(F32), 32 * i, 1) if i else VT[y, i].astype(F32) for i in range(4)
    ).astype(BF16)
    vec_last = net.send([(near, near, peer("y", step)) for step in (1, 2, 3)], span(3, LEN))
    for copy in loads:
        copy.wait()
    flows = {}

    def begin(part, route):
        flows[part, route] = gather_start([some for some in PARTS[part] if some[1] == route])

    def sharing(part, routes="xyz"):
        for route in routes:
            flows[part, route] = gather_share(flows[part, route])

    z_strips[0].wait_recv()
    begin(0, "z")
    x_strips.wait_recv()
    begin(0, "x")
    y_strips.wait_recv()
    order_strips(3, every)
    begin(0, "y")
    z_strips[1].wait_recv()
    begin(1, "z")
    x_rest.wait_recv()
    begin(1, "x")
    begin(1, "y")
    y_rest.wait_recv()
    order_strips(5, p2)
    for route in "zxy":
        begin(2, route)
    vec_last.wait_recv()
    net.sent(vec_strips)
    for i in range(4):
        block_i = packed[i].astype(F32)
        for j in range(4):
            VT[i, j] = (pltpu.roll(block_i, LEN - 32 * j, 1) if j else block_i).astype(BF16)
    V[...] = VT[...].reshape(D, LEN).astype(F32).T[0:16]
    shares = [gather_share(starts[key]) for key in (("x", 0), ("y", 0))]
    net.sent(att_strips[2])
    shares += [gather_share(starts[key]) for key in (("x", 1), ("y", 1), ("t", 0))]
    for copy in shares:
        copy.wait_recv()
    qkv(W, V, xb, q, k, v)
    net.sent(x_rest)
    sharing(0)
    attend(q, k, v, s["bias"], p, ctx)
    sharing(1)
    first_norm(W, V, xb, ctx, A, inv1, F, y1b)
    turn(y1b, turned.at[1])

    def arrived(part):
        for route in "xyz":
            flows[part, route].wait_recv()

    arrived(0)
    net.sent(att_strips[1])
    net.sent(y_strips)
    net.sent(y_rest)
    up(W, V, y1b, h, gp, 0)
    down_(W, h, FP, 0)
    sharing(2)
    arrived(1)
    up(W, V, y1b, h, gp, 1)
    down_(W, h, FP, 1)
    arrived(2)
    up(W, V, y1b, h, gp, 2)
    down_(W, h, FP, 2)
    second_norm(V, perm, FP, F, gb, gb, dfb, sums)
    stores = []
    for i in range(SLOTS):
        stores.append(pltpu.make_async_copy(gb.at[pl.ds(i * LEN, LEN)], out_hbm.at[i], s["store_sem"].at[i]))
        stores[-1].start()
    to_down_order(dfb, perm, dfp)
    dfpT = turned.at[0]
    y1T = turned.at[1]
    turn(dfp, dfpT)
    net.close()

    pair_in, pair_out = s["pair_in"], s["pair_out"]
    G_half = s["half_in"]
    G_block = pair_in
    slots = [None] * 8

    def send_tiles(tiles):
        for slot, _, _, _ in tiles:
            if slots[slot] is not None:
                net.sent(slots[slot])
        values = [value() for _, _, _, value in tiles]
        for (slot, _, _, _), value in zip(tiles, values):
            pair_out[slot] = value.astype(BF16).reshape(4, 4, 48, TILE)
        group = net.send(
            [(pair_out.at[slot], pair_in.at[l, :, :, :, cols], sibling) for slot, l, cols, _ in tiles],
            span(16 * len(tiles), TILE),
        )
        for slot, _, _, _ in tiles:
            slots[slot] = group
        return group

    def add_into(ref, index, *others):
        total = ref[index].astype(F32)
        for other_ref, other_index in others:
            total = total + other_ref[other_index].astype(F32)
        ref[index] = total.astype(BF16)

    def cell(l, route, index, i, cols):
        return (l, i, index, slice(None), cols) if route == "x" else (l, index, i, slice(None), cols)

    def reduce_start(some):
        copies = []
        for l, route, cols in some:
            across = wrap(HERE[route] + 2)
            for half, step in ((0, 1), (1, 3)):
                copies.append((region(G, l, route, across, half, cols), G_half.at[l - 2, half, :, :, cols], peer(route, step)))
        return some, net.send(copies, span(4 * len(some), TILE))

    def reduce_pass(state):
        some, group = state
        group.wait_recv()
        copies = []
        for l, route, cols in some:
            here = HERE[route]
            for i in range(2):
                add_into(G, cell(l, route, wrap(here + 1), i, cols), (G_half, (l - 2, 0, i, slice(None), cols)))
                add_into(G, cell(l, route, wrap(here - 1), 2 + i, cols), (G_half, (l - 2, 1, i, slice(None), cols)))
            for half, step in ((0, 1), (1, 3)):
                copies.append(
                    (region(G, l, route, wrap(here + step), None, cols), G_block.at[l, half, :, :, cols], peer(route, step))
                )
        return some, net.send(copies, span(8 * len(some), TILE))

    def direct_start(some):
        copies = []
        for l, route, cols in some:
            for step in (1, 2, 3):
                source = region(G, l, route, wrap(HERE[route] + step), None, cols)
                copies.append((source, W.at[2 + l, step - 1, :, :, cols], peer(route, step)))
        return some, net.send(copies, span(12 * len(some), TILE))

    strip_in = s["strip_in"]

    def strip_place(l, route, moved):
        return (l, moved, x) if route == "x" else (l, z, moved)

    def reduce_end(state):
        some, group = state
        group.wait_recv()
        copies = []
        for l, route, cols in some:
            arrived = [(W, 2 + l, i) for i in range(3)] if l < 2 else [(G_block, l, i) for i in range(2)]
            for i in range(4):
                add_into(
                    G,
                    cell(l, route, HERE[route], i, cols),
                    *[(ref, (place, block, i, slice(None), cols)) for ref, place, block in arrived],
                )
            if route == "y":
                for i in range(4):
                    FP[48 * i : 48 * i + 48, 0:TILE] = G[l, y, i, :, cols].astype(F32)
                for j in range(4):
                    for i in range(4):
                        line[12 * i : 12 * i + 12, 0:TILE] = FP[48 * i + 12 * j : 48 * i + 12 * j + 12, 0:TILE]
                    stage(h, l, j)[:, cols] = line[:, 0:TILE].astype(BF16)
            for step in (1, 2, 3):
                target = wrap(HERE[SECOND[route]] + step)
                if route == "y":
                    source = stage(h, l, target).at[:, cols]
                else:
                    source = G.at[strip_place(l, route, target) + (slice(None), cols)]
                copies.append((source, strip_in.at[l, step - 1, :, cols], peer(SECOND[route], step)))
        return some, net.send(copies, span(3 * len(some), TILE))

    piece_out, piece_in = pieces, s["piece_in"]

    def strips_sum(state):
        some, group = state
        group.wait_recv()
        for l, route, cols in some:
            if route == "y":
                own = stage(h, l, z)[:, cols]
            else:
                own = G[strip_place(l, route, HERE[SECOND[route]]) + (slice(None), cols)]
            total = own.astype(F32)
            for i in range(3):
                total = total + strip_in[l, i, :, cols].astype(F32)
            line[:, 0:TILE] = total
            gap = jnp.zeros((4, TILE), F32)
            for i in range(4):
                rows = jnp.concatenate([line[12 * i : 12 * i + 12, 0:TILE], gap], 0)
                piece_out[i, l, :, cols] = rows.astype(BF16)

    def pieces_out(some, units):
        copies = []
        for l, route, cols in some:
            for step in (1, 2, 3):
                source = piece_out.at[wrap(HERE[FIRST[route]] + step), l, :, cols]
                copies.append((source, piece_in.at[step - 1, l, :, cols], peer(FIRST[route], step)))
        return net.send(copies, span(units, D))

    rows_out, rows_own, rows_in = s["first_out"], s["first_own"], s["first_in"]

    def pieces_sum(l, route, cols):
        total = piece_out[HERE[FIRST[route]], l, :, cols].astype(F32)
        for i in range(3):
            total = total + piece_in[i, l, :, cols].astype(F32)
        line[0:16, cols] = total
        top, bottom = line[0:6, cols], line[6:12, cols]
        rows_own[l, 0:6, cols] = jnp.where(c == 0, top, bottom)
        rows_out[l, 0:6, cols] = jnp.where(c == 0, bottom, top)
        return jnp.sum(top * top + bottom * bottom, keepdims=True)

    def hidden_slopes(core, part):
        places = [pl.ds(pl.multiple_of((2 * core + e) * D + part * TILE, LEN), TILE) for e in range(2)]
        slopes = []
        for e in range(2):
            dh = dot(dfp[...], columns(W, 6 * core + 4 + e, part * TILE, TILE))
            du = (dh * gp[:, places[e]].astype(F32)).astype(BF16)
            slopes.append(du)
            sums[pl.ds(V_B1 + 2 * core + e, 1), part_cols[part]] = jnp.sum(du.astype(F32), 0, keepdims=True)
        return places, slopes

    def keep_tiles(group, tiles):
        group.wait_recv()
        for l, cols, value in tiles:
            total = value() + pair_in[l, :, :, :, cols].reshape(D, TILE).astype(F32)
            G[l, :, :, :, cols] = total.astype(BF16).reshape(4, 4, 48, TILE)

    def hidden_tiles(places, slopes, cols):
        tiles = [(4 + e, cols, lambda e=e: dot(dfpT[...], h[:, places[e]])) for e in range(2)]
        return tiles + [(2 + e, cols, lambda e=e: dot(y1T[...], slopes[e])) for e in range(2)]

    shared = {}

    def others(part):
        places, slopes = hidden_slopes(other, part)
        tiles = hidden_tiles(places, slopes, part_cols[part])
        shared[part] = send_tiles([(4 * (part % 2) + i,) + tile for i, tile in enumerate(tiles)])
        for e in range(2):
            gp[:, places[e]] = slopes[e]

    def own_slopes(part):
        places, slopes = hidden_slopes(c, part)
        for e in range(2):
            gp[:, places[e]] = slopes[e]

    def own_tiles(part):
        places = [pl.ds(pl.multiple_of((2 * c + e) * D + part * TILE, LEN), TILE) for e in range(2)]
        keep_tiles(shared[part], hidden_tiles(places, [gp[:, place] for place in places], part_cols[part]))
        for l, route, cols in PARTS[part]:
            if turns(l, route):
                turn_rows(G, l, cols)
        return reduce_start(PARTS[part])

    others(0)
    others(1)
    own_slopes(0)
    flows[0] = own_tiles(0)
    others(2)
    own_slopes(1)
    flows[1] = own_tiles(1)
    flows[0] = reduce_pass(flows[0])
    own_slopes(2)
    flows[2] = own_tiles(2)
    first_back_product(W, gp, F)
    flows[1] = reduce_pass(flows[1])
    first_back(V, A, inv1, F, dfb, sums)
    flows[2] = reduce_pass(flows[2])
    flows[0] = reduce_end(flows[0])

    sums[VECTORS:16, :] = jnp.zeros((16 - VECTORS, D), F32)
    sums_in, sums_out = s["sums_in"], s["sums_out"]

    def sums_step(place, stage_, group, axis):
        if group is None:
            total = sums[8 * place : 8 * place + 8, :]
        else:
            total = sums_out[place, stage_ - 1]
            group.wait_recv()
            for i in range(1 if stage_ == 1 else 3):
                total = total + sums_in[place, 0 if stage_ == 1 else 3 * stage_ - 5 + i]
        if axis is None:
            return total
        sums_out[place, stage_] = total
        near = sums_out.at[place, stage_]
        if stage_ == 0:
            return net.send([(near, sums_in.at[place, 0], sibling)], near)
        base = 3 * stage_ - 3
        return net.send(
            [(near, sums_in.at[place, base + step], peer(axis, step)) for step in (1, 2, 3)],
            sums_in.at[place, pl.ds(0, 3)],
        )

    up_sums = sums_step(1, 0, None, "sibling")
    doT = turned.at[1]
    turn(dfb, doT)
    output_back(W, dfb, y1b)
    up_sums = sums_step(1, 1, up_sums, "z")
    attend_back(q, k, v, p, y1b)
    column_sums(q, sums, V_BQ)
    column_sums(v, sums, V_BV)
    first_sums = sums_step(0, 0, None, "sibling")
    turn(xb, turned.at[0])
    flows[1] = reduce_end(flows[1])
    first_sums = sums_step(0, 1, first_sums, "z")
    up_sums = sums_step(1, 2, up_sums, "x")

    def projection_grad(core, l, n):
        left = core if l == 1 else 0
        return dot(turned[left], act[2 * core + l, :, n * TILE : (n + 1) * TILE])

    def projection_tiles(core, n):
        return [(l, part_cols[n], lambda l=l: projection_grad(core, l, n)) for l in (0, 1)]

    ORDER = (2, 0, 1)
    for n in ORDER:
        shared["p", n] = send_tiles([(2 * n + i,) + tile for i, tile in enumerate(projection_tiles(other, n))])
    flows[2] = reduce_end(flows[2])
    for group in pair + [att_pieces, hid_pieces]:
        net.sent(group)
    strips_sum(flows[0])
    first_sums = sums_step(0, 2, first_sums, "x")
    last = []
    for n in ORDER:
        keep_tiles(shared["p", n], projection_tiles(c, n))
        if n == 2:
            for l in (0, 1):
                turn_rows(G, l, third)
        last.append(direct_start([(l, "z" if n == 2 else "xy"[l], part_cols[n]) for l in (0, 1)]))
    strips_sum(flows[1])
    up_sums = sums_step(1, 3, up_sums, "y")
    input_back(W, q, k, v, F)
    for i in range(SLOTS):
        stores.append(pltpu.make_async_copy(F.at[pl.ds(i * LEN, LEN)], grad_hbm.at[i], s["store_sem"].at[4 + i]))
        stores[-1].start()
    first_sums = sums_step(0, 3, first_sums, "y")
    strips_sum(flows[2])
    hid_pieces = pieces_out(HID, 4)
    for n in range(3):
        last[n] = reduce_end(last[n])
    hid_pieces.wait_recv()
    squares = jnp.zeros((1, 1), F32)
    for some in HID:
        squares = squares + pieces_sum(*some)
    rows_copies = [net.send([(rows_out.at[pl.ds(2, 4)], rows_in.at[pl.ds(2, 4)], sibling)], rows_out.at[pl.ds(2, 4)])]
    for n in range(3):
        strips_sum(last[n])
    att_pieces = pieces_out(ATT, 2)
    vec_total = jnp.concatenate([sums_step(0, 4, first_sums, None), sums_step(1, 4, up_sums, None)], 0)
    place = lax.broadcasted_iota(jnp.int32, (8, D), 1) - 6 * me
    pick = (place == lax.broadcasted_iota(jnp.int32, (8, D), 0)).astype(BF16)
    vec_grad = jnp.zeros((8, 16), F32)
    for _ in range(3):
        low = vec_total.astype(BF16)
        vec_grad = vec_grad + dot(pick, low, NT)
        vec_total = vec_total - low.astype(F32)
    vec_grad = vec_grad[0:6, 0:VECTORS]
    squares = squares + jnp.sum(vec_grad * vec_grad, keepdims=True)
    att_pieces.wait_recv()
    for some in ATT:
        squares = squares + pieces_sum(*some)
    norm_out, norm_in = s["norm_out"], s["norm_in"]
    norm_out[0] = jnp.broadcast_to(squares, (8, LEN))
    plane = [(norm_out.at[0], norm_in.at[0, i], device) for i, device in enumerate(plane_peers)]
    norm_group = net.send(plane, norm_in.at[0])
    rows_copies.append(
        net.send([(rows_out.at[pl.ds(0, 2)], rows_in.at[pl.ds(0, 2)], sibling)], rows_out.at[pl.ds(0, 2)])
    )
    for copy in rows_copies:
        copy.wait_recv()
    att_grad, hid_grad, vec_grad_at = att_w, hid_w, vec_w
    vec_grad_at[...] = vec_grad
    for core in range(2):
        for l in range(SHARE):
            value = jnp.where(c == core, rows_own[l, 0:6], rows_in[l, 0:6])
            if l < 2:
                att_grad[:, 2 * core + l, :] = value
            else:
                i, j = (l - 2) // 2, 2 * core + l % 2
                hid_grad[:, i, j * D : (j + 1) * D] = value
    for i, (source, target) in enumerate(((att_grad, att_out), (hid_grad, hid_out), (vec_grad_at, vec_out))):
        stores.append(pltpu.make_async_copy(source, target, s["store_sem"].at[8 + i]))
        stores[-1].start()

    def norm_step(index, group, count):
        group.wait_recv()
        total = norm_out[index]
        for i in range(count):
            total = total + norm_in[index, i]
        return total

    norm_out[1] = norm_step(0, norm_group, 15)
    copies = [(norm_out.at[1], norm_in.at[1, 0], sibling)]
    for step in (1, 2, 3):
        copies.append((norm_out.at[1], norm_in.at[1, step], peer("z", step)))
        copies.append((norm_out.at[1], norm_in.at[1, 3 + step], far_peer(step)))
    norm_group = net.send(copies, norm_in.at[1, pl.ds(0, 7)])
    norm = jnp.sqrt(norm_step(1, norm_group, 7))
    norm_out_ref[...] = norm[0:1, 0:1]
    for copy in stores:
        copy.wait()
    net.close()


def rates(values, shape):
    index = lax.broadcasted_iota(jnp.int32, shape, 1)
    rate = jnp.full(shape, values[0], F32)
    for i, value in enumerate(values[1:]):
        rate = jnp.where(index == i + 1, value, rate)
    return rate


def update_kernel(out_in, grad_in, norm, *refs):
    sources, (out_hbm, grad_hbm), targets = refs[:12], refs[12:14], refs[14:23]
    out_at, grad_at = refs[23:25]
    held, sems = refs[25:37], refs[37]
    loads = [pltpu.make_async_copy(a, b, sems.at[i]) for i, (a, b) in enumerate(zip(sources, held))]
    passing = [pltpu.make_async_copy(out_in, out_at, sems.at[12]), pltpu.make_async_copy(grad_in, grad_at, sems.at[13])]
    for copy in loads + passing:
        copy.start()
    stores = [pltpu.make_async_copy(out_at, out_hbm, sems.at[14]), pltpu.make_async_copy(grad_at, grad_hbm, sems.at[15])]
    factor = CLIP_NORM / jnp.maximum(norm[...], CLIP_NORM)
    settings = (
        (rates(ATTENTION_RATES, (6, 4, D)), WEIGHT_DECAY),
        (rates(HIDDEN_RATES, (6, 2, FF)), WEIGHT_DECAY),
        (VECTOR_RATE, 0.0),
    )
    for i in (1, 0, 2):
        for j in (i, 3 + 3 * i, 4 + 3 * i, 5 + 3 * i):
            loads[j].wait()
        state = held[3 + 3 * i : 6 + 3 * i]
        new = adam(state[0][...], state[1][...], state[2][...], held[i][...] * factor, *settings[i])
        for j in range(3):
            state[j][...] = new[j]
            stores.append(pltpu.make_async_copy(state[j], targets[3 * i + j], sems.at[16 + 3 * i + j]))
        if i == 1:
            for load, copy in zip(passing, stores):
                load.wait()
                copy.start()
        for copy in stores[-3:]:
            copy.start()
    for copy in stores:
        copy.wait()


def on_device(
    inputs,
    cotangent,
    joined,
    half_lengths,
    attention_master,
    attention_first,
    attention_second,
    hidden_master,
    hidden_first,
    hidden_second,
    vector_master,
    vector_first,
    vector_second,
):
    any_space = pl.BlockSpec(memory_space=pl.ANY)
    vmem = pl.BlockSpec(memory_space=pltpu.VMEM)
    smem = pl.BlockSpec(memory_space=pltpu.SMEM)
    like = lambda a: jax.ShapeDtypeStruct(a.shape, a.dtype)
    swap = lambda a: jnp.transpose(a, (1, 0, 2))
    attention = [swap(a) for a in (attention_master, attention_first, attention_second)]
    hidden = [swap(a) for a in (hidden_master, hidden_first, hidden_second)]
    vectors = [a.T for a in (vector_master, vector_first, vector_second)]
    params = attention + hidden + vectors
    out_like = jax.ShapeDtypeStruct(inputs.shape, BF16)
    grad_like = jax.ShapeDtypeStruct(inputs.shape, F32)
    results = pl.pallas_call(
        step_kernel,
        out_shape=(
            out_like,
            grad_like,
            jax.ShapeDtypeStruct((1, 1), F32),
            like(attention[0]),
            like(hidden[0]),
            like(vectors[0]),
        ),
        in_specs=[any_space] * 3 + [smem] * 2 + [any_space] * 3,
        out_specs=(any_space, any_space, vmem) + (any_space,) * 3,
        scratch_shapes=list(SCRATCH.values()),
        compiler_params=pltpu.CompilerParams(collective_id=0, has_side_effects=True, vmem_limit_bytes=64 << 20),
        cost_estimate=pl.CostEstimate(flops=22 * 10**9, bytes_accessed=6 * 10**6, transcendentals=4 * 10**6),
    )(
        inputs,
        cotangent,
        jnp.asarray(permutation(), BF16),
        joined.T,
        jnp.transpose(half_lengths, (1, 2, 0)),
        attention[0],
        hidden[0],
        vectors[0],
    )
    outs = pl.pallas_call(
        update_kernel,
        out_shape=(out_like, grad_like) + tuple(like(a) for a in params),
        in_specs=[any_space] * 2 + [vmem] + [any_space] * 12,
        out_specs=(any_space,) * 11,
        scratch_shapes=[
            pltpu.VMEM(inputs.shape, BF16),
            pltpu.VMEM(inputs.shape, F32),
            *[pltpu.VMEM(a.shape, F32) for a in (attention[0], hidden[0], vectors[0], *params)],
            pltpu.SemaphoreType.DMA((25,)),
        ],
        cost_estimate=pl.CostEstimate(flops=2 * 10**6, bytes_accessed=7 * 10**6, transcendentals=10**5),
    )(*results, *params)
    output, input_grad, *new = outs
    norm = results[2].reshape(())
    return (output, input_grad, norm, *[swap(a) for a in new[:6]], *[a.T for a in new[6:]])


def solution(mesh):
    shard = P(None, "dp", None)
    flat = P(None, "dp")
    return jax.shard_map(
        on_device,
        mesh=mesh,
        in_specs=(shard, shard, flat, shard, shard, shard, shard, shard, shard, shard, flat, flat, flat),
        out_specs=(shard, shard, P(), shard, shard, shard, shard, shard, shard, flat, flat, flat),
        check_vma=False,
    )
```

```python
import functools
import jax
import jax.numpy as jnp
import numpy as np
from jax import lax
from jax.experimental import pallas as pl
from jax.experimental.pallas import tpu as pltpu
from jax.sharding import PartitionSpec as P

F32 = jnp.float32
BF16 = jnp.bfloat16
D = 768
FF = 3072
ROWS = 512
SLOTS = 4
LEN = 128
PAIRS = 6
TILE = 256
NORM_EPS = 1e-05
MASKED = -1e30
NN = (((1,), (0,)), ((), ()))
NT = (((1,), (1,)), ((), ()))
TN = (((0,), (0,)), ((), ()))
PLACE_Q, PLACE_K, PLACE_V, PLACE_O = 0, 1, 6, 7
PLACE_UP = (2, 3, 8, 9)
PLACE_DOWN = (4, 5, 10, 11)
V_BQ, V_BV, V_BO, V_G1, V_C1, V_G2, V_C2, V_B2, V_B1 = range(9)


def dot(a, b, dims=NN):
    return lax.dot_general(a, b, dims, preferred_element_type=F32)


def block(ref, place):
    return ref[place].reshape(D, D)


def columns(ref, place, start, size):
    return ref[place, :, :, :, pl.ds(start, size)].reshape(D, size)


def put_columns(ref, place, start, size, value):
    ref[place, :, :, :, pl.ds(start, size)] = value.reshape(4, 4, 48, size)


def loop(count, body):
    lax.fori_loop(0, count, lambda i, c: (body(i), c)[1], 0)


def at(i, size):
    return pl.ds(pl.multiple_of(i * size, size), size)


def qkv(W, V, xb, q, k, v):
    x = xb[...]
    for n in range(D // TILE):
        cols = pl.ds(n * TILE, TILE)
        q[:, cols] = ((dot(x, columns(W, PLACE_Q, n * TILE, TILE)) + V[V_BQ, cols]).astype(BF16) * 0.125).astype(BF16)
        k[:, cols] = dot(x, columns(W, PLACE_K, n * TILE, TILE)).astype(BF16)
        v[:, cols] = (dot(x, columns(W, PLACE_V, n * TILE, TILE)) + V[V_BV, cols]).astype(BF16)


def halves(value):
    lane = lax.broadcasted_iota(jnp.int32, value.shape, 1)
    zero = jnp.zeros_like(value)
    return jnp.concatenate([jnp.where(lane < 64, value, zero), jnp.where(lane < 64, zero, value)], 0)


def joined_halves(value):
    lane = lax.broadcasted_iota(jnp.int32, (LEN, LEN), 1)
    return jnp.where(lane < 64, value[:LEN], value[LEN:])


def fill_masks(joined, half_lengths, bias):
    query = lax.broadcasted_iota(jnp.int32, (LEN, LEN), 0)
    key = lax.broadcasted_iota(jnp.int32, (LEN, LEN), 1)
    for slot in range(SLOTS):
        is_joined = joined[0, slot]
        low = half_lengths[0, 0, slot]
        high = half_lengths[0, 1, slot]
        upper = (key >= 64).astype(jnp.int32)
        limit = is_joined * (64 + high) + (1 - is_joined) * (upper * (64 + high) + (1 - upper) * low)
        apart = (1 - is_joined) * jnp.abs((query >= 64).astype(jnp.int32) - upper)
        bias[slot] = jnp.where((key < limit) & (apart == 0), 0.0, MASKED)


GROUP = 6


def attend(q, k, v, bias, p, ctx):
    def units(slot):
        rows = at(slot, LEN)
        m = bias[slot]
        hidden = jnp.concatenate([m, m], 0) < 0
        cols = [pl.ds(pair * LEN, LEN) for pair in range(PAIRS)]
        for start in range(0, PAIRS, GROUP):
            some = range(start, start + GROUP)
            s = [dot(halves(q[rows, cols[i]]), k[rows, cols[i]], NT) for i in some]
            values = [v[rows, cols[i]] for i in some]
            s = [jnp.where(hidden, MASKED, one) for one in s]
            e = [jnp.exp(one - jnp.max(one, -1, keepdims=True)) for one in s]
            low = [(one * (1.0 / jnp.sum(one, -1, keepdims=True))).astype(BF16) for one in e]
            out = [joined_halves(dot(one, value)).astype(BF16) for one, value in zip(low, values)]
            for i, one, result in zip(some, low, out):
                p[slot * PAIRS + i] = one
                ctx[rows, cols[i]] = result

    loop(SLOTS, units)


def attend_back(q, k, v, p, dctx, n):
    def units(step):
        some = [(2 * step + slot, pair) for slot in range(2) for pair in (2 * n, 2 * n + 1)]
        places = [(at(slot, LEN), pl.ds(pair * LEN, LEN)) for slot, pair in some]
        low = [p[slot * PAIRS + pair] for slot, pair in some]
        two = [halves(dctx[place]) for place in places]
        q2 = [halves(q[place]) for place in places]
        keys = [k[place] for place in places]
        dp = [dot(a, v[place], NT) for a, place in zip(two, places)]
        dv = [dot(a, b, TN) for a, b in zip(low, two)]
        full = [a.astype(F32) for a in low]
        ds = [(a * (b - jnp.sum(a * b, -1, keepdims=True))).astype(BF16) for a, b in zip(full, dp)]
        dq = [joined_halves(dot(a, b)) * 0.125 for a, b in zip(ds, keys)]
        dk = [dot(a, b, TN) for a, b in zip(ds, q2)]
        for a, b, d, place in zip(dv, dq, dk, places):
            v[place] = a.astype(BF16)
            q[place] = b.astype(BF16)
            k[place] = d.astype(BF16)

    loop(2, units)


STRIP = 256


def first_norm(W, V, xb, ctx, A, inv1, F, y1b):
    A[...] = dot(ctx[...], block(W, PLACE_O), NT)

    def strip(i):
        rows = at(i, STRIP)
        a = xb[rows, :].astype(F32) + A[rows, :] + V[V_BO : V_BO + 1, :]
        center = a - jnp.mean(a, -1, keepdims=True)
        inverse = lax.rsqrt(jnp.mean(center * center, -1, keepdims=True) + NORM_EPS)
        n = center * inverse
        A[rows, :] = n
        inv1[rows, :] = inverse
        y = n * V[V_G1 : V_G1 + 1, :] + V[V_C1 : V_C1 + 1, :]
        y1b[rows, :] = y.astype(BF16)
        F[rows, :] = y + V[V_B2 : V_B2 + 1, :]

    loop(ROWS // STRIP, strip)


def gelu_parts(u):
    e = jnp.exp(-0.5 * (u * u))
    t = pl.reciprocal(1.0 + 0.23164190 * jnp.abs(u), approx=True)
    poly = ((((0.5307027145 * t - 0.726576013) * t + 0.7107068705) * t - 0.142248368) * t + 0.127414796) * t
    tail = poly * e
    cdf = jnp.where(u >= 0, 1.0 - tail, tail)
    return u * cdf, cdf + (u * 0.3989422804014327) * e


def up(W, V, y1b, h, gp, part):
    for j, place in enumerate(PLACE_UP):
        cols = pl.ds(j * D + part * TILE, TILE)
        u = dot(y1b[...], columns(W, place, part * TILE, TILE)) + V[V_B1 + j : V_B1 + j + 1, pl.ds(part * TILE, TILE)]
        value, slope = gelu_parts(u)
        h[:, cols] = value.astype(BF16)
        gp[:, cols] = slope.astype(BF16)


def down_(W, h, FP, part):
    left = jnp.concatenate([h[:, pl.ds(j * D + part * TILE, TILE)] for j in range(4)], 1)
    right = jnp.concatenate([columns(W, place, part * TILE, TILE) for place in PLACE_DOWN], 1)
    total = dot(left, right, NT)
    FP[...] = total if part == 0 else FP[...] + total


def second_norm(V, perm, FP, F, gb, outb, dfb, sums):
    F[...] += dot(FP[...].astype(BF16), perm[...])

    def strip(i, carry):
        dg, dc, db = carry
        rows = at(i, STRIP)
        z = F[rows, :]
        center = z - jnp.mean(z, -1, keepdims=True)
        inverse = lax.rsqrt(jnp.mean(center * center, -1, keepdims=True) + NORM_EPS)
        n = center * inverse
        gain = V[V_G2 : V_G2 + 1, :]
        g = gb[rows, :].astype(F32)
        outb[rows, :] = (n * gain + V[V_C2 : V_C2 + 1, :]).astype(BF16)
        gn = g * n
        e = g * gain
        dz = inverse * (e - jnp.mean(e, -1, keepdims=True) - n * jnp.mean(gn * gain, -1, keepdims=True))
        low = dz.astype(BF16)
        F[rows, :] = dz
        dfb[rows, :] = low
        return (
            dg + jnp.sum(gn, 0, keepdims=True),
            dc + jnp.sum(g, 0, keepdims=True),
            db + jnp.sum(low.astype(F32), 0, keepdims=True),
        )

    zero = jnp.zeros((1, D), F32)
    dg, dc, db = lax.fori_loop(0, ROWS // STRIP, strip, (zero, zero, zero))
    sums[V_G2 : V_G2 + 1, :] = dg
    sums[V_C2 : V_C2 + 1, :] = dc
    sums[V_B2 : V_B2 + 1, :] = db


def turn(source, target):
    for i in range(ROWS // LEN):
        target[:, i * LEN : (i + 1) * LEN] = source[i * LEN : (i + 1) * LEN, :].T


def first_back_product(W, gp, F):
    for i in range(ROWS // TILE):
        rows = pl.ds(i * TILE, TILE)
        F[rows, :] += dot(gp[rows, :], jnp.concatenate([block(W, place) for place in PLACE_UP], 1), NT)


def first_back(V, A, inv1, F, dob, sums):
    def strip(i, carry):
        dg, dc, db = carry
        rows = at(i, STRIP)
        dy = F[rows, :]
        n = A[rows, :]
        gain = V[V_G1 : V_G1 + 1, :]
        dyn = dy * n
        e = dy * gain
        da = inv1[rows, :] * (e - jnp.mean(e, -1, keepdims=True) - n * jnp.mean(dyn * gain, -1, keepdims=True))
        low = da.astype(BF16)
        F[rows, :] = da
        dob[rows, :] = low
        return (
            dg + jnp.sum(dyn, 0, keepdims=True),
            dc + jnp.sum(dy, 0, keepdims=True),
            db + jnp.sum(low.astype(F32), 0, keepdims=True),
        )

    zero = jnp.zeros((1, D), F32)
    dg, dc, db = lax.fori_loop(0, ROWS // STRIP, strip, (zero, zero, zero))
    sums[V_G1 : V_G1 + 1, :] = dg
    sums[V_C1 : V_C1 + 1, :] = dc
    sums[V_BO : V_BO + 1, :] = db


def output_back(W, dob, dctx):
    def tile(n):
        cols = at(n, TILE)
        dctx[:, cols] = dot(dob[...], columns(W, PLACE_O, cols.start, TILE)).astype(BF16)

    loop(D // TILE, tile)


def column_sums(source, sums, row):
    sums[row : row + 1, :] = jnp.sum(source[...].astype(F32), 0, keepdims=True)


def input_back(W, q, k, v, F):
    for i in range(ROWS // TILE):
        rows = pl.ds(i * TILE, TILE)
        left = jnp.concatenate([q[rows, :], k[rows, :], v[rows, :]], 1)
        right = jnp.concatenate([block(W, place) for place in (PLACE_Q, PLACE_K, PLACE_V)], 1)
        F[rows, :] += dot(left, right, NT)


def to_down_order(dfb, perm, dfp):
    dfp[...] = dot(dfb[...], perm[...], NT).astype(BF16)


def permutation():
    r = np.arange(D)
    y, x, z, j = r // 192, r // 48 % 4, r // 12 % 4, r % 12
    p = np.zeros((D, D), np.float32)
    p[192 * z + 48 * x + 12 * y + j, r] = 1
    return p


MESH = pl.DeviceIdType.MESH
STEP = 10
ADAM_EPS = 1e-08
BETA_ONE = 0.9
BETA_TWO = 0.999
CLIP_NORM = 1.0
WEIGHT_DECAY = 0.01
ATTENTION_RATES = (0.02, 0.02, 0.04, 0.3)
HIDDEN_RATES = (0.04, 0.02)
VECTOR_RATE = 0.5
COPIES = 85
VECTORS = 12
SHARE = 6


class Net:
    def __init__(self, send_sem, recv_sem):
        self.send_sem, self.recv_sem, self.count, self.open = send_sem, recv_sem, 0, []

    def send(self, copies, whole):
        assert self.count < COPIES
        sems = dict(send_sem=self.send_sem.at[self.count], recv_sem=self.recv_sem.at[self.count])
        self.count += 1
        made = [
            pltpu.make_async_remote_copy(src_ref=a, dst_ref=b, device_id=(d,), device_id_type=MESH, **sems)
            for a, b, d in copies
        ]
        for copy in made:
            copy.start()
        group = pltpu.make_async_remote_copy(
            src_ref=whole, dst_ref=whole, device_id=(copies[0][2],), device_id_type=MESH, **sems
        )
        self.open.append(group)
        return group

    def sent(self, group):
        if any(one is group for one in self.open):
            group.wait_send()
            self.open = [one for one in self.open if one is not group]

    def close(self):
        for group in self.open:
            group.wait_send()
        self.open = []


def adam(master, first, second, gradient, rate, decay):
    first_new = BETA_ONE * first + (1.0 - BETA_ONE) * gradient
    second_new = BETA_TWO * second + (1.0 - BETA_TWO) * gradient * gradient
    first_hat = first_new * (1.0 / (1.0 - BETA_ONE**STEP))
    second_hat = second_new * (1.0 / (1.0 - BETA_TWO**STEP))
    step = first_hat * pl.reciprocal(jnp.sqrt(second_hat) + ADAM_EPS, approx=True)
    master_new = master - rate * (step + decay * master)
    return master_new, first_new, second_new


SCRATCH = dict(
    W=pltpu.VMEM((12, 4, 4, 48, D), BF16),
    G=pltpu.VMEM((SHARE, 4, 4, 48, D), BF16),
    pair_in=pltpu.VMEM((SHARE, 4, 4, 48, D), BF16),
    pair_out=pltpu.VMEM((8, 4, 4, 48, TILE), BF16),
    half_in=pltpu.VMEM((SHARE, 2, 2, 48, D), BF16),
    strip_in=pltpu.VMEM((SHARE, 3, 48, D), BF16),
    piece_in=pltpu.VMEM((3, SHARE, 16, D), BF16),
    first_out=pltpu.VMEM((SHARE, 8, D), F32),
    first_own=pltpu.VMEM((SHARE, 8, D), F32),
    first_in=pltpu.VMEM((SHARE, 8, D), F32),
    vec_own=pltpu.VMEM((8, LEN), F32),
    vec_in=pltpu.VMEM((8, LEN), F32),
    pieces=pltpu.VMEM((4, SHARE, 16, D), BF16),
    vec_pieces=pltpu.VMEM((4, 16, LEN), BF16),
    VT=pltpu.VMEM((4, 4, 48, LEN), BF16),
    line=pltpu.VMEM((48, D), F32),
    sums_in=pltpu.VMEM((2, 10, 8, D), F32),
    sums_out=pltpu.VMEM((2, 4, 8, D), F32),
    packed=pltpu.VMEM((4, 48, LEN), BF16),
    norm_out=pltpu.VMEM((2, 8, LEN), F32),
    norm_in=pltpu.VMEM((2, 15, 8, LEN), F32),
    V=pltpu.VMEM((16, D), F32),
    sums=pltpu.VMEM((16, D), F32),
    bias=pltpu.VMEM((SLOTS, LEN, LEN), F32),
    act=pltpu.VMEM((4, ROWS, D), BF16),
    p=pltpu.VMEM((SLOTS * PAIRS, 2 * LEN, LEN), BF16),
    A=pltpu.VMEM((ROWS, D), F32),
    F=pltpu.VMEM((ROWS, D), F32),
    FP=pltpu.VMEM((ROWS, D), F32),
    inv1=pltpu.VMEM((ROWS, 1), F32),
    y1b=pltpu.VMEM((ROWS, D), BF16),
    turned=pltpu.VMEM((2, D, ROWS), BF16),
    h=pltpu.VMEM((ROWS, FF), BF16),
    gp=pltpu.VMEM((ROWS, FF), BF16),
    dfb=pltpu.VMEM((ROWS, D), BF16),
    xb=pltpu.VMEM((ROWS, D), BF16),
    gb=pltpu.VMEM((ROWS, D), BF16),
    perm=pltpu.VMEM((D, D), BF16),
    att_w=pltpu.VMEM((6, 4, D), F32),
    hid_w=pltpu.VMEM((6, 2, FF), F32),
    vec_w=pltpu.VMEM((6, VECTORS), F32),
    load_sem=pltpu.SemaphoreType.DMA((12,)),
    store_sem=pltpu.SemaphoreType.DMA((11,)),
    send_sem=pltpu.SemaphoreType.DMA((COPIES,)),
    recv_sem=pltpu.SemaphoreType.DMA((COPIES,)),
)
NAMES = tuple(SCRATCH)


def step_kernel(
    x_hbm,
    g_hbm,
    perm_hbm,
    joined,
    half_lengths,
    att_hbm,
    hid_hbm,
    vec_hbm,
    out_hbm,
    grad_hbm,
    norm_out_ref,
    att_out,
    hid_out,
    vec_out,
    *scratch,
):
    s = dict(zip(NAMES, scratch))
    W, G, V = s["W"], s["G"], s["V"]
    xb, gb, perm = s["xb"], s["gb"], s["perm"]
    net = Net(s["send_sem"], s["recv_sem"])

    me = lax.axis_index("dp")
    c = lax.rem(me, 2)
    z = lax.rem(lax.div(me, 2), 4)
    x = lax.rem(lax.div(me, 8), 4)
    y = lax.div(me, 32)
    other = 1 - c

    def wrap(value):
        return lax.rem(value + 4, 4)

    def peer(axis, step):
        moved = {"x": x, "y": y, "z": z}
        moved[axis] = wrap(moved[axis] + step)
        return ((moved["y"] * 4 + moved["x"]) * 4 + moved["z"]) * 2 + c

    sibling = me + 1 - 2 * c

    def far_peer(step):
        return ((y * 4 + x) * 4 + wrap(z + step)) * 2 + other

    plane_peers = [((wrap(y + i // 4) * 4 + wrap(x + i % 4)) * 4 + z) * 2 + c for i in range(1, 16)]

    att_w, hid_w, vec_w = s["att_w"], s["hid_w"], s["vec_w"]
    masters_in = [
        pltpu.make_async_copy(source, target, s["load_sem"].at[9 + i])
        for i, (source, target) in enumerate(((att_hbm, att_w), (hid_hbm, hid_w), (vec_hbm, vec_w)))
    ]
    loads = []
    for i in range(SLOTS):
        loads.append(pltpu.make_async_copy(x_hbm.at[i], xb.at[pl.ds(i * LEN, LEN)], s["load_sem"].at[i]))
        loads.append(pltpu.make_async_copy(g_hbm.at[i], gb.at[pl.ds(i * LEN, LEN)], s["load_sem"].at[4 + i]))
    loads.append(pltpu.make_async_copy(perm_hbm, perm, s["load_sem"].at[8]))
    for copy in masters_in + loads:
        copy.start()

    barrier = pltpu.get_barrier_semaphore()
    partners = [sibling] + [peer(axis, step) for axis in "xyz" for step in (1, 2, 3)]
    for partner in partners:
        pl.semaphore_signal(barrier, inc=1, device_id=(partner,), device_id_type=MESH)

    for copy in masters_in:
        copy.wait()
    masters = [[att_w[:, 2 * core + l, :] for l in range(2)] for core in range(2)]
    for core in range(2):
        masters[core] += [hid_w[:, i, (2 * core + l) * D : (2 * core + l + 1) * D] for i in range(2) for l in range(2)]
    for l in range(SHARE):
        s["first_own"][l, 0:6, :] = jnp.where(c == 0, masters[0][l], masters[1][l])
        s["first_out"][l, 0:6, :] = jnp.where(c == 0, masters[1][l], masters[0][l])
    s["vec_own"][...] = jnp.zeros((8, LEN), F32)
    s["vec_own"][0:6, 0:VECTORS] = vec_w[...]
    line = s["line"]
    line[...] = jnp.zeros((48, D), F32)
    pl.semaphore_wait(barrier, len(partners))

    FIRST = {"x": "z", "y": "x", "z": "y"}
    SECOND = {"x": "y", "y": "z", "z": "x"}
    HERE = {"x": x, "y": y, "z": z}
    every = pl.ds(0, D)
    wide = pl.ds(0, 2 * TILE)
    part_cols = [pl.ds(part * TILE, TILE) for part in range(3)]
    third = part_cols[2]

    def span(count, size):
        for n in (4, 3, 2, 1):
            for k in (4, 3, 2, 1):
                if count % (n * k) == 0 and count // (n * k) <= 12:
                    return W.at[pl.ds(0, count // (n * k)), pl.ds(0, k), pl.ds(0, n), :, pl.ds(0, size)]
        raise ValueError

    def to_three(axis, copies):
        return [(source(step), target(step), peer(axis, step)) for source, target in copies for step in (1, 2, 3)]

    pair = [
        net.send([(a, b, sibling)], a)
        for a, b in (
            (s["first_out"].at[pl.ds(0, 2)], s["first_in"].at[pl.ds(0, 2)]),
            (s["vec_own"], s["vec_in"]),
            (s["first_out"].at[pl.ds(2, 4)], s["first_in"].at[pl.ds(2, 4)]),
        )
    ]
    fill_masks(joined, half_lengths, s["bias"])
    pieces, vec_pieces = s["pieces"], s["vec_pieces"]
    ATT = ((0, "x", wide), (1, "y", wide), (0, "z", third), (1, "z", third))
    p0, p1, p2 = part_cols
    PARTS = (
        ((2, "x", p0), (3, "y", p0), (4, "z", p0), (5, "z", p0)),
        ((2, "x", p1), (4, "x", p1), (3, "y", p1), (5, "z", p1)),
        ((2, "x", p2), (3, "y", p2), (5, "y", p2), (4, "z", p2)),
    )
    HID = (
        (2, "x", every),
        (3, "y", every),
        (4, "z", p0),
        (4, "x", p1),
        (4, "z", p2),
        (5, "z", pl.ds(0, 2 * TILE)),
        (5, "y", p2),
    )

    def turns(l, route):
        return (route == "z") != (l >= 4)

    def make_piece(l, route, cols):
        own, far = s["first_own"][l, 0:6, cols], s["first_in"][l, 0:6, cols]
        line[0:6, cols] = jnp.where(c == 0, own, far)
        line[6:12, cols] = jnp.where(c == 0, far, own)
        pieces[HERE[FIRST[route]], l, :, cols] = line[0:16, cols].astype(BF16)

    def send_pieces(some, units):
        copies = []
        for l, route, cols in some:
            near = pieces.at[HERE[FIRST[route]], l, :, cols]
            copies += [(near, near, peer(FIRST[route], step)) for step in (1, 2, 3)]
        return net.send(copies, span(units, D))

    pair[0].wait_recv()
    for some in ATT:
        make_piece(*some)
    att_pieces = send_pieces(ATT, 2)
    pair[2].wait_recv()
    for some in HID:
        make_piece(*some)
    hid_pieces = send_pieces(HID, 4)
    pair[1].wait_recv()
    own, far = s["vec_own"][0:6], s["vec_in"][0:6]
    line[0:6, 0:LEN] = jnp.where(c == 0, own, far)
    line[6:12, 0:LEN] = jnp.where(c == 0, far, own)
    vec_pieces[z] = line[0:16, 0:LEN].astype(BF16)
    near = vec_pieces.at[z]
    vec_copies = net.send([(near, near, peer("z", step)) for step in (1, 2, 3)], span(1, LEN))

    VT, packed = s["VT"], s["packed"]

    def stage(ref, l, index):
        return ref.at[pl.ds(pl.multiple_of(index * 48, 16), 48), pl.ds((l // 2) * D, D)]

    def spread(l, route, cols):
        for i in range(4):
            line[12 * i : 12 * i + 12, cols] = pieces[i, l, :, cols].astype(F32)[0:12]
        rows = line[:, cols].astype(BF16)
        if route == "x":
            W[6 * c + l, y, x, :, cols] = rows
        elif route == "y":
            stage(s["gp"], l, z)[:, cols] = rows
        else:
            W[6 * c + l, z, x, :, cols] = rows

    def strips(some, units):
        copies = []
        for l, route, cols in some:
            if route == "x":
                near = W.at[6 * c + l, y, x, :, cols]
            elif route == "y":
                near = stage(s["gp"], l, z).at[:, cols]
            else:
                near = W.at[6 * c + l, z, x, :, cols]
            copies += [(near, near, peer(SECOND[route], step)) for step in (1, 2, 3)]
        return net.send(copies, span(3 * units, copies[0][0].shape[-1]))

    def order_strips(l, cols):
        size = cols.size
        for i in range(4):
            FP[48 * i : 48 * i + 48, 0:size] = stage(s["gp"], l, i)[:, cols].astype(F32)
        for i in range(4):
            for j in range(4):
                line[12 * j : 12 * j + 12, 0:size] = FP[48 * j + 12 * i : 48 * j + 12 * i + 12, 0:size]
            W[6 * c + l, y, i, :, cols] = line[:, 0:size].astype(BF16)

    def turn_rows(ref, place, cols):
        rows = ref[place, :, :, :, cols].reshape(D, cols.size)
        ref[place, :, :, :, cols] = dot(perm[...], rows).astype(BF16).reshape(4, 4, 48, cols.size)

    def region(ref, place, route, index, half, cols):
        part = pl.ds(0, 4) if half is None else pl.ds(2 * half, 2)
        if route == "x":
            return ref.at[place, part, index, :, cols]
        return ref.at[place, index, part, :, cols]

    def gather_start(some):
        copies = []
        for l, route, cols in some:
            near = region(W, 6 * c + l, route, HERE[route], None, cols)
            copies += [(near, near, peer(route, step)) for step in (1, 2, 3)]
        return some, net.send(copies, span(12 * len(some), some[0][2].size))

    def gather_share(state):
        some, group = state
        group.wait_recv()
        if any(turns(l, route) for l, route, _ in some):
            net.sent(group)
        copies = []
        for l, route, cols in some:
            if turns(l, route):
                turn_rows(W, 6 * c + l, cols)
            near = W.at[6 * c + l, :, :, :, cols]
            copies.append((near, near, sibling))
        return net.send(copies, span(16 * len(some), some[0][2].size))

    act, p = s["act"], s["p"]
    q, k, v, ctx = (act.at[i] for i in range(4))
    A, F, FP, inv1, y1b = s["A"], s["F"], s["FP"], s["inv1"], s["y1b"]
    h, gp, dfb, dfp, sums = s["h"], s["gp"], s["dfb"], y1b, s["sums"]
    turned = s["turned"]

    att_pieces.wait_recv()
    att_strips = []
    for group in (ATT[:1], ATT[1:2], ATT[2:]):
        for some in group:
            spread(*some)
        att_strips.append(strips(group, len(group)))
    hid_pieces.wait_recv()
    for some in HID:
        spread(*some)
    z_strips = [strips(PARTS[0][2:], 2)]
    x_strips = strips(HID[:1], 1)
    y_strips = strips(HID[1:2], 1)
    z_strips.append(strips([(5, "z", p1), (4, "z", p2)], 2))
    x_rest = strips([(4, "x", p1)], 1)
    y_rest = strips([(5, "y", p2)], 1)
    vec_copies.wait_recv()
    for i in range(4):
        line[12 * i : 12 * i + 12, 0:LEN] = vec_pieces[i].astype(F32)[0:12]
    VT[y, x] = line[:, 0:LEN].astype(BF16)
    near = VT.at[y, x]
    vec_strips = net.send([(near, near, peer("x", step)) for step in (1, 2, 3)], span(3, LEN))
    starts = {}
    att_strips[0].wait_recv()
    for part in range(2):
        starts["x", part] = gather_start([(0, "x", part_cols[part])])
    att_strips[1].wait_recv()
    order_strips(1, wide)
    for part in range(2):
        starts["y", part] = gather_start([(1, "y", part_cols[part])])
    att_strips[2].wait_recv()
    for l in range(2):
        starts["t", l] = gather_start(ATT[2 + l : 3 + l])
    vec_strips.wait_recv()
    near = packed.at[y]
    packed[y] = sum(
        pltpu.roll(VT[y, i].astype(F32), 32 * i, 1) if i else VT[y, i].astype(F32) for i in range(4)
    ).astype(BF16)
    vec_last = net.send([(near, near, peer("y", step)) for step in (1, 2, 3)], span(3, LEN))
    for copy in loads:
        copy.wait()
    flows = {}

    def begin(part, route):
        flows[part, route] = gather_start([some for some in PARTS[part] if some[1] == route])

    def sharing(part, routes="xyz"):
        for route in routes:
            flows[part, route] = gather_share(flows[part, route])

    z_strips[0].wait_recv()
    begin(0, "z")
    x_strips.wait_recv()
    begin(0, "x")
    y_strips.wait_recv()
    order_strips(3, every)
    begin(0, "y")
    z_strips[1].wait_recv()
    begin(1, "z")
    x_rest.wait_recv()
    begin(1, "x")
    begin(1, "y")
    y_rest.wait_recv()
    order_strips(5, p2)
    for route in "zxy":
        begin(2, route)
    net.sent(att_strips[2])
    shares = [gather_share(starts[key]) for key in (("x", 0), ("y", 0), ("t", 0))]
    vec_last.wait_recv()
    net.sent(vec_strips)
    for i in range(4):
        block_i = packed[i].astype(F32)
        for j in range(4):
            VT[i, j] = (pltpu.roll(block_i, LEN - 32 * j, 1) if j else block_i).astype(BF16)
    V[...] = VT[...].reshape(D, LEN).astype(F32).T[0:16]
    shares += [gather_share(starts[key]) for key in (("x", 1), ("y", 1), ("t", 1))]
    for copy in shares:
        copy.wait_recv()
    qkv(W, V, xb, q, k, v)
    attend(q, k, v, s["bias"], p, ctx)
    net.sent(x_rest)
    sharing(0)
    first_norm(W, V, xb, ctx, A, inv1, F, y1b)
    turn(y1b, turned.at[1])
    sharing(1)

    def arrived(part):
        for route in "xyz":
            flows[part, route].wait_recv()

    arrived(0)
    net.sent(att_strips[1])
    net.sent(y_strips)
    net.sent(y_rest)
    up(W, V, y1b, h, gp, 0)
    down_(W, h, FP, 0)
    sharing(2)
    arrived(1)
    up(W, V, y1b, h, gp, 1)
    down_(W, h, FP, 1)
    arrived(2)
    up(W, V, y1b, h, gp, 2)
    down_(W, h, FP, 2)
    second_norm(V, perm, FP, F, gb, gb, dfb, sums)
    stores = []
    for i in range(SLOTS):
        stores.append(pltpu.make_async_copy(gb.at[pl.ds(i * LEN, LEN)], out_hbm.at[i], s["store_sem"].at[i]))
        stores[-1].start()
    to_down_order(dfb, perm, dfp)
    dfpT = turned.at[0]
    y1T = turned.at[1]
    turn(dfp, dfpT)
    net.close()

    pair_in, pair_out = s["pair_in"], s["pair_out"]
    G_half = s["half_in"]
    G_block = pair_in
    slots = [None] * 8

    def send_tiles(tiles):
        for slot, _, _, _ in tiles:
            if slots[slot] is not None:
                net.sent(slots[slot])
        values = [value() for _, _, _, value in tiles]
        for (slot, _, _, _), value in zip(tiles, values):
            pair_out[slot] = value.astype(BF16).reshape(4, 4, 48, TILE)
        group = net.send(
            [(pair_out.at[slot], pair_in.at[l, :, :, :, cols], sibling) for slot, l, cols, _ in tiles],
            span(16 * len(tiles), TILE),
        )
        for slot, _, _, _ in tiles:
            slots[slot] = group
        return group

    def add_into(ref, index, *others):
        total = ref[index].astype(F32)
        for other_ref, other_index in others:
            total = total + other_ref[other_index].astype(F32)
        ref[index] = total.astype(BF16)

    def cell(l, route, index, i, cols):
        return (l, i, index, slice(None), cols) if route == "x" else (l, index, i, slice(None), cols)

    def reduce_start(some):
        copies = []
        for l, route, cols in some:
            across = wrap(HERE[route] + 2)
            for half, step in ((0, 1), (1, 3)):
                copies.append((region(G, l, route, across, half, cols), G_half.at[l, half, :, :, cols], peer(route, step)))
        return some, net.send(copies, span(4 * len(some), TILE))

    def reduce_pass(state):
        some, group = state
        group.wait_recv()
        copies = []
        for l, route, cols in some:
            here = HERE[route]
            for i in range(2):
                add_into(G, cell(l, route, wrap(here + 1), i, cols), (G_half, (l, 0, i, slice(None), cols)))
                add_into(G, cell(l, route, wrap(here - 1), 2 + i, cols), (G_half, (l, 1, i, slice(None), cols)))
            for half, step in ((0, 1), (1, 3)):
                copies.append(
                    (region(G, l, route, wrap(here + step), None, cols), G_block.at[l, half, :, :, cols], peer(route, step))
                )
        return some, net.send(copies, span(8 * len(some), TILE))

    strip_in = s["strip_in"]

    def strip_place(l, route, moved):
        return (l, moved, x) if route == "x" else (l, z, moved)

    def reduce_end(state):
        some, group = state
        group.wait_recv()
        copies = []
        for l, route, cols in some:
            for i in range(4):
                add_into(
                    G,
                    cell(l, route, HERE[route], i, cols),
                    (G_block, (l, 0, i, slice(None), cols)),
                    (G_block, (l, 1, i, slice(None), cols)),
                )
            if route == "y":
                for i in range(4):
                    FP[48 * i : 48 * i + 48, 0:TILE] = G[l, y, i, :, cols].astype(F32)
                for j in range(4):
                    for i in range(4):
                        line[12 * i : 12 * i + 12, 0:TILE] = FP[48 * i + 12 * j : 48 * i + 12 * j + 12, 0:TILE]
                    stage(h, l, j)[:, cols] = line[:, 0:TILE].astype(BF16)
            for step in (1, 2, 3):
                target = wrap(HERE[SECOND[route]] + step)
                if route == "y":
                    source = stage(h, l, target).at[:, cols]
                else:
                    source = G.at[strip_place(l, route, target) + (slice(None), cols)]
                copies.append((source, strip_in.at[l, step - 1, :, cols], peer(SECOND[route], step)))
        return some, net.send(copies, span(3 * len(some), TILE))

    piece_out, piece_in = pieces, s["piece_in"]

    def strips_sum(state):
        some, group = state
        group.wait_recv()
        for l, route, cols in some:
            if route == "y":
                own = stage(h, l, z)[:, cols]
            else:
                own = G[strip_place(l, route, HERE[SECOND[route]]) + (slice(None), cols)]
            total = own.astype(F32)
            for i in range(3):
                total = total + strip_in[l, i, :, cols].astype(F32)
            line[:, 0:TILE] = total
            gap = jnp.zeros((4, TILE), F32)
            for i in range(4):
                rows = jnp.concatenate([line[12 * i : 12 * i + 12, 0:TILE], gap], 0)
                piece_out[i, l, :, cols] = rows.astype(BF16)

    def pieces_out(some, units):
        copies = []
        for l, route, cols in some:
            for step in (1, 2, 3):
                source = piece_out.at[wrap(HERE[FIRST[route]] + step), l, :, cols]
                copies.append((source, piece_in.at[step - 1, l, :, cols], peer(FIRST[route], step)))
        return net.send(copies, span(units, D))

    rows_out, rows_own, rows_in = s["first_out"], s["first_own"], s["first_in"]

    def pieces_sum(l, route, cols):
        total = piece_out[HERE[FIRST[route]], l, :, cols].astype(F32)
        for i in range(3):
            total = total + piece_in[i, l, :, cols].astype(F32)
        line[0:16, cols] = total
        top, bottom = line[0:6, cols], line[6:12, cols]
        rows_own[l, 0:6, cols] = jnp.where(c == 0, top, bottom)
        rows_out[l, 0:6, cols] = jnp.where(c == 0, bottom, top)
        return jnp.sum(top * top + bottom * bottom, keepdims=True)

    def hidden_slopes(core, part):
        places = [pl.ds(pl.multiple_of((2 * core + e) * D + part * TILE, LEN), TILE) for e in range(2)]
        slopes = []
        for e in range(2):
            dh = dot(dfp[...], columns(W, 6 * core + 4 + e, part * TILE, TILE))
            du = (dh * gp[:, places[e]].astype(F32)).astype(BF16)
            slopes.append(du)
            sums[pl.ds(V_B1 + 2 * core + e, 1), part_cols[part]] = jnp.sum(du.astype(F32), 0, keepdims=True)
        return places, slopes

    def keep_tiles(group, tiles):
        group.wait_recv()
        for l, cols, value in tiles:
            total = value() + pair_in[l, :, :, :, cols].reshape(D, TILE).astype(F32)
            G[l, :, :, :, cols] = total.astype(BF16).reshape(4, 4, 48, TILE)

    def hidden_tiles(places, slopes, cols):
        tiles = [(4 + e, cols, lambda e=e: dot(dfpT[...], h[:, places[e]])) for e in range(2)]
        return tiles + [(2 + e, cols, lambda e=e: dot(y1T[...], slopes[e])) for e in range(2)]

    shared = {}

    def others(part):
        places, slopes = hidden_slopes(other, part)
        tiles = hidden_tiles(places, slopes, part_cols[part])
        shared[part] = send_tiles([(4 * (part % 2) + i,) + tile for i, tile in enumerate(tiles)])
        for e in range(2):
            gp[:, places[e]] = slopes[e]

    def own_slopes(part):
        places, slopes = hidden_slopes(c, part)
        for e in range(2):
            gp[:, places[e]] = slopes[e]

    def own_tiles(part):
        places = [pl.ds(pl.multiple_of((2 * c + e) * D + part * TILE, LEN), TILE) for e in range(2)]
        keep_tiles(shared[part], hidden_tiles(places, [gp[:, place] for place in places], part_cols[part]))
        for l, route, cols in PARTS[part]:
            if turns(l, route):
                turn_rows(G, l, cols)
        return reduce_start(PARTS[part])

    others(0)
    others(1)
    own_slopes(0)
    flows[0] = own_tiles(0)
    others(2)
    own_slopes(1)
    flows[1] = own_tiles(1)
    flows[0] = reduce_pass(flows[0])
    own_slopes(2)
    flows[2] = own_tiles(2)
    first_back_product(W, gp, F)
    flows[1] = reduce_pass(flows[1])
    first_back(V, A, inv1, F, dfb, sums)
    flows[2] = reduce_pass(flows[2])
    flows[0] = reduce_end(flows[0])

    sums[VECTORS:16, :] = jnp.zeros((16 - VECTORS, D), F32)
    sums_in, sums_out = s["sums_in"], s["sums_out"]

    def sums_step(place, stage_, group, axis):
        if group is None:
            total = sums[8 * place : 8 * place + 8, :]
        else:
            total = sums_out[place, stage_ - 1]
            group.wait_recv()
            for i in range(1 if stage_ == 1 else 3):
                total = total + sums_in[place, 0 if stage_ == 1 else 3 * stage_ - 5 + i]
        if axis is None:
            return total
        sums_out[place, stage_] = total
        near = sums_out.at[place, stage_]
        if stage_ == 0:
            return net.send([(near, sums_in.at[place, 0], sibling)], near)
        base = 3 * stage_ - 3
        return net.send(
            [(near, sums_in.at[place, base + step], peer(axis, step)) for step in (1, 2, 3)],
            sums_in.at[place, pl.ds(0, 3)],
        )

    up_sums = sums_step(1, 0, None, "sibling")
    doT = turned.at[1]
    turn(dfb, doT)
    output_back(W, dfb, y1b)
    up_sums = sums_step(1, 1, up_sums, "z")
    turn(xb, turned.at[0])

    def projection_grad(core, l, n):
        left = core if l == 1 else 0
        return dot(turned[left], act[2 * core + l, :, n * TILE : (n + 1) * TILE])

    def projection_tiles(core, n):
        return [(l, part_cols[n], lambda l=l: projection_grad(core, l, n)) for l in (0, 1)]

    last = []

    def other_projections(n):
        attend_back(q, k, v, p, y1b, n)
        tiles = projection_tiles(other, n)
        shared["p", n] = send_tiles([(2 * n + i,) + tile for i, tile in enumerate(tiles)])

    def own_projections(n):
        keep_tiles(shared["p", n], projection_tiles(c, n))
        if n == 2:
            for l in (0, 1):
                turn_rows(G, l, third)
        last.append(reduce_start([(l, "z" if n == 2 else "xy"[l], part_cols[n]) for l in (0, 1)]))

    other_projections(2)
    other_projections(0)
    flows[1] = reduce_end(flows[1])
    up_sums = sums_step(1, 2, up_sums, "x")
    own_projections(2)
    other_projections(1)
    column_sums(q, sums, V_BQ)
    column_sums(v, sums, V_BV)
    first_sums = sums_step(0, 0, None, "sibling")
    own_projections(0)
    flows[2] = reduce_end(flows[2])
    first_sums = sums_step(0, 1, first_sums, "z")
    own_projections(1)
    last[0] = reduce_pass(last[0])
    for group in pair + [att_pieces, hid_pieces]:
        net.sent(group)
    strips_sum(flows[0])
    strips_sum(flows[1])
    last[1] = reduce_pass(last[1])
    input_back(W, q, k, v, F)
    for i in range(SLOTS):
        stores.append(pltpu.make_async_copy(F.at[pl.ds(i * LEN, LEN)], grad_hbm.at[i], s["store_sem"].at[4 + i]))
        stores[-1].start()
    last[2] = reduce_pass(last[2])
    first_sums = sums_step(0, 2, first_sums, "x")
    up_sums = sums_step(1, 3, up_sums, "y")
    strips_sum(flows[2])
    hid_pieces = pieces_out(HID, 4)
    for n in range(3):
        last[n] = reduce_end(last[n])
    first_sums = sums_step(0, 3, first_sums, "y")
    hid_pieces.wait_recv()
    squares = jnp.zeros((1, 1), F32)
    for some in HID:
        squares = squares + pieces_sum(*some)
    rows_copies = [net.send([(rows_out.at[pl.ds(2, 4)], rows_in.at[pl.ds(2, 4)], sibling)], rows_out.at[pl.ds(2, 4)])]
    for n in range(3):
        strips_sum(last[n])
    att_pieces = pieces_out(ATT, 2)
    vec_total = jnp.concatenate([sums_step(0, 4, first_sums, None), sums_step(1, 4, up_sums, None)], 0)
    place = lax.broadcasted_iota(jnp.int32, (8, D), 1) - 6 * me
    pick = (place == lax.broadcasted_iota(jnp.int32, (8, D), 0)).astype(BF16)
    vec_grad = jnp.zeros((8, 16), F32)
    for _ in range(3):
        low = vec_total.astype(BF16)
        vec_grad = vec_grad + dot(pick, low, NT)
        vec_total = vec_total - low.astype(F32)
    vec_grad = vec_grad[0:6, 0:VECTORS]
    squares = squares + jnp.sum(vec_grad * vec_grad, keepdims=True)
    att_pieces.wait_recv()
    for some in ATT:
        squares = squares + pieces_sum(*some)
    norm_out, norm_in = s["norm_out"], s["norm_in"]
    norm_out[0] = jnp.broadcast_to(squares, (8, LEN))
    plane = [(norm_out.at[0], norm_in.at[0, i], device) for i, device in enumerate(plane_peers)]
    norm_group = net.send(plane, norm_in.at[0])
    rows_copies.append(
        net.send([(rows_out.at[pl.ds(0, 2)], rows_in.at[pl.ds(0, 2)], sibling)], rows_out.at[pl.ds(0, 2)])
    )
    for copy in rows_copies:
        copy.wait_recv()
    att_grad, hid_grad, vec_grad_at = att_w, hid_w, vec_w
    vec_grad_at[...] = vec_grad
    for core in range(2):
        for l in range(SHARE):
            value = jnp.where(c == core, rows_own[l, 0:6], rows_in[l, 0:6])
            if l < 2:
                att_grad[:, 2 * core + l, :] = value
            else:
                i, j = (l - 2) // 2, 2 * core + l % 2
                hid_grad[:, i, j * D : (j + 1) * D] = value
    for i, (source, target) in enumerate(((att_grad, att_out), (hid_grad, hid_out), (vec_grad_at, vec_out))):
        stores.append(pltpu.make_async_copy(source, target, s["store_sem"].at[8 + i]))
        stores[-1].start()

    def norm_step(index, group, count):
        group.wait_recv()
        total = norm_out[index]
        for i in range(count):
            total = total + norm_in[index, i]
        return total

    norm_out[1] = norm_step(0, norm_group, 15)
    copies = [(norm_out.at[1], norm_in.at[1, 0], sibling)]
    for step in (1, 2, 3):
        copies.append((norm_out.at[1], norm_in.at[1, step], peer("z", step)))
        copies.append((norm_out.at[1], norm_in.at[1, 3 + step], far_peer(step)))
    norm_group = net.send(copies, norm_in.at[1, pl.ds(0, 7)])
    norm = jnp.sqrt(norm_step(1, norm_group, 7))
    norm_out_ref[...] = norm[0:1, 0:1]
    for copy in stores:
        copy.wait()
    net.close()


def rates(values, shape):
    index = lax.broadcasted_iota(jnp.int32, shape, 1)
    rate = jnp.full(shape, values[0], F32)
    for i, value in enumerate(values[1:]):
        rate = jnp.where(index == i + 1, value, rate)
    return rate


def update_kernel(out_in, grad_in, norm, *refs):
    sources, (out_hbm, grad_hbm), targets = refs[:12], refs[12:14], refs[14:23]
    out_at, grad_at = refs[23:25]
    held, sems = refs[25:37], refs[37]
    loads = [pltpu.make_async_copy(a, b, sems.at[i]) for i, (a, b) in enumerate(zip(sources, held))]
    passing = [pltpu.make_async_copy(out_in, out_at, sems.at[12]), pltpu.make_async_copy(grad_in, grad_at, sems.at[13])]
    for copy in loads + passing:
        copy.start()
    stores = [pltpu.make_async_copy(out_at, out_hbm, sems.at[14]), pltpu.make_async_copy(grad_at, grad_hbm, sems.at[15])]
    factor = CLIP_NORM / jnp.maximum(norm[...], CLIP_NORM)
    settings = (
        (rates(ATTENTION_RATES, (6, 4, D)), WEIGHT_DECAY),
        (rates(HIDDEN_RATES, (6, 2, FF)), WEIGHT_DECAY),
        (VECTOR_RATE, 0.0),
    )
    for i in (1, 0, 2):
        for j in (i, 3 + 3 * i, 4 + 3 * i, 5 + 3 * i):
            loads[j].wait()
        state = held[3 + 3 * i : 6 + 3 * i]
        new = adam(state[0][...], state[1][...], state[2][...], held[i][...] * factor, *settings[i])
        for j in range(3):
            state[j][...] = new[j]
            stores.append(pltpu.make_async_copy(state[j], targets[3 * i + j], sems.at[16 + 3 * i + j]))
        if i == 1:
            for load, copy in zip(passing, stores):
                load.wait()
                copy.start()
        for copy in stores[-3:]:
            copy.start()
    for copy in stores:
        copy.wait()


def on_device(
    inputs,
    cotangent,
    joined,
    half_lengths,
    attention_master,
    attention_first,
    attention_second,
    hidden_master,
    hidden_first,
    hidden_second,
    vector_master,
    vector_first,
    vector_second,
):
    any_space = pl.BlockSpec(memory_space=pl.ANY)
    vmem = pl.BlockSpec(memory_space=pltpu.VMEM)
    smem = pl.BlockSpec(memory_space=pltpu.SMEM)
    like = lambda a: jax.ShapeDtypeStruct(a.shape, a.dtype)
    swap = lambda a: jnp.transpose(a, (1, 0, 2))
    attention = [swap(a) for a in (attention_master, attention_first, attention_second)]
    hidden = [swap(a) for a in (hidden_master, hidden_first, hidden_second)]
    vectors = [a.T for a in (vector_master, vector_first, vector_second)]
    params = attention + hidden + vectors
    out_like = jax.ShapeDtypeStruct(inputs.shape, BF16)
    grad_like = jax.ShapeDtypeStruct(inputs.shape, F32)
    results = pl.pallas_call(
        step_kernel,
        out_shape=(
            out_like,
            grad_like,
            jax.ShapeDtypeStruct((1, 1), F32),
            like(attention[0]),
            like(hidden[0]),
            like(vectors[0]),
        ),
        in_specs=[any_space] * 3 + [smem] * 2 + [any_space] * 3,
        out_specs=(any_space, any_space, vmem) + (any_space,) * 3,
        scratch_shapes=list(SCRATCH.values()),
        compiler_params=pltpu.CompilerParams(collective_id=0, has_side_effects=True, vmem_limit_bytes=64 << 20),
        cost_estimate=pl.CostEstimate(flops=22 * 10**9, bytes_accessed=6 * 10**6, transcendentals=4 * 10**6),
    )(
        inputs,
        cotangent,
        jnp.asarray(permutation(), BF16),
        joined.T,
        jnp.transpose(half_lengths, (1, 2, 0)),
        attention[0],
        hidden[0],
        vectors[0],
    )
    outs = pl.pallas_call(
        update_kernel,
        out_shape=(out_like, grad_like) + tuple(like(a) for a in params),
        in_specs=[any_space] * 2 + [vmem] + [any_space] * 12,
        out_specs=(any_space,) * 11,
        scratch_shapes=[
            pltpu.VMEM(inputs.shape, BF16),
            pltpu.VMEM(inputs.shape, F32),
            *[pltpu.VMEM(a.shape, F32) for a in (attention[0], hidden[0], vectors[0], *params)],
            pltpu.SemaphoreType.DMA((25,)),
        ],
        cost_estimate=pl.CostEstimate(flops=2 * 10**6, bytes_accessed=7 * 10**6, transcendentals=10**5),
    )(*results, *params)
    output, input_grad, *new = outs
    norm = results[2].reshape(())
    return (output, input_grad, norm, *[swap(a) for a in new[:6]], *[a.T for a in new[6:]])


def solution(mesh):
    shard = P(None, "dp", None)
    flat = P(None, "dp")
    return jax.shard_map(
        on_device,
        mesh=mesh,
        in_specs=(shard, shard, flat, shard, shard, shard, shard, shard, shard, shard, flat, flat, flat),
        out_specs=(shard, shard, P(), shard, shard, shard, shard, shard, shard, flat, flat, flat),
        check_vma=False,
    )
```

```python
import functools
import jax
import jax.numpy as jnp
import numpy as np
from jax import lax
from jax.experimental import pallas as pl
from jax.experimental.pallas import tpu as pltpu
from jax.sharding import PartitionSpec as P

F32 = jnp.float32
BF16 = jnp.bfloat16
D = 768
FF = 3072
ROWS = 512
SLOTS = 4
LEN = 128
PAIRS = 6
TILE = 256
NORM_EPS = 1e-05
MASKED = -1e30
NN = (((1,), (0,)), ((), ()))
NT = (((1,), (1,)), ((), ()))
TN = (((0,), (0,)), ((), ()))
PLACE_Q, PLACE_K, PLACE_V, PLACE_O = 0, 1, 6, 7
PLACE_UP = (2, 3, 8, 9)
PLACE_DOWN = (4, 5, 10, 11)
V_BQ, V_BV, V_BO, V_G1, V_C1, V_G2, V_C2, V_B2, V_B1 = range(9)


def dot(a, b, dims=NN):
    return lax.dot_general(a, b, dims, preferred_element_type=F32)


def block(ref, place):
    return ref[place].reshape(D, D)


def columns(ref, place, start, size):
    return ref[place, :, :, :, pl.ds(start, size)].reshape(D, size)


def put_columns(ref, place, start, size, value):
    ref[place, :, :, :, pl.ds(start, size)] = value.reshape(4, 4, 48, size)


def loop(count, body):
    lax.fori_loop(0, count, lambda i, c: (body(i), c)[1], 0)


def at(i, size):
    return pl.ds(pl.multiple_of(i * size, size), size)


def qkv(W, V, xb, q, k, v):
    x = xb[...]
    for n in range(D // TILE):
        cols = pl.ds(n * TILE, TILE)
        q[:, cols] = ((dot(x, columns(W, PLACE_Q, n * TILE, TILE)) + V[V_BQ, cols]).astype(BF16) * 0.125).astype(BF16)
        k[:, cols] = dot(x, columns(W, PLACE_K, n * TILE, TILE)).astype(BF16)
        v[:, cols] = (dot(x, columns(W, PLACE_V, n * TILE, TILE)) + V[V_BV, cols]).astype(BF16)


def halves(value):
    lane = lax.broadcasted_iota(jnp.int32, value.shape, 1)
    zero = jnp.zeros_like(value)
    return jnp.concatenate([jnp.where(lane < 64, value, zero), jnp.where(lane < 64, zero, value)], 0)


def joined_halves(value):
    lane = lax.broadcasted_iota(jnp.int32, (LEN, LEN), 1)
    return jnp.where(lane < 64, value[:LEN], value[LEN:])


def fill_masks(joined, half_lengths, bias):
    query = lax.broadcasted_iota(jnp.int32, (LEN, LEN), 0)
    key = lax.broadcasted_iota(jnp.int32, (LEN, LEN), 1)
    for slot in range(SLOTS):
        is_joined = joined[0, slot]
        low = half_lengths[0, 0, slot]
        high = half_lengths[0, 1, slot]
        upper = (key >= 64).astype(jnp.int32)
        limit = is_joined * (64 + high) + (1 - is_joined) * (upper * (64 + high) + (1 - upper) * low)
        apart = (1 - is_joined) * jnp.abs((query >= 64).astype(jnp.int32) - upper)
        bias[slot] = jnp.where((key < limit) & (apart == 0), 0.0, MASKED)


GROUP = 6


def attend(q, k, v, bias, p, ctx):
    def units(slot):
        rows = at(slot, LEN)
        m = bias[slot]
        hidden = jnp.concatenate([m, m], 0) < 0
        cols = [pl.ds(pair * LEN, LEN) for pair in range(PAIRS)]
        for start in range(0, PAIRS, GROUP):
            some = range(start, start + GROUP)
            s = [dot(halves(q[rows, cols[i]]), k[rows, cols[i]], NT) for i in some]
            values = [v[rows, cols[i]] for i in some]
            s = [jnp.where(hidden, MASKED, one) for one in s]
            e = [jnp.exp(one - jnp.max(one, -1, keepdims=True)) for one in s]
            low = [(one * (1.0 / jnp.sum(one, -1, keepdims=True))).astype(BF16) for one in e]
            out = [joined_halves(dot(one, value)).astype(BF16) for one, value in zip(low, values)]
            for i, one, result in zip(some, low, out):
                p[slot * PAIRS + i] = one
                ctx[rows, cols[i]] = result

    loop(SLOTS, units)


def attend_back(q, k, v, p, dctx, n):
    def units(step):
        some = [(2 * step + slot, pair) for slot in range(2) for pair in (2 * n, 2 * n + 1)]
        places = [(at(slot, LEN), pl.ds(pair * LEN, LEN)) for slot, pair in some]
        low = [p[slot * PAIRS + pair] for slot, pair in some]
        two = [halves(dctx[place]) for place in places]
        q2 = [halves(q[place]) for place in places]
        keys = [k[place] for place in places]
        dp = [dot(a, v[place], NT) for a, place in zip(two, places)]
        dv = [dot(a, b, TN) for a, b in zip(low, two)]
        full = [a.astype(F32) for a in low]
        ds = [(a * (b - jnp.sum(a * b, -1, keepdims=True))).astype(BF16) for a, b in zip(full, dp)]
        dq = [joined_halves(dot(a, b)) * 0.125 for a, b in zip(ds, keys)]
        dk = [dot(a, b, TN) for a, b in zip(ds, q2)]
        for a, b, d, place in zip(dv, dq, dk, places):
            v[place] = a.astype(BF16)
            q[place] = b.astype(BF16)
            k[place] = d.astype(BF16)

    loop(2, units)


STRIP = 256


def first_norm(W, V, xb, ctx, A, inv1, F, y1b):
    A[...] = dot(ctx[...], block(W, PLACE_O), NT)

    def strip(i):
        rows = at(i, STRIP)
        a = xb[rows, :].astype(F32) + A[rows, :] + V[V_BO : V_BO + 1, :]
        center = a - jnp.mean(a, -1, keepdims=True)
        inverse = lax.rsqrt(jnp.mean(center * center, -1, keepdims=True) + NORM_EPS)
        n = center * inverse
        A[rows, :] = n
        inv1[rows, :] = inverse
        y = n * V[V_G1 : V_G1 + 1, :] + V[V_C1 : V_C1 + 1, :]
        y1b[rows, :] = y.astype(BF16)
        F[rows, :] = y + V[V_B2 : V_B2 + 1, :]

    loop(ROWS // STRIP, strip)


def gelu_parts(u):
    e = jnp.exp(-0.5 * (u * u))
    t = pl.reciprocal(1.0 + 0.23164190 * jnp.abs(u), approx=True)
    poly = ((((0.5307027145 * t - 0.726576013) * t + 0.7107068705) * t - 0.142248368) * t + 0.127414796) * t
    tail = poly * e
    cdf = jnp.where(u >= 0, 1.0 - tail, tail)
    return u * cdf, cdf + (u * 0.3989422804014327) * e


def up(W, V, y1b, h, gp, part):
    for j, place in enumerate(PLACE_UP):
        cols = pl.ds(j * D + part * TILE, TILE)
        u = dot(y1b[...], columns(W, place, part * TILE, TILE)) + V[V_B1 + j : V_B1 + j + 1, pl.ds(part * TILE, TILE)]
        value, slope = gelu_parts(u)
        h[:, cols] = value.astype(BF16)
        gp[:, cols] = slope.astype(BF16)


def down_(W, h, FP, part):
    left = jnp.concatenate([h[:, pl.ds(j * D + part * TILE, TILE)] for j in range(4)], 1)
    right = jnp.concatenate([columns(W, place, part * TILE, TILE) for place in PLACE_DOWN], 1)
    total = dot(left, right, NT)
    FP[...] = total if part == 0 else FP[...] + total


def second_norm(V, perm, FP, F, gb, outb, dfb, sums):
    F[...] += dot(FP[...].astype(BF16), perm[...])

    def strip(i, carry):
        dg, dc, db = carry
        rows = at(i, STRIP)
        z = F[rows, :]
        center = z - jnp.mean(z, -1, keepdims=True)
        inverse = lax.rsqrt(jnp.mean(center * center, -1, keepdims=True) + NORM_EPS)
        n = center * inverse
        gain = V[V_G2 : V_G2 + 1, :]
        g = gb[rows, :].astype(F32)
        outb[rows, :] = (n * gain + V[V_C2 : V_C2 + 1, :]).astype(BF16)
        gn = g * n
        e = g * gain
        dz = inverse * (e - jnp.mean(e, -1, keepdims=True) - n * jnp.mean(gn * gain, -1, keepdims=True))
        low = dz.astype(BF16)
        F[rows, :] = dz
        dfb[rows, :] = low
        return (
            dg + jnp.sum(gn, 0, keepdims=True),
            dc + jnp.sum(g, 0, keepdims=True),
            db + jnp.sum(low.astype(F32), 0, keepdims=True),
        )

    zero = jnp.zeros((1, D), F32)
    dg, dc, db = lax.fori_loop(0, ROWS // STRIP, strip, (zero, zero, zero))
    sums[V_G2 : V_G2 + 1, :] = dg
    sums[V_C2 : V_C2 + 1, :] = dc
    sums[V_B2 : V_B2 + 1, :] = db


def turn(source, target):
    for i in range(ROWS // LEN):
        target[:, i * LEN : (i + 1) * LEN] = source[i * LEN : (i + 1) * LEN, :].T


def first_back_product(W, gp, F):
    for i in range(ROWS // TILE):
        rows = pl.ds(i * TILE, TILE)
        F[rows, :] += dot(gp[rows, :], jnp.concatenate([block(W, place) for place in PLACE_UP], 1), NT)


def first_back(V, A, inv1, F, dob, sums):
    def strip(i, carry):
        dg, dc, db = carry
        rows = at(i, STRIP)
        dy = F[rows, :]
        n = A[rows, :]
        gain = V[V_G1 : V_G1 + 1, :]
        dyn = dy * n
        e = dy * gain
        da = inv1[rows, :] * (e - jnp.mean(e, -1, keepdims=True) - n * jnp.mean(dyn * gain, -1, keepdims=True))
        low = da.astype(BF16)
        F[rows, :] = da
        dob[rows, :] = low
        return (
            dg + jnp.sum(dyn, 0, keepdims=True),
            dc + jnp.sum(dy, 0, keepdims=True),
            db + jnp.sum(low.astype(F32), 0, keepdims=True),
        )

    zero = jnp.zeros((1, D), F32)
    dg, dc, db = lax.fori_loop(0, ROWS // STRIP, strip, (zero, zero, zero))
    sums[V_G1 : V_G1 + 1, :] = dg
    sums[V_C1 : V_C1 + 1, :] = dc
    sums[V_BO : V_BO + 1, :] = db


def output_back(W, dob, dctx):
    def tile(n):
        cols = at(n, TILE)
        dctx[:, cols] = dot(dob[...], columns(W, PLACE_O, cols.start, TILE)).astype(BF16)

    loop(D // TILE, tile)


def column_sums(source, sums, row):
    sums[row : row + 1, :] = jnp.sum(source[...].astype(F32), 0, keepdims=True)


def input_back(W, q, k, v, F, i):
    rows = pl.ds(i * TILE, TILE)
    left = jnp.concatenate([q[rows, :], k[rows, :], v[rows, :]], 1)
    right = jnp.concatenate([block(W, place) for place in (PLACE_Q, PLACE_K, PLACE_V)], 1)
    F[rows, :] += dot(left, right, NT)


def to_down_order(dfb, perm, dfp):
    dfp[...] = dot(dfb[...], perm[...], NT).astype(BF16)


def permutation():
    r = np.arange(D)
    y, x, z, j = r // 192, r // 48 % 4, r // 12 % 4, r % 12
    p = np.zeros((D, D), np.float32)
    p[192 * z + 48 * x + 12 * y + j, r] = 1
    return p


MESH = pl.DeviceIdType.MESH
STEP = 10
ADAM_EPS = 1e-08
BETA_ONE = 0.9
BETA_TWO = 0.999
CLIP_NORM = 1.0
WEIGHT_DECAY = 0.01
ATTENTION_RATES = (0.02, 0.02, 0.04, 0.3)
HIDDEN_RATES = (0.04, 0.02)
VECTOR_RATE = 0.5
COPIES = 85
VECTORS = 12
SHARE = 6


class Net:
    def __init__(self, send_sem, recv_sem):
        self.send_sem, self.recv_sem, self.count, self.open = send_sem, recv_sem, 0, []

    def send(self, copies, whole):
        assert self.count < COPIES
        sems = dict(send_sem=self.send_sem.at[self.count], recv_sem=self.recv_sem.at[self.count])
        self.count += 1
        made = [
            pltpu.make_async_remote_copy(src_ref=a, dst_ref=b, device_id=(d,), device_id_type=MESH, **sems)
            for a, b, d in copies
        ]
        for copy in made:
            copy.start()
        group = pltpu.make_async_remote_copy(
            src_ref=whole, dst_ref=whole, device_id=(copies[0][2],), device_id_type=MESH, **sems
        )
        self.open.append(group)
        return group

    def sent(self, group):
        if any(one is group for one in self.open):
            group.wait_send()
            self.open = [one for one in self.open if one is not group]

    def close(self):
        for group in self.open:
            group.wait_send()
        self.open = []


def adam(master, first, second, gradient, rate, decay):
    first_new = BETA_ONE * first + (1.0 - BETA_ONE) * gradient
    second_new = BETA_TWO * second + (1.0 - BETA_TWO) * gradient * gradient
    first_hat = first_new * (1.0 / (1.0 - BETA_ONE**STEP))
    second_hat = second_new * (1.0 / (1.0 - BETA_TWO**STEP))
    step = first_hat * pl.reciprocal(jnp.sqrt(second_hat) + ADAM_EPS, approx=True)
    master_new = master - rate * (step + decay * master)
    return master_new, first_new, second_new


SCRATCH = dict(
    W=pltpu.VMEM((12, 4, 4, 48, D), BF16),
    G=pltpu.VMEM((SHARE, 4, 4, 48, D), BF16),
    pair_in=pltpu.VMEM((SHARE, 4, 4, 48, D), BF16),
    pair_out=pltpu.VMEM((8, 4, 4, 48, TILE), BF16),
    half_in=pltpu.VMEM((SHARE, 2, 2, 48, D), BF16),
    strip_in=pltpu.VMEM((SHARE, 3, 48, D), BF16),
    piece_in=pltpu.VMEM((3, SHARE, 16, D), BF16),
    first_out=pltpu.VMEM((SHARE, 8, D), F32),
    first_own=pltpu.VMEM((SHARE, 8, D), F32),
    first_in=pltpu.VMEM((SHARE, 8, D), F32),
    vec_own=pltpu.VMEM((8, LEN), F32),
    vec_in=pltpu.VMEM((8, LEN), F32),
    pieces=pltpu.VMEM((4, SHARE, 16, D), BF16),
    vec_pieces=pltpu.VMEM((4, 16, LEN), BF16),
    VT=pltpu.VMEM((4, 4, 48, LEN), BF16),
    line=pltpu.VMEM((48, D), F32),
    sums_in=pltpu.VMEM((2, 10, 8, D), F32),
    sums_out=pltpu.VMEM((2, 4, 8, D), F32),
    packed=pltpu.VMEM((4, 48, LEN), BF16),
    norm_out=pltpu.VMEM((2, 8, LEN), F32),
    norm_in=pltpu.VMEM((2, 15, 8, LEN), F32),
    V=pltpu.VMEM((16, D), F32),
    sums=pltpu.VMEM((16, D), F32),
    bias=pltpu.VMEM((SLOTS, LEN, LEN), F32),
    act=pltpu.VMEM((4, ROWS, D), BF16),
    p=pltpu.VMEM((SLOTS * PAIRS, 2 * LEN, LEN), BF16),
    A=pltpu.VMEM((ROWS, D), F32),
    F=pltpu.VMEM((ROWS, D), F32),
    FP=pltpu.VMEM((ROWS, D), F32),
    inv1=pltpu.VMEM((ROWS, 1), F32),
    y1b=pltpu.VMEM((ROWS, D), BF16),
    turned=pltpu.VMEM((2, D, ROWS), BF16),
    h=pltpu.VMEM((ROWS, FF), BF16),
    gp=pltpu.VMEM((ROWS, FF), BF16),
    dfb=pltpu.VMEM((ROWS, D), BF16),
    xb=pltpu.VMEM((ROWS, D), BF16),
    gb=pltpu.VMEM((ROWS, D), BF16),
    perm=pltpu.VMEM((D, D), BF16),
    att_w=pltpu.VMEM((6, 4, D), F32),
    hid_w=pltpu.VMEM((6, 2, FF), F32),
    vec_w=pltpu.VMEM((6, VECTORS), F32),
    load_sem=pltpu.SemaphoreType.DMA((12,)),
    store_sem=pltpu.SemaphoreType.DMA((11,)),
    send_sem=pltpu.SemaphoreType.DMA((COPIES,)),
    recv_sem=pltpu.SemaphoreType.DMA((COPIES,)),
)
NAMES = tuple(SCRATCH)


def step_kernel(
    x_hbm,
    g_hbm,
    perm_hbm,
    joined,
    half_lengths,
    att_hbm,
    hid_hbm,
    vec_hbm,
    out_hbm,
    grad_hbm,
    norm_out_ref,
    att_out,
    hid_out,
    vec_out,
    *scratch,
):
    s = dict(zip(NAMES, scratch))
    W, G, V = s["W"], s["G"], s["V"]
    xb, gb, perm = s["xb"], s["gb"], s["perm"]
    net = Net(s["send_sem"], s["recv_sem"])

    me = lax.axis_index("dp")
    c = lax.rem(me, 2)
    z = lax.rem(lax.div(me, 2), 4)
    x = lax.rem(lax.div(me, 8), 4)
    y = lax.div(me, 32)
    other = 1 - c

    def wrap(value):
        return lax.rem(value + 4, 4)

    def peer(axis, step):
        moved = {"x": x, "y": y, "z": z}
        moved[axis] = wrap(moved[axis] + step)
        return ((moved["y"] * 4 + moved["x"]) * 4 + moved["z"]) * 2 + c

    sibling = me + 1 - 2 * c

    def far_peer(step):
        return ((y * 4 + x) * 4 + wrap(z + step)) * 2 + other

    plane_peers = [((wrap(y + i // 4) * 4 + wrap(x + i % 4)) * 4 + z) * 2 + c for i in range(1, 16)]

    att_w, hid_w, vec_w = s["att_w"], s["hid_w"], s["vec_w"]
    masters_in = [
        pltpu.make_async_copy(source, target, s["load_sem"].at[9 + i])
        for i, (source, target) in enumerate(((att_hbm, att_w), (hid_hbm, hid_w), (vec_hbm, vec_w)))
    ]
    loads = []
    for i in range(SLOTS):
        loads.append(pltpu.make_async_copy(x_hbm.at[i], xb.at[pl.ds(i * LEN, LEN)], s["load_sem"].at[i]))
        loads.append(pltpu.make_async_copy(g_hbm.at[i], gb.at[pl.ds(i * LEN, LEN)], s["load_sem"].at[4 + i]))
    loads.append(pltpu.make_async_copy(perm_hbm, perm, s["load_sem"].at[8]))
    for copy in masters_in + loads:
        copy.start()

    barrier = pltpu.get_barrier_semaphore()
    partners = [sibling] + [peer(axis, step) for axis in "xyz" for step in (1, 2, 3)]
    for partner in partners:
        pl.semaphore_signal(barrier, inc=1, device_id=(partner,), device_id_type=MESH)

    for copy in masters_in:
        copy.wait()
    masters = [[att_w[:, 2 * core + l, :] for l in range(2)] for core in range(2)]
    for core in range(2):
        masters[core] += [hid_w[:, i, (2 * core + l) * D : (2 * core + l + 1) * D] for i in range(2) for l in range(2)]
    for l in range(SHARE):
        s["first_own"][l, 0:6, :] = jnp.where(c == 0, masters[0][l], masters[1][l])
        s["first_out"][l, 0:6, :] = jnp.where(c == 0, masters[1][l], masters[0][l])
    s["vec_own"][...] = jnp.zeros((8, LEN), F32)
    s["vec_own"][0:6, 0:VECTORS] = vec_w[...]
    line = s["line"]
    line[...] = jnp.zeros((48, D), F32)
    pl.semaphore_wait(barrier, len(partners))

    FIRST = {"x": "z", "y": "x", "z": "y"}
    SECOND = {"x": "y", "y": "z", "z": "x"}
    HERE = {"x": x, "y": y, "z": z}
    every = pl.ds(0, D)
    wide = pl.ds(0, 2 * TILE)
    part_cols = [pl.ds(part * TILE, TILE) for part in range(3)]
    third = part_cols[2]

    def span(count, size):
        for n in (4, 3, 2, 1):
            for k in (4, 3, 2, 1):
                if count % (n * k) == 0 and count // (n * k) <= 12:
                    return W.at[pl.ds(0, count // (n * k)), pl.ds(0, k), pl.ds(0, n), :, pl.ds(0, size)]
        raise ValueError

    def to_three(axis, copies):
        return [(source(step), target(step), peer(axis, step)) for source, target in copies for step in (1, 2, 3)]

    pair = [
        net.send([(a, b, sibling)], a)
        for a, b in (
            (s["first_out"].at[pl.ds(0, 2)], s["first_in"].at[pl.ds(0, 2)]),
            (s["vec_own"], s["vec_in"]),
            (s["first_out"].at[pl.ds(2, 4)], s["first_in"].at[pl.ds(2, 4)]),
        )
    ]
    fill_masks(joined, half_lengths, s["bias"])
    pieces, vec_pieces = s["pieces"], s["vec_pieces"]
    ATT = ((0, "x", wide), (1, "y", wide), (0, "z", third), (1, "z", third))
    p0, p1, p2 = part_cols
    PARTS = (
        ((2, "x", p0), (3, "y", p0), (4, "z", p0), (5, "z", p0)),
        ((2, "x", p1), (4, "x", p1), (3, "y", p1), (5, "z", p1)),
        ((2, "x", p2), (3, "y", p2), (5, "y", p2), (4, "z", p2)),
    )
    HID = (
        (2, "x", every),
        (3, "y", every),
        (4, "z", p0),
        (4, "x", p1),
        (4, "z", p2),
        (5, "z", pl.ds(0, 2 * TILE)),
        (5, "y", p2),
    )

    def turns(l, route):
        return (route == "z") != (l >= 4)

    def make_piece(l, route, cols):
        own, far = s["first_own"][l, 0:6, cols], s["first_in"][l, 0:6, cols]
        line[0:6, cols] = jnp.where(c == 0, own, far)
        line[6:12, cols] = jnp.where(c == 0, far, own)
        pieces[HERE[FIRST[route]], l, :, cols] = line[0:16, cols].astype(BF16)

    def send_pieces(some, units):
        copies = []
        for l, route, cols in some:
            near = pieces.at[HERE[FIRST[route]], l, :, cols]
            copies += [(near, near, peer(FIRST[route], step)) for step in (1, 2, 3)]
        return net.send(copies, span(units, D))

    pair[0].wait_recv()
    for some in ATT:
        make_piece(*some)
    att_pieces = send_pieces(ATT, 2)
    pair[2].wait_recv()
    for some in HID:
        make_piece(*some)
    hid_pieces = send_pieces(HID, 4)
    pair[1].wait_recv()
    own, far = s["vec_own"][0:6], s["vec_in"][0:6]
    line[0:6, 0:LEN] = jnp.where(c == 0, own, far)
    line[6:12, 0:LEN] = jnp.where(c == 0, far, own)
    vec_pieces[z] = line[0:16, 0:LEN].astype(BF16)
    near = vec_pieces.at[z]
    vec_copies = net.send([(near, near, peer("z", step)) for step in (1, 2, 3)], span(1, LEN))

    VT, packed = s["VT"], s["packed"]

    def stage(ref, l, index):
        return ref.at[pl.ds(pl.multiple_of(index * 48, 16), 48), pl.ds((l // 2) * D, D)]

    def spread(l, route, cols):
        for i in range(4):
            line[12 * i : 12 * i + 12, cols] = pieces[i, l, :, cols].astype(F32)[0:12]
        rows = line[:, cols].astype(BF16)
        if route == "x":
            W[6 * c + l, y, x, :, cols] = rows
        elif route == "y":
            stage(s["gp"], l, z)[:, cols] = rows
        else:
            W[6 * c + l, z, x, :, cols] = rows

    def strips(some, units):
        copies = []
        for l, route, cols in some:
            if route == "x":
                near = W.at[6 * c + l, y, x, :, cols]
            elif route == "y":
                near = stage(s["gp"], l, z).at[:, cols]
            else:
                near = W.at[6 * c + l, z, x, :, cols]
            copies += [(near, near, peer(SECOND[route], step)) for step in (1, 2, 3)]
        return net.send(copies, span(3 * units, copies[0][0].shape[-1]))

    def order_strips(l, cols):
        size = cols.size
        for i in range(4):
            FP[48 * i : 48 * i + 48, 0:size] = stage(s["gp"], l, i)[:, cols].astype(F32)
        for i in range(4):
            for j in range(4):
                line[12 * j : 12 * j + 12, 0:size] = FP[48 * j + 12 * i : 48 * j + 12 * i + 12, 0:size]
            W[6 * c + l, y, i, :, cols] = line[:, 0:size].astype(BF16)

    def turn_rows(ref, place, cols):
        rows = ref[place, :, :, :, cols].reshape(D, cols.size)
        ref[place, :, :, :, cols] = dot(perm[...], rows).astype(BF16).reshape(4, 4, 48, cols.size)

    def region(ref, place, route, index, half, cols):
        part = pl.ds(0, 4) if half is None else pl.ds(2 * half, 2)
        if route == "x":
            return ref.at[place, part, index, :, cols]
        return ref.at[place, index, part, :, cols]

    def gather_start(some):
        copies = []
        for l, route, cols in some:
            near = region(W, 6 * c + l, route, HERE[route], None, cols)
            copies += [(near, near, peer(route, step)) for step in (1, 2, 3)]
        return some, net.send(copies, span(12 * len(some), some[0][2].size))

    def gather_share(state):
        some, group = state
        group.wait_recv()
        if any(turns(l, route) for l, route, _ in some):
            net.sent(group)
        copies = []
        for l, route, cols in some:
            if turns(l, route):
                turn_rows(W, 6 * c + l, cols)
            near = W.at[6 * c + l, :, :, :, cols]
            copies.append((near, near, sibling))
        return net.send(copies, span(16 * len(some), some[0][2].size))

    act, p = s["act"], s["p"]
    q, k, v, ctx = (act.at[i] for i in range(4))
    A, F, FP, inv1, y1b = s["A"], s["F"], s["FP"], s["inv1"], s["y1b"]
    h, gp, dfb, dfp, sums = s["h"], s["gp"], s["dfb"], y1b, s["sums"]
    turned = s["turned"]

    att_pieces.wait_recv()
    att_strips = []
    for group in (ATT[:1], ATT[1:2], ATT[2:]):
        for some in group:
            spread(*some)
        att_strips.append(strips(group, len(group)))
    hid_pieces.wait_recv()
    for some in HID:
        spread(*some)
    z_strips = [strips(PARTS[0][2:], 2)]
    x_strips = strips(HID[:1], 1)
    y_strips = strips(HID[1:2], 1)
    z_strips.append(strips([(5, "z", p1), (4, "z", p2)], 2))
    x_rest = strips([(4, "x", p1)], 1)
    y_rest = strips([(5, "y", p2)], 1)
    vec_copies.wait_recv()
    for i in range(4):
        line[12 * i : 12 * i + 12, 0:LEN] = vec_pieces[i].astype(F32)[0:12]
    VT[y, x] = line[:, 0:LEN].astype(BF16)
    near = VT.at[y, x]
    vec_strips = net.send([(near, near, peer("x", step)) for step in (1, 2, 3)], span(3, LEN))
    starts = {}
    att_strips[0].wait_recv()
    for part in range(2):
        starts["x", part] = gather_start([(0, "x", part_cols[part])])
    att_strips[1].wait_recv()
    order_strips(1, wide)
    for part in range(2):
        starts["y", part] = gather_start([(1, "y", part_cols[part])])
    att_strips[2].wait_recv()
    for l in range(2):
        starts["t", l] = gather_start(ATT[2 + l : 3 + l])
    vec_strips.wait_recv()
    near = packed.at[y]
    packed[y] = sum(
        pltpu.roll(VT[y, i].astype(F32), 32 * i, 1) if i else VT[y, i].astype(F32) for i in range(4)
    ).astype(BF16)
    vec_last = net.send([(near, near, peer("y", step)) for step in (1, 2, 3)], span(3, LEN))
    for copy in loads:
        copy.wait()
    flows = {}

    def begin(part, route):
        flows[part, route] = gather_start([some for some in PARTS[part] if some[1] == route])

    def sharing(part, routes="xyz"):
        for route in routes:
            flows[part, route] = gather_share(flows[part, route])

    z_strips[0].wait_recv()
    begin(0, "z")
    x_strips.wait_recv()
    begin(0, "x")
    y_strips.wait_recv()
    order_strips(3, every)
    begin(0, "y")
    z_strips[1].wait_recv()
    begin(1, "z")
    x_rest.wait_recv()
    begin(1, "x")
    begin(1, "y")
    y_rest.wait_recv()
    order_strips(5, p2)
    for route in "zxy":
        begin(2, route)
    net.sent(att_strips[2])
    shares = [gather_share(starts[key]) for key in (("x", 0), ("y", 0), ("t", 0))]
    vec_last.wait_recv()
    net.sent(vec_strips)
    for i in range(4):
        block_i = packed[i].astype(F32)
        for j in range(4):
            VT[i, j] = (pltpu.roll(block_i, LEN - 32 * j, 1) if j else block_i).astype(BF16)
    V[...] = VT[...].reshape(D, LEN).astype(F32).T[0:16]
    shares += [gather_share(starts[key]) for key in (("x", 1), ("y", 1), ("t", 1))]
    for copy in shares:
        copy.wait_recv()
    qkv(W, V, xb, q, k, v)
    attend(q, k, v, s["bias"], p, ctx)
    net.sent(x_rest)
    sharing(0)
    first_norm(W, V, xb, ctx, A, inv1, F, y1b)
    turn(y1b, turned.at[1])
    sharing(1)

    def arrived(part):
        for route in "xyz":
            flows[part, route].wait_recv()

    arrived(0)
    net.sent(att_strips[1])
    net.sent(y_strips)
    net.sent(y_rest)
    up(W, V, y1b, h, gp, 0)
    down_(W, h, FP, 0)
    sharing(2)
    arrived(1)
    up(W, V, y1b, h, gp, 1)
    down_(W, h, FP, 1)
    arrived(2)
    up(W, V, y1b, h, gp, 2)
    down_(W, h, FP, 2)
    second_norm(V, perm, FP, F, gb, gb, dfb, sums)
    stores = []
    for i in range(SLOTS):
        stores.append(pltpu.make_async_copy(gb.at[pl.ds(i * LEN, LEN)], out_hbm.at[i], s["store_sem"].at[i]))
        stores[-1].start()
    to_down_order(dfb, perm, dfp)
    dfpT = turned.at[0]
    y1T = turned.at[1]
    turn(dfp, dfpT)
    net.close()

    pair_in, pair_out = s["pair_in"], s["pair_out"]
    G_half = s["half_in"]
    G_block = pair_in
    slots = [None] * 8

    def send_tiles(tiles):
        for slot, _, _, _ in tiles:
            if slots[slot] is not None:
                net.sent(slots[slot])
        values = [value() for _, _, _, value in tiles]
        for (slot, _, _, _), value in zip(tiles, values):
            pair_out[slot] = value.astype(BF16).reshape(4, 4, 48, TILE)
        group = net.send(
            [(pair_out.at[slot], pair_in.at[l, :, :, :, cols], sibling) for slot, l, cols, _ in tiles],
            span(16 * len(tiles), TILE),
        )
        for slot, _, _, _ in tiles:
            slots[slot] = group
        return group

    def add_into(ref, index, *others):
        total = ref[index].astype(F32)
        for other_ref, other_index in others:
            total = total + other_ref[other_index].astype(F32)
        ref[index] = total.astype(BF16)

    def cell(l, route, index, i, cols):
        return (l, i, index, slice(None), cols) if route == "x" else (l, index, i, slice(None), cols)

    def reduce_start(some):
        copies = []
        for l, route, cols in some:
            across = wrap(HERE[route] + 2)
            for half, step in ((0, 1), (1, 3)):
                copies.append((region(G, l, route, across, half, cols), G_half.at[l, half, :, :, cols], peer(route, step)))
        return some, net.send(copies, span(4 * len(some), TILE))

    def reduce_pass(state):
        some, group = state
        group.wait_recv()
        copies = []
        for l, route, cols in some:
            here = HERE[route]
            for i in range(2):
                add_into(G, cell(l, route, wrap(here + 1), i, cols), (G_half, (l, 0, i, slice(None), cols)))
                add_into(G, cell(l, route, wrap(here - 1), 2 + i, cols), (G_half, (l, 1, i, slice(None), cols)))
            for half, step in ((0, 1), (1, 3)):
                copies.append(
                    (region(G, l, route, wrap(here + step), None, cols), G_block.at[l, half, :, :, cols], peer(route, step))
                )
        return some, net.send(copies, span(8 * len(some), TILE))

    strip_in = s["strip_in"]

    def strip_place(l, route, moved):
        return (l, moved, x) if route == "x" else (l, z, moved)

    def reduce_end(state):
        some, group = state
        group.wait_recv()
        copies = []
        for l, route, cols in some:
            for i in range(4):
                add_into(
                    G,
                    cell(l, route, HERE[route], i, cols),
                    (G_block, (l, 0, i, slice(None), cols)),
                    (G_block, (l, 1, i, slice(None), cols)),
                )
            if route == "y":
                for i in range(4):
                    FP[48 * i : 48 * i + 48, 0:TILE] = G[l, y, i, :, cols].astype(F32)
                for j in range(4):
                    for i in range(4):
                        line[12 * i : 12 * i + 12, 0:TILE] = FP[48 * i + 12 * j : 48 * i + 12 * j + 12, 0:TILE]
                    stage(h, l, j)[:, cols] = line[:, 0:TILE].astype(BF16)
            for step in (1, 2, 3):
                target = wrap(HERE[SECOND[route]] + step)
                if route == "y":
                    source = stage(h, l, target).at[:, cols]
                else:
                    source = G.at[strip_place(l, route, target) + (slice(None), cols)]
                copies.append((source, strip_in.at[l, step - 1, :, cols], peer(SECOND[route], step)))
        return some, net.send(copies, span(3 * len(some), TILE))

    piece_out, piece_in = pieces, s["piece_in"]

    def strips_sum(state):
        some, group = state
        group.wait_recv()
        for l, route, cols in some:
            if route == "y":
                own = stage(h, l, z)[:, cols]
            else:
                own = G[strip_place(l, route, HERE[SECOND[route]]) + (slice(None), cols)]
            total = own.astype(F32)
            for i in range(3):
                total = total + strip_in[l, i, :, cols].astype(F32)
            line[:, 0:TILE] = total
            gap = jnp.zeros((4, TILE), F32)
            for i in range(4):
                rows = jnp.concatenate([line[12 * i : 12 * i + 12, 0:TILE], gap], 0)
                piece_out[i, l, :, cols] = rows.astype(BF16)

    def pieces_out(some, units):
        copies = []
        for l, route, cols in some:
            for step in (1, 2, 3):
                source = piece_out.at[wrap(HERE[FIRST[route]] + step), l, :, cols]
                copies.append((source, piece_in.at[step - 1, l, :, cols], peer(FIRST[route], step)))
        return net.send(copies, span(units, D))

    rows_out, rows_own, rows_in = s["first_out"], s["first_own"], s["first_in"]

    def pieces_sum(l, route, cols):
        total = piece_out[HERE[FIRST[route]], l, :, cols].astype(F32)
        for i in range(3):
            total = total + piece_in[i, l, :, cols].astype(F32)
        line[0:16, cols] = total
        top, bottom = line[0:6, cols], line[6:12, cols]
        rows_own[l, 0:6, cols] = jnp.where(c == 0, top, bottom)
        rows_out[l, 0:6, cols] = jnp.where(c == 0, bottom, top)
        return jnp.sum(top * top + bottom * bottom, keepdims=True)

    def hidden_slopes(core, part):
        places = [pl.ds(pl.multiple_of((2 * core + e) * D + part * TILE, LEN), TILE) for e in range(2)]
        slopes = []
        for e in range(2):
            dh = dot(dfp[...], columns(W, 6 * core + 4 + e, part * TILE, TILE))
            du = (dh * gp[:, places[e]].astype(F32)).astype(BF16)
            slopes.append(du)
            sums[pl.ds(V_B1 + 2 * core + e, 1), part_cols[part]] = jnp.sum(du.astype(F32), 0, keepdims=True)
        return places, slopes

    def keep_tiles(group, tiles):
        group.wait_recv()
        for l, cols, value in tiles:
            total = value() + pair_in[l, :, :, :, cols].reshape(D, TILE).astype(F32)
            G[l, :, :, :, cols] = total.astype(BF16).reshape(4, 4, 48, TILE)

    def hidden_tiles(places, slopes, cols):
        tiles = [(4 + e, cols, lambda e=e: dot(dfpT[...], h[:, places[e]])) for e in range(2)]
        return tiles + [(2 + e, cols, lambda e=e: dot(y1T[...], slopes[e])) for e in range(2)]

    shared = {}

    def others(part):
        places, slopes = hidden_slopes(other, part)
        tiles = hidden_tiles(places, slopes, part_cols[part])
        shared[part] = send_tiles([(4 * (part % 2) + i,) + tile for i, tile in enumerate(tiles)])
        for e in range(2):
            gp[:, places[e]] = slopes[e]

    def own_slopes(part):
        places, slopes = hidden_slopes(c, part)
        for e in range(2):
            gp[:, places[e]] = slopes[e]

    def own_tiles(part):
        places = [pl.ds(pl.multiple_of((2 * c + e) * D + part * TILE, LEN), TILE) for e in range(2)]
        keep_tiles(shared[part], hidden_tiles(places, [gp[:, place] for place in places], part_cols[part]))
        for l, route, cols in PARTS[part]:
            if turns(l, route):
                turn_rows(G, l, cols)
        return reduce_start(PARTS[part])

    others(0)
    others(1)
    own_slopes(0)
    flows[0] = own_tiles(0)
    others(2)
    own_slopes(1)
    flows[1] = own_tiles(1)
    flows[0] = reduce_pass(flows[0])
    own_slopes(2)
    flows[2] = own_tiles(2)
    first_back_product(W, gp, F)
    flows[1] = reduce_pass(flows[1])
    first_back(V, A, inv1, F, dfb, sums)

    sums[VECTORS:16, :] = jnp.zeros((16 - VECTORS, D), F32)
    sums_in, sums_out = s["sums_in"], s["sums_out"]

    def sums_step(place, stage_, group, axis):
        if group is None:
            total = sums[8 * place : 8 * place + 8, :]
        else:
            total = sums_out[place, stage_ - 1]
            group.wait_recv()
            for i in range(1 if stage_ == 1 else 3):
                total = total + sums_in[place, 0 if stage_ == 1 else 3 * stage_ - 5 + i]
        if axis is None:
            return total
        sums_out[place, stage_] = total
        near = sums_out.at[place, stage_]
        if stage_ == 0:
            return net.send([(near, sums_in.at[place, 0], sibling)], near)
        base = 3 * stage_ - 3
        return net.send(
            [(near, sums_in.at[place, base + step], peer(axis, step)) for step in (1, 2, 3)],
            sums_in.at[place, pl.ds(0, 3)],
        )

    up_sums = sums_step(1, 0, None, "sibling")
    doT = turned.at[1]
    turn(dfb, doT)
    output_back(W, dfb, y1b)
    up_sums = sums_step(1, 1, up_sums, "z")
    turn(xb, turned.at[0])
    flows[2] = reduce_pass(flows[2])
    flows[0] = reduce_end(flows[0])

    def projection_grad(core, l, n):
        left = core if l == 1 else 0
        return dot(turned[left], act[2 * core + l, :, n * TILE : (n + 1) * TILE])

    def projection_tiles(core, n):
        return [(l, part_cols[n], lambda l=l: projection_grad(core, l, n)) for l in (0, 1)]

    last = []

    def other_projections(n):
        attend_back(q, k, v, p, y1b, n)
        tiles = projection_tiles(other, n)
        shared["p", n] = send_tiles([(2 * n + i,) + tile for i, tile in enumerate(tiles)])

    def own_projections(n):
        keep_tiles(shared["p", n], projection_tiles(c, n))
        if n == 2:
            for l in (0, 1):
                turn_rows(G, l, third)
        last.append(reduce_start([(l, "z" if n == 2 else "xy"[l], part_cols[n]) for l in (0, 1)]))

    other_projections(2)
    other_projections(0)
    own_projections(2)
    flows[1] = reduce_end(flows[1])
    up_sums = sums_step(1, 2, up_sums, "x")
    other_projections(1)
    column_sums(q, sums, V_BQ)
    column_sums(v, sums, V_BV)
    first_sums = sums_step(0, 0, None, "sibling")
    own_projections(0)
    own_projections(1)
    first_sums = sums_step(0, 1, first_sums, "z")
    flows[2] = reduce_end(flows[2])
    last[0] = reduce_pass(last[0])
    for group in pair + [att_pieces, hid_pieces]:
        net.sent(group)
    last[1] = reduce_pass(last[1])
    input_back(W, q, k, v, F, 0)
    last[2] = reduce_pass(last[2])
    input_back(W, q, k, v, F, 1)
    for i in range(SLOTS):
        stores.append(pltpu.make_async_copy(F.at[pl.ds(i * LEN, LEN)], grad_hbm.at[i], s["store_sem"].at[4 + i]))
        stores[-1].start()
    strips_sum(flows[0])
    strips_sum(flows[1])
    first_sums = sums_step(0, 2, first_sums, "x")
    up_sums = sums_step(1, 3, up_sums, "y")
    strips_sum(flows[2])
    hid_pieces = pieces_out(HID, 4)
    for n in range(3):
        last[n] = reduce_end(last[n])
    first_sums = sums_step(0, 3, first_sums, "y")
    hid_pieces.wait_recv()
    squares = jnp.zeros((1, 1), F32)
    for some in HID:
        squares = squares + pieces_sum(*some)
    rows_copies = [net.send([(rows_out.at[pl.ds(2, 4)], rows_in.at[pl.ds(2, 4)], sibling)], rows_out.at[pl.ds(2, 4)])]
    for n in range(3):
        strips_sum(last[n])
    att_pieces = pieces_out(ATT, 2)
    vec_total = jnp.concatenate([sums_step(0, 4, first_sums, None), sums_step(1, 4, up_sums, None)], 0)
    place = lax.broadcasted_iota(jnp.int32, (8, D), 1) - 6 * me
    pick = (place == lax.broadcasted_iota(jnp.int32, (8, D), 0)).astype(BF16)
    vec_grad = jnp.zeros((8, 16), F32)
    for _ in range(3):
        low = vec_total.astype(BF16)
        vec_grad = vec_grad + dot(pick, low, NT)
        vec_total = vec_total - low.astype(F32)
    vec_grad = vec_grad[0:6, 0:VECTORS]
    squares = squares + jnp.sum(vec_grad * vec_grad, keepdims=True)
    att_pieces.wait_recv()
    for some in ATT:
        squares = squares + pieces_sum(*some)
    norm_out, norm_in = s["norm_out"], s["norm_in"]
    norm_out[0] = jnp.broadcast_to(squares, (8, LEN))
    plane = [(norm_out.at[0], norm_in.at[0, i], device) for i, device in enumerate(plane_peers)]
    norm_group = net.send(plane, norm_in.at[0])
    rows_copies.append(
        net.send([(rows_out.at[pl.ds(0, 2)], rows_in.at[pl.ds(0, 2)], sibling)], rows_out.at[pl.ds(0, 2)])
    )
    for copy in rows_copies:
        copy.wait_recv()
    att_grad, hid_grad, vec_grad_at = att_w, hid_w, vec_w
    vec_grad_at[...] = vec_grad
    for core in range(2):
        for l in range(SHARE):
            value = jnp.where(c == core, rows_own[l, 0:6], rows_in[l, 0:6])
            if l < 2:
                att_grad[:, 2 * core + l, :] = value
            else:
                i, j = (l - 2) // 2, 2 * core + l % 2
                hid_grad[:, i, j * D : (j + 1) * D] = value
    for i, (source, target) in enumerate(((att_grad, att_out), (hid_grad, hid_out), (vec_grad_at, vec_out))):
        stores.append(pltpu.make_async_copy(source, target, s["store_sem"].at[8 + i]))
        stores[-1].start()

    def norm_step(index, group, count):
        group.wait_recv()
        total = norm_out[index]
        for i in range(count):
            total = total + norm_in[index, i]
        return total

    norm_out[1] = norm_step(0, norm_group, 15)
    copies = [(norm_out.at[1], norm_in.at[1, 0], sibling)]
    for step in (1, 2, 3):
        copies.append((norm_out.at[1], norm_in.at[1, step], peer("z", step)))
        copies.append((norm_out.at[1], norm_in.at[1, 3 + step], far_peer(step)))
    norm_group = net.send(copies, norm_in.at[1, pl.ds(0, 7)])
    norm = jnp.sqrt(norm_step(1, norm_group, 7))
    norm_out_ref[...] = norm[0:1, 0:1]
    for copy in stores:
        copy.wait()
    net.close()


def rates(values, shape):
    index = lax.broadcasted_iota(jnp.int32, shape, 1)
    rate = jnp.full(shape, values[0], F32)
    for i, value in enumerate(values[1:]):
        rate = jnp.where(index == i + 1, value, rate)
    return rate


def update_kernel(out_in, grad_in, norm, *refs):
    sources, (out_hbm, grad_hbm), targets = refs[:12], refs[12:14], refs[14:23]
    out_at, grad_at = refs[23:25]
    held, sems = refs[25:37], refs[37]
    loads = [pltpu.make_async_copy(a, b, sems.at[i]) for i, (a, b) in enumerate(zip(sources, held))]
    passing = []
    stores = []
    for i in range(SLOTS):
        for j, (source, middle, target) in enumerate(((grad_in, grad_at, grad_hbm), (out_in, out_at, out_hbm))):
            n = 12 + 4 * i + 2 * j
            passing.append(pltpu.make_async_copy(source.at[i], middle.at[i], sems.at[n]))
            stores.append(pltpu.make_async_copy(middle.at[i], target.at[i], sems.at[n + 1]))
    for copy in loads + passing:
        copy.start()
    factor = CLIP_NORM / jnp.maximum(norm[...], CLIP_NORM)
    settings = (
        (rates(ATTENTION_RATES, (6, 4, D)), WEIGHT_DECAY),
        (rates(HIDDEN_RATES, (6, 2, FF)), WEIGHT_DECAY),
        (VECTOR_RATE, 0.0),
    )
    for i in (1, 0, 2):
        for j in (i, 3 + 3 * i, 4 + 3 * i, 5 + 3 * i):
            loads[j].wait()
        state = held[3 + 3 * i : 6 + 3 * i]
        new = adam(state[0][...], state[1][...], state[2][...], held[i][...] * factor, *settings[i])
        for j in range(3):
            state[j][...] = new[j]
            stores.append(pltpu.make_async_copy(state[j], targets[3 * i + j], sems.at[28 + 3 * i + j]))
        if i == 1:
            for load, copy in zip(passing, stores):
                load.wait()
                copy.start()
        for copy in stores[-3:]:
            copy.start()
    for copy in stores:
        copy.wait()


def on_device(
    inputs,
    cotangent,
    joined,
    half_lengths,
    attention_master,
    attention_first,
    attention_second,
    hidden_master,
    hidden_first,
    hidden_second,
    vector_master,
    vector_first,
    vector_second,
):
    any_space = pl.BlockSpec(memory_space=pl.ANY)
    vmem = pl.BlockSpec(memory_space=pltpu.VMEM)
    smem = pl.BlockSpec(memory_space=pltpu.SMEM)
    like = lambda a: jax.ShapeDtypeStruct(a.shape, a.dtype)
    swap = lambda a: jnp.transpose(a, (1, 0, 2))
    attention = [swap(a) for a in (attention_master, attention_first, attention_second)]
    hidden = [swap(a) for a in (hidden_master, hidden_first, hidden_second)]
    vectors = [a.T for a in (vector_master, vector_first, vector_second)]
    params = attention + hidden + vectors
    out_like = jax.ShapeDtypeStruct(inputs.shape, BF16)
    grad_like = jax.ShapeDtypeStruct(inputs.shape, F32)
    results = pl.pallas_call(
        step_kernel,
        out_shape=(
            out_like,
            grad_like,
            jax.ShapeDtypeStruct((1, 1), F32),
            like(attention[0]),
            like(hidden[0]),
            like(vectors[0]),
        ),
        in_specs=[any_space] * 3 + [smem] * 2 + [any_space] * 3,
        out_specs=(any_space, any_space, vmem) + (any_space,) * 3,
        scratch_shapes=list(SCRATCH.values()),
        compiler_params=pltpu.CompilerParams(collective_id=0, has_side_effects=True, vmem_limit_bytes=64 << 20),
        cost_estimate=pl.CostEstimate(flops=22 * 10**9, bytes_accessed=6 * 10**6, transcendentals=4 * 10**6),
    )(
        inputs,
        cotangent,
        jnp.asarray(permutation(), BF16),
        joined.T,
        jnp.transpose(half_lengths, (1, 2, 0)),
        attention[0],
        hidden[0],
        vectors[0],
    )
    outs = pl.pallas_call(
        update_kernel,
        out_shape=(out_like, grad_like) + tuple(like(a) for a in params),
        in_specs=[any_space] * 2 + [vmem] + [any_space] * 12,
        out_specs=(any_space,) * 11,
        scratch_shapes=[
            pltpu.VMEM(inputs.shape, BF16),
            pltpu.VMEM(inputs.shape, F32),
            *[pltpu.VMEM(a.shape, F32) for a in (attention[0], hidden[0], vectors[0], *params)],
            pltpu.SemaphoreType.DMA((37,)),
        ],
        cost_estimate=pl.CostEstimate(flops=2 * 10**6, bytes_accessed=7 * 10**6, transcendentals=10**5),
    )(*results, *params)
    output, input_grad, *new = outs
    norm = results[2].reshape(())
    return (output, input_grad, norm, *[swap(a) for a in new[:6]], *[a.T for a in new[6:]])


def solution(mesh):
    shard = P(None, "dp", None)
    flat = P(None, "dp")
    return jax.shard_map(
        on_device,
        mesh=mesh,
        in_specs=(shard, shard, flat, shard, shard, shard, shard, shard, shard, shard, flat, flat, flat),
        out_specs=(shard, shard, P(), shard, shard, shard, shard, shard, shard, flat, flat, flat),
        check_vma=False,
    )
```

```python
import functools
import jax
import jax.numpy as jnp
import numpy as np
from jax import lax
from jax.experimental import pallas as pl
from jax.experimental.pallas import tpu as pltpu
from jax.sharding import PartitionSpec as P

F32 = jnp.float32
BF16 = jnp.bfloat16
D = 768
FF = 3072
ROWS = 512
SLOTS = 4
LEN = 128
PAIRS = 6
TILE = 256
NORM_EPS = 1e-05
MASKED = -1e30
NN = (((1,), (0,)), ((), ()))
NT = (((1,), (1,)), ((), ()))
TN = (((0,), (0,)), ((), ()))
PLACE_Q, PLACE_K, PLACE_V, PLACE_O = 0, 1, 6, 7
PLACE_UP = (2, 3, 8, 9)
PLACE_DOWN = (4, 5, 10, 11)
V_BQ, V_BV, V_BO, V_G1, V_C1, V_G2, V_C2, V_B2, V_B1 = range(9)


def dot(a, b, dims=NN):
    return lax.dot_general(a, b, dims, preferred_element_type=F32)


def block(ref, place):
    return ref[place].reshape(D, D)


def columns(ref, place, start, size):
    return ref[place, :, :, :, pl.ds(start, size)].reshape(D, size)


def put_columns(ref, place, start, size, value):
    ref[place, :, :, :, pl.ds(start, size)] = value.reshape(4, 4, 48, size)


def loop(count, body):
    lax.fori_loop(0, count, lambda i, c: (body(i), c)[1], 0)


def at(i, size):
    return pl.ds(pl.multiple_of(i * size, size), size)


def qkv(W, V, xb, q, k, v):
    x = xb[...]
    for n in range(D // TILE):
        cols = pl.ds(n * TILE, TILE)
        q[:, cols] = ((dot(x, columns(W, PLACE_Q, n * TILE, TILE)) + V[V_BQ, cols]).astype(BF16) * 0.125).astype(BF16)
        k[:, cols] = dot(x, columns(W, PLACE_K, n * TILE, TILE)).astype(BF16)
        v[:, cols] = (dot(x, columns(W, PLACE_V, n * TILE, TILE)) + V[V_BV, cols]).astype(BF16)


def halves(value):
    lane = lax.broadcasted_iota(jnp.int32, value.shape, 1)
    zero = jnp.zeros_like(value)
    return jnp.concatenate([jnp.where(lane < 64, value, zero), jnp.where(lane < 64, zero, value)], 0)


def joined_halves(value):
    lane = lax.broadcasted_iota(jnp.int32, (LEN, LEN), 1)
    return jnp.where(lane < 64, value[:LEN], value[LEN:])


def fill_masks(joined, half_lengths, bias):
    query = lax.broadcasted_iota(jnp.int32, (LEN, LEN), 0)
    key = lax.broadcasted_iota(jnp.int32, (LEN, LEN), 1)
    for slot in range(SLOTS):
        is_joined = joined[0, slot]
        low = half_lengths[0, 0, slot]
        high = half_lengths[0, 1, slot]
        upper = (key >= 64).astype(jnp.int32)
        limit = is_joined * (64 + high) + (1 - is_joined) * (upper * (64 + high) + (1 - upper) * low)
        apart = (1 - is_joined) * jnp.abs((query >= 64).astype(jnp.int32) - upper)
        bias[slot] = jnp.where((key < limit) & (apart == 0), 0.0, MASKED)


GROUP = 6


def attend(q, k, v, bias, p, ctx):
    def units(slot):
        rows = at(slot, LEN)
        m = bias[slot]
        hidden = jnp.concatenate([m, m], 0) < 0
        cols = [pl.ds(pair * LEN, LEN) for pair in range(PAIRS)]
        for start in range(0, PAIRS, GROUP):
            some = range(start, start + GROUP)
            s = [dot(halves(q[rows, cols[i]]), k[rows, cols[i]], NT) for i in some]
            values = [v[rows, cols[i]] for i in some]
            s = [jnp.where(hidden, MASKED, one) for one in s]
            e = [jnp.exp(one - jnp.max(one, -1, keepdims=True)) for one in s]
            low = [(one * (1.0 / jnp.sum(one, -1, keepdims=True))).astype(BF16) for one in e]
            out = [joined_halves(dot(one, value)).astype(BF16) for one, value in zip(low, values)]
            for i, one, result in zip(some, low, out):
                p[slot * PAIRS + i] = one
                ctx[rows, cols[i]] = result

    loop(SLOTS, units)


def attend_back(q, k, v, p, dctx, n):
    def units(step):
        some = [(2 * step + slot, pair) for slot in range(2) for pair in (2 * n, 2 * n + 1)]
        places = [(at(slot, LEN), pl.ds(pair * LEN, LEN)) for slot, pair in some]
        low = [p[slot * PAIRS + pair] for slot, pair in some]
        two = [halves(dctx[place]) for place in places]
        q2 = [halves(q[place]) for place in places]
        keys = [k[place] for place in places]
        dp = [dot(a, v[place], NT) for a, place in zip(two, places)]
        dv = [dot(a, b, TN) for a, b in zip(low, two)]
        full = [a.astype(F32) for a in low]
        ds = [(a * (b - jnp.sum(a * b, -1, keepdims=True))).astype(BF16) for a, b in zip(full, dp)]
        dq = [joined_halves(dot(a, b)) * 0.125 for a, b in zip(ds, keys)]
        dk = [dot(a, b, TN) for a, b in zip(ds, q2)]
        for a, b, d, place in zip(dv, dq, dk, places):
            v[place] = a.astype(BF16)
            q[place] = b.astype(BF16)
            k[place] = d.astype(BF16)

    loop(2, units)


STRIP = 256


def first_norm(W, V, xb, ctx, A, inv1, F, y1b):
    A[...] = dot(ctx[...], block(W, PLACE_O), NT)

    def strip(i):
        rows = at(i, STRIP)
        a = xb[rows, :].astype(F32) + A[rows, :] + V[V_BO : V_BO + 1, :]
        center = a - jnp.mean(a, -1, keepdims=True)
        inverse = lax.rsqrt(jnp.mean(center * center, -1, keepdims=True) + NORM_EPS)
        n = center * inverse
        A[rows, :] = n
        inv1[rows, :] = inverse
        y = n * V[V_G1 : V_G1 + 1, :] + V[V_C1 : V_C1 + 1, :]
        y1b[rows, :] = y.astype(BF16)
        F[rows, :] = y + V[V_B2 : V_B2 + 1, :]

    loop(ROWS // STRIP, strip)


def gelu_parts(u):
    e = jnp.exp(-0.5 * (u * u))
    t = pl.reciprocal(1.0 + 0.23164190 * jnp.abs(u), approx=True)
    poly = ((((0.5307027145 * t - 0.726576013) * t + 0.7107068705) * t - 0.142248368) * t + 0.127414796) * t
    tail = poly * e
    cdf = jnp.where(u >= 0, 1.0 - tail, tail)
    return u * cdf, cdf + (u * 0.3989422804014327) * e


def up(W, V, y1b, h, gp, part):
    for j, place in enumerate(PLACE_UP):
        cols = pl.ds(j * D + part * TILE, TILE)
        u = dot(y1b[...], columns(W, place, part * TILE, TILE)) + V[V_B1 + j : V_B1 + j + 1, pl.ds(part * TILE, TILE)]
        value, slope = gelu_parts(u)
        h[:, cols] = value.astype(BF16)
        gp[:, cols] = slope.astype(BF16)


def down_(W, h, FP, part):
    left = jnp.concatenate([h[:, pl.ds(j * D + part * TILE, TILE)] for j in range(4)], 1)
    right = jnp.concatenate([columns(W, place, part * TILE, TILE) for place in PLACE_DOWN], 1)
    total = dot(left, right, NT)
    FP[...] = total if part == 0 else FP[...] + total


def second_norm(V, perm, FP, F, gb, outb, dfb, sums):
    F[...] += dot(FP[...].astype(BF16), perm[...])

    def strip(i, carry):
        dg, dc, db = carry
        rows = at(i, STRIP)
        z = F[rows, :]
        center = z - jnp.mean(z, -1, keepdims=True)
        inverse = lax.rsqrt(jnp.mean(center * center, -1, keepdims=True) + NORM_EPS)
        n = center * inverse
        gain = V[V_G2 : V_G2 + 1, :]
        g = gb[rows, :].astype(F32)
        outb[rows, :] = (n * gain + V[V_C2 : V_C2 + 1, :]).astype(BF16)
        gn = g * n
        e = g * gain
        dz = inverse * (e - jnp.mean(e, -1, keepdims=True) - n * jnp.mean(gn * gain, -1, keepdims=True))
        low = dz.astype(BF16)
        F[rows, :] = dz
        dfb[rows, :] = low
        return (
            dg + jnp.sum(gn, 0, keepdims=True),
            dc + jnp.sum(g, 0, keepdims=True),
            db + jnp.sum(low.astype(F32), 0, keepdims=True),
        )

    zero = jnp.zeros((1, D), F32)
    dg, dc, db = lax.fori_loop(0, ROWS // STRIP, strip, (zero, zero, zero))
    sums[V_G2 : V_G2 + 1, :] = dg
    sums[V_C2 : V_C2 + 1, :] = dc
    sums[V_B2 : V_B2 + 1, :] = db


def turn(source, target):
    for i in range(ROWS // LEN):
        target[:, i * LEN : (i + 1) * LEN] = source[i * LEN : (i + 1) * LEN, :].T


def first_back_product(W, gp, F):
    for i in range(ROWS // TILE):
        rows = pl.ds(i * TILE, TILE)
        F[rows, :] += dot(gp[rows, :], jnp.concatenate([block(W, place) for place in PLACE_UP], 1), NT)


def first_back(V, A, inv1, F, dob, sums):
    def strip(i, carry):
        dg, dc, db = carry
        rows = at(i, STRIP)
        dy = F[rows, :]
        n = A[rows, :]
        gain = V[V_G1 : V_G1 + 1, :]
        dyn = dy * n
        e = dy * gain
        da = inv1[rows, :] * (e - jnp.mean(e, -1, keepdims=True) - n * jnp.mean(dyn * gain, -1, keepdims=True))
        low = da.astype(BF16)
        F[rows, :] = da
        dob[rows, :] = low
        return (
            dg + jnp.sum(dyn, 0, keepdims=True),
            dc + jnp.sum(dy, 0, keepdims=True),
            db + jnp.sum(low.astype(F32), 0, keepdims=True),
        )

    zero = jnp.zeros((1, D), F32)
    dg, dc, db = lax.fori_loop(0, ROWS // STRIP, strip, (zero, zero, zero))
    sums[V_G1 : V_G1 + 1, :] = dg
    sums[V_C1 : V_C1 + 1, :] = dc
    sums[V_BO : V_BO + 1, :] = db


def output_back(W, dob, dctx):
    def tile(n):
        cols = at(n, TILE)
        dctx[:, cols] = dot(dob[...], columns(W, PLACE_O, cols.start, TILE)).astype(BF16)

    loop(D // TILE, tile)


def column_sums(source, sums, row):
    sums[row : row + 1, :] = jnp.sum(source[...].astype(F32), 0, keepdims=True)


def input_back(W, q, k, v, F, i):
    rows = pl.ds(i * TILE, TILE)
    left = jnp.concatenate([q[rows, :], k[rows, :], v[rows, :]], 1)
    right = jnp.concatenate([block(W, place) for place in (PLACE_Q, PLACE_K, PLACE_V)], 1)
    F[rows, :] += dot(left, right, NT)


def to_down_order(dfb, perm, dfp):
    dfp[...] = dot(dfb[...], perm[...], NT).astype(BF16)


def permutation():
    r = np.arange(D)
    y, x, z, j = r // 192, r // 48 % 4, r // 12 % 4, r % 12
    p = np.zeros((D, D), np.float32)
    p[192 * z + 48 * x + 12 * y + j, r] = 1
    return p


MESH = pl.DeviceIdType.MESH
STEP = 10
ADAM_EPS = 1e-08
BETA_ONE = 0.9
BETA_TWO = 0.999
CLIP_NORM = 1.0
WEIGHT_DECAY = 0.01
ATTENTION_RATES = (0.02, 0.02, 0.04, 0.3)
HIDDEN_RATES = (0.04, 0.02)
VECTOR_RATE = 0.5
COPIES = 85
VECTORS = 12
SHARE = 6


class Net:
    def __init__(self, send_sem, recv_sem):
        self.send_sem, self.recv_sem, self.count, self.open = send_sem, recv_sem, 0, []

    def send(self, copies, whole):
        assert self.count < COPIES
        sems = dict(send_sem=self.send_sem.at[self.count], recv_sem=self.recv_sem.at[self.count])
        self.count += 1
        made = [
            pltpu.make_async_remote_copy(src_ref=a, dst_ref=b, device_id=(d,), device_id_type=MESH, **sems)
            for a, b, d in copies
        ]
        for copy in made:
            copy.start()
        group = pltpu.make_async_remote_copy(
            src_ref=whole, dst_ref=whole, device_id=(copies[0][2],), device_id_type=MESH, **sems
        )
        self.open.append(group)
        return group

    def sent(self, group):
        if any(one is group for one in self.open):
            group.wait_send()
            self.open = [one for one in self.open if one is not group]

    def close(self):
        for group in self.open:
            group.wait_send()
        self.open = []


def adam(master, first, second, gradient, rate, decay):
    first_new = BETA_ONE * first + (1.0 - BETA_ONE) * gradient
    second_new = BETA_TWO * second + (1.0 - BETA_TWO) * gradient * gradient
    first_hat = first_new * (1.0 / (1.0 - BETA_ONE**STEP))
    second_hat = second_new * (1.0 / (1.0 - BETA_TWO**STEP))
    step = first_hat * pl.reciprocal(jnp.sqrt(second_hat) + ADAM_EPS, approx=True)
    master_new = master - rate * (step + decay * master)
    return master_new, first_new, second_new


SCRATCH = dict(
    W=pltpu.VMEM((12, 4, 4, 48, D), BF16),
    G=pltpu.VMEM((SHARE, 4, 4, 48, D), BF16),
    pair_in=pltpu.VMEM((SHARE, 4, 4, 48, D), BF16),
    pair_out=pltpu.VMEM((8, 4, 4, 48, TILE), BF16),
    half_in=pltpu.VMEM((SHARE, 2, 2, 48, D), BF16),
    strip_in=pltpu.VMEM((SHARE, 3, 48, D), BF16),
    piece_in=pltpu.VMEM((3, SHARE, 16, D), BF16),
    first_out=pltpu.VMEM((SHARE, 8, D), F32),
    first_own=pltpu.VMEM((SHARE, 8, D), F32),
    first_in=pltpu.VMEM((SHARE, 8, D), F32),
    vec_own=pltpu.VMEM((8, LEN), F32),
    vec_in=pltpu.VMEM((8, LEN), F32),
    pieces=pltpu.VMEM((4, SHARE, 16, D), BF16),
    vec_pieces=pltpu.VMEM((4, 16, LEN), BF16),
    VT=pltpu.VMEM((4, 4, 48, LEN), BF16),
    line=pltpu.VMEM((48, D), F32),
    sums_in=pltpu.VMEM((2, 10, 8, D), F32),
    sums_out=pltpu.VMEM((2, 4, 8, D), F32),
    packed=pltpu.VMEM((4, 48, LEN), BF16),
    norm_out=pltpu.VMEM((2, 8, LEN), F32),
    norm_in=pltpu.VMEM((2, 15, 8, LEN), F32),
    V=pltpu.VMEM((16, D), F32),
    sums=pltpu.VMEM((16, D), F32),
    bias=pltpu.VMEM((SLOTS, LEN, LEN), F32),
    act=pltpu.VMEM((4, ROWS, D), BF16),
    p=pltpu.VMEM((SLOTS * PAIRS, 2 * LEN, LEN), BF16),
    A=pltpu.VMEM((ROWS, D), F32),
    F=pltpu.VMEM((ROWS, D), F32),
    FP=pltpu.VMEM((ROWS, D), F32),
    inv1=pltpu.VMEM((ROWS, 1), F32),
    y1b=pltpu.VMEM((ROWS, D), BF16),
    turned=pltpu.VMEM((2, D, ROWS), BF16),
    h=pltpu.VMEM((ROWS, FF), BF16),
    gp=pltpu.VMEM((ROWS, FF), BF16),
    dfb=pltpu.VMEM((ROWS, D), BF16),
    xb=pltpu.VMEM((ROWS, D), BF16),
    gb=pltpu.VMEM((ROWS, D), BF16),
    perm=pltpu.VMEM((D, D), BF16),
    att_w=pltpu.VMEM((6, 4, D), F32),
    hid_w=pltpu.VMEM((6, 2, FF), F32),
    vec_w=pltpu.VMEM((6, VECTORS), F32),
    joined=pltpu.SMEM((1, SLOTS), jnp.int32),
    half_lengths=pltpu.SMEM((1, 2, SLOTS), jnp.int32),
    load_sem=pltpu.SemaphoreType.DMA((14,)),
    store_sem=pltpu.SemaphoreType.DMA((11,)),
    send_sem=pltpu.SemaphoreType.DMA((COPIES,)),
    recv_sem=pltpu.SemaphoreType.DMA((COPIES,)),
)
NAMES = tuple(SCRATCH)


def step_kernel(
    x_hbm,
    g_hbm,
    perm_hbm,
    joined_hbm,
    half_hbm,
    att_hbm,
    hid_hbm,
    vec_hbm,
    out_hbm,
    grad_hbm,
    norm_out_ref,
    att_out,
    hid_out,
    vec_out,
    *scratch,
):
    s = dict(zip(NAMES, scratch))
    W, G, V = s["W"], s["G"], s["V"]
    xb, gb, perm = s["xb"], s["gb"], s["perm"]
    net = Net(s["send_sem"], s["recv_sem"])

    me = lax.axis_index("dp")
    c = lax.rem(me, 2)
    z = lax.rem(lax.div(me, 2), 4)
    x = lax.rem(lax.div(me, 8), 4)
    y = lax.div(me, 32)
    other = 1 - c

    def wrap(value):
        return lax.rem(value + 4, 4)

    def peer(axis, step):
        moved = {"x": x, "y": y, "z": z}
        moved[axis] = wrap(moved[axis] + step)
        return ((moved["y"] * 4 + moved["x"]) * 4 + moved["z"]) * 2 + c

    sibling = me + 1 - 2 * c

    def far_peer(step):
        return ((y * 4 + x) * 4 + wrap(z + step)) * 2 + other

    plane_peers = [((wrap(y + i // 4) * 4 + wrap(x + i % 4)) * 4 + z) * 2 + c for i in range(1, 16)]

    att_w, hid_w, vec_w = s["att_w"], s["hid_w"], s["vec_w"]
    masters_in = [
        pltpu.make_async_copy(source, target, s["load_sem"].at[9 + i])
        for i, (source, target) in enumerate(((att_hbm, att_w), (hid_hbm, hid_w), (vec_hbm, vec_w)))
    ]
    loads = []
    for i in range(SLOTS):
        loads.append(pltpu.make_async_copy(x_hbm.at[i], xb.at[pl.ds(i * LEN, LEN)], s["load_sem"].at[i]))
        loads.append(pltpu.make_async_copy(g_hbm.at[i], gb.at[pl.ds(i * LEN, LEN)], s["load_sem"].at[4 + i]))
    loads.append(pltpu.make_async_copy(perm_hbm, perm, s["load_sem"].at[8]))
    joined, half_lengths = s["joined"], s["half_lengths"]
    lengths_in = [
        pltpu.make_async_copy(joined_hbm, joined, s["load_sem"].at[12]),
        pltpu.make_async_copy(half_hbm, half_lengths, s["load_sem"].at[13]),
    ]
    for copy in masters_in + lengths_in + loads:
        copy.start()

    barrier = pltpu.get_barrier_semaphore()
    partners = [sibling] + [peer(axis, step) for axis in "xyz" for step in (1, 2, 3)]
    for partner in partners:
        pl.semaphore_signal(barrier, inc=1, device_id=(partner,), device_id_type=MESH)

    for copy in masters_in:
        copy.wait()
    masters = [[att_w[:, 2 * core + l, :] for l in range(2)] for core in range(2)]
    for core in range(2):
        masters[core] += [hid_w[:, i, (2 * core + l) * D : (2 * core + l + 1) * D] for i in range(2) for l in range(2)]
    for l in range(SHARE):
        s["first_own"][l, 0:6, :] = jnp.where(c == 0, masters[0][l], masters[1][l])
        s["first_out"][l, 0:6, :] = jnp.where(c == 0, masters[1][l], masters[0][l])
    s["vec_own"][...] = jnp.zeros((8, LEN), F32)
    s["vec_own"][0:6, 0:VECTORS] = vec_w[...]
    line = s["line"]
    line[...] = jnp.zeros((48, D), F32)
    pl.semaphore_wait(barrier, len(partners))

    FIRST = {"x": "z", "y": "x", "z": "y"}
    SECOND = {"x": "y", "y": "z", "z": "x"}
    HERE = {"x": x, "y": y, "z": z}
    every = pl.ds(0, D)
    wide = pl.ds(0, 2 * TILE)
    part_cols = [pl.ds(part * TILE, TILE) for part in range(3)]
    third = part_cols[2]

    def span(count, size):
        for n in (4, 3, 2, 1):
            for k in (4, 3, 2, 1):
                if count % (n * k) == 0 and count // (n * k) <= 12:
                    return W.at[pl.ds(0, count // (n * k)), pl.ds(0, k), pl.ds(0, n), :, pl.ds(0, size)]
        raise ValueError

    def to_three(axis, copies):
        return [(source(step), target(step), peer(axis, step)) for source, target in copies for step in (1, 2, 3)]

    pair = [
        net.send([(a, b, sibling)], a)
        for a, b in (
            (s["first_out"].at[pl.ds(0, 2)], s["first_in"].at[pl.ds(0, 2)]),
            (s["vec_own"], s["vec_in"]),
            (s["first_out"].at[pl.ds(2, 4)], s["first_in"].at[pl.ds(2, 4)]),
        )
    ]
    for copy in lengths_in:
        copy.wait()
    fill_masks(joined, half_lengths, s["bias"])
    pieces, vec_pieces = s["pieces"], s["vec_pieces"]
    ATT = ((0, "x", wide), (1, "y", wide), (0, "z", third), (1, "z", third))
    p0, p1, p2 = part_cols
    PARTS = (
        ((2, "x", p0), (3, "y", p0), (4, "z", p0), (5, "z", p0)),
        ((2, "x", p1), (4, "x", p1), (3, "y", p1), (5, "z", p1)),
        ((2, "x", p2), (3, "y", p2), (5, "y", p2), (4, "z", p2)),
    )
    HID = (
        (2, "x", every),
        (3, "y", every),
        (4, "z", p0),
        (4, "x", p1),
        (4, "z", p2),
        (5, "z", pl.ds(0, 2 * TILE)),
        (5, "y", p2),
    )

    def turns(l, route):
        return (route == "z") != (l >= 4)

    def make_piece(l, route, cols):
        own, far = s["first_own"][l, 0:6, cols], s["first_in"][l, 0:6, cols]
        line[0:6, cols] = jnp.where(c == 0, own, far)
        line[6:12, cols] = jnp.where(c == 0, far, own)
        pieces[HERE[FIRST[route]], l, :, cols] = line[0:16, cols].astype(BF16)

    def send_pieces(some, units):
        copies = []
        for l, route, cols in some:
            near = pieces.at[HERE[FIRST[route]], l, :, cols]
            copies += [(near, near, peer(FIRST[route], step)) for step in (1, 2, 3)]
        return net.send(copies, span(units, D))

    pair[0].wait_recv()
    for some in ATT:
        make_piece(*some)
    att_pieces = send_pieces(ATT, 2)
    pair[2].wait_recv()
    for some in HID:
        make_piece(*some)
    hid_pieces = send_pieces(HID, 4)
    pair[1].wait_recv()
    own, far = s["vec_own"][0:6], s["vec_in"][0:6]
    line[0:6, 0:LEN] = jnp.where(c == 0, own, far)
    line[6:12, 0:LEN] = jnp.where(c == 0, far, own)
    vec_pieces[z] = line[0:16, 0:LEN].astype(BF16)
    near = vec_pieces.at[z]
    vec_copies = net.send([(near, near, peer("z", step)) for step in (1, 2, 3)], span(1, LEN))

    VT, packed = s["VT"], s["packed"]

    def stage(ref, l, index):
        return ref.at[pl.ds(pl.multiple_of(index * 48, 16), 48), pl.ds((l // 2) * D, D)]

    def spread(l, route, cols):
        for i in range(4):
            line[12 * i : 12 * i + 12, cols] = pieces[i, l, :, cols].astype(F32)[0:12]
        rows = line[:, cols].astype(BF16)
        if route == "x":
            W[6 * c + l, y, x, :, cols] = rows
        elif route == "y":
            stage(s["gp"], l, z)[:, cols] = rows
        else:
            W[6 * c + l, z, x, :, cols] = rows

    def strips(some, units):
        copies = []
        for l, route, cols in some:
            if route == "x":
                near = W.at[6 * c + l, y, x, :, cols]
            elif route == "y":
                near = stage(s["gp"], l, z).at[:, cols]
            else:
                near = W.at[6 * c + l, z, x, :, cols]
            copies += [(near, near, peer(SECOND[route], step)) for step in (1, 2, 3)]
        return net.send(copies, span(3 * units, copies[0][0].shape[-1]))

    def order_strips(l, cols):
        size = cols.size
        for i in range(4):
            FP[48 * i : 48 * i + 48, 0:size] = stage(s["gp"], l, i)[:, cols].astype(F32)
        for i in range(4):
            for j in range(4):
                line[12 * j : 12 * j + 12, 0:size] = FP[48 * j + 12 * i : 48 * j + 12 * i + 12, 0:size]
            W[6 * c + l, y, i, :, cols] = line[:, 0:size].astype(BF16)

    def turn_rows(ref, place, cols):
        rows = ref[place, :, :, :, cols].reshape(D, cols.size)
        ref[place, :, :, :, cols] = dot(perm[...], rows).astype(BF16).reshape(4, 4, 48, cols.size)

    def region(ref, place, route, index, half, cols):
        part = pl.ds(0, 4) if half is None else pl.ds(2 * half, 2)
        if route == "x":
            return ref.at[place, part, index, :, cols]
        return ref.at[place, index, part, :, cols]

    def gather_start(some):
        copies = []
        for l, route, cols in some:
            near = region(W, 6 * c + l, route, HERE[route], None, cols)
            copies += [(near, near, peer(route, step)) for step in (1, 2, 3)]
        return some, net.send(copies, span(12 * len(some), some[0][2].size))

    def gather_share(state):
        some, group = state
        group.wait_recv()
        if any(turns(l, route) for l, route, _ in some):
            net.sent(group)
        copies = []
        for l, route, cols in some:
            if turns(l, route):
                turn_rows(W, 6 * c + l, cols)
            near = W.at[6 * c + l, :, :, :, cols]
            copies.append((near, near, sibling))
        return net.send(copies, span(16 * len(some), some[0][2].size))

    act, p = s["act"], s["p"]
    q, k, v, ctx = (act.at[i] for i in range(4))
    A, F, FP, inv1, y1b = s["A"], s["F"], s["FP"], s["inv1"], s["y1b"]
    h, gp, dfb, dfp, sums = s["h"], s["gp"], s["dfb"], y1b, s["sums"]
    turned = s["turned"]

    att_pieces.wait_recv()
    att_strips = []
    for group in (ATT[:1], ATT[1:2], ATT[2:]):
        for some in group:
            spread(*some)
        att_strips.append(strips(group, len(group)))
    hid_pieces.wait_recv()
    for some in HID:
        spread(*some)
    z_strips = [strips(PARTS[0][2:], 2)]
    x_strips = strips(HID[:1], 1)
    y_strips = strips(HID[1:2], 1)
    z_strips.append(strips([(5, "z", p1), (4, "z", p2)], 2))
    x_rest = strips([(4, "x", p1)], 1)
    y_rest = strips([(5, "y", p2)], 1)
    vec_copies.wait_recv()
    for i in range(4):
        line[12 * i : 12 * i + 12, 0:LEN] = vec_pieces[i].astype(F32)[0:12]
    VT[y, x] = line[:, 0:LEN].astype(BF16)
    near = VT.at[y, x]
    vec_strips = net.send([(near, near, peer("x", step)) for step in (1, 2, 3)], span(3, LEN))
    starts = {}
    att_strips[0].wait_recv()
    for part in range(2):
        starts["x", part] = gather_start([(0, "x", part_cols[part])])
    att_strips[1].wait_recv()
    order_strips(1, wide)
    for part in range(2):
        starts["y", part] = gather_start([(1, "y", part_cols[part])])
    att_strips[2].wait_recv()
    for l in range(2):
        starts["t", l] = gather_start(ATT[2 + l : 3 + l])
    vec_strips.wait_recv()
    near = packed.at[y]
    packed[y] = sum(
        pltpu.roll(VT[y, i].astype(F32), 32 * i, 1) if i else VT[y, i].astype(F32) for i in range(4)
    ).astype(BF16)
    vec_last = net.send([(near, near, peer("y", step)) for step in (1, 2, 3)], span(3, LEN))
    for copy in loads:
        copy.wait()
    flows = {}

    def begin(part, route):
        flows[part, route] = gather_start([some for some in PARTS[part] if some[1] == route])

    def sharing(part, routes="xyz"):
        for route in routes:
            flows[part, route] = gather_share(flows[part, route])

    z_strips[0].wait_recv()
    begin(0, "z")
    x_strips.wait_recv()
    begin(0, "x")
    y_strips.wait_recv()
    order_strips(3, every)
    begin(0, "y")
    z_strips[1].wait_recv()
    begin(1, "z")
    x_rest.wait_recv()
    begin(1, "x")
    begin(1, "y")
    y_rest.wait_recv()
    order_strips(5, p2)
    for route in "zxy":
        begin(2, route)
    net.sent(att_strips[2])
    shares = [gather_share(starts[key]) for key in (("x", 0), ("y", 0), ("t", 0))]
    vec_last.wait_recv()
    net.sent(vec_strips)
    for i in range(4):
        block_i = packed[i].astype(F32)
        for j in range(4):
            VT[i, j] = (pltpu.roll(block_i, LEN - 32 * j, 1) if j else block_i).astype(BF16)
    V[...] = VT[...].reshape(D, LEN).astype(F32).T[0:16]
    shares += [gather_share(starts[key]) for key in (("x", 1), ("y", 1), ("t", 1))]
    for copy in shares:
        copy.wait_recv()
    qkv(W, V, xb, q, k, v)
    attend(q, k, v, s["bias"], p, ctx)
    net.sent(x_rest)
    sharing(0)
    first_norm(W, V, xb, ctx, A, inv1, F, y1b)
    turn(y1b, turned.at[1])
    sharing(1)

    def arrived(part):
        for route in "xyz":
            flows[part, route].wait_recv()

    arrived(0)
    net.sent(att_strips[1])
    net.sent(y_strips)
    net.sent(y_rest)
    up(W, V, y1b, h, gp, 0)
    down_(W, h, FP, 0)
    sharing(2)
    arrived(1)
    up(W, V, y1b, h, gp, 1)
    down_(W, h, FP, 1)
    arrived(2)
    up(W, V, y1b, h, gp, 2)
    down_(W, h, FP, 2)
    second_norm(V, perm, FP, F, gb, gb, dfb, sums)
    stores = []
    for i in range(SLOTS):
        stores.append(pltpu.make_async_copy(gb.at[pl.ds(i * LEN, LEN)], out_hbm.at[i], s["store_sem"].at[i]))
        stores[-1].start()
    to_down_order(dfb, perm, dfp)
    dfpT = turned.at[0]
    y1T = turned.at[1]
    turn(dfp, dfpT)
    net.close()

    pair_in, pair_out = s["pair_in"], s["pair_out"]
    G_half = s["half_in"]
    G_block = pair_in
    slots = [None] * 8

    def send_tiles(tiles):
        for slot, _, _, _ in tiles:
            if slots[slot] is not None:
                net.sent(slots[slot])
        values = [value() for _, _, _, value in tiles]
        for (slot, _, _, _), value in zip(tiles, values):
            pair_out[slot] = value.astype(BF16).reshape(4, 4, 48, TILE)
        group = net.send(
            [(pair_out.at[slot], pair_in.at[l, :, :, :, cols], sibling) for slot, l, cols, _ in tiles],
            span(16 * len(tiles), TILE),
        )
        for slot, _, _, _ in tiles:
            slots[slot] = group
        return group

    def add_into(ref, index, *others):
        total = ref[index].astype(F32)
        for other_ref, other_index in others:
            total = total + other_ref[other_index].astype(F32)
        ref[index] = total.astype(BF16)

    def cell(l, route, index, i, cols):
        return (l, i, index, slice(None), cols) if route == "x" else (l, index, i, slice(None), cols)

    def reduce_start(some):
        copies = []
        for l, route, cols in some:
            across = wrap(HERE[route] + 2)
            for half, step in ((0, 1), (1, 3)):
                copies.append((region(G, l, route, across, half, cols), G_half.at[l, half, :, :, cols], peer(route, step)))
        return some, net.send(copies, span(4 * len(some), TILE))

    def reduce_pass(state):
        some, group = state
        group.wait_recv()
        copies = []
        for l, route, cols in some:
            here = HERE[route]
            for i in range(2):
                add_into(G, cell(l, route, wrap(here + 1), i, cols), (G_half, (l, 0, i, slice(None), cols)))
                add_into(G, cell(l, route, wrap(here - 1), 2 + i, cols), (G_half, (l, 1, i, slice(None), cols)))
            for half, step in ((0, 1), (1, 3)):
                copies.append(
                    (region(G, l, route, wrap(here + step), None, cols), G_block.at[l, half, :, :, cols], peer(route, step))
                )
        return some, net.send(copies, span(8 * len(some), TILE))

    strip_in = s["strip_in"]

    def strip_place(l, route, moved):
        return (l, moved, x) if route == "x" else (l, z, moved)

    def reduce_end(state):
        some, group = state
        group.wait_recv()
        copies = []
        for l, route, cols in some:
            for i in range(4):
                add_into(
                    G,
                    cell(l, route, HERE[route], i, cols),
                    (G_block, (l, 0, i, slice(None), cols)),
                    (G_block, (l, 1, i, slice(None), cols)),
                )
            if route == "y":
                for i in range(4):
                    FP[48 * i : 48 * i + 48, 0:TILE] = G[l, y, i, :, cols].astype(F32)
                for j in range(4):
                    for i in range(4):
                        line[12 * i : 12 * i + 12, 0:TILE] = FP[48 * i + 12 * j : 48 * i + 12 * j + 12, 0:TILE]
                    stage(h, l, j)[:, cols] = line[:, 0:TILE].astype(BF16)
            for step in (1, 2, 3):
                target = wrap(HERE[SECOND[route]] + step)
                if route == "y":
                    source = stage(h, l, target).at[:, cols]
                else:
                    source = G.at[strip_place(l, route, target) + (slice(None), cols)]
                copies.append((source, strip_in.at[l, step - 1, :, cols], peer(SECOND[route], step)))
        return some, net.send(copies, span(3 * len(some), TILE))

    piece_out, piece_in = pieces, s["piece_in"]

    def strips_sum(state):
        some, group = state
        group.wait_recv()
        for l, route, cols in some:
            if route == "y":
                own = stage(h, l, z)[:, cols]
            else:
                own = G[strip_place(l, route, HERE[SECOND[route]]) + (slice(None), cols)]
            total = own.astype(F32)
            for i in range(3):
                total = total + strip_in[l, i, :, cols].astype(F32)
            line[:, 0:TILE] = total
            gap = jnp.zeros((4, TILE), F32)
            for i in range(4):
                rows = jnp.concatenate([line[12 * i : 12 * i + 12, 0:TILE], gap], 0)
                piece_out[i, l, :, cols] = rows.astype(BF16)

    def pieces_out(some, units):
        copies = []
        for l, route, cols in some:
            for step in (1, 2, 3):
                source = piece_out.at[wrap(HERE[FIRST[route]] + step), l, :, cols]
                copies.append((source, piece_in.at[step - 1, l, :, cols], peer(FIRST[route], step)))
        return net.send(copies, span(units, D))

    rows_out, rows_own, rows_in = s["first_out"], s["first_own"], s["first_in"]

    def pieces_sum(l, route, cols):
        total = piece_out[HERE[FIRST[route]], l, :, cols].astype(F32)
        for i in range(3):
            total = total + piece_in[i, l, :, cols].astype(F32)
        line[0:16, cols] = total
        top, bottom = line[0:6, cols], line[6:12, cols]
        rows_own[l, 0:6, cols] = jnp.where(c == 0, top, bottom)
        rows_out[l, 0:6, cols] = jnp.where(c == 0, bottom, top)
        return jnp.sum(top * top + bottom * bottom, keepdims=True)

    def hidden_slopes(core, part):
        places = [pl.ds(pl.multiple_of((2 * core + e) * D + part * TILE, LEN), TILE) for e in range(2)]
        slopes = []
        for e in range(2):
            dh = dot(dfp[...], columns(W, 6 * core + 4 + e, part * TILE, TILE))
            du = (dh * gp[:, places[e]].astype(F32)).astype(BF16)
            slopes.append(du)
            sums[pl.ds(V_B1 + 2 * core + e, 1), part_cols[part]] = jnp.sum(du.astype(F32), 0, keepdims=True)
        return places, slopes

    def keep_tiles(group, tiles):
        group.wait_recv()
        for l, cols, value in tiles:
            total = value() + pair_in[l, :, :, :, cols].reshape(D, TILE).astype(F32)
            G[l, :, :, :, cols] = total.astype(BF16).reshape(4, 4, 48, TILE)

    def hidden_tiles(places, slopes, cols):
        tiles = [(4 + e, cols, lambda e=e: dot(dfpT[...], h[:, places[e]])) for e in range(2)]
        return tiles + [(2 + e, cols, lambda e=e: dot(y1T[...], slopes[e])) for e in range(2)]

    shared = {}

    def others(part):
        places, slopes = hidden_slopes(other, part)
        tiles = hidden_tiles(places, slopes, part_cols[part])
        shared[part] = send_tiles([(4 * (part % 2) + i,) + tile for i, tile in enumerate(tiles)])
        for e in range(2):
            gp[:, places[e]] = slopes[e]

    def own_slopes(part):
        places, slopes = hidden_slopes(c, part)
        for e in range(2):
            gp[:, places[e]] = slopes[e]

    def own_tiles(part):
        places = [pl.ds(pl.multiple_of((2 * c + e) * D + part * TILE, LEN), TILE) for e in range(2)]
        keep_tiles(shared[part], hidden_tiles(places, [gp[:, place] for place in places], part_cols[part]))
        for l, route, cols in PARTS[part]:
            if turns(l, route):
                turn_rows(G, l, cols)
        return reduce_start(PARTS[part])

    others(0)
    others(1)
    own_slopes(0)
    flows[0] = own_tiles(0)
    others(2)
    own_slopes(1)
    flows[1] = own_tiles(1)
    flows[0] = reduce_pass(flows[0])
    own_slopes(2)
    flows[2] = own_tiles(2)
    first_back_product(W, gp, F)
    flows[1] = reduce_pass(flows[1])
    first_back(V, A, inv1, F, dfb, sums)

    sums[VECTORS:16, :] = jnp.zeros((16 - VECTORS, D), F32)
    sums_in, sums_out = s["sums_in"], s["sums_out"]

    def sums_step(place, stage_, group, axis):
        if group is None:
            total = sums[8 * place : 8 * place + 8, :]
        else:
            total = sums_out[place, stage_ - 1]
            group.wait_recv()
            for i in range(1 if stage_ == 1 else 3):
                total = total + sums_in[place, 0 if stage_ == 1 else 3 * stage_ - 5 + i]
        if axis is None:
            return total
        sums_out[place, stage_] = total
        near = sums_out.at[place, stage_]
        if stage_ == 0:
            return net.send([(near, sums_in.at[place, 0], sibling)], near)
        base = 3 * stage_ - 3
        return net.send(
            [(near, sums_in.at[place, base + step], peer(axis, step)) for step in (1, 2, 3)],
            sums_in.at[place, pl.ds(0, 3)],
        )

    up_sums = sums_step(1, 0, None, "sibling")
    doT = turned.at[1]
    turn(dfb, doT)
    output_back(W, dfb, y1b)
    up_sums = sums_step(1, 1, up_sums, "z")
    turn(xb, turned.at[0])
    flows[2] = reduce_pass(flows[2])
    flows[0] = reduce_end(flows[0])

    def projection_grad(core, l, n):
        left = core if l == 1 else 0
        return dot(turned[left], act[2 * core + l, :, n * TILE : (n + 1) * TILE])

    def projection_tiles(core, n):
        return [(l, part_cols[n], lambda l=l: projection_grad(core, l, n)) for l in (0, 1)]

    last = []

    def other_projections(n):
        attend_back(q, k, v, p, y1b, n)
        tiles = projection_tiles(other, n)
        shared["p", n] = send_tiles([(2 * n + i,) + tile for i, tile in enumerate(tiles)])

    def own_projections(n):
        keep_tiles(shared["p", n], projection_tiles(c, n))
        if n == 2:
            for l in (0, 1):
                turn_rows(G, l, third)
        last.append(reduce_start([(l, "z" if n == 2 else "xy"[l], part_cols[n]) for l in (0, 1)]))

    other_projections(2)
    other_projections(0)
    own_projections(2)
    flows[1] = reduce_end(flows[1])
    up_sums = sums_step(1, 2, up_sums, "x")
    other_projections(1)
    column_sums(q, sums, V_BQ)
    column_sums(v, sums, V_BV)
    first_sums = sums_step(0, 0, None, "sibling")
    own_projections(0)
    own_projections(1)
    first_sums = sums_step(0, 1, first_sums, "z")
    flows[2] = reduce_end(flows[2])
    last[0] = reduce_pass(last[0])
    for group in pair + [att_pieces, hid_pieces]:
        net.sent(group)
    last[1] = reduce_pass(last[1])
    input_back(W, q, k, v, F, 0)
    last[2] = reduce_pass(last[2])
    input_back(W, q, k, v, F, 1)
    for i in range(SLOTS):
        stores.append(pltpu.make_async_copy(F.at[pl.ds(i * LEN, LEN)], grad_hbm.at[i], s["store_sem"].at[4 + i]))
        stores[-1].start()
    strips_sum(flows[0])
    strips_sum(flows[1])
    first_sums = sums_step(0, 2, first_sums, "x")
    up_sums = sums_step(1, 3, up_sums, "y")
    strips_sum(flows[2])
    hid_pieces = pieces_out(HID, 4)
    for n in range(3):
        last[n] = reduce_end(last[n])
    first_sums = sums_step(0, 3, first_sums, "y")
    hid_pieces.wait_recv()
    squares = jnp.zeros((1, 1), F32)
    for some in HID:
        squares = squares + pieces_sum(*some)
    rows_copies = [net.send([(rows_out.at[pl.ds(2, 4)], rows_in.at[pl.ds(2, 4)], sibling)], rows_out.at[pl.ds(2, 4)])]
    for n in range(3):
        strips_sum(last[n])
    att_pieces = pieces_out(ATT, 2)
    vec_total = jnp.concatenate([sums_step(0, 4, first_sums, None), sums_step(1, 4, up_sums, None)], 0)
    place = lax.broadcasted_iota(jnp.int32, (8, D), 1) - 6 * me
    pick = (place == lax.broadcasted_iota(jnp.int32, (8, D), 0)).astype(BF16)
    vec_grad = jnp.zeros((8, 16), F32)
    for _ in range(3):
        low = vec_total.astype(BF16)
        vec_grad = vec_grad + dot(pick, low, NT)
        vec_total = vec_total - low.astype(F32)
    vec_grad = vec_grad[0:6, 0:VECTORS]
    squares = squares + jnp.sum(vec_grad * vec_grad, keepdims=True)
    att_pieces.wait_recv()
    for some in ATT:
        squares = squares + pieces_sum(*some)
    norm_out, norm_in = s["norm_out"], s["norm_in"]
    norm_out[0] = jnp.broadcast_to(squares, (8, LEN))
    plane = [(norm_out.at[0], norm_in.at[0, i], device) for i, device in enumerate(plane_peers)]
    norm_group = net.send(plane, norm_in.at[0])
    rows_copies.append(
        net.send([(rows_out.at[pl.ds(0, 2)], rows_in.at[pl.ds(0, 2)], sibling)], rows_out.at[pl.ds(0, 2)])
    )
    for copy in rows_copies:
        copy.wait_recv()
    att_grad, hid_grad, vec_grad_at = att_w, hid_w, vec_w
    vec_grad_at[...] = vec_grad
    for core in range(2):
        for l in range(SHARE):
            value = jnp.where(c == core, rows_own[l, 0:6], rows_in[l, 0:6])
            if l < 2:
                att_grad[:, 2 * core + l, :] = value
            else:
                i, j = (l - 2) // 2, 2 * core + l % 2
                hid_grad[:, i, j * D : (j + 1) * D] = value
    for i, (source, target) in enumerate(((att_grad, att_out), (hid_grad, hid_out), (vec_grad_at, vec_out))):
        stores.append(pltpu.make_async_copy(source, target, s["store_sem"].at[8 + i]))
        stores[-1].start()

    def norm_step(index, group, count):
        group.wait_recv()
        total = norm_out[index]
        for i in range(count):
            total = total + norm_in[index, i]
        return total

    norm_out[1] = norm_step(0, norm_group, 15)
    copies = [(norm_out.at[1], norm_in.at[1, 0], sibling)]
    for step in (1, 2, 3):
        copies.append((norm_out.at[1], norm_in.at[1, step], peer("z", step)))
        copies.append((norm_out.at[1], norm_in.at[1, 3 + step], far_peer(step)))
    norm_group = net.send(copies, norm_in.at[1, pl.ds(0, 7)])
    norm = jnp.sqrt(norm_step(1, norm_group, 7))
    norm_out_ref[...] = norm[0:1, 0:1]
    for copy in stores:
        copy.wait()
    net.close()


def rates(values, shape):
    index = lax.broadcasted_iota(jnp.int32, shape, 1)
    rate = jnp.full(shape, values[0], F32)
    for i, value in enumerate(values[1:]):
        rate = jnp.where(index == i + 1, value, rate)
    return rate


def update_kernel(out_in, grad_in, norm_in, *refs):
    sources, (out_hbm, grad_hbm), targets = refs[:12], refs[12:14], refs[14:23]
    out_at, grad_at = refs[23:25]
    held, norm, sems = refs[25:37], refs[37], refs[38]
    norm_load = pltpu.make_async_copy(norm_in, norm, sems.at[37])
    norm_load.start()
    loads = [pltpu.make_async_copy(a, b, sems.at[i]) for i, (a, b) in enumerate(zip(sources, held))]
    passing = []
    stores = []
    for i in range(SLOTS):
        for j, (source, middle, target) in enumerate(((grad_in, grad_at, grad_hbm), (out_in, out_at, out_hbm))):
            n = 12 + 4 * i + 2 * j
            passing.append(pltpu.make_async_copy(source.at[i], middle.at[i], sems.at[n]))
            stores.append(pltpu.make_async_copy(middle.at[i], target.at[i], sems.at[n + 1]))
    for copy in loads + passing:
        copy.start()
    norm_load.wait()
    factor = CLIP_NORM / jnp.maximum(norm[...], CLIP_NORM)
    settings = (
        (rates(ATTENTION_RATES, (6, 4, D)), WEIGHT_DECAY),
        (rates(HIDDEN_RATES, (6, 2, FF)), WEIGHT_DECAY),
        (VECTOR_RATE, 0.0),
    )
    for i in (1, 0, 2):
        for j in (i, 3 + 3 * i, 4 + 3 * i, 5 + 3 * i):
            loads[j].wait()
        state = held[3 + 3 * i : 6 + 3 * i]
        new = adam(state[0][...], state[1][...], state[2][...], held[i][...] * factor, *settings[i])
        for j in range(3):
            state[j][...] = new[j]
            stores.append(pltpu.make_async_copy(state[j], targets[3 * i + j], sems.at[28 + 3 * i + j]))
        if i == 1:
            for load, copy in zip(passing, stores):
                load.wait()
                copy.start()
        for copy in stores[-3:]:
            copy.start()
    for copy in stores:
        copy.wait()


def on_device(
    inputs,
    cotangent,
    joined,
    half_lengths,
    attention_master,
    attention_first,
    attention_second,
    hidden_master,
    hidden_first,
    hidden_second,
    vector_master,
    vector_first,
    vector_second,
):
    any_space = pl.BlockSpec(memory_space=pl.ANY)
    vmem = pl.BlockSpec(memory_space=pltpu.VMEM)
    like = lambda a: jax.ShapeDtypeStruct(a.shape, a.dtype)
    swap = lambda a: jnp.transpose(a, (1, 0, 2))
    attention = [swap(a) for a in (attention_master, attention_first, attention_second)]
    hidden = [swap(a) for a in (hidden_master, hidden_first, hidden_second)]
    vectors = [a.T for a in (vector_master, vector_first, vector_second)]
    params = attention + hidden + vectors
    out_like = jax.ShapeDtypeStruct(inputs.shape, BF16)
    grad_like = jax.ShapeDtypeStruct(inputs.shape, F32)
    results = pl.pallas_call(
        step_kernel,
        out_shape=(
            out_like,
            grad_like,
            jax.ShapeDtypeStruct((1, 1), F32),
            like(attention[0]),
            like(hidden[0]),
            like(vectors[0]),
        ),
        in_specs=[any_space] * 8,
        out_specs=(any_space, any_space, vmem) + (any_space,) * 3,
        scratch_shapes=list(SCRATCH.values()),
        compiler_params=pltpu.CompilerParams(collective_id=0, has_side_effects=True, vmem_limit_bytes=64 << 20),
        cost_estimate=pl.CostEstimate(flops=22 * 10**9, bytes_accessed=6 * 10**6, transcendentals=4 * 10**6),
    )(
        inputs,
        cotangent,
        jnp.asarray(permutation(), BF16),
        joined.T,
        jnp.transpose(half_lengths, (1, 2, 0)),
        attention[0],
        hidden[0],
        vectors[0],
    )
    outs = pl.pallas_call(
        update_kernel,
        out_shape=(out_like, grad_like) + tuple(like(a) for a in params),
        in_specs=[any_space] * 15,
        out_specs=(any_space,) * 11,
        scratch_shapes=[
            pltpu.VMEM(inputs.shape, BF16),
            pltpu.VMEM(inputs.shape, F32),
            *[pltpu.VMEM(a.shape, F32) for a in (attention[0], hidden[0], vectors[0], *params)],
            pltpu.VMEM((1, 1), F32),
            pltpu.SemaphoreType.DMA((38,)),
        ],
        cost_estimate=pl.CostEstimate(flops=2 * 10**6, bytes_accessed=7 * 10**6, transcendentals=10**5),
    )(*results, *params)
    output, input_grad, *new = outs
    norm = results[2].reshape(())
    return (output, input_grad, norm, *[swap(a) for a in new[:6]], *[a.T for a in new[6:]])


def solution(mesh):
    shard = P(None, "dp", None)
    flat = P(None, "dp")
    return jax.shard_map(
        on_device,
        mesh=mesh,
        in_specs=(shard, shard, flat, shard, shard, shard, shard, shard, shard, shard, flat, flat, flat),
        out_specs=(shard, shard, P(), shard, shard, shard, shard, shard, shard, flat, flat, flat),
        check_vma=False,
    )
```

```python
import functools
import jax
import jax.numpy as jnp
import numpy as np
from jax import lax
from jax.experimental import pallas as pl
from jax.experimental.pallas import tpu as pltpu
from jax.sharding import PartitionSpec as P

F32 = jnp.float32
BF16 = jnp.bfloat16
D = 768
FF = 3072
ROWS = 512
SLOTS = 4
LEN = 128
PAIRS = 6
TILE = 256
NORM_EPS = 1e-05
MASKED = -1e30
NN = (((1,), (0,)), ((), ()))
NT = (((1,), (1,)), ((), ()))
TN = (((0,), (0,)), ((), ()))
PLACE_Q, PLACE_K, PLACE_V, PLACE_O = 0, 1, 6, 7
PLACE_UP = (2, 3, 8, 9)
PLACE_DOWN = (4, 5, 10, 11)
V_BQ, V_BV, V_BO, V_G1, V_C1, V_G2, V_C2, V_B2, V_B1 = range(9)


def dot(a, b, dims=NN):
    return lax.dot_general(a, b, dims, preferred_element_type=F32)


def block(ref, place):
    return ref[place].reshape(D, D)


def columns(ref, place, start, size):
    return ref[place, :, :, :, pl.ds(start, size)].reshape(D, size)


def put_columns(ref, place, start, size, value):
    ref[place, :, :, :, pl.ds(start, size)] = value.reshape(4, 4, 48, size)


def loop(count, body):
    lax.fori_loop(0, count, lambda i, c: (body(i), c)[1], 0)


def at(i, size):
    return pl.ds(pl.multiple_of(i * size, size), size)


def qkv(W, V, xb, q, k, v):
    x = xb[...]
    for n in range(D // TILE):
        cols = pl.ds(n * TILE, TILE)
        q[:, cols] = ((dot(x, columns(W, PLACE_Q, n * TILE, TILE)) + V[V_BQ, cols]).astype(BF16) * 0.125).astype(BF16)
        k[:, cols] = dot(x, columns(W, PLACE_K, n * TILE, TILE)).astype(BF16)
        v[:, cols] = (dot(x, columns(W, PLACE_V, n * TILE, TILE)) + V[V_BV, cols]).astype(BF16)


def halves(value):
    lane = lax.broadcasted_iota(jnp.int32, value.shape, 1)
    zero = jnp.zeros_like(value)
    return jnp.concatenate([jnp.where(lane < 64, value, zero), jnp.where(lane < 64, zero, value)], 0)


def joined_halves(value):
    lane = lax.broadcasted_iota(jnp.int32, (LEN, LEN), 1)
    return jnp.where(lane < 64, value[:LEN], value[LEN:])


def fill_masks(joined, half_lengths, bias):
    query = lax.broadcasted_iota(jnp.int32, (LEN, LEN), 0)
    key = lax.broadcasted_iota(jnp.int32, (LEN, LEN), 1)
    for slot in range(SLOTS):
        is_joined = joined[0, slot]
        low = half_lengths[0, 0, slot]
        high = half_lengths[0, 1, slot]
        upper = (key >= 64).astype(jnp.int32)
        limit = is_joined * (64 + high) + (1 - is_joined) * (upper * (64 + high) + (1 - upper) * low)
        apart = (1 - is_joined) * jnp.abs((query >= 64).astype(jnp.int32) - upper)
        bias[slot] = jnp.where((key < limit) & (apart == 0), 0.0, MASKED)


GROUP = 6


def attend(q, k, v, bias, p, ctx):
    def units(slot):
        rows = at(slot, LEN)
        m = bias[slot]
        hidden = jnp.concatenate([m, m], 0) < 0
        cols = [pl.ds(pair * LEN, LEN) for pair in range(PAIRS)]
        for start in range(0, PAIRS, GROUP):
            some = range(start, start + GROUP)
            s = [dot(halves(q[rows, cols[i]]), k[rows, cols[i]], NT) for i in some]
            values = [v[rows, cols[i]] for i in some]
            s = [jnp.where(hidden, MASKED, one) for one in s]
            e = [jnp.exp(one - jnp.max(one, -1, keepdims=True)) for one in s]
            low = [(one * (1.0 / jnp.sum(one, -1, keepdims=True))).astype(BF16) for one in e]
            out = [joined_halves(dot(one, value)).astype(BF16) for one, value in zip(low, values)]
            for i, one, result in zip(some, low, out):
                p[slot * PAIRS + i] = one
                ctx[rows, cols[i]] = result

    loop(SLOTS, units)


def attend_back(q, k, v, p, dctx, n):
    def units(step):
        some = [(2 * step + slot, pair) for slot in range(2) for pair in (2 * n, 2 * n + 1)]
        places = [(at(slot, LEN), pl.ds(pair * LEN, LEN)) for slot, pair in some]
        low = [p[slot * PAIRS + pair] for slot, pair in some]
        two = [halves(dctx[place]) for place in places]
        q2 = [halves(q[place]) for place in places]
        keys = [k[place] for place in places]
        dp = [dot(a, v[place], NT) for a, place in zip(two, places)]
        dv = [dot(a, b, TN) for a, b in zip(low, two)]
        full = [a.astype(F32) for a in low]
        ds = [(a * (b - jnp.sum(a * b, -1, keepdims=True))).astype(BF16) for a, b in zip(full, dp)]
        dq = [joined_halves(dot(a, b)) * 0.125 for a, b in zip(ds, keys)]
        dk = [dot(a, b, TN) for a, b in zip(ds, q2)]
        for a, b, d, place in zip(dv, dq, dk, places):
            v[place] = a.astype(BF16)
            q[place] = b.astype(BF16)
            k[place] = d.astype(BF16)

    loop(2, units)


STRIP = 256


def first_norm(W, V, xb, ctx, A, inv1, F, y1b):
    A[...] = dot(ctx[...], block(W, PLACE_O), NT)

    def strip(i):
        rows = at(i, STRIP)
        a = xb[rows, :].astype(F32) + A[rows, :] + V[V_BO : V_BO + 1, :]
        center = a - jnp.mean(a, -1, keepdims=True)
        inverse = lax.rsqrt(jnp.mean(center * center, -1, keepdims=True) + NORM_EPS)
        n = center * inverse
        A[rows, :] = n
        inv1[rows, :] = inverse
        y = n * V[V_G1 : V_G1 + 1, :] + V[V_C1 : V_C1 + 1, :]
        y1b[rows, :] = y.astype(BF16)
        F[rows, :] = y + V[V_B2 : V_B2 + 1, :]

    loop(ROWS // STRIP, strip)


def gelu_parts(u):
    e = jnp.exp(-0.5 * (u * u))
    t = pl.reciprocal(1.0 + 0.23164190 * jnp.abs(u), approx=True)
    poly = ((((0.5307027145 * t - 0.726576013) * t + 0.7107068705) * t - 0.142248368) * t + 0.127414796) * t
    tail = poly * e
    cdf = jnp.where(u >= 0, 1.0 - tail, tail)
    return u * cdf, cdf + (u * 0.3989422804014327) * e


def up(W, V, y1b, h, gp, part):
    for j, place in enumerate(PLACE_UP):
        cols = pl.ds(j * D + part * TILE, TILE)
        u = dot(y1b[...], columns(W, place, part * TILE, TILE)) + V[V_B1 + j : V_B1 + j + 1, pl.ds(part * TILE, TILE)]
        value, slope = gelu_parts(u)
        h[:, cols] = value.astype(BF16)
        gp[:, cols] = slope.astype(BF16)


def down_(W, h, FP, part):
    left = jnp.concatenate([h[:, pl.ds(j * D + part * TILE, TILE)] for j in range(4)], 1)
    right = jnp.concatenate([columns(W, place, part * TILE, TILE) for place in PLACE_DOWN], 1)
    total = dot(left, right, NT)
    FP[...] = total if part == 0 else FP[...] + total


def second_norm(V, perm, FP, F, gb, outb, dfb, sums):
    F[...] += dot(FP[...].astype(BF16), perm[...])

    def strip(i, carry):
        dg, dc, db = carry
        rows = at(i, STRIP)
        z = F[rows, :]
        center = z - jnp.mean(z, -1, keepdims=True)
        inverse = lax.rsqrt(jnp.mean(center * center, -1, keepdims=True) + NORM_EPS)
        n = center * inverse
        gain = V[V_G2 : V_G2 + 1, :]
        g = gb[rows, :].astype(F32)
        outb[rows, :] = (n * gain + V[V_C2 : V_C2 + 1, :]).astype(BF16)
        gn = g * n
        e = g * gain
        dz = inverse * (e - jnp.mean(e, -1, keepdims=True) - n * jnp.mean(gn * gain, -1, keepdims=True))
        low = dz.astype(BF16)
        F[rows, :] = dz
        dfb[rows, :] = low
        return (
            dg + jnp.sum(gn, 0, keepdims=True),
            dc + jnp.sum(g, 0, keepdims=True),
            db + jnp.sum(low.astype(F32), 0, keepdims=True),
        )

    zero = jnp.zeros((1, D), F32)
    dg, dc, db = lax.fori_loop(0, ROWS // STRIP, strip, (zero, zero, zero))
    sums[V_G2 : V_G2 + 1, :] = dg
    sums[V_C2 : V_C2 + 1, :] = dc
    sums[V_B2 : V_B2 + 1, :] = db


def turn(source, target):
    for i in range(ROWS // LEN):
        target[:, i * LEN : (i + 1) * LEN] = source[i * LEN : (i + 1) * LEN, :].T


def first_back_product(W, gp, F):
    for i in range(ROWS // TILE):
        rows = pl.ds(i * TILE, TILE)
        F[rows, :] += dot(gp[rows, :], jnp.concatenate([block(W, place) for place in PLACE_UP], 1), NT)


def first_back(V, A, inv1, F, dob, sums):
    def strip(i, carry):
        dg, dc, db = carry
        rows = at(i, STRIP)
        dy = F[rows, :]
        n = A[rows, :]
        gain = V[V_G1 : V_G1 + 1, :]
        dyn = dy * n
        e = dy * gain
        da = inv1[rows, :] * (e - jnp.mean(e, -1, keepdims=True) - n * jnp.mean(dyn * gain, -1, keepdims=True))
        low = da.astype(BF16)
        F[rows, :] = da
        dob[rows, :] = low
        return (
            dg + jnp.sum(dyn, 0, keepdims=True),
            dc + jnp.sum(dy, 0, keepdims=True),
            db + jnp.sum(low.astype(F32), 0, keepdims=True),
        )

    zero = jnp.zeros((1, D), F32)
    dg, dc, db = lax.fori_loop(0, ROWS // STRIP, strip, (zero, zero, zero))
    sums[V_G1 : V_G1 + 1, :] = dg
    sums[V_C1 : V_C1 + 1, :] = dc
    sums[V_BO : V_BO + 1, :] = db


def output_back(W, dob, dctx):
    def tile(n):
        cols = at(n, TILE)
        dctx[:, cols] = dot(dob[...], columns(W, PLACE_O, cols.start, TILE)).astype(BF16)

    loop(D // TILE, tile)


def column_sums(source, sums, row):
    sums[row : row + 1, :] = jnp.sum(source[...].astype(F32), 0, keepdims=True)


def input_back(W, q, k, v, F, i):
    rows = pl.ds(i * TILE, TILE)
    left = jnp.concatenate([q[rows, :], k[rows, :], v[rows, :]], 1)
    right = jnp.concatenate([block(W, place) for place in (PLACE_Q, PLACE_K, PLACE_V)], 1)
    F[rows, :] += dot(left, right, NT)


def to_down_order(dfb, perm, dfp):
    dfp[...] = dot(dfb[...], perm[...], NT).astype(BF16)


def permutation():
    r = np.arange(D)
    y, x, z, j = r // 192, r // 48 % 4, r // 12 % 4, r % 12
    p = np.zeros((D, D), np.float32)
    p[192 * z + 48 * x + 12 * y + j, r] = 1
    return p


MESH = pl.DeviceIdType.MESH
STEP = 10
ADAM_EPS = 1e-08
BETA_ONE = 0.9
BETA_TWO = 0.999
CLIP_NORM = 1.0
WEIGHT_DECAY = 0.01
ATTENTION_RATES = (0.02, 0.02, 0.04, 0.3)
HIDDEN_RATES = (0.04, 0.02)
VECTOR_RATE = 0.5
COPIES = 85
VECTORS = 12
SHARE = 6


class Net:
    def __init__(self, send_sem, recv_sem):
        self.send_sem, self.recv_sem, self.count, self.open = send_sem, recv_sem, 0, []

    def send(self, copies, whole):
        assert self.count < COPIES
        sems = dict(send_sem=self.send_sem.at[self.count], recv_sem=self.recv_sem.at[self.count])
        self.count += 1
        made = [
            pltpu.make_async_remote_copy(src_ref=a, dst_ref=b, device_id=(d,), device_id_type=MESH, **sems)
            for a, b, d in copies
        ]
        for copy in made:
            copy.start()
        group = pltpu.make_async_remote_copy(
            src_ref=whole, dst_ref=whole, device_id=(copies[0][2],), device_id_type=MESH, **sems
        )
        self.open.append(group)
        return group

    def sent(self, group):
        if any(one is group for one in self.open):
            group.wait_send()
            self.open = [one for one in self.open if one is not group]

    def close(self):
        for group in self.open:
            group.wait_send()
        self.open = []


def adam(master, first, second, gradient, rate, decay):
    first_new = BETA_ONE * first + (1.0 - BETA_ONE) * gradient
    second_new = BETA_TWO * second + (1.0 - BETA_TWO) * gradient * gradient
    first_hat = first_new * (1.0 / (1.0 - BETA_ONE**STEP))
    second_hat = second_new * (1.0 / (1.0 - BETA_TWO**STEP))
    step = first_hat * pl.reciprocal(jnp.sqrt(second_hat) + ADAM_EPS, approx=True)
    master_new = master - rate * (step + decay * master)
    return master_new, first_new, second_new


SCRATCH = dict(
    W=pltpu.VMEM((12, 4, 4, 48, D), BF16),
    G=pltpu.VMEM((SHARE, 4, 4, 48, D), BF16),
    pair_in=pltpu.VMEM((SHARE, 4, 4, 48, D), BF16),
    pair_out=pltpu.VMEM((8, 4, 4, 48, TILE), BF16),
    half_in=pltpu.VMEM((SHARE, 2, 2, 48, D), BF16),
    strip_in=pltpu.VMEM((SHARE, 3, 48, D), BF16),
    piece_in=pltpu.VMEM((3, SHARE, 16, D), BF16),
    first_out=pltpu.VMEM((SHARE, 8, D), F32),
    first_own=pltpu.VMEM((SHARE, 8, D), F32),
    first_in=pltpu.VMEM((SHARE, 8, D), F32),
    vec_own=pltpu.VMEM((8, LEN), F32),
    vec_in=pltpu.VMEM((8, LEN), F32),
    pieces=pltpu.VMEM((4, SHARE, 16, D), BF16),
    vec_pieces=pltpu.VMEM((4, 16, LEN), BF16),
    VT=pltpu.VMEM((4, 4, 48, LEN), BF16),
    line=pltpu.VMEM((48, D), F32),
    sums_in=pltpu.VMEM((2, 10, 8, D), F32),
    sums_out=pltpu.VMEM((2, 4, 8, D), F32),
    packed=pltpu.VMEM((4, 48, LEN), BF16),
    norm_out=pltpu.VMEM((2, 8, LEN), F32),
    norm_in=pltpu.VMEM((2, 15, 8, LEN), F32),
    V=pltpu.VMEM((16, D), F32),
    sums=pltpu.VMEM((16, D), F32),
    bias=pltpu.VMEM((SLOTS, LEN, LEN), F32),
    act=pltpu.VMEM((4, ROWS, D), BF16),
    p=pltpu.VMEM((SLOTS * PAIRS, 2 * LEN, LEN), BF16),
    A=pltpu.VMEM((ROWS, D), F32),
    F=pltpu.VMEM((ROWS, D), F32),
    FP=pltpu.VMEM((ROWS, D), F32),
    inv1=pltpu.VMEM((ROWS, 1), F32),
    y1b=pltpu.VMEM((ROWS, D), BF16),
    turned=pltpu.VMEM((2, D, ROWS), BF16),
    h=pltpu.VMEM((ROWS, FF), BF16),
    gp=pltpu.VMEM((ROWS, FF), BF16),
    dfb=pltpu.VMEM((ROWS, D), BF16),
    xb=pltpu.VMEM((ROWS, D), BF16),
    gb=pltpu.VMEM((ROWS, D), BF16),
    perm=pltpu.VMEM((D, D), BF16),
    att_w=pltpu.VMEM((6, 4, D), F32),
    hid_w=pltpu.VMEM((6, 2, FF), F32),
    vec_w=pltpu.VMEM((6, VECTORS), F32),
    joined=pltpu.SMEM((1, SLOTS), jnp.int32),
    half_lengths=pltpu.SMEM((1, 2, SLOTS), jnp.int32),
    load_sem=pltpu.SemaphoreType.DMA((14,)),
    store_sem=pltpu.SemaphoreType.DMA((11,)),
    send_sem=pltpu.SemaphoreType.DMA((COPIES,)),
    recv_sem=pltpu.SemaphoreType.DMA((COPIES,)),
)
NAMES = tuple(SCRATCH)


def step_kernel(
    x_hbm,
    g_hbm,
    perm_hbm,
    joined_hbm,
    half_hbm,
    att_hbm,
    hid_hbm,
    vec_hbm,
    out_hbm,
    grad_hbm,
    norm_out_ref,
    att_out,
    hid_out,
    vec_out,
    *scratch,
):
    s = dict(zip(NAMES, scratch))
    W, G, V = s["W"], s["G"], s["V"]
    xb, gb, perm = s["xb"], s["gb"], s["perm"]
    net = Net(s["send_sem"], s["recv_sem"])

    me = lax.axis_index("dp")
    c = lax.rem(me, 2)
    z = lax.rem(lax.div(me, 2), 4)
    x = lax.rem(lax.div(me, 8), 4)
    y = lax.div(me, 32)
    other = 1 - c

    def wrap(value):
        return lax.rem(value + 4, 4)

    def peer(axis, step):
        moved = {"x": x, "y": y, "z": z}
        moved[axis] = wrap(moved[axis] + step)
        return ((moved["y"] * 4 + moved["x"]) * 4 + moved["z"]) * 2 + c

    sibling = me + 1 - 2 * c

    def far_peer(step):
        return ((y * 4 + x) * 4 + wrap(z + step)) * 2 + other

    plane_peers = [((wrap(y + i // 4) * 4 + wrap(x + i % 4)) * 4 + z) * 2 + c for i in range(1, 16)]

    att_w, hid_w, vec_w = s["att_w"], s["hid_w"], s["vec_w"]
    masters_in = [
        pltpu.make_async_copy(source, target, s["load_sem"].at[9 + i])
        for i, (source, target) in enumerate(((att_hbm, att_w), (hid_hbm, hid_w), (vec_hbm, vec_w)))
    ]
    loads = []
    for i in range(SLOTS):
        loads.append(pltpu.make_async_copy(x_hbm.at[i], xb.at[pl.ds(i * LEN, LEN)], s["load_sem"].at[i]))
        loads.append(pltpu.make_async_copy(g_hbm.at[i], gb.at[pl.ds(i * LEN, LEN)], s["load_sem"].at[4 + i]))
    loads.append(pltpu.make_async_copy(perm_hbm, perm, s["load_sem"].at[8]))
    joined, half_lengths = s["joined"], s["half_lengths"]
    lengths_in = [
        pltpu.make_async_copy(joined_hbm, joined, s["load_sem"].at[12]),
        pltpu.make_async_copy(half_hbm, half_lengths, s["load_sem"].at[13]),
    ]
    for copy in masters_in + lengths_in + loads:
        copy.start()

    barrier = pltpu.get_barrier_semaphore()
    partners = [sibling] + [peer(axis, step) for axis in "xyz" for step in (1, 2, 3)]
    for partner in partners:
        pl.semaphore_signal(barrier, inc=1, device_id=(partner,), device_id_type=MESH)

    for copy in masters_in:
        copy.wait()
    masters = [[att_w[:, 2 * core + l, :] for l in range(2)] for core in range(2)]
    for core in range(2):
        masters[core] += [hid_w[:, i, (2 * core + l) * D : (2 * core + l + 1) * D] for i in range(2) for l in range(2)]
    for l in range(SHARE):
        s["first_own"][l, 0:6, :] = jnp.where(c == 0, masters[0][l], masters[1][l])
        s["first_out"][l, 0:6, :] = jnp.where(c == 0, masters[1][l], masters[0][l])
    s["vec_own"][...] = jnp.zeros((8, LEN), F32)
    s["vec_own"][0:6, 0:VECTORS] = vec_w[...]
    line = s["line"]
    line[...] = jnp.zeros((48, D), F32)
    pl.semaphore_wait(barrier, len(partners))

    FIRST = {"x": "z", "y": "x", "z": "y"}
    SECOND = {"x": "y", "y": "z", "z": "x"}
    HERE = {"x": x, "y": y, "z": z}
    every = pl.ds(0, D)
    wide = pl.ds(0, 2 * TILE)
    part_cols = [pl.ds(part * TILE, TILE) for part in range(3)]
    third = part_cols[2]

    def span(count, size):
        for n in (4, 3, 2, 1):
            for k in (4, 3, 2, 1):
                if count % (n * k) == 0 and count // (n * k) <= 12:
                    return W.at[pl.ds(0, count // (n * k)), pl.ds(0, k), pl.ds(0, n), :, pl.ds(0, size)]
        raise ValueError

    def to_three(axis, copies):
        return [(source(step), target(step), peer(axis, step)) for source, target in copies for step in (1, 2, 3)]

    pair = [
        net.send([(a, b, sibling)], a)
        for a, b in (
            (s["first_out"].at[pl.ds(0, 2)], s["first_in"].at[pl.ds(0, 2)]),
            (s["vec_own"], s["vec_in"]),
            (s["first_out"].at[pl.ds(2, 4)], s["first_in"].at[pl.ds(2, 4)]),
        )
    ]
    for copy in lengths_in:
        copy.wait()
    fill_masks(joined, half_lengths, s["bias"])
    pieces, vec_pieces = s["pieces"], s["vec_pieces"]
    ATT = ((0, "x", wide), (1, "y", wide), (0, "z", third), (1, "z", third))
    p0, p1, p2 = part_cols
    PARTS = (
        ((2, "x", p0), (3, "y", p0), (4, "z", p0), (5, "z", p0)),
        ((2, "x", p1), (4, "x", p1), (3, "y", p1), (5, "z", p1)),
        ((2, "x", p2), (3, "y", p2), (5, "y", p2), (4, "z", p2)),
    )
    HID = (
        (2, "x", every),
        (3, "y", every),
        (4, "z", p0),
        (4, "x", p1),
        (4, "z", p2),
        (5, "z", pl.ds(0, 2 * TILE)),
        (5, "y", p2),
    )

    def turns(l, route):
        return (route == "z") != (l >= 4)

    def make_piece(l, route, cols):
        own, far = s["first_own"][l, 0:6, cols], s["first_in"][l, 0:6, cols]
        line[0:6, cols] = jnp.where(c == 0, own, far)
        line[6:12, cols] = jnp.where(c == 0, far, own)
        pieces[HERE[FIRST[route]], l, :, cols] = line[0:16, cols].astype(BF16)

    def send_pieces(some, units):
        copies = []
        for l, route, cols in some:
            near = pieces.at[HERE[FIRST[route]], l, :, cols]
            copies += [(near, near, peer(FIRST[route], step)) for step in (1, 2, 3)]
        return net.send(copies, span(units, D))

    pair[0].wait_recv()
    for some in ATT:
        make_piece(*some)
    att_pieces = send_pieces(ATT, 2)
    pair[2].wait_recv()
    for some in HID:
        make_piece(*some)
    hid_pieces = send_pieces(HID, 4)
    pair[1].wait_recv()
    own, far = s["vec_own"][0:6], s["vec_in"][0:6]
    line[0:6, 0:LEN] = jnp.where(c == 0, own, far)
    line[6:12, 0:LEN] = jnp.where(c == 0, far, own)
    vec_pieces[z] = line[0:16, 0:LEN].astype(BF16)
    near = vec_pieces.at[z]
    vec_copies = net.send([(near, near, peer("z", step)) for step in (1, 2, 3)], span(1, LEN))

    VT, packed = s["VT"], s["packed"]

    def stage(ref, l, index):
        return ref.at[pl.ds(pl.multiple_of(index * 48, 16), 48), pl.ds((l // 2) * D, D)]

    def spread(l, route, cols):
        for i in range(4):
            line[12 * i : 12 * i + 12, cols] = pieces[i, l, :, cols].astype(F32)[0:12]
        rows = line[:, cols].astype(BF16)
        if route == "x":
            W[6 * c + l, y, x, :, cols] = rows
        elif route == "y":
            stage(s["gp"], l, z)[:, cols] = rows
        else:
            W[6 * c + l, z, x, :, cols] = rows

    def strips(some, units):
        copies = []
        for l, route, cols in some:
            if route == "x":
                near = W.at[6 * c + l, y, x, :, cols]
            elif route == "y":
                near = stage(s["gp"], l, z).at[:, cols]
            else:
                near = W.at[6 * c + l, z, x, :, cols]
            copies += [(near, near, peer(SECOND[route], step)) for step in (1, 2, 3)]
        return net.send(copies, span(3 * units, copies[0][0].shape[-1]))

    def order_strips(l, cols):
        size = cols.size
        for i in range(4):
            FP[48 * i : 48 * i + 48, 0:size] = stage(s["gp"], l, i)[:, cols].astype(F32)
        for i in range(4):
            for j in range(4):
                line[12 * j : 12 * j + 12, 0:size] = FP[48 * j + 12 * i : 48 * j + 12 * i + 12, 0:size]
            W[6 * c + l, y, i, :, cols] = line[:, 0:size].astype(BF16)

    def turn_rows(ref, place, cols):
        rows = ref[place, :, :, :, cols].reshape(D, cols.size)
        ref[place, :, :, :, cols] = dot(perm[...], rows).astype(BF16).reshape(4, 4, 48, cols.size)

    def region(ref, place, route, index, half, cols):
        part = pl.ds(0, 4) if half is None else pl.ds(2 * half, 2)
        if route == "x":
            return ref.at[place, part, index, :, cols]
        return ref.at[place, index, part, :, cols]

    def gather_start(some):
        copies = []
        for l, route, cols in some:
            near = region(W, 6 * c + l, route, HERE[route], None, cols)
            copies += [(near, near, peer(route, step)) for step in (1, 2, 3)]
        return some, net.send(copies, span(12 * len(some), some[0][2].size))

    def gather_share(state):
        some, group = state
        group.wait_recv()
        if any(turns(l, route) for l, route, _ in some):
            net.sent(group)
        copies = []
        for l, route, cols in some:
            if turns(l, route):
                turn_rows(W, 6 * c + l, cols)
            near = W.at[6 * c + l, :, :, :, cols]
            copies.append((near, near, sibling))
        return net.send(copies, span(16 * len(some), some[0][2].size))

    act, p = s["act"], s["p"]
    q, k, v, ctx = (act.at[i] for i in range(4))
    A, F, FP, inv1, y1b = s["A"], s["F"], s["FP"], s["inv1"], s["y1b"]
    h, gp, dfb, dfp, sums = s["h"], s["gp"], s["dfb"], y1b, s["sums"]
    turned = s["turned"]

    att_pieces.wait_recv()
    att_strips = []
    for group in (ATT[:1], ATT[1:2], ATT[2:]):
        for some in group:
            spread(*some)
        att_strips.append(strips(group, len(group)))
    hid_pieces.wait_recv()
    for some in HID:
        spread(*some)
    z_strips = [strips(PARTS[0][2:], 2)]
    x_strips = strips(HID[:1], 1)
    y_strips = strips(HID[1:2], 1)
    z_strips.append(strips([(5, "z", p1), (4, "z", p2)], 2))
    x_rest = strips([(4, "x", p1)], 1)
    y_rest = strips([(5, "y", p2)], 1)
    vec_copies.wait_recv()
    for i in range(4):
        line[12 * i : 12 * i + 12, 0:LEN] = vec_pieces[i].astype(F32)[0:12]
    VT[y, x] = line[:, 0:LEN].astype(BF16)
    near = VT.at[y, x]
    vec_strips = net.send([(near, near, peer("x", step)) for step in (1, 2, 3)], span(3, LEN))
    starts = {}
    att_strips[0].wait_recv()
    for part in range(2):
        starts["x", part] = gather_start([(0, "x", part_cols[part])])
    att_strips[1].wait_recv()
    order_strips(1, wide)
    for part in range(2):
        starts["y", part] = gather_start([(1, "y", part_cols[part])])
    att_strips[2].wait_recv()
    for l in range(2):
        starts["t", l] = gather_start(ATT[2 + l : 3 + l])
    vec_strips.wait_recv()
    near = packed.at[y]
    packed[y] = sum(
        pltpu.roll(VT[y, i].astype(F32), 32 * i, 1) if i else VT[y, i].astype(F32) for i in range(4)
    ).astype(BF16)
    vec_last = net.send([(near, near, peer("y", step)) for step in (1, 2, 3)], span(3, LEN))
    for copy in loads:
        copy.wait()
    flows = {}

    def begin(part, route):
        flows[part, route] = gather_start([some for some in PARTS[part] if some[1] == route])

    def sharing(part, routes="xyz"):
        for route in routes:
            flows[part, route] = gather_share(flows[part, route])

    z_strips[0].wait_recv()
    begin(0, "z")
    x_strips.wait_recv()
    begin(0, "x")
    y_strips.wait_recv()
    order_strips(3, every)
    begin(0, "y")
    z_strips[1].wait_recv()
    begin(1, "z")
    x_rest.wait_recv()
    begin(1, "x")
    begin(1, "y")
    y_rest.wait_recv()
    order_strips(5, p2)
    for route in "zxy":
        begin(2, route)
    net.sent(att_strips[2])
    shares = [gather_share(starts[key]) for key in (("x", 0), ("y", 0), ("t", 0))]
    vec_last.wait_recv()
    net.sent(vec_strips)
    for i in range(4):
        block_i = packed[i].astype(F32)
        for j in range(4):
            VT[i, j] = (pltpu.roll(block_i, LEN - 32 * j, 1) if j else block_i).astype(BF16)
    V[...] = VT[...].reshape(D, LEN).astype(F32).T[0:16]
    shares += [gather_share(starts[key]) for key in (("x", 1), ("y", 1), ("t", 1))]
    for copy in shares:
        copy.wait_recv()
    qkv(W, V, xb, q, k, v)
    attend(q, k, v, s["bias"], p, ctx)
    net.sent(x_rest)
    sharing(0)
    first_norm(W, V, xb, ctx, A, inv1, F, y1b)
    turn(y1b, turned.at[1])
    sharing(1)

    def arrived(part):
        for route in "xyz":
            flows[part, route].wait_recv()

    arrived(0)
    net.sent(att_strips[1])
    net.sent(y_strips)
    net.sent(y_rest)
    up(W, V, y1b, h, gp, 0)
    down_(W, h, FP, 0)
    sharing(2)
    arrived(1)
    up(W, V, y1b, h, gp, 1)
    down_(W, h, FP, 1)
    arrived(2)
    up(W, V, y1b, h, gp, 2)
    down_(W, h, FP, 2)
    second_norm(V, perm, FP, F, gb, gb, dfb, sums)
    stores = []
    for i in range(SLOTS):
        stores.append(pltpu.make_async_copy(gb.at[pl.ds(i * LEN, LEN)], out_hbm.at[i], s["store_sem"].at[i]))
        stores[-1].start()
    to_down_order(dfb, perm, dfp)
    dfpT = turned.at[0]
    y1T = turned.at[1]
    turn(dfp, dfpT)

    pair_in, pair_out = s["pair_in"], s["pair_out"]
    G_half = s["half_in"]
    G_block = pair_in
    slots = [None] * 8

    def send_tiles(tiles):
        for slot, _, _, _ in tiles:
            if slots[slot] is not None:
                net.sent(slots[slot])
        values = [value() for _, _, _, value in tiles]
        for (slot, _, _, _), value in zip(tiles, values):
            pair_out[slot] = value.astype(BF16).reshape(4, 4, 48, TILE)
        group = net.send(
            [(pair_out.at[slot], pair_in.at[l, :, :, :, cols], sibling) for slot, l, cols, _ in tiles],
            span(16 * len(tiles), TILE),
        )
        for slot, _, _, _ in tiles:
            slots[slot] = group
        return group

    def add_into(ref, index, *others):
        total = ref[index].astype(F32)
        for other_ref, other_index in others:
            total = total + other_ref[other_index].astype(F32)
        ref[index] = total.astype(BF16)

    def cell(l, route, index, i, cols):
        return (l, i, index, slice(None), cols) if route == "x" else (l, index, i, slice(None), cols)

    def reduce_start(some):
        copies = []
        for l, route, cols in some:
            across = wrap(HERE[route] + 2)
            for half, step in ((0, 1), (1, 3)):
                copies.append((region(G, l, route, across, half, cols), G_half.at[l, half, :, :, cols], peer(route, step)))
        return some, net.send(copies, span(4 * len(some), TILE))

    def reduce_pass(state):
        some, group = state
        group.wait_recv()
        copies = []
        for l, route, cols in some:
            here = HERE[route]
            for i in range(2):
                add_into(G, cell(l, route, wrap(here + 1), i, cols), (G_half, (l, 0, i, slice(None), cols)))
                add_into(G, cell(l, route, wrap(here - 1), 2 + i, cols), (G_half, (l, 1, i, slice(None), cols)))
            for half, step in ((0, 1), (1, 3)):
                copies.append(
                    (region(G, l, route, wrap(here + step), None, cols), G_block.at[l, half, :, :, cols], peer(route, step))
                )
        return some, net.send(copies, span(8 * len(some), TILE))

    strip_in = s["strip_in"]

    def strip_place(l, route, moved):
        return (l, moved, x) if route == "x" else (l, z, moved)

    def reduce_end(state):
        some, group = state
        group.wait_recv()
        copies = []
        for l, route, cols in some:
            for i in range(4):
                add_into(
                    G,
                    cell(l, route, HERE[route], i, cols),
                    (G_block, (l, 0, i, slice(None), cols)),
                    (G_block, (l, 1, i, slice(None), cols)),
                )
            if route == "y":
                for i in range(4):
                    FP[48 * i : 48 * i + 48, 0:TILE] = G[l, y, i, :, cols].astype(F32)
                for j in range(4):
                    for i in range(4):
                        line[12 * i : 12 * i + 12, 0:TILE] = FP[48 * i + 12 * j : 48 * i + 12 * j + 12, 0:TILE]
                    stage(h, l, j)[:, cols] = line[:, 0:TILE].astype(BF16)
            for step in (1, 2, 3):
                target = wrap(HERE[SECOND[route]] + step)
                if route == "y":
                    source = stage(h, l, target).at[:, cols]
                else:
                    source = G.at[strip_place(l, route, target) + (slice(None), cols)]
                copies.append((source, strip_in.at[l, step - 1, :, cols], peer(SECOND[route], step)))
        return some, net.send(copies, span(3 * len(some), TILE))

    piece_out, piece_in = pieces, s["piece_in"]

    def strips_sum(state):
        some, group = state
        group.wait_recv()
        for l, route, cols in some:
            if route == "y":
                own = stage(h, l, z)[:, cols]
            else:
                own = G[strip_place(l, route, HERE[SECOND[route]]) + (slice(None), cols)]
            total = own.astype(F32)
            for i in range(3):
                total = total + strip_in[l, i, :, cols].astype(F32)
            line[:, 0:TILE] = total
            gap = jnp.zeros((4, TILE), F32)
            for i in range(4):
                rows = jnp.concatenate([line[12 * i : 12 * i + 12, 0:TILE], gap], 0)
                piece_out[i, l, :, cols] = rows.astype(BF16)

    def pieces_out(some, units):
        copies = []
        for l, route, cols in some:
            for step in (1, 2, 3):
                source = piece_out.at[wrap(HERE[FIRST[route]] + step), l, :, cols]
                copies.append((source, piece_in.at[step - 1, l, :, cols], peer(FIRST[route], step)))
        return net.send(copies, span(units, D))

    rows_out, rows_own, rows_in = s["first_out"], s["first_own"], s["first_in"]

    def pieces_sum(l, route, cols):
        total = piece_out[HERE[FIRST[route]], l, :, cols].astype(F32)
        for i in range(3):
            total = total + piece_in[i, l, :, cols].astype(F32)
        line[0:16, cols] = total
        top, bottom = line[0:6, cols], line[6:12, cols]
        rows_own[l, 0:6, cols] = jnp.where(c == 0, top, bottom)
        rows_out[l, 0:6, cols] = jnp.where(c == 0, bottom, top)
        return jnp.sum(top * top + bottom * bottom, keepdims=True)

    def hidden_slopes(core, part):
        places = [pl.ds(pl.multiple_of((2 * core + e) * D + part * TILE, LEN), TILE) for e in range(2)]
        slopes = []
        for e in range(2):
            dh = dot(dfp[...], columns(W, 6 * core + 4 + e, part * TILE, TILE))
            du = (dh * gp[:, places[e]].astype(F32)).astype(BF16)
            slopes.append(du)
            sums[pl.ds(V_B1 + 2 * core + e, 1), part_cols[part]] = jnp.sum(du.astype(F32), 0, keepdims=True)
        return places, slopes

    def keep_tiles(group, tiles):
        group.wait_recv()
        for l, cols, value in tiles:
            total = value() + pair_in[l, :, :, :, cols].reshape(D, TILE).astype(F32)
            G[l, :, :, :, cols] = total.astype(BF16).reshape(4, 4, 48, TILE)

    def hidden_tiles(places, slopes, cols):
        tiles = [(4 + e, cols, lambda e=e: dot(dfpT[...], h[:, places[e]])) for e in range(2)]
        return tiles + [(2 + e, cols, lambda e=e: dot(y1T[...], slopes[e])) for e in range(2)]

    shared = {}

    def others(part):
        places, slopes = hidden_slopes(other, part)
        tiles = hidden_tiles(places, slopes, part_cols[part])
        shared[part] = send_tiles([(4 * (part % 2) + i,) + tile for i, tile in enumerate(tiles)])
        for e in range(2):
            gp[:, places[e]] = slopes[e]

    def own_slopes(part):
        places, slopes = hidden_slopes(c, part)
        for e in range(2):
            gp[:, places[e]] = slopes[e]

    def own_tiles(part):
        places = [pl.ds(pl.multiple_of((2 * c + e) * D + part * TILE, LEN), TILE) for e in range(2)]
        keep_tiles(shared[part], hidden_tiles(places, [gp[:, place] for place in places], part_cols[part]))
        for l, route, cols in PARTS[part]:
            if turns(l, route):
                turn_rows(G, l, cols)
        return reduce_start(PARTS[part])

    others(0)
    others(1)
    own_slopes(0)
    own_slopes(1)
    flows[0] = own_tiles(0)
    others(2)
    flows[1] = own_tiles(1)
    flows[0] = reduce_pass(flows[0])
    own_slopes(2)
    flows[2] = own_tiles(2)
    first_back_product(W, gp, F)
    flows[1] = reduce_pass(flows[1])
    first_back(V, A, inv1, F, dfb, sums)

    sums[VECTORS:16, :] = jnp.zeros((16 - VECTORS, D), F32)
    sums_in, sums_out = s["sums_in"], s["sums_out"]

    def sums_step(place, stage_, group, axis):
        if group is None:
            total = sums[8 * place : 8 * place + 8, :]
        else:
            total = sums_out[place, stage_ - 1]
            group.wait_recv()
            for i in range(1 if stage_ == 1 else 3):
                total = total + sums_in[place, 0 if stage_ == 1 else 3 * stage_ - 5 + i]
        if axis is None:
            return total
        sums_out[place, stage_] = total
        near = sums_out.at[place, stage_]
        if stage_ == 0:
            return net.send([(near, sums_in.at[place, 0], sibling)], near)
        base = 3 * stage_ - 3
        return net.send(
            [(near, sums_in.at[place, base + step], peer(axis, step)) for step in (1, 2, 3)],
            sums_in.at[place, pl.ds(0, 3)],
        )

    up_sums = sums_step(1, 0, None, "sibling")
    doT = turned.at[1]
    turn(dfb, doT)
    output_back(W, dfb, y1b)
    up_sums = sums_step(1, 1, up_sums, "z")
    turn(xb, turned.at[0])
    flows[2] = reduce_pass(flows[2])
    flows[0] = reduce_end(flows[0])

    def projection_grad(core, l, n):
        left = core if l == 1 else 0
        return dot(turned[left], act[2 * core + l, :, n * TILE : (n + 1) * TILE])

    def projection_tiles(core, n):
        return [(l, part_cols[n], lambda l=l: projection_grad(core, l, n)) for l in (0, 1)]

    last = []

    def other_projections(n):
        attend_back(q, k, v, p, y1b, n)
        tiles = projection_tiles(other, n)
        shared["p", n] = send_tiles([(2 * n + i,) + tile for i, tile in enumerate(tiles)])

    def own_projections(n):
        keep_tiles(shared["p", n], projection_tiles(c, n))
        if n == 2:
            for l in (0, 1):
                turn_rows(G, l, third)
        last.append(reduce_start([(l, "z" if n == 2 else "xy"[l], part_cols[n]) for l in (0, 1)]))

    other_projections(2)
    other_projections(0)
    own_projections(2)
    flows[1] = reduce_end(flows[1])
    up_sums = sums_step(1, 2, up_sums, "x")
    other_projections(1)
    column_sums(q, sums, V_BQ)
    column_sums(v, sums, V_BV)
    first_sums = sums_step(0, 0, None, "sibling")
    own_projections(0)
    own_projections(1)
    first_sums = sums_step(0, 1, first_sums, "z")
    flows[2] = reduce_end(flows[2])
    last[0] = reduce_pass(last[0])
    for group in pair + [att_pieces, hid_pieces]:
        net.sent(group)
    last[1] = reduce_pass(last[1])
    input_back(W, q, k, v, F, 0)
    last[2] = reduce_pass(last[2])
    input_back(W, q, k, v, F, 1)
    for i in range(SLOTS):
        stores.append(pltpu.make_async_copy(F.at[pl.ds(i * LEN, LEN)], grad_hbm.at[i], s["store_sem"].at[4 + i]))
        stores[-1].start()
    strips_sum(flows[0])
    strips_sum(flows[1])
    first_sums = sums_step(0, 2, first_sums, "x")
    up_sums = sums_step(1, 3, up_sums, "y")
    strips_sum(flows[2])
    hid_pieces = pieces_out(HID, 4)
    net.close()
    for n in range(3):
        last[n] = reduce_end(last[n])
    first_sums = sums_step(0, 3, first_sums, "y")
    hid_pieces.wait_recv()
    squares = jnp.zeros((1, 1), F32)
    for some in HID:
        squares = squares + pieces_sum(*some)
    rows_copies = [net.send([(rows_out.at[pl.ds(2, 4)], rows_in.at[pl.ds(2, 4)], sibling)], rows_out.at[pl.ds(2, 4)])]
    for n in range(3):
        strips_sum(last[n])
    att_pieces = pieces_out(ATT, 2)
    vec_total = jnp.concatenate([sums_step(0, 4, first_sums, None), sums_step(1, 4, up_sums, None)], 0)
    place = lax.broadcasted_iota(jnp.int32, (8, D), 1) - 6 * me
    pick = (place == lax.broadcasted_iota(jnp.int32, (8, D), 0)).astype(BF16)
    vec_grad = jnp.zeros((8, 16), F32)
    for _ in range(3):
        low = vec_total.astype(BF16)
        vec_grad = vec_grad + dot(pick, low, NT)
        vec_total = vec_total - low.astype(F32)
    vec_grad = vec_grad[0:6, 0:VECTORS]
    squares = squares + jnp.sum(vec_grad * vec_grad, keepdims=True)
    att_pieces.wait_recv()
    for some in ATT:
        squares = squares + pieces_sum(*some)
    norm_out, norm_in = s["norm_out"], s["norm_in"]
    norm_out[0] = jnp.broadcast_to(squares, (8, LEN))
    plane = [(norm_out.at[0], norm_in.at[0, i], device) for i, device in enumerate(plane_peers)]
    norm_group = net.send(plane, norm_in.at[0])
    rows_copies.append(
        net.send([(rows_out.at[pl.ds(0, 2)], rows_in.at[pl.ds(0, 2)], sibling)], rows_out.at[pl.ds(0, 2)])
    )
    for copy in rows_copies:
        copy.wait_recv()
    att_grad, hid_grad, vec_grad_at = att_w, hid_w, vec_w
    vec_grad_at[...] = vec_grad
    for core in range(2):
        for l in range(SHARE):
            value = jnp.where(c == core, rows_own[l, 0:6], rows_in[l, 0:6])
            if l < 2:
                att_grad[:, 2 * core + l, :] = value
            else:
                i, j = (l - 2) // 2, 2 * core + l % 2
                hid_grad[:, i, j * D : (j + 1) * D] = value
    for i, (source, target) in enumerate(((att_grad, att_out), (hid_grad, hid_out), (vec_grad_at, vec_out))):
        stores.append(pltpu.make_async_copy(source, target, s["store_sem"].at[8 + i]))
        stores[-1].start()

    def norm_step(index, group, count):
        group.wait_recv()
        total = norm_out[index]
        for i in range(count):
            total = total + norm_in[index, i]
        return total

    norm_out[1] = norm_step(0, norm_group, 15)
    copies = [(norm_out.at[1], norm_in.at[1, 0], sibling)]
    for step in (1, 2, 3):
        copies.append((norm_out.at[1], norm_in.at[1, step], peer("z", step)))
        copies.append((norm_out.at[1], norm_in.at[1, 3 + step], far_peer(step)))
    norm_group = net.send(copies, norm_in.at[1, pl.ds(0, 7)])
    norm = jnp.sqrt(norm_step(1, norm_group, 7))
    norm_out_ref[...] = norm[0:1, 0:1]
    for copy in stores:
        copy.wait()
    net.close()


def rates(values, shape):
    index = lax.broadcasted_iota(jnp.int32, shape, 1)
    rate = jnp.full(shape, values[0], F32)
    for i, value in enumerate(values[1:]):
        rate = jnp.where(index == i + 1, value, rate)
    return rate


def update_kernel(out_in, grad_in, norm_in, *refs):
    sources, (out_hbm, grad_hbm), targets = refs[:12], refs[12:14], refs[14:23]
    out_at, grad_at = refs[23:25]
    held, norm, sems = refs[25:37], refs[37], refs[38]
    norm_load = pltpu.make_async_copy(norm_in, norm, sems.at[37])
    norm_load.start()
    loads = [pltpu.make_async_copy(a, b, sems.at[i]) for i, (a, b) in enumerate(zip(sources, held))]
    passing = []
    stores = []
    for i in range(SLOTS):
        for j, (source, middle, target) in enumerate(((grad_in, grad_at, grad_hbm), (out_in, out_at, out_hbm))):
            n = 12 + 4 * i + 2 * j
            passing.append(pltpu.make_async_copy(source.at[i], middle.at[i], sems.at[n]))
            stores.append(pltpu.make_async_copy(middle.at[i], target.at[i], sems.at[n + 1]))
    for copy in loads + passing:
        copy.start()
    norm_load.wait()
    factor = CLIP_NORM / jnp.maximum(norm[...], CLIP_NORM)
    settings = (
        (rates(ATTENTION_RATES, (6, 4, D)), WEIGHT_DECAY),
        (rates(HIDDEN_RATES, (6, 2, FF)), WEIGHT_DECAY),
        (VECTOR_RATE, 0.0),
    )
    for i in (1, 0, 2):
        for j in (i, 3 + 3 * i, 4 + 3 * i, 5 + 3 * i):
            loads[j].wait()
        state = held[3 + 3 * i : 6 + 3 * i]
        new = adam(state[0][...], state[1][...], state[2][...], held[i][...] * factor, *settings[i])
        for j in range(3):
            state[j][...] = new[j]
            stores.append(pltpu.make_async_copy(state[j], targets[3 * i + j], sems.at[28 + 3 * i + j]))
        if i == 1:
            for load, copy in zip(passing, stores):
                load.wait()
                copy.start()
        for copy in stores[-3:]:
            copy.start()
    for copy in stores:
        copy.wait()


def on_device(
    inputs,
    cotangent,
    joined,
    half_lengths,
    attention_master,
    attention_first,
    attention_second,
    hidden_master,
    hidden_first,
    hidden_second,
    vector_master,
    vector_first,
    vector_second,
):
    any_space = pl.BlockSpec(memory_space=pl.ANY)
    vmem = pl.BlockSpec(memory_space=pltpu.VMEM)
    like = lambda a: jax.ShapeDtypeStruct(a.shape, a.dtype)
    swap = lambda a: jnp.transpose(a, (1, 0, 2))
    attention = [swap(a) for a in (attention_master, attention_first, attention_second)]
    hidden = [swap(a) for a in (hidden_master, hidden_first, hidden_second)]
    vectors = [a.T for a in (vector_master, vector_first, vector_second)]
    params = attention + hidden + vectors
    out_like = jax.ShapeDtypeStruct(inputs.shape, BF16)
    grad_like = jax.ShapeDtypeStruct(inputs.shape, F32)
    results = pl.pallas_call(
        step_kernel,
        out_shape=(
            out_like,
            grad_like,
            jax.ShapeDtypeStruct((1, 1), F32),
            like(attention[0]),
            like(hidden[0]),
            like(vectors[0]),
        ),
        in_specs=[any_space] * 8,
        out_specs=(any_space, any_space, vmem) + (any_space,) * 3,
        scratch_shapes=list(SCRATCH.values()),
        compiler_params=pltpu.CompilerParams(collective_id=0, has_side_effects=True, vmem_limit_bytes=64 << 20),
        cost_estimate=pl.CostEstimate(flops=22 * 10**9, bytes_accessed=6 * 10**6, transcendentals=4 * 10**6),
    )(
        inputs,
        cotangent,
        jnp.asarray(permutation(), BF16),
        joined.T,
        jnp.transpose(half_lengths, (1, 2, 0)),
        attention[0],
        hidden[0],
        vectors[0],
    )
    outs = pl.pallas_call(
        update_kernel,
        out_shape=(out_like, grad_like) + tuple(like(a) for a in params),
        in_specs=[any_space] * 15,
        out_specs=(any_space,) * 11,
        scratch_shapes=[
            pltpu.VMEM(inputs.shape, BF16),
            pltpu.VMEM(inputs.shape, F32),
            *[pltpu.VMEM(a.shape, F32) for a in (attention[0], hidden[0], vectors[0], *params)],
            pltpu.VMEM((1, 1), F32),
            pltpu.SemaphoreType.DMA((38,)),
        ],
        cost_estimate=pl.CostEstimate(flops=2 * 10**6, bytes_accessed=7 * 10**6, transcendentals=10**5),
    )(*results, *params)
    output, input_grad, *new = outs
    norm = results[2].reshape(())
    return (output, input_grad, norm, *[swap(a) for a in new[:6]], *[a.T for a in new[6:]])


def solution(mesh):
    shard = P(None, "dp", None)
    flat = P(None, "dp")
    return jax.shard_map(
        on_device,
        mesh=mesh,
        in_specs=(shard, shard, flat, shard, shard, shard, shard, shard, shard, shard, flat, flat, flat),
        out_specs=(shard, shard, P(), shard, shard, shard, shard, shard, shard, flat, flat, flat),
        check_vma=False,
    )
```
